32 devices in a mesh: dp: 16 (over z, y, core), seq: 2 (over x).
Axes of the slice: x: 2, y: 2, z: 4, core: 2. Of those that a mesh axis runs over, the one named last changes fastest.
Arguments:
- inputs: bfloat16 [16, 1024, 768], P('dp', 'seq'), may hold values from -6 to 6
- modality: int32 [16, 1024], P('dp'), may hold values from 0 to 2, never falling along the last dimension, each value on 1 to 512 neighbouring positions
- key_valid_mask: int32 [16, 1024], P('dp'), may hold values 0 or 1
- output_gradient: bfloat16 [16, 1024, 768], P('dp', 'seq'), may hold values from -6 to 6
- mats: float32 [768, 9216], P('dp'), may hold values from -2 to 2
- mats_momentum: float32 [768, 9216], P('dp')
- mats_average: float32 [768, 9216], P('dp'), may hold values from -2 to 2
- smalls: float32 [768, 15], P('dp'), may hold values from -2 to 2
- smalls_momentum: float32 [768, 15], P('dp')
- smalls_average: float32 [768, 15], P('dp'), may hold values from -2 to 2
Outputs:
- block_out: bfloat16 [16, 1024, 768], P('dp', 'seq')
- input_grad: bfloat16 [16, 1024, 768], P('dp', 'seq')
- mats_grad: float32 [768, 9216], P('dp')
- new_mats: float32 [768, 9216], P('dp')
- new_mats_momentum: float32 [768, 9216], P('dp')
- new_mats_average: float32 [768, 9216], P('dp')
- smalls_grad: float32 [768, 15], P('dp')
- out_bias_grad: float32 [768], P('dp')
- new_smalls: float32 [768, 15], P('dp')
- new_smalls_momentum: float32 [768, 15], P('dp')
- new_smalls_average: float32 [768, 15], P('dp')
The draws below stay inside these ranges and needn't reach their ends.
Inputs may be any that keep to these rules, and one draw needn't show every extreme that they name: Along a document's positions the modality never falls; each of the three fills 1 to 512 positions, one of them exactly that many.
All inputs are finite; a program needn't handle non-finite values. No bound on the sum of `key_valid_mask` on one device may be relied on, other than what follows from the above.
Results may differ from the reference program's by a relative error of at most 0.019.
Values may be sent and summed in bfloat16 or wider, within the bound.
No kernel may reach another device: no remote copies, remote signals or barrier semaphores. Data moves between devices by JAX's collectives and lax.ppermute only.
A program may use at most 192 MiB of HBM per device.

```python
import math
import jax
import jax.numpy as jnp
import numpy as np
from jax import lax

MODEL_WIDTH = 768
H = 12
HD = 64
FF = 3072
DOCUMENT_LENGTH = 1024
SMALL = 15
MATCOLS = 9216
DOCS = 16
TOKENS = 16384


def column_scales():
    column = jnp.arange(MATCOLS)
    base = jnp.float32(MODEL_WIDTH) ** (-0.5)
    scale = jnp.where(column < MODEL_WIDTH, 1.3 * base, base)
    scale = jnp.where((column >= 3 * MODEL_WIDTH) & (column < 4 * MODEL_WIDTH), (DOCUMENT_LENGTH / 16.0) ** 0.5 * base, scale)
    scale = jnp.where(column >= 4 * MODEL_WIDTH + FF, jnp.float32(FF) ** (-0.5), scale)
    return scale


def momentum_scales():
    column = jnp.arange(MATCOLS)
    scale = jnp.where(column < 3 * MODEL_WIDTH, 1.0, 0.2)
    scale = jnp.where(column >= 4 * MODEL_WIDTH, 0.3, scale)
    scale = jnp.where(column >= 4 * MODEL_WIDTH + FF, 0.6, scale)
    return scale * jnp.float32(TOKENS) ** 0.5


def matrix_draw(key):
    noise = jax.random.truncated_normal(key, -4.0, 4.0, (MODEL_WIDTH, MATCOLS), jnp.float32)
    return noise * column_scales()[None, :]


def small_draw(key):
    column = jnp.arange(SMALL)
    noise = jax.random.truncated_normal(key, -4.0, 4.0, (MODEL_WIDTH, SMALL), jnp.float32)
    spread = jnp.where(column >= 12, 0.5, 0.2)
    gains = jax.random.uniform(jax.random.fold_in(key, 5), (MODEL_WIDTH, SMALL), jnp.float32, 0.6, 1.4)
    is_gain = (column == 4) | (column == 6)
    return jnp.where(is_gain[None, :], gains, noise * spread[None, :])


def draw_mats(key, part):
    return matrix_draw(jax.random.fold_in(key, 11))


def draw_mats_average(key, part):
    return matrix_draw(jax.random.fold_in(key, 23))


def draw_mats_momentum(key, part):
    noise = jax.random.truncated_normal(jax.random.fold_in(key, 37), -4.0, 4.0, (MODEL_WIDTH, MATCOLS), jnp.float32)
    return noise * momentum_scales()[None, :]


def draw_smalls(key, part):
    return small_draw(jax.random.fold_in(key, 41))


def draw_smalls_average(key, part):
    return small_draw(jax.random.fold_in(key, 43))


def draw_smalls_momentum(key, part):
    noise = jax.random.truncated_normal(jax.random.fold_in(key, 47), -4.0, 4.0, (MODEL_WIDTH, SMALL), jnp.float32)
    return noise * jnp.float32(TOKENS) ** 0.5


def touch_ends(values, stream_key, low, high):
    shape = values.shape
    place = [jax.random.randint(jax.random.fold_in(stream_key, axis), (), 0, shape[axis]) for axis in range(len(shape))]
    values = values.at[tuple(place)].set(low)
    longest = shape.index(max(shape))
    place[longest] = (place[longest] + 1) % shape[longest]
    return values.at[tuple(place)].set(high)


def steps_of(own_key, shape, split, low, top_value):
    def one(position, shards_of):
        steps = jax.random.uniform(jax.random.fold_in(jax.random.fold_in(own_key, 6), position), (shards_of,), jnp.float32, low / len(split), top_value / len(split))
        return jnp.repeat(jnp.exp(steps), shape[position] // shards_of).reshape((-1,) + (1,) * (len(shape) - position - 1))

    level = one(*split[0])
    for cut in split[1:]:
        level = level * one(*cut)
    return level


def profile(count, total, reach, lean):
    portions = [(1 << 20) // math.isqrt(rank ** lean) + 1 for rank in range(2, count + 1)]
    spare, holding = total - reach - (count - 1), [1] * (count - 1)
    while spare > 0:
        candidates = [i for i in range(count - 1) if holding[i] < reach]
        whole, remaining = sum([portions[i] for i in candidates]), spare
        for i in candidates:
            addition = min(reach - holding[i], max(1, remaining * portions[i] // whole), spare)
            holding[i] = holding[i] + addition
            spare = spare - addition
    return np.array([reach] + holding)


def uneven(stream_key, amount, total, bound, skew):
    if amount == 2:
        one = jax.random.randint(stream_key, (), max(1, total - bound), min(bound, total - 1) + 1)
        return jnp.stack([one, total - one])
    lengths = jnp.asarray(profile(amount, total, bound, skew), jnp.int32)
    pairs = (amount - 1) // 2
    giver, receiver = lengths[1:1 + 2 * pairs:2], lengths[2:2 + 2 * pairs:2]
    margin = jnp.minimum(giver - 1, bound - receiver)
    shifted = jax.random.randint(jax.random.fold_in(stream_key, 1), (pairs,), 0, 1 << 20) % (margin + 1)
    lengths = lengths.at[1:1 + 2 * pairs:2].set(giver - shifted).at[2:2 + 2 * pairs:2].set(receiver + shifted)
    return lengths[jax.random.permutation(jax.random.fold_in(stream_key, 2), amount)]


def bell_draw(key, shape, width, reach, shards=(), kind=jnp.bfloat16):
    entries = width * jax.random.normal(key, shape, jnp.float32)
    if shards:
        entries = entries * steps_of(key, shape, shards, -0.22, 0.18)
    return jnp.clip(entries, -reach, reach).astype(kind)


def setup_inputs(seed: int = 0) -> dict:
    seeds = jax.random.split(jax.random.key(seed), 11)
    return {
        "inputs": bell_draw(seeds[0], (DOCS, DOCUMENT_LENGTH, MODEL_WIDTH), 1.0, 6.0, ((0, 16), (1, 2))),
        "modality": jax.vmap(lambda own: jnp.searchsorted(jnp.cumsum(uneven(own, 3, DOCUMENT_LENGTH, DOCUMENT_LENGTH // 2, 0)), jnp.arange(DOCUMENT_LENGTH), side="right"))(jax.random.split(seeds[1], DOCS)).reshape((DOCS, DOCUMENT_LENGTH)).astype(jnp.int32),
        "key_valid_mask": touch_ends((jax.random.randint(seeds[2], (DOCS, DOCUMENT_LENGTH), 0, 100) < 85).astype(jnp.int32), jax.random.fold_in(seeds[2], 1), 0, 1),
        "output_gradient": bell_draw(seeds[3], (DOCS, DOCUMENT_LENGTH, MODEL_WIDTH), 1.0, 6.0, ((0, 16), (1, 2))),
        "mats": draw_mats(jax.random.fold_in(seeds[10], 71), 0),
        "mats_momentum": draw_mats_momentum(jax.random.fold_in(seeds[10], 71), 0),
        "mats_average": draw_mats_average(jax.random.fold_in(seeds[10], 71), 0),
        "smalls": draw_smalls(jax.random.fold_in(seeds[10], 71), 0),
        "smalls_momentum": draw_smalls_momentum(jax.random.fold_in(seeds[10], 71), 0),
        "smalls_average": draw_smalls_average(jax.random.fold_in(seeds[10], 71), 0),
    }


epsilon = 1e-06
momentum_rate = 0.9
decay_rate = 0.0001
average_rate = 0.75
base_rate = 0.03
masked_score = -1e+30

@jax.custom_vjp
def low(v):
    return lax.optimization_barrier(v.astype(jnp.bfloat16)).astype(jnp.float32)

@jax.custom_vjp
def low_back(v):
    return v

def low_keep(v):
    return (low(v), None)

def low_pass(kept, grad):
    return (grad,)

def back_keep(v):
    return (v, None)

def back_low(kept, grad):
    return (low(grad),)
low.defvjp(low_keep, low_pass)
low_back.defvjp(back_keep, back_low)

def product(left, right):
    return jnp.dot(left, right, precision=lax.Precision.HIGHEST, preferred_element_type=jnp.float32)

def product_nt(left, right):
    return lax.dot_general(left, right, (((1,), (1,)), ((), ())), precision=lax.Precision.HIGHEST, preferred_element_type=jnp.float32)

def normalize(rows, gain, shift):
    mean = lax.optimization_barrier(jnp.mean(rows, axis=-1, keepdims=True))
    centred = rows - mean
    spread = lax.optimization_barrier(jnp.mean(centred * centred, axis=-1, keepdims=True))
    return centred * lax.rsqrt(spread + epsilon) * gain + shift

def attend_doc(query_doc, keys_doc, values_doc, live_doc):
    length = query_doc.shape[0]
    query_heads = query_doc.reshape(length, H, HD)
    key_heads = keys_doc.reshape(length, H, HD)
    value_heads = values_doc.reshape(length, H, HD)
    scores = jnp.einsum('qhe,khe->hqk', query_heads, key_heads, precision=lax.Precision.HIGHEST) * 0.125
    scores = low_back(jnp.where(live_doc[None, None, :] > 0, scores, masked_score))
    top = lax.optimization_barrier(jnp.max(scores, axis=-1, keepdims=True))
    expd = jnp.exp(scores - top)
    prob = expd / lax.optimization_barrier(jnp.sum(expd, axis=-1, keepdims=True))
    attention_output = jnp.einsum('hqk,khe->qhe', low(prob), value_heads, precision=lax.Precision.HIGHEST)
    return attention_output.reshape(length, H * HD)

def forward_group(mats, smalls, inputs_group, modality_group, live_group):
    document_group = inputs_group.shape[0]
    rows = document_group * DOCUMENT_LENGTH
    weights = low(mats)
    params = low(smalls)
    w_query = weights[:, 0:MODEL_WIDTH]
    w_key = weights[:, MODEL_WIDTH:2 * MODEL_WIDTH]
    w_value = weights[:, 2 * MODEL_WIDTH:3 * MODEL_WIDTH]
    w_out = weights[:, 3 * MODEL_WIDTH:4 * MODEL_WIDTH]
    w_up = weights[:, 4 * MODEL_WIDTH:4 * MODEL_WIDTH + FF]
    w_down = weights[:, 4 * MODEL_WIDTH + FF:]
    bias_up = jnp.transpose(params[:, 8:12]).reshape(FF)
    embed = jnp.transpose(params[:, 12:15])
    onehot = (modality_group[..., None] == jnp.arange(3, dtype=jnp.int32)).astype(inputs_group.dtype)
    x_in = inputs_group.reshape(rows, MODEL_WIDTH) + product(onehot.reshape(rows, 3), embed)
    x_low = low(x_in)
    query = low(low_back(product(x_low, w_query) + params[:, 0]))
    keys = low(low_back(product(x_low, w_key)))
    values = low(low_back(product(x_low, w_value) + params[:, 1]))
    checked = jax.checkpoint(attend_doc)

    def attend_item(item):
        return checked(item[0], item[1], item[2], item[3])
    attention_output = lax.map(attend_item, (query.reshape(document_group, DOCUMENT_LENGTH, MODEL_WIDTH), keys.reshape(document_group, DOCUMENT_LENGTH, MODEL_WIDTH), values.reshape(document_group, DOCUMENT_LENGTH, MODEL_WIDTH), live_group))
    out_low = low(low_back(attention_output.reshape(rows, MODEL_WIDTH)))
    mixed = low_back(product(out_low, w_out) + params[:, 2])
    first = normalize(x_in + mixed, params[:, 4], params[:, 5])
    up = low_back(product(low(first), w_up) + bias_up)
    act = low(jax.nn.gelu(up, approximate=False))
    ffo = low_back(product_nt(act, w_down) + params[:, 3])
    result = normalize(first + ffo, params[:, 6], params[:, 7])
    return result.reshape(document_group, DOCUMENT_LENGTH, MODEL_WIDTH)

def reference(inputs, modality, key_valid_mask, output_gradient, mats, mats_momentum, mats_average, smalls, smalls_momentum, smalls_average):
    document_group = math.gcd(DOCS, max(1, 4096 // DOCUMENT_LENGTH))
    element_count = DOCS // document_group
    leading_key = (jnp.arange(DOCUMENT_LENGTH) == 0).astype(jnp.int32)
    valid_positions = jnp.maximum(key_valid_mask, leading_key[None, :])

    def one_group(totals, item):
        inputs_group, modality_group, live_group, cot_group = item

        def forward(mats_in, smalls_in, inputs_in):
            return forward_group(mats_in, smalls_in, inputs_in, modality_group, live_group)
        result, pull = jax.vjp(forward, mats, smalls, inputs_group.astype(jnp.float32))
        grad_mats, grad_smalls, grad_inputs = pull(cot_group.astype(jnp.float32))
        return ((totals[0] + grad_mats, totals[1] + grad_smalls), (result.astype(jnp.bfloat16), grad_inputs.astype(jnp.bfloat16)))
    entry_list = (inputs.reshape(element_count, document_group, DOCUMENT_LENGTH, MODEL_WIDTH), modality.reshape(element_count, document_group, DOCUMENT_LENGTH), valid_positions.reshape(element_count, document_group, DOCUMENT_LENGTH), output_gradient.reshape(element_count, document_group, DOCUMENT_LENGTH, MODEL_WIDTH))
    totals, outputs = lax.scan(one_group, (jnp.zeros_like(mats), jnp.zeros_like(smalls)), entry_list)
    mats_grad, smalls_grad = totals
    block_out = outputs[0].reshape(DOCS, DOCUMENT_LENGTH, MODEL_WIDTH)
    input_grad = outputs[1].reshape(DOCS, DOCUMENT_LENGTH, MODEL_WIDTH)
    out_bias_grad = smalls_grad[:, 2]
    rate = base_rate / math.sqrt(DOCS * DOCUMENT_LENGTH)
    decayed = mats_grad + decay_rate * mats
    new_mats_momentum = momentum_rate * mats_momentum + decayed
    new_mats = mats - rate * (decayed + momentum_rate * new_mats_momentum)
    new_mats_average = average_rate * mats_average + (1.0 - average_rate) * new_mats
    new_smalls_momentum = momentum_rate * smalls_momentum + smalls_grad
    new_smalls = smalls - rate * (smalls_grad + momentum_rate * new_smalls_momentum)
    new_smalls_average = average_rate * smalls_average + (1.0 - average_rate) * new_smalls
    return (block_out, input_grad, mats_grad, new_mats, new_mats_momentum, new_mats_average, smalls_grad, out_bias_grad, new_smalls, new_smalls_momentum, new_smalls_average)
```

```python
import functools
import math

import jax
import jax.numpy as jnp
from jax import lax
from jax.experimental import pallas as pl
from jax.experimental.pallas import tpu as pltpu
from jax.sharding import PartitionSpec as P

MODEL_WIDTH = 768
H = 12
HD = 64
FF = 3072


epsilon = 1e-06
momentum_rate = 0.9
decay_rate = 0.0001
average_rate = 0.75
base_rate = 0.03
masked_score = -1e30


def product(left, right):
    return jnp.dot(left, right, preferred_element_type=jnp.float32)


def product_tn(left, right):
    return lax.dot_general(
        left, right, (((0,), (0,)), ((), ())), preferred_element_type=jnp.float32
    )


def product_nt(left, right):
    return lax.dot_general(
        left, right, (((1,), (1,)), ((), ())), preferred_element_type=jnp.float32
    )


def normalize(rows, gain, shift):
    mean = jnp.mean(rows, axis=-1, keepdims=True)
    centred = rows - mean
    spread = jnp.mean(centred * centred, axis=-1, keepdims=True)
    return centred * lax.rsqrt(spread + epsilon) * gain + shift


def exact_gelu(values):
    return jax.nn.gelu(values, approximate=False)


def head_scores(query_heads, key_heads, live_doc):
    scores = (
        jnp.einsum("qhe,khe->hqk", query_heads, key_heads, preferred_element_type=jnp.float32)
        * 0.125
    )
    return jnp.where(live_doc[None, None, :] > 0, scores, masked_score)


def attention_forward_pass(item):
    query_doc, keys_doc, values_doc, live_doc = item
    query_heads = query_doc.reshape(query_doc.shape[0], H, HD)
    key_heads = keys_doc.reshape(keys_doc.shape[0], H, HD)
    value_heads = values_doc.reshape(values_doc.shape[0], H, HD)
    scores = head_scores(query_heads, key_heads, live_doc)
    top = jnp.max(scores, axis=-1, keepdims=True)
    expd = jnp.exp(scores - top)
    total = jnp.sum(expd, axis=-1, keepdims=True)
    prob = (expd / total).astype(jnp.bfloat16)
    attention_output = jnp.einsum(
        "hqk,khe->qhe", prob, value_heads, preferred_element_type=jnp.float32
    )
    return (attention_output.reshape(query_doc.shape[0], H * HD), (top + jnp.log(total))[..., 0])


def attention_backward_pass(item):
    query_doc, keys_doc, values_doc, live_doc, log_sum_normalizer, grad_doc = item
    element_count = query_doc.shape[0]
    length = keys_doc.shape[0]
    query_heads = query_doc.reshape(element_count, H, HD)
    key_heads = keys_doc.reshape(length, H, HD)
    value_heads = values_doc.reshape(length, H, HD)
    grad_heads = grad_doc.reshape(element_count, H, HD)
    scores = head_scores(query_heads, key_heads, live_doc)
    prob = jnp.exp(scores - log_sum_normalizer[..., None])
    grad_prob = jnp.einsum(
        "qhe,khe->hqk", grad_heads, value_heads, preferred_element_type=jnp.float32
    )
    grad_values = jnp.einsum(
        "hqk,qhe->khe", prob.astype(jnp.bfloat16), grad_heads, preferred_element_type=jnp.float32
    )
    inner = jnp.sum(prob * grad_prob, axis=-1, keepdims=True)
    grad_scores = (prob * (grad_prob - inner)).astype(jnp.bfloat16)
    grad_query = (
        jnp.einsum("hqk,khe->qhe", grad_scores, key_heads, preferred_element_type=jnp.float32)
        * 0.125
    )
    grad_keys = (
        jnp.einsum("hqk,qhe->khe", grad_scores, query_heads, preferred_element_type=jnp.float32)
        * 0.125
    )
    return (
        grad_query.reshape(element_count, H * HD),
        grad_keys.reshape(length, H * HD),
        grad_values.reshape(length, H * HD),
    )


def per_device(
    inputs,
    modality,
    key_valid_mask,
    output_gradient,
    mats,
    mats_momentum,
    mats_average,
    smalls,
    smalls_momentum,
    smalls_average,
):
    docs, local_len, width = inputs.shape
    seq_len = modality.shape[1]
    rows = docs * local_len
    low_mats = mats.astype(jnp.bfloat16)
    w_qkv, w_out, w_up, w_down, whole_smalls = (
        lax.all_gather(low_mats[:, 0 : 3 * MODEL_WIDTH], "dp", axis=0, tiled=True),
        lax.all_gather(low_mats[:, 3 * MODEL_WIDTH : 4 * MODEL_WIDTH], "dp", axis=0, tiled=True),
        lax.all_gather(
            low_mats[:, 4 * MODEL_WIDTH : 4 * MODEL_WIDTH + FF], "dp", axis=0, tiled=True
        ),
        lax.all_gather(low_mats[:, 4 * MODEL_WIDTH + FF :], "dp", axis=0, tiled=True),
        lax.all_gather(smalls.astype(jnp.bfloat16), "dp", axis=0, tiled=True),
    )
    params = whole_smalls.astype(jnp.float32)
    bias_qkv = jnp.concatenate([params[:, 0], jnp.zeros_like(params[:, 0]), params[:, 1]])
    bias_up = jnp.transpose(params[:, 8:12]).reshape(FF)
    embed = jnp.transpose(whole_smalls[:, 12:15])
    leading_key = (jnp.arange(seq_len) == 0).astype(jnp.int32)
    valid_positions = jnp.maximum(key_valid_mask, leading_key[None, :])
    local_start = lax.axis_index("seq") * local_len
    local_modality = lax.dynamic_slice_in_dim(modality, local_start, local_len, 1)
    onehot = (
        local_modality.reshape(rows)[:, None] == jnp.arange(3, dtype=jnp.int32)[None, :]
    ).astype(jnp.bfloat16)
    x_in = inputs.reshape(rows, width).astype(jnp.float32) + product(onehot, embed)
    x_low = x_in.astype(jnp.bfloat16)
    qkv = (product(x_low, w_qkv) + bias_qkv).astype(jnp.bfloat16)
    query_documents = qkv[:, 0:width].reshape(docs, local_len, width)
    keys_local = qkv[:, width : 2 * width].reshape(docs, local_len, width)
    values_local = qkv[:, 2 * width :].reshape(docs, local_len, width)
    every_key, every_value = (
        lax.all_gather(keys_local, "seq", axis=1, tiled=True),
        lax.all_gather(values_local, "seq", axis=1, tiled=True),
    )
    attention_output, log_sum_normalizer = lax.map(
        attention_forward_pass, (query_documents, every_key, every_value, valid_positions)
    )
    out_low = attention_output.reshape(rows, width).astype(jnp.bfloat16)
    mixed = product(out_low, w_out) + params[:, 2]
    first_in = x_in + mixed
    first = normalize(first_in, params[:, 4], params[:, 5])
    first_low = first.astype(jnp.bfloat16)
    up = product(first_low, w_up) + bias_up
    act_low = exact_gelu(up).astype(jnp.bfloat16)
    ffo = product_nt(act_low, w_down) + params[:, 3]
    second_in = first + ffo
    result = normalize(second_in, params[:, 6], params[:, 7])
    block_out = result.astype(jnp.bfloat16).reshape(docs, local_len, width)
    w_qkv, w_out, w_up, w_down = (
        lax.all_gather(low_mats[:, 0 : 3 * MODEL_WIDTH], "dp", axis=0, tiled=True),
        lax.all_gather(low_mats[:, 3 * MODEL_WIDTH : 4 * MODEL_WIDTH], "dp", axis=0, tiled=True),
        lax.all_gather(
            low_mats[:, 4 * MODEL_WIDTH : 4 * MODEL_WIDTH + FF], "dp", axis=0, tiled=True
        ),
        lax.all_gather(low_mats[:, 4 * MODEL_WIDTH + FF :], "dp", axis=0, tiled=True),
    )
    grad_rows = output_gradient.reshape(rows, width).astype(jnp.float32)
    second_out, second_pull = jax.vjp(normalize, second_in, params[:, 6], params[:, 7])
    grad_second, grad_gain2, grad_shift2 = second_pull(grad_rows)
    grad_ffo = grad_second.astype(jnp.bfloat16)
    grad_bias_down = jnp.sum(grad_ffo.astype(jnp.float32), axis=0)
    grad_w_down = product_tn(grad_ffo, act_low)
    grad_act = product(grad_ffo, w_down)
    gelu_out, gelu_pull = jax.vjp(exact_gelu, up)
    grad_up = gelu_pull(grad_act)[0].astype(jnp.bfloat16)
    grad_bias_up = jnp.sum(grad_up.astype(jnp.float32), axis=0)
    grad_w_up = product_tn(first_low, grad_up)
    grad_first = grad_second + product_nt(grad_up, w_up)
    first_out, first_pull = jax.vjp(normalize, first_in, params[:, 4], params[:, 5])
    grad_first_in, grad_gain1, grad_shift1 = first_pull(grad_first)
    grad_mixed = grad_first_in.astype(jnp.bfloat16)
    grad_bias_out = jnp.sum(grad_mixed.astype(jnp.float32), axis=0)
    grad_w_out = product_tn(out_low, grad_mixed)
    grad_out = product_nt(grad_mixed, w_out).astype(jnp.bfloat16)
    output_gradient_documents = grad_out.reshape(docs, local_len, width)
    grad_query, grad_keys_all, grad_values_all = lax.map(
        attention_backward_pass,
        (
            query_documents,
            every_key,
            every_value,
            valid_positions,
            log_sum_normalizer,
            output_gradient_documents,
        ),
    )
    grad_keys, grad_values = (
        lax.psum_scatter(
            grad_keys_all.astype(jnp.bfloat16), "seq", scatter_dimension=1, tiled=True
        ).astype(jnp.float32),
        lax.psum_scatter(
            grad_values_all.astype(jnp.bfloat16), "seq", scatter_dimension=1, tiled=True
        ).astype(jnp.float32),
    )
    grad_qkv = jnp.concatenate(
        [
            grad_query.reshape(rows, width).astype(jnp.bfloat16),
            grad_keys.reshape(rows, width).astype(jnp.bfloat16),
            grad_values.reshape(rows, width).astype(jnp.bfloat16),
        ],
        axis=1,
    )
    grad_bias_qkv = jnp.sum(grad_qkv.astype(jnp.float32), axis=0)
    grad_w_qkv = product_tn(x_low, grad_qkv)
    grad_x_in = grad_first_in + product_nt(grad_qkv, w_qkv)
    grad_embed = lax.dot_general(
        onehot.astype(jnp.float32),
        grad_x_in,
        (((0,), (0,)), ((), ())),
        precision=lax.Precision.HIGHEST,
        preferred_element_type=jnp.float32,
    )
    input_grad = grad_x_in.astype(jnp.bfloat16).reshape(docs, local_len, width)
    grad_columns = jnp.stack(
        [
            grad_bias_qkv[0:width],
            grad_bias_qkv[2 * width :],
            grad_bias_out,
            grad_bias_down,
            grad_gain1,
            grad_shift1,
            grad_gain2,
            grad_shift2,
        ],
        axis=1,
    )
    grad_smalls = jnp.concatenate(
        [
            grad_columns,
            jnp.transpose(grad_bias_up.reshape(FF // width, width)),
            jnp.transpose(grad_embed),
        ],
        axis=1,
    )
    qkv_shard, out_shard, up_shard, down_shard, small_shard = (
        lax.psum_scatter(
            grad_w_qkv.astype(jnp.bfloat16), "dp", scatter_dimension=0, tiled=True
        ).astype(jnp.float32),
        lax.psum_scatter(
            grad_w_out.astype(jnp.bfloat16), "dp", scatter_dimension=0, tiled=True
        ).astype(jnp.float32),
        lax.psum_scatter(
            grad_w_up.astype(jnp.bfloat16), "dp", scatter_dimension=0, tiled=True
        ).astype(jnp.float32),
        lax.psum_scatter(
            grad_w_down.astype(jnp.bfloat16), "dp", scatter_dimension=0, tiled=True
        ).astype(jnp.float32),
        lax.psum_scatter(
            grad_smalls.astype(jnp.bfloat16), "dp", scatter_dimension=0, tiled=True
        ).astype(jnp.float32),
    )
    mats_shard = jnp.concatenate([qkv_shard, out_shard, up_shard, down_shard], axis=1)
    mats_grad, smalls_grad = (
        lax.psum(mats_shard.astype(jnp.bfloat16), "seq").astype(jnp.float32),
        lax.psum(small_shard.astype(jnp.bfloat16), "seq").astype(jnp.float32),
    )
    out_bias_grad = smalls_grad[:, 2]
    total_tokens = rows * lax.axis_size("dp") * lax.axis_size("seq")
    rate = base_rate / math.sqrt(total_tokens)
    decayed = mats_grad + decay_rate * mats
    new_mats_momentum = momentum_rate * mats_momentum + decayed
    new_mats = mats - rate * (decayed + momentum_rate * new_mats_momentum)
    new_mats_average = average_rate * mats_average + (1.0 - average_rate) * new_mats
    new_smalls_momentum = momentum_rate * smalls_momentum + smalls_grad
    new_smalls = smalls - rate * (smalls_grad + momentum_rate * new_smalls_momentum)
    new_smalls_average = average_rate * smalls_average + (1.0 - average_rate) * new_smalls
    return (
        block_out,
        input_grad,
        mats_grad,
        new_mats,
        new_mats_momentum,
        new_mats_average,
        smalls_grad,
        out_bias_grad,
        new_smalls,
        new_smalls_momentum,
        new_smalls_average,
    )


LN2 = math.log(2.0)
NT = (((1,), (1,)), ((), ()))
NN = (((1,), (0,)), ((), ()))


def mxu(left, right, dims):
    return lax.dot_general(left, right, dims, preferred_element_type=jnp.float32)


def three_parts(value):
    high = value.astype(jnp.bfloat16)
    rest = value - high.astype(jnp.float32)
    middle = rest.astype(jnp.bfloat16)
    return high, middle, (rest - middle.astype(jnp.float32)).astype(jnp.bfloat16)


def attend_kernel(q_ref, k_ref, v_ref, masked_ref, out_ref, log_ref, *, block):
    length = k_ref.shape[0]
    lane = lax.broadcasted_iota(jnp.int32, (1, 128), 1)
    keys = jnp.concatenate([k_ref[...], masked_ref[...]], axis=1)
    values = jnp.concatenate([v_ref[...], jnp.ones((length, 128), jnp.bfloat16)], axis=1)
    one = jnp.broadcast_to(jnp.where(lane == 0, 1.0, 0.0).astype(jnp.bfloat16), (block, 128))
    for i in range(q_ref.shape[0] // block):
        span = slice(i * block, (i + 1) * block)
        query = q_ref[span, :]
        outs, logs = [], []
        for head in range(2):
            here = (lane < 64) if head == 0 else (lane >= 64)
            only = jnp.where(here, query, jnp.zeros_like(query))
            scores = mxu(jnp.concatenate([only, one], axis=1), keys, NT)
            top = jnp.max(scores, axis=1, keepdims=True)
            weight = jnp.exp2(scores - top).astype(jnp.bfloat16)
            mixed = mxu(weight, values, NN)
            total = mixed[:, 128:]
            outs.append(mixed[:, :128] / total)
            logs.append(top + jnp.log2(total[:, 0:1]))
        out_ref[span, :] = jnp.where(lane < 64, outs[0], outs[1]).astype(jnp.bfloat16)
        log_ref[span, :] = jnp.where(lane == 0, logs[0], jnp.where(lane == 1, logs[1], 0.0))


def attend(qkv, masked, block=256):
    length, columns = qkv.shape
    pairs = columns // 3 // 128

    def spec(first):
        return pl.BlockSpec((length, 128), lambda i: (0, first + i))

    return pl.pallas_call(
        functools.partial(attend_kernel, block=block),
        grid=(pairs,),
        in_specs=[
            spec(0),
            spec(pairs),
            spec(2 * pairs),
            pl.BlockSpec((length, 128), lambda i: (0, 0)),
        ],
        out_specs=[spec(0), spec(0)],
        out_shape=[
            jax.ShapeDtypeStruct((length, pairs * 128), jnp.bfloat16),
            jax.ShapeDtypeStruct((length, pairs * 128), jnp.float32),
        ],
        compiler_params=pltpu.CompilerParams(vmem_limit_bytes=24 * 2**20),
        cost_estimate=pl.CostEstimate(
            flops=length * length * pairs * 2 * 128 * 8,
            bytes_accessed=length * columns * 4,
            transcendentals=length * length * pairs * 2,
        ),
        name="attend",
    )(qkv, qkv, qkv, masked)


def attend_back_kernel(
    q_ref, k_ref, v_ref, o_ref, g_ref, log_ref, masked_ref, dq_ref, dk_ref, dv_ref, dk_sum, dv_sum, *, block
):
    length = k_ref.shape[0]
    bf16 = jnp.bfloat16
    lane = lax.broadcasted_iota(jnp.int32, (1, 128), 1)
    ones = jnp.where((lane >= 1) & (lane <= 3), 1.0, 0.0).astype(bf16)
    masked = masked_ref[...]
    keys = jnp.concatenate(
        [k_ref[...], jnp.where(lane == 0, masked, jnp.broadcast_to(ones, masked.shape))], axis=1
    )
    three = jnp.broadcast_to(jnp.where(lane <= 2, 1.0, 0.0).astype(bf16), (length, 128))
    values = jnp.concatenate([v_ref[...], three], axis=1)
    keys_t = k_ref[...].T
    one = jnp.ones((block, 128), bf16)
    zero = jnp.zeros((block, 128), bf16)
    row = lax.broadcasted_iota(jnp.int32, (128, 1), 0)
    for i in range(q_ref.shape[0] // block):
        span = slice(i * block, (i + 1) * block)
        query, grad = q_ref[span, :], g_ref[span, :]
        both = grad.astype(jnp.float32) * o_ref[span, :].astype(jnp.float32)
        logs = log_ref[span, :]
        turned = []
        for head in range(2):
            here = (lane < 64) if head == 0 else (lane >= 64)
            inner = jnp.sum(jnp.where(here, both, 0.0), axis=1, keepdims=True)
            wide = lambda t: jnp.broadcast_to(t, (block, 128))
            i0, i1, i2 = (wide(t) for t in three_parts(-inner))
            l0, l1, l2 = (wide(t) for t in three_parts(-logs[:, head : head + 1]))
            query_h = jnp.where(here, query, zero)
            grad_h = jnp.where(here, grad, zero)
            tail_q = jnp.where(
                lane == 0,
                one,
                jnp.where(lane == 1, l0, jnp.where(lane == 2, l1, jnp.where(lane == 3, l2, zero))),
            )
            tail_g = jnp.where(lane == 0, i0, jnp.where(lane == 1, i1, jnp.where(lane == 2, i2, zero)))
            prob = jnp.exp2(mxu(keys, jnp.concatenate([query_h, tail_q], axis=1), NT))
            slope = mxu(values, jnp.concatenate([grad_h, tail_g], axis=1), NT)
            grad_scores = (prob * slope).astype(bf16)
            add_v = mxu(prob.astype(bf16), grad_h, NN)
            add_k = mxu(grad_scores, query_h, NN)
            if i == 0 and head == 0:
                dv_sum[...] = add_v
                dk_sum[...] = add_k
            else:
                dv_sum[...] += add_v
                dk_sum[...] += add_k
            turned.append(mxu(keys_t, grad_scores, NN))
        dq_ref[span, :] = (jnp.where(row < 64, turned[0], turned[1]) * 0.125).T.astype(bf16)
    dk_ref[...] = (dk_sum[...] * LN2).astype(bf16)
    dv_ref[...] = dv_sum[...].astype(bf16)


def attend_back(qkv, out, grad, log_sum, masked, block=512):
    length, columns = qkv.shape
    pairs = columns // 3 // 128

    def spec(first):
        return pl.BlockSpec((length, 128), lambda i: (0, first + i))

    return pl.pallas_call(
        functools.partial(attend_back_kernel, block=block),
        grid=(pairs,),
        in_specs=[
            spec(0),
            spec(pairs),
            spec(2 * pairs),
            spec(0),
            spec(0),
            spec(0),
            pl.BlockSpec((length, 128), lambda i: (0, 0)),
        ],
        out_specs=[spec(0)] * 3,
        out_shape=[jax.ShapeDtypeStruct((length, pairs * 128), jnp.bfloat16)] * 3,
        scratch_shapes=[pltpu.VMEM((length, 128), jnp.float32)] * 2,
        compiler_params=pltpu.CompilerParams(vmem_limit_bytes=32 * 2**20),
        cost_estimate=pl.CostEstimate(
            flops=length * length * pairs * 2 * 128 * 20,
            bytes_accessed=length * columns * 8,
            transcendentals=length * length * pairs * 2,
        ),
        name="attend_back",
    )(qkv, qkv, qkv, out, grad, log_sum, masked)


SEQ_SWAP = [(0, 1), (1, 0)]
CORE_SWAP = [(i, i ^ 1) for i in range(16)]
Y_SWAP = [(i, i ^ 2) for i in range(16)]
Z_LINES = [[r + 4 * z for z in range(4)] for r in range(4)]
HALF = MODEL_WIDTH // 2
FHALF = FF // 2
QCOLS = 5 * 128
BF16 = jnp.bfloat16
F32 = jnp.float32


def over_seq(value):
    return lax.ppermute(value, "seq", SEQ_SWAP)


def over_core(value):
    return lax.ppermute(value, "dp", CORE_SWAP)


def over_y(value):
    return lax.ppermute(value, "dp", Y_SWAP)


def over_z(blocks):
    return lax.all_to_all(blocks, "dp", 0, 0, axis_index_groups=Z_LINES)


def ordered(flag, mine, theirs, axis):
    return jnp.where(
        flag == 0,
        jnp.concatenate([mine, theirs], axis=axis),
        jnp.concatenate([theirs, mine], axis=axis),
    )


def part(value, index, size, axis):
    return lax.dynamic_slice_in_dim(value, index * size, size, axis)


def gelu_and_slope(up):
    size = jnp.abs(up)
    t = 1.0 / (1.0 + (0.3275911 * math.sqrt(0.5)) * size)
    bell = jnp.exp(-0.5 * up * up)
    poly = t * (
        0.5 * 0.254829592
        + t
        * (
            0.5 * -0.284496736
            + t * (0.5 * 1.421413741 + t * (0.5 * -1.453152027 + t * (0.5 * 1.061405429)))
        )
    )
    tail = poly * bell
    below = jnp.where(up < 0, tail, 1.0 - tail)
    return up * below, below + up * bell * (1.0 / math.sqrt(2.0 * math.pi))


def norm_parts(rows):
    mean = jnp.mean(rows, axis=-1, keepdims=True)
    centred = rows - mean
    spread = jnp.mean(centred * centred, axis=-1, keepdims=True)
    scale = lax.rsqrt(spread + epsilon)
    return centred * scale, scale


def norm_back(grad, unit, scale, gain):
    grad_gain = jnp.sum(unit * grad, axis=0)
    grad_shift = jnp.sum(grad, axis=0)
    inner = grad * gain
    mean_one = jnp.mean(inner, axis=-1, keepdims=True)
    mean_two = jnp.mean(inner * unit, axis=-1, keepdims=True)
    return scale * (inner - mean_one - unit * mean_two), grad_gain, grad_shift


def reduce_rows(grad, y):
    n = grad.shape[1]
    grouped = grad.reshape(4, 2, 96, n)
    mine = lax.dynamic_index_in_dim(grouped, y, 1, keepdims=False)
    theirs = lax.dynamic_index_in_dim(grouped, 1 - y, 1, keepdims=False)
    got = over_y(theirs)
    summed = (mine.astype(F32) + got.astype(F32)).astype(BF16)
    lines = over_z(summed)
    return jnp.sum(lines.astype(F32), axis=0)


def tuned(
    inputs,
    modality,
    key_valid_mask,
    output_gradient,
    mats,
    mats_momentum,
    mats_average,
    smalls,
    smalls_momentum,
    smalls_average,
):
    width = MODEL_WIDTH
    rows = inputs.shape[1]
    dp = lax.axis_index("dp")
    x = lax.axis_index("seq")
    core = dp % 2
    y = (dp // 2) % 2
    low = mats.astype(BF16)

    attention_block = jnp.concatenate(
        [part(low[:, j * width : (j + 1) * width], x, HALF, 1) for j in range(3)]
        + [low[:, 3 * width : 4 * width], jnp.pad(smalls.astype(BF16), ((0, 0), (0, 113)))],
        axis=1,
    )
    shared = low[:, 4 * width :].reshape(48, 2, 2, FHALF)
    keep = lax.dynamic_index_in_dim(shared, core, 2, keepdims=False)
    give = lax.dynamic_index_in_dim(shared, 1 - core, 2, keepdims=False)
    other_inputs = over_seq(inputs[0])
    att_z = over_z(jnp.broadcast_to(attention_block[None], (4,) + attention_block.shape))
    took = over_core(give)
    pair = ordered(core, keep[None], took[None], 0)
    up_block = pair[:, :, 0].reshape(96, FHALF)
    down_block = pair[:, :, 1].reshape(96, FHALF)
    att_y = ordered(y, att_z[:, None], over_y(att_z)[:, None], 1)
    att_w = ordered(core, att_y[:, :, None], over_core(att_y)[:, :, None], 2).reshape(width, -1)
    up_z = over_z(jnp.broadcast_to(up_block[None], (4, 96, FHALF)))
    down_z = over_z(jnp.broadcast_to(down_block[None], (4, 96, FHALF)))
    w_up = ordered(y, up_z[:, None], over_y(up_z)[:, None], 1).reshape(width, FHALF)
    w_down = ordered(y, down_z[:, None], over_y(down_z)[:, None], 1).reshape(width, FHALF)
    w_qkv = att_w[:, 0 : 3 * HALF]
    w_out = att_w[:, 3 * HALF : 3 * HALF + width]
    whole_smalls = att_w[:, 3 * HALF + width : 3 * HALF + width + 15]
    params = whole_smalls.astype(F32).T
    bias_up = part(params[8:12].reshape(FF), core, FHALF, 0)
    embed = whole_smalls[:, 12:15].T

    leading_key = (jnp.arange(2 * rows) == 0).astype(jnp.int32)
    live = jnp.maximum(key_valid_mask[0], leading_key)
    own_first = lambda v: jnp.concatenate([part(v, x, rows, 0), part(v, 1 - x, rows, 0)])
    live = own_first(live)
    kinds = own_first(modality[0])
    onehot = (kinds[:, None] == jnp.arange(3, dtype=jnp.int32)[None, :]).astype(BF16)
    both_inputs = jnp.concatenate([inputs[0], other_inputs], axis=0)
    x_all = both_inputs.astype(F32) + product(onehot, embed)
    x_low = x_all.astype(BF16)
    x_in = x_all[0:rows]
    bias_q = part(params[0], x, HALF, 0)
    bias_v = part(params[1], x, HALF, 0)
    bias_qkv = jnp.concatenate([bias_q, jnp.zeros_like(bias_q), bias_v])
    q_scale = jnp.where(jnp.arange(3 * HALF) < HALF, 0.125 / LN2, 1.0)
    qkv = ((product(x_low, w_qkv) + bias_qkv) * q_scale).astype(BF16)
    masked = jnp.where(
        (live == 0)[:, None] & (jnp.arange(128) == 0)[None, :], masked_score, 0.0
    ).astype(BF16)
    out_heads, log_sum = attend(qkv, masked)
    got_heads = over_seq(out_heads[rows:])
    out_low = ordered(x, out_heads[0:rows], got_heads, 1)
    first_in = x_in + (product(out_low, w_out) + params[2])
    unit1, scale1 = norm_parts(first_in)
    first = unit1 * params[4] + params[5]
    first_low = first.astype(BF16)

    first_both = jnp.concatenate([first_low, over_core(first_low)], axis=0)
    up = product(first_both, w_up) + bias_up
    act, slope = gelu_and_slope(up)
    act_low = act.astype(BF16)
    slope = slope.astype(BF16)
    ffo_other = product_nt(act_low[rows:], w_down).astype(BF16)
    ffo_got = over_core(ffo_other)
    ffo_own = product_nt(act_low[0:rows], w_down)
    second_in = first + (ffo_own + ffo_got.astype(F32) + params[3])
    unit2, scale2 = norm_parts(second_in)
    block_out = (unit2 * params[6] + params[7]).astype(BF16)[None]

    grad_rows = output_gradient[0].astype(F32)
    grad_second, grad_gain2, grad_shift2 = norm_back(grad_rows, unit2, scale2, params[6])
    grad_ffo = grad_second.astype(BF16)
    grad_bias_down = jnp.sum(grad_ffo.astype(F32), axis=0)
    ffo_both = jnp.concatenate([grad_ffo, over_core(grad_ffo)], axis=0)
    grad_act = product(ffo_both, w_down)
    grad_up_f = grad_act * slope.astype(F32)
    grad_up = grad_up_f.astype(BF16)
    grad_bias_up = jnp.sum(grad_up.astype(F32), axis=0)
    grad_w_down = product_tn(ffo_both, act_low).astype(BF16)
    down_rows = reduce_rows(grad_w_down, y)
    back_other = over_core(product_nt(grad_up[rows:], w_up).astype(BF16))
    back_own = product_nt(grad_up[0:rows], w_up)
    grad_first = grad_second + back_own + back_other.astype(F32)
    grad_w_up = product_tn(first_both, grad_up).astype(BF16)
    grad_first_in, grad_gain1, grad_shift1 = norm_back(grad_first, unit1, scale1, params[4])
    grad_mixed = grad_first_in.astype(BF16)
    grad_bias_out = jnp.sum(grad_mixed.astype(F32), axis=0)
    grad_out = product_nt(grad_mixed, w_out).astype(BF16)
    got_grad = over_seq(part(grad_out, 1 - x, HALF, 1))
    grad_heads = jnp.concatenate([part(grad_out, x, HALF, 1), got_grad], axis=0)
    out_both = jnp.concatenate([out_low, over_core(out_low)], axis=0)
    mixed_half = jnp.concatenate(
        [part(grad_mixed, core, HALF, 1), over_core(part(grad_mixed, 1 - core, HALF, 1))], axis=0
    )
    grad_w_out = product_tn(out_both, mixed_half).astype(BF16)
    up_rows = reduce_rows(jnp.concatenate([grad_w_up, grad_w_out], axis=1), y)

    gq, gk, gv = attend_back(qkv, out_heads, grad_heads, log_sum, masked)
    grad_qkv = jnp.concatenate([gq, gk, gv], axis=1)
    x_both = jnp.concatenate([x_low, over_core(x_low)], axis=0)
    padded = jnp.pad(grad_qkv, ((0, 0), (0, 128)))
    qkv_half = jnp.concatenate(
        [part(padded, core, QCOLS, 1), over_core(part(padded, 1 - core, QCOLS, 1))], axis=0
    )
    grad_w_qkv = product_tn(x_both, qkv_half)
    grad_x = product_nt(grad_qkv, w_qkv)
    got_x = over_seq(grad_x[rows:].astype(BF16))
    grad_x_in = grad_first_in + grad_x[0:rows] + got_x.astype(F32)
    input_grad = grad_x_in.astype(BF16)[None]

    hot = onehot.astype(F32)
    high = dict(precision=lax.Precision.HIGHEST, preferred_element_type=F32)
    rows_t = (((0,), (0,)), ((), ()))
    grad_embed = lax.dot_general(hot, grad_x, rows_t, **high) + lax.dot_general(
        hot[0:rows], grad_first_in, rows_t, **high
    )
    spread = lambda v: lax.dynamic_update_slice(jnp.zeros((width,), F32), v, (x * HALF,))
    bias_up_all = lax.dynamic_update_slice(jnp.zeros((FF,), F32), grad_bias_up, (core * FHALF,))
    small_rows = jnp.concatenate(
        [
            jnp.stack(
                [
                    spread(jnp.sum(gq.astype(F32), axis=0)),
                    spread(jnp.sum(gv.astype(F32), axis=0)),
                    grad_bias_out,
                    grad_bias_down,
                    grad_gain1,
                    grad_shift1,
                    grad_gain2,
                    grad_shift2,
                ]
            ),
            bias_up_all.reshape(4, width),
            grad_embed,
            jnp.zeros((1, width), F32),
        ],
        axis=0,
    )
    small_chip = small_rows + over_core(small_rows)
    small_tile = jnp.pad(small_chip.T, ((0, 0), (0, 112)))
    last = jnp.where(core == 0, grad_w_qkv[:, 4 * 128 :], small_tile)
    q_rows = reduce_rows(
        jnp.concatenate([grad_w_qkv[:, 0 : 4 * 128], last], axis=1).astype(BF16), y
    )

    def finish(value):
        mine = part(value, core, 48, 0)
        theirs = part(value, 1 - core, 48, 0)
        return ordered(core, mine[:, None], over_core(theirs)[:, None], 1)

    def add_seq(value):
        sent = value.astype(BF16)
        return (value + over_seq(sent).astype(F32)).astype(BF16)

    down_own = finish(add_seq(down_rows)).reshape(48, FF)
    up_own = finish(add_seq(up_rows))
    q_low = q_rows.astype(BF16)
    q_pair = jnp.concatenate([q_low, over_seq(q_low)], axis=1)
    q_own = finish(q_pair).reshape(48, 2, 2, QCOLS)
    mine_q = q_own[:, :, 0].reshape(48, 2 * QCOLS)
    other_q = q_own[:, :, 1].reshape(48, 2 * QCOLS)
    pieces = [
        ordered(x, mine_q[:, j * HALF : (j + 1) * HALF], other_q[:, j * HALF : (j + 1) * HALF], 1)
        for j in range(3)
    ]
    mats_grad = jnp.concatenate(
        pieces
        + [up_own[:, :, FHALF:].reshape(48, width), up_own[:, :, 0:FHALF].reshape(48, FF), down_own],
        axis=1,
    ).astype(F32)
    smalls_grad = mine_q[:, 3 * HALF : 3 * HALF + 15].astype(F32) + other_q[
        :, 3 * HALF : 3 * HALF + 15
    ].astype(F32)

    out_bias_grad = smalls_grad[:, 2]
    total_tokens = rows * lax.axis_size("dp") * lax.axis_size("seq")
    rate = base_rate / math.sqrt(total_tokens)
    decayed = mats_grad + decay_rate * mats
    new_mats_momentum = momentum_rate * mats_momentum + decayed
    new_mats = mats - rate * (decayed + momentum_rate * new_mats_momentum)
    new_mats_average = average_rate * mats_average + (1.0 - average_rate) * new_mats
    new_smalls_momentum = momentum_rate * smalls_momentum + smalls_grad
    new_smalls = smalls - rate * (smalls_grad + momentum_rate * new_smalls_momentum)
    new_smalls_average = average_rate * smalls_average + (1.0 - average_rate) * new_smalls
    return (
        block_out,
        input_grad,
        mats_grad,
        new_mats,
        new_mats_momentum,
        new_mats_average,
        smalls_grad,
        out_bias_grad,
        new_smalls,
        new_smalls_momentum,
        new_smalls_average,
    )


def solution(mesh):
    placed = (
        P("dp", "seq", None),
        P("dp", None),
        P("dp", None),
        P("dp", "seq", None),
        P("dp", None),
        P("dp", None),
        P("dp", None),
        P("dp", None),
        P("dp", None),
        P("dp", None),
    )
    plan = tuned if tuple(mesh.shape.values()) == (16, 2) else per_device
    return jax.shard_map(
        plan,
        mesh=mesh,
        in_specs=placed,
        out_specs=(
            P("dp", "seq", None),
            P("dp", "seq", None),
            P("dp", None),
            P("dp", None),
            P("dp", None),
            P("dp", None),
            P("dp", None),
            P("dp"),
            P("dp", None),
            P("dp", None),
            P("dp", None),
        ),
        check_vma=False,
    )
```

```python
import functools
import math

import jax
import jax.numpy as jnp
from jax import lax
from jax.experimental import pallas as pl
from jax.experimental.pallas import tpu as pltpu
from jax.sharding import PartitionSpec as P

MODEL_WIDTH = 768
H = 12
HD = 64
FF = 3072


epsilon = 1e-06
momentum_rate = 0.9
decay_rate = 0.0001
average_rate = 0.75
base_rate = 0.03
masked_score = -1e30


def product(left, right):
    return jnp.dot(left, right, preferred_element_type=jnp.float32)


def product_tn(left, right):
    return lax.dot_general(
        left, right, (((0,), (0,)), ((), ())), preferred_element_type=jnp.float32
    )


def product_nt(left, right):
    return lax.dot_general(
        left, right, (((1,), (1,)), ((), ())), preferred_element_type=jnp.float32
    )


def normalize(rows, gain, shift):
    mean = jnp.mean(rows, axis=-1, keepdims=True)
    centred = rows - mean
    spread = jnp.mean(centred * centred, axis=-1, keepdims=True)
    return centred * lax.rsqrt(spread + epsilon) * gain + shift


def exact_gelu(values):
    return jax.nn.gelu(values, approximate=False)


def head_scores(query_heads, key_heads, live_doc):
    scores = (
        jnp.einsum("qhe,khe->hqk", query_heads, key_heads, preferred_element_type=jnp.float32)
        * 0.125
    )
    return jnp.where(live_doc[None, None, :] > 0, scores, masked_score)


def attention_forward_pass(item):
    query_doc, keys_doc, values_doc, live_doc = item
    query_heads = query_doc.reshape(query_doc.shape[0], H, HD)
    key_heads = keys_doc.reshape(keys_doc.shape[0], H, HD)
    value_heads = values_doc.reshape(values_doc.shape[0], H, HD)
    scores = head_scores(query_heads, key_heads, live_doc)
    top = jnp.max(scores, axis=-1, keepdims=True)
    expd = jnp.exp(scores - top)
    total = jnp.sum(expd, axis=-1, keepdims=True)
    prob = (expd / total).astype(jnp.bfloat16)
    attention_output = jnp.einsum(
        "hqk,khe->qhe", prob, value_heads, preferred_element_type=jnp.float32
    )
    return (attention_output.reshape(query_doc.shape[0], H * HD), (top + jnp.log(total))[..., 0])


def attention_backward_pass(item):
    query_doc, keys_doc, values_doc, live_doc, log_sum_normalizer, grad_doc = item
    element_count = query_doc.shape[0]
    length = keys_doc.shape[0]
    query_heads = query_doc.reshape(element_count, H, HD)
    key_heads = keys_doc.reshape(length, H, HD)
    value_heads = values_doc.reshape(length, H, HD)
    grad_heads = grad_doc.reshape(element_count, H, HD)
    scores = head_scores(query_heads, key_heads, live_doc)
    prob = jnp.exp(scores - log_sum_normalizer[..., None])
    grad_prob = jnp.einsum(
        "qhe,khe->hqk", grad_heads, value_heads, preferred_element_type=jnp.float32
    )
    grad_values = jnp.einsum(
        "hqk,qhe->khe", prob.astype(jnp.bfloat16), grad_heads, preferred_element_type=jnp.float32
    )
    inner = jnp.sum(prob * grad_prob, axis=-1, keepdims=True)
    grad_scores = (prob * (grad_prob - inner)).astype(jnp.bfloat16)
    grad_query = (
        jnp.einsum("hqk,khe->qhe", grad_scores, key_heads, preferred_element_type=jnp.float32)
        * 0.125
    )
    grad_keys = (
        jnp.einsum("hqk,qhe->khe", grad_scores, query_heads, preferred_element_type=jnp.float32)
        * 0.125
    )
    return (
        grad_query.reshape(element_count, H * HD),
        grad_keys.reshape(length, H * HD),
        grad_values.reshape(length, H * HD),
    )


def per_device(
    inputs,
    modality,
    key_valid_mask,
    output_gradient,
    mats,
    mats_momentum,
    mats_average,
    smalls,
    smalls_momentum,
    smalls_average,
):
    docs, local_len, width = inputs.shape
    seq_len = modality.shape[1]
    rows = docs * local_len
    low_mats = mats.astype(jnp.bfloat16)
    w_qkv, w_out, w_up, w_down, whole_smalls = (
        lax.all_gather(low_mats[:, 0 : 3 * MODEL_WIDTH], "dp", axis=0, tiled=True),
        lax.all_gather(low_mats[:, 3 * MODEL_WIDTH : 4 * MODEL_WIDTH], "dp", axis=0, tiled=True),
        lax.all_gather(
            low_mats[:, 4 * MODEL_WIDTH : 4 * MODEL_WIDTH + FF], "dp", axis=0, tiled=True
        ),
        lax.all_gather(low_mats[:, 4 * MODEL_WIDTH + FF :], "dp", axis=0, tiled=True),
        lax.all_gather(smalls.astype(jnp.bfloat16), "dp", axis=0, tiled=True),
    )
    params = whole_smalls.astype(jnp.float32)
    bias_qkv = jnp.concatenate([params[:, 0], jnp.zeros_like(params[:, 0]), params[:, 1]])
    bias_up = jnp.transpose(params[:, 8:12]).reshape(FF)
    embed = jnp.transpose(whole_smalls[:, 12:15])
    leading_key = (jnp.arange(seq_len) == 0).astype(jnp.int32)
    valid_positions = jnp.maximum(key_valid_mask, leading_key[None, :])
    local_start = lax.axis_index("seq") * local_len
    local_modality = lax.dynamic_slice_in_dim(modality, local_start, local_len, 1)
    onehot = (
        local_modality.reshape(rows)[:, None] == jnp.arange(3, dtype=jnp.int32)[None, :]
    ).astype(jnp.bfloat16)
    x_in = inputs.reshape(rows, width).astype(jnp.float32) + product(onehot, embed)
    x_low = x_in.astype(jnp.bfloat16)
    qkv = (product(x_low, w_qkv) + bias_qkv).astype(jnp.bfloat16)
    query_documents = qkv[:, 0:width].reshape(docs, local_len, width)
    keys_local = qkv[:, width : 2 * width].reshape(docs, local_len, width)
    values_local = qkv[:, 2 * width :].reshape(docs, local_len, width)
    every_key, every_value = (
        lax.all_gather(keys_local, "seq", axis=1, tiled=True),
        lax.all_gather(values_local, "seq", axis=1, tiled=True),
    )
    attention_output, log_sum_normalizer = lax.map(
        attention_forward_pass, (query_documents, every_key, every_value, valid_positions)
    )
    out_low = attention_output.reshape(rows, width).astype(jnp.bfloat16)
    mixed = product(out_low, w_out) + params[:, 2]
    first_in = x_in + mixed
    first = normalize(first_in, params[:, 4], params[:, 5])
    first_low = first.astype(jnp.bfloat16)
    up = product(first_low, w_up) + bias_up
    act_low = exact_gelu(up).astype(jnp.bfloat16)
    ffo = product_nt(act_low, w_down) + params[:, 3]
    second_in = first + ffo
    result = normalize(second_in, params[:, 6], params[:, 7])
    block_out = result.astype(jnp.bfloat16).reshape(docs, local_len, width)
    w_qkv, w_out, w_up, w_down = (
        lax.all_gather(low_mats[:, 0 : 3 * MODEL_WIDTH], "dp", axis=0, tiled=True),
        lax.all_gather(low_mats[:, 3 * MODEL_WIDTH : 4 * MODEL_WIDTH], "dp", axis=0, tiled=True),
        lax.all_gather(
            low_mats[:, 4 * MODEL_WIDTH : 4 * MODEL_WIDTH + FF], "dp", axis=0, tiled=True
        ),
        lax.all_gather(low_mats[:, 4 * MODEL_WIDTH + FF :], "dp", axis=0, tiled=True),
    )
    grad_rows = output_gradient.reshape(rows, width).astype(jnp.float32)
    second_out, second_pull = jax.vjp(normalize, second_in, params[:, 6], params[:, 7])
    grad_second, grad_gain2, grad_shift2 = second_pull(grad_rows)
    grad_ffo = grad_second.astype(jnp.bfloat16)
    grad_bias_down = jnp.sum(grad_ffo.astype(jnp.float32), axis=0)
    grad_w_down = product_tn(grad_ffo, act_low)
    grad_act = product(grad_ffo, w_down)
    gelu_out, gelu_pull = jax.vjp(exact_gelu, up)
    grad_up = gelu_pull(grad_act)[0].astype(jnp.bfloat16)
    grad_bias_up = jnp.sum(grad_up.astype(jnp.float32), axis=0)
    grad_w_up = product_tn(first_low, grad_up)
    grad_first = grad_second + product_nt(grad_up, w_up)
    first_out, first_pull = jax.vjp(normalize, first_in, params[:, 4], params[:, 5])
    grad_first_in, grad_gain1, grad_shift1 = first_pull(grad_first)
    grad_mixed = grad_first_in.astype(jnp.bfloat16)
    grad_bias_out = jnp.sum(grad_mixed.astype(jnp.float32), axis=0)
    grad_w_out = product_tn(out_low, grad_mixed)
    grad_out = product_nt(grad_mixed, w_out).astype(jnp.bfloat16)
    output_gradient_documents = grad_out.reshape(docs, local_len, width)
    grad_query, grad_keys_all, grad_values_all = lax.map(
        attention_backward_pass,
        (
            query_documents,
            every_key,
            every_value,
            valid_positions,
            log_sum_normalizer,
            output_gradient_documents,
        ),
    )
    grad_keys, grad_values = (
        lax.psum_scatter(
            grad_keys_all.astype(jnp.bfloat16), "seq", scatter_dimension=1, tiled=True
        ).astype(jnp.float32),
        lax.psum_scatter(
            grad_values_all.astype(jnp.bfloat16), "seq", scatter_dimension=1, tiled=True
        ).astype(jnp.float32),
    )
    grad_qkv = jnp.concatenate(
        [
            grad_query.reshape(rows, width).astype(jnp.bfloat16),
            grad_keys.reshape(rows, width).astype(jnp.bfloat16),
            grad_values.reshape(rows, width).astype(jnp.bfloat16),
        ],
        axis=1,
    )
    grad_bias_qkv = jnp.sum(grad_qkv.astype(jnp.float32), axis=0)
    grad_w_qkv = product_tn(x_low, grad_qkv)
    grad_x_in = grad_first_in + product_nt(grad_qkv, w_qkv)
    grad_embed = lax.dot_general(
        onehot.astype(jnp.float32),
        grad_x_in,
        (((0,), (0,)), ((), ())),
        precision=lax.Precision.HIGHEST,
        preferred_element_type=jnp.float32,
    )
    input_grad = grad_x_in.astype(jnp.bfloat16).reshape(docs, local_len, width)
    grad_columns = jnp.stack(
        [
            grad_bias_qkv[0:width],
            grad_bias_qkv[2 * width :],
            grad_bias_out,
            grad_bias_down,
            grad_gain1,
            grad_shift1,
            grad_gain2,
            grad_shift2,
        ],
        axis=1,
    )
    grad_smalls = jnp.concatenate(
        [
            grad_columns,
            jnp.transpose(grad_bias_up.reshape(FF // width, width)),
            jnp.transpose(grad_embed),
        ],
        axis=1,
    )
    qkv_shard, out_shard, up_shard, down_shard, small_shard = (
        lax.psum_scatter(
            grad_w_qkv.astype(jnp.bfloat16), "dp", scatter_dimension=0, tiled=True
        ).astype(jnp.float32),
        lax.psum_scatter(
            grad_w_out.astype(jnp.bfloat16), "dp", scatter_dimension=0, tiled=True
        ).astype(jnp.float32),
        lax.psum_scatter(
            grad_w_up.astype(jnp.bfloat16), "dp", scatter_dimension=0, tiled=True
        ).astype(jnp.float32),
        lax.psum_scatter(
            grad_w_down.astype(jnp.bfloat16), "dp", scatter_dimension=0, tiled=True
        ).astype(jnp.float32),
        lax.psum_scatter(
            grad_smalls.astype(jnp.bfloat16), "dp", scatter_dimension=0, tiled=True
        ).astype(jnp.float32),
    )
    mats_shard = jnp.concatenate([qkv_shard, out_shard, up_shard, down_shard], axis=1)
    mats_grad, smalls_grad = (
        lax.psum(mats_shard.astype(jnp.bfloat16), "seq").astype(jnp.float32),
        lax.psum(small_shard.astype(jnp.bfloat16), "seq").astype(jnp.float32),
    )
    out_bias_grad = smalls_grad[:, 2]
    total_tokens = rows * lax.axis_size("dp") * lax.axis_size("seq")
    rate = base_rate / math.sqrt(total_tokens)
    decayed = mats_grad + decay_rate * mats
    new_mats_momentum = momentum_rate * mats_momentum + decayed
    new_mats = mats - rate * (decayed + momentum_rate * new_mats_momentum)
    new_mats_average = average_rate * mats_average + (1.0 - average_rate) * new_mats
    new_smalls_momentum = momentum_rate * smalls_momentum + smalls_grad
    new_smalls = smalls - rate * (smalls_grad + momentum_rate * new_smalls_momentum)
    new_smalls_average = average_rate * smalls_average + (1.0 - average_rate) * new_smalls
    return (
        block_out,
        input_grad,
        mats_grad,
        new_mats,
        new_mats_momentum,
        new_mats_average,
        smalls_grad,
        out_bias_grad,
        new_smalls,
        new_smalls_momentum,
        new_smalls_average,
    )


LN2 = math.log(2.0)
NT = (((1,), (1,)), ((), ()))
NN = (((1,), (0,)), ((), ()))
TN = (((0,), (0,)), ((), ()))
BF16 = jnp.bfloat16
F32 = jnp.float32
HALF = MODEL_WIDTH // 2
QUARTER = MODEL_WIDTH
QCOLS = 5 * 128
COST = 1000


def mxu(left, right, dims):
    return lax.dot_general(left, right, dims, preferred_element_type=jnp.float32)


def three_parts(value):
    high = value.astype(jnp.bfloat16)
    rest = value - high.astype(jnp.float32)
    middle = rest.astype(jnp.bfloat16)
    return high, middle, (rest - middle.astype(jnp.float32)).astype(jnp.bfloat16)


def run(kernel, name, ins, outs, scratch=(), flops=0, moved=0, special=0, limit=12):
    spaces = {"vmem": pltpu.VMEM, "any": pl.ANY, "smem": pltpu.SMEM}
    return pl.pallas_call(
        kernel,
        in_specs=[pl.BlockSpec(memory_space=spaces[kind]) for _, kind in ins],
        out_specs=[pl.BlockSpec(memory_space=pltpu.VMEM) for _ in outs],
        out_shape=[jax.ShapeDtypeStruct(shape, dtype) for shape, dtype in outs],
        scratch_shapes=list(scratch),
        compiler_params=pltpu.CompilerParams(vmem_limit_bytes=limit * 2**20),
        cost_estimate=pl.CostEstimate(flops=COST, bytes_accessed=0, transcendentals=0),
        name=name,
    )(*[array for array, _ in ins])


def fetch(pieces, whole, sems):
    copies = []
    for i, (source, first) in enumerate(pieces):
        copy = pltpu.make_async_copy(source, whole.at[pl.ds(first, source.shape[0])], sems.at[i])
        copy.start()
        copies.append(copy)
    return copies


def xor2(z):
    return lax.rem(z + 2, 4)


def xor1(z):
    return z + 1 - 2 * lax.rem(z, 2)


def near_far(place, y_last):
    y, z = place[1], place[3]
    if y_last:
        line = (z, xor2(z), xor1(z), xor1(xor2(z)))
        return [(zz, y) for zz in line], [(zz, 1 - y) for zz in line]
    one, two = (z, xor2(z)), (xor1(z), xor1(xor2(z)))
    return [(zz, yy) for yy in (y, 1 - y) for zz in one], [(zz, yy) for yy in (y, 1 - y) for zz in two]


def eight(place, block):
    mine, theirs, y_last = block
    near, far = near_far(place, y_last)
    pieces = []
    for ref, chips in ((mine, near), (theirs, far)):
        for i, (zz, yy) in enumerate(chips):
            pieces.append((ref.at[i, :, pl.ds(0, QUARTER)], pl.multiple_of((2 * zz + yy) * 96, 32)))
    return pieces


def sixteen(place, blocks):
    core = place[2]
    near, far = near_far(place, True)
    pieces = []
    for chips, cc, ref in zip((near, near, far, far), (core, 1 - core, core, 1 - core), blocks):
        for i, (zz, yy) in enumerate(chips):
            pieces.append((ref.at[i], pl.multiple_of((zz * 4 + yy * 2 + cc) * 48, 16)))
    return pieces


def fetch_out(place, mine, theirs, whole, sems):
    core = place[2]
    near, far = near_far(place, True)
    copies = []
    for j, (ref, cc) in enumerate(((mine, core), (theirs, 1 - core))):
        for i, (zz, yy) in enumerate(near + far):
            row = pl.multiple_of((2 * zz + yy) * 96, 32)
            lanes = pl.ds(pl.multiple_of(cc * HALF, 128), HALF)
            copy = pltpu.make_async_copy(ref.at[i], whole.at[pl.ds(row, 96), lanes], sems.at[8 * j + i])
            copy.start()
            copies.append(copy)
    return copies


def split_rows(whole, mine, theirs, place, y_last):
    near, far = near_far(place, y_last)
    for ref, chips in ((mine, near), (theirs, far)):
        for i, (zz, yy) in enumerate(chips):
            row = pl.multiple_of((2 * zz + yy) * 96, 32)
            ref[i] = whole[pl.ds(row, 96), :].astype(ref.dtype)


def pack_heads_kernel(place, mats, smalls_t, block, wide, narrow, sems):
    width = MODEL_WIDTH
    copies = []
    for j in range(3):
        lanes = pl.ds(pl.multiple_of(j * width + place[0] * HALF, 128), HALF)
        copy = pltpu.make_async_copy(mats.at[:, lanes], wide.at[:, pl.ds(j * HALF, HALF)], sems.at[j])
        copy.start()
        copies.append(copy)
    narrow[...] = jnp.zeros_like(narrow)
    narrow[0:15, :] = smalls_t[...]
    block[:, 3 * HALF :] = narrow[...].T.astype(BF16)
    for copy in copies:
        copy.wait()
    block[:, 0 : 3 * HALF] = wide[...].astype(BF16)


def pack_heads(place, mats, smalls_t):
    rows = mats.shape[0]
    return run(
        pack_heads_kernel,
        "pack_heads",
        [(place, "smem"), (mats, "any"), (smalls_t, "vmem")],
        [((rows, 3 * HALF + 128), BF16)],
        [
            pltpu.VMEM((rows, 3 * HALF), F32),
            pltpu.VMEM((128, rows), F32),
            pltpu.SemaphoreType.DMA((3,)),
        ],
        moved=2**19,
        limit=4,
    )[0]


CUTS = (0, QUARTER + HALF, 2 * QUARTER + HALF, 3 * QUARTER + HALF, 4 * QUARTER + HALF)


def pack_rest_kernel(place, mats, keep, give):
    width = MODEL_WIDTH
    for core, ref in ((place[2], keep), (1 - place[2], give)):
        take = lambda first, n: mats[:, pl.ds(pl.multiple_of(first, 128), n)].astype(BF16)
        ref[:, 0:QUARTER] = take(4 * width + 2 * core * QUARTER, QUARTER)
        ref[:, QUARTER : CUTS[1]] = take(3 * width + core * HALF, HALF)
        ref[:, CUTS[1] : CUTS[2]] = take(4 * width + (2 * core + 1) * QUARTER, QUARTER)
        ref[:, CUTS[2] : CUTS[3]] = take(8 * width + 2 * core * QUARTER, QUARTER)
        ref[:, CUTS[3] :] = take(8 * width + (2 * core + 1) * QUARTER, QUARTER)


def pack_rest(place, mats):
    rows = mats.shape[0]
    return run(
        pack_rest_kernel,
        "pack_rest",
        [(place, "smem"), (mats, "vmem")],
        [((rows, CUTS[4]), BF16)] * 2,
        moved=4 * 2**20,
        limit=4,
    )


def unit_rows(rows):
    mean = jnp.mean(rows, axis=-1, keepdims=True)
    centred = rows - mean
    spread = jnp.mean(centred * centred, axis=-1, keepdims=True)
    scale = lax.rsqrt(spread + epsilon)
    return centred * scale, scale


def unit_back(grad, unit, scale, gain):
    inner = grad * gain
    mean_one = jnp.mean(inner, axis=-1, keepdims=True)
    mean_two = jnp.mean(inner * unit, axis=-1, keepdims=True)
    return scale * (inner - mean_one - unit * mean_two)


def down_sum(value):
    return jnp.sum(value, axis=0, keepdims=True)


def project_kernel(
    place, own, other, kinds, mask, w0, w1, w2, w3, x_low, x_in, qkv, masked, params, whole, sems
):
    x, y, core = place[0], place[1], place[2]
    rows = own.shape[0]
    copies = fetch(sixteen(place, (w0, w1, w2, w3)), whole, sems)
    lane_row = lax.broadcasted_iota(jnp.int32, (8, rows), 0)
    lane = lax.broadcasted_iota(jnp.int32, (8, 128), 1)
    first_row = lax.broadcasted_iota(jnp.int32, (8, 128), 0)
    pick = jnp.where((lane == 0) & (first_row == 0), 1.0, 0.0).astype(BF16)
    position = lax.broadcasted_iota(jnp.int32, (1, rows), 1)
    for side in range(2):
        start = pl.multiple_of((x if side == 0 else 1 - x) * rows, 128)
        alive = (mask[:, pl.ds(start, rows)] > 0) | (position + start == 0)
        bias = jnp.where(alive, 0.0, masked_score)
        bias = jnp.where(lane_row == 0, jnp.broadcast_to(bias, (8, rows)), 0.0).astype(BF16)
        masked[side * rows : (side + 1) * rows, :] = mxu(bias, pick, TN).astype(BF16)
    for copy in copies:
        copy.wait()
    params[...] = whole[:, 3 * HALF :].astype(F32).T[0:16]
    embed = params[8:16, :].astype(BF16)
    start_q = pl.multiple_of(x * HALF, 128)
    bias_q = params[0:1, pl.ds(start_q, HALF)]
    bias_v = params[1:2, pl.ds(start_q, HALF)]
    scale = 0.125 / LN2
    step = 256
    for side in range(2):
        start = pl.multiple_of((x if side == 0 else 1 - x) * rows, 128)
        hot = jnp.where(kinds[:, pl.ds(start, rows)] + 4 == lane_row, 1.0, 0.0).astype(BF16)
        source = own if side == 0 else other
        for i in range(rows // step):
            span = slice(i * step, (i + 1) * step)
            out = slice(side * rows + i * step, side * rows + (i + 1) * step)
            value = source[span, :].astype(F32) + mxu(hot[:, span], embed, TN)
            if side == 0:
                x_in[span, :] = value
            low = value.astype(BF16)
            x_low[out, :] = low
            q = mxu(low, whole[:, 0:HALF], NN)
            qkv[out, 0:HALF] = ((q + bias_q) * scale).astype(BF16)
            k = mxu(low, whole[:, HALF : 2 * HALF], NN)
            qkv[out, HALF : 2 * HALF] = k.astype(BF16)
            v = mxu(low, whole[:, 2 * HALF : 3 * HALF], NN)
            qkv[out, 2 * HALF :] = (v + bias_v).astype(BF16)


def project(place, own, other, kinds, mask, blocks):
    rows, width = own.shape
    return run(
        project_kernel,
        "project",
        [(place, "smem"), (own, "vmem"), (other, "vmem"), (kinds, "vmem"), (mask, "vmem")]
        + [(block, "any") for block in blocks],
        [
            ((2 * rows, width), BF16),
            ((rows, width), F32),
            ((2 * rows, 3 * HALF), BF16),
            ((2 * rows, 128), BF16),
            ((16, width), F32),
        ],
        [pltpu.VMEM((width, 3 * HALF + 128), BF16), pltpu.SemaphoreType.DMA((16,))],
        flops=4 * rows * width * 3 * HALF,
        moved=12 * 2**20,
    )


def attend_kernel(q_ref, k_ref, v_ref, masked_ref, out_ref, log_ref, *, block):
    length = k_ref.shape[0]
    lane = lax.broadcasted_iota(jnp.int32, (1, 128), 1)
    keys = jnp.concatenate([k_ref[...], masked_ref[...]], axis=1)
    values = jnp.concatenate([v_ref[...], jnp.ones((length, 128), jnp.bfloat16)], axis=1)
    one = jnp.broadcast_to(jnp.where(lane == 0, 1.0, 0.0).astype(jnp.bfloat16), (block, 128))
    for i in range(q_ref.shape[0] // block):
        span = slice(i * block, (i + 1) * block)
        query = q_ref[span, :]
        outs, logs = [], []
        for head in range(2):
            here = (lane < 64) if head == 0 else (lane >= 64)
            only = jnp.where(here, query, jnp.zeros_like(query))
            scores = mxu(jnp.concatenate([only, one], axis=1), keys, NT)
            top = jnp.max(scores, axis=1, keepdims=True)
            weight = jnp.exp2(scores - top).astype(jnp.bfloat16)
            mixed = mxu(weight, values, NN)
            total = mixed[:, 128:]
            outs.append(mixed[:, :128] / total)
            logs.append(top + jnp.log2(total[:, 0:1]))
        out_ref[span, :] = jnp.where(lane < 64, outs[0], outs[1]).astype(jnp.bfloat16)
        log_ref[span, :] = jnp.where(lane == 0, logs[0], jnp.where(lane == 1, logs[1], 0.0))


def attend(qkv, masked, block=256):
    length, columns = qkv.shape
    pairs = columns // 3 // 128

    def spec(first):
        return pl.BlockSpec((length, 128), lambda i: (0, first + i))

    return pl.pallas_call(
        functools.partial(attend_kernel, block=block),
        grid=(pairs,),
        in_specs=[
            spec(0),
            spec(pairs),
            spec(2 * pairs),
            pl.BlockSpec((length, 128), lambda i: (0, 0)),
        ],
        out_specs=[spec(0), spec(0)],
        out_shape=[
            jax.ShapeDtypeStruct((length, pairs * 128), jnp.bfloat16),
            jax.ShapeDtypeStruct((length, pairs * 128), jnp.float32),
        ],
        compiler_params=pltpu.CompilerParams(vmem_limit_bytes=24 * 2**20),
        cost_estimate=pl.CostEstimate(
            flops=COST, bytes_accessed=0, transcendentals=0
        ),
        name="attend",
    )(qkv, qkv, qkv, masked)


def attend_back_kernel(
    q_ref, k_ref, v_ref, o_ref, g_ref, log_ref, masked_ref, dq_ref, dk_ref, dv_ref, dk_sum, dv_sum, *, block
):
    length = k_ref.shape[0]
    bf16 = jnp.bfloat16
    lane = lax.broadcasted_iota(jnp.int32, (1, 128), 1)
    ones = jnp.where((lane >= 1) & (lane <= 3), 1.0, 0.0).astype(bf16)
    masked = masked_ref[...]
    keys = jnp.concatenate(
        [k_ref[...], jnp.where(lane == 0, masked, jnp.broadcast_to(ones, masked.shape))], axis=1
    )
    three = jnp.broadcast_to(jnp.where(lane <= 2, 1.0, 0.0).astype(bf16), (length, 128))
    values = jnp.concatenate([v_ref[...], three], axis=1)
    keys_t = k_ref[...].T
    one = jnp.ones((block, 128), bf16)
    zero = jnp.zeros((block, 128), bf16)
    row = lax.broadcasted_iota(jnp.int32, (128, 1), 0)
    for i in range(q_ref.shape[0] // block):
        span = slice(i * block, (i + 1) * block)
        query, grad = q_ref[span, :], g_ref[span, :]
        both = grad.astype(jnp.float32) * o_ref[span, :].astype(jnp.float32)
        logs = log_ref[span, :]
        turned = []
        for head in range(2):
            here = (lane < 64) if head == 0 else (lane >= 64)
            inner = jnp.sum(jnp.where(here, both, 0.0), axis=1, keepdims=True)
            wide = lambda t: jnp.broadcast_to(t, (block, 128))
            i0, i1, i2 = (wide(t) for t in three_parts(-inner))
            l0, l1, l2 = (wide(t) for t in three_parts(-logs[:, head : head + 1]))
            query_h = jnp.where(here, query, zero)
            grad_h = jnp.where(here, grad, zero)
            tail_q = jnp.where(
                lane == 0,
                one,
                jnp.where(lane == 1, l0, jnp.where(lane == 2, l1, jnp.where(lane == 3, l2, zero))),
            )
            tail_g = jnp.where(lane == 0, i0, jnp.where(lane == 1, i1, jnp.where(lane == 2, i2, zero)))
            prob = jnp.exp2(mxu(keys, jnp.concatenate([query_h, tail_q], axis=1), NT))
            slope = mxu(values, jnp.concatenate([grad_h, tail_g], axis=1), NT)
            grad_scores = (prob * slope).astype(bf16)
            add_v = mxu(prob.astype(bf16), grad_h, NN)
            add_k = mxu(grad_scores, query_h, NN)
            if i == 0 and head == 0:
                dv_sum[...] = add_v
                dk_sum[...] = add_k
            else:
                dv_sum[...] += add_v
                dk_sum[...] += add_k
            turned.append(mxu(keys_t, grad_scores, NN))
        dq_ref[span, :] = (jnp.where(row < 64, turned[0], turned[1]) * 0.125).T.astype(bf16)
    dk_ref[...] = (dk_sum[...] * LN2).astype(bf16)
    dv_ref[...] = dv_sum[...].astype(bf16)


def attend_back(qkv, out, grad, log_sum, masked, pair, block=512):
    length, columns = qkv.shape
    pairs = columns // 3 // 128

    def spec(column):
        return pl.BlockSpec((length, 128), lambda i: (0, column))

    return pl.pallas_call(
        functools.partial(attend_back_kernel, block=block),
        grid=(1,),
        in_specs=[
            spec(pair),
            spec(pairs + pair),
            spec(2 * pairs + pair),
            spec(pair),
            spec(pair),
            spec(pair),
            spec(0),
        ],
        out_specs=[spec(0)] * 3,
        out_shape=[jax.ShapeDtypeStruct((length, 128), jnp.bfloat16)] * 3,
        scratch_shapes=[pltpu.VMEM((length, 128), jnp.float32)] * 2,
        compiler_params=pltpu.CompilerParams(vmem_limit_bytes=28 * 2**20),
        cost_estimate=pl.CostEstimate(flops=COST, bytes_accessed=0, transcendentals=0),
        name="attend_back",
    )(qkv, qkv, qkv, out, grad, log_sum, masked)


def mix_kernel(
    place, heads, got, x_in, params, w0, w1, out_low, unit, scale, first_low, whole, sems
):
    x, y, core = place[0], place[1], place[2]
    rows = x_in.shape[0]
    copies = fetch_out(place, w0, w1, whole, sems)
    mine = pl.multiple_of(x * HALF, 128)
    theirs = pl.multiple_of((1 - x) * HALF, 128)
    out_low[:, pl.ds(mine, HALF)] = heads[0:rows, :]
    out_low[:, pl.ds(theirs, HALF)] = got[...]
    for copy in copies:
        copy.wait()
    step = 256
    for i in range(rows // step):
        span = slice(i * step, (i + 1) * step)
        mixed = mxu(out_low[span, :], whole[...], NN) + params[2:3, :]
        ones, size = unit_rows(x_in[span, :] + mixed)
        unit[span, :] = ones
        scale[span, :] = jnp.broadcast_to(size, (step, 128))
        first_low[span, :] = (ones * params[4:5, :] + params[5:6, :]).astype(BF16)


def mix(place, heads, got, x_in, params, blocks):
    rows, width = x_in.shape
    return run(
        mix_kernel,
        "mix",
        [(place, "smem"), (heads, "vmem"), (got, "vmem"), (x_in, "vmem"), (params, "vmem")]
        + [(block, "any") for block in blocks],
        [
            ((rows, width), BF16),
            ((rows, width), F32),
            ((rows, 128), F32),
            ((rows, width), BF16),
        ],
        [pltpu.VMEM((width, width), BF16), pltpu.SemaphoreType.DMA((16,))],
        flops=2 * rows * width * width,
        moved=8 * 2**20,
    )


def gelu_and_slope(up):
    size = jnp.abs(up)
    t = 1.0 / (1.0 + (0.3275911 * math.sqrt(0.5)) * size)
    bell = jnp.exp(-0.5 * up * up)
    poly = t * (
        0.5 * 0.254829592
        + t
        * (
            0.5 * -0.284496736
            + t * (0.5 * 1.421413741 + t * (0.5 * -1.453152027 + t * (0.5 * 1.061405429)))
        )
    )
    tail = poly * bell
    below = jnp.where(up < 0, tail, 1.0 - tail)
    return up * below, below + up * bell * (1.0 / math.sqrt(2.0 * math.pi))


def up_kernel(place, own, other, params, w0, w1, act, slope, whole, sems, *, which, y_last):
    core = place[2]
    rows = own.shape[0]
    for copy in fetch(eight(place, (w0, w1, y_last)), whole, sems):
        copy.wait()
    bias = params[pl.ds(8 + 2 * core + which, 1), :]
    step = 128
    for side in range(2):
        source = own if side == 0 else other
        for i in range(rows // step):
            out = slice(side * rows + i * step, side * rows + (i + 1) * step)
            up = mxu(source[i * step : (i + 1) * step, :], whole[...], NN) + bias
            value, change = gelu_and_slope(up)
            act[out, :] = value.astype(BF16)
            slope[out, :] = change.astype(BF16)


def raise_up(place, own, other, params, block, which):
    rows, width = own.shape
    *refs, y_last = block
    return run(
        functools.partial(up_kernel, which=which, y_last=y_last),
        "raise_up",
        [(place, "smem"), (own, "vmem"), (other, "vmem"), (params, "vmem")] + [(r, "any") for r in refs],
        [((2 * rows, QUARTER), BF16), ((2 * rows, QUARTER), BF16)],
        [pltpu.VMEM((width, QUARTER), BF16), pltpu.SemaphoreType.DMA((8,))],
        flops=4 * rows * width * QUARTER,
        moved=8 * 2**20,
        special=4 * rows * QUARTER,
        limit=8,
    )


def lower_kernel(place, act, w0, w1, out, whole, sems, *, y_last):
    for copy in fetch(eight(place, (w0, w1, y_last)), whole, sems):
        copy.wait()
    step = 256
    for i in range(act.shape[0] // step):
        span = slice(i * step, (i + 1) * step)
        out[span, :] = mxu(act[span, :], whole[...], NT)


def lower(place, act, block):
    rows, columns = act.shape
    *refs, y_last = block
    return run(
        functools.partial(lower_kernel, y_last=y_last),
        "lower",
        [(place, "smem"), (act, "vmem")] + [(r, "any") for r in refs],
        [((rows, MODEL_WIDTH), F32)],
        [pltpu.VMEM((MODEL_WIDTH, columns), BF16), pltpu.SemaphoreType.DMA((8,))],
        flops=2 * rows * columns * MODEL_WIDTH,
        moved=6 * 2**20,
        limit=8,
    )[0]


def lower_other_kernel(place, act, so_far, w0, w1, out, whole, sems, *, y_last):
    for copy in fetch(eight(place, (w0, w1, y_last)), whole, sems):
        copy.wait()
    rows = out.shape[0]
    step = 256
    for i in range(rows // step):
        span = slice(rows + i * step, rows + (i + 1) * step)
        value = so_far[span, :] + mxu(act[span, :], whole[...], NT)
        out[i * step : (i + 1) * step, :] = value.astype(BF16)


def lower_other(place, act, so_far, block):
    rows, columns = act.shape
    *refs, y_last = block
    return run(
        functools.partial(lower_other_kernel, y_last=y_last),
        "lower_other",
        [(place, "smem"), (act, "vmem"), (so_far, "vmem")] + [(r, "any") for r in refs],
        [((rows // 2, MODEL_WIDTH), BF16)],
        [pltpu.VMEM((MODEL_WIDTH, columns), BF16), pltpu.SemaphoreType.DMA((8,))],
        flops=rows * columns * MODEL_WIDTH,
        moved=4 * 2**20,
        limit=8,
    )[0]


def turn_kernel(
    place,
    act,
    so_far,
    got,
    unit1,
    params,
    grad,
    w0,
    w1,
    block_out,
    grad_second,
    grad_low,
    sums,
    whole,
    sems,
    *,
    y_last,
):
    for copy in fetch(eight(place, (w0, w1, y_last)), whole, sems):
        copy.wait()
    rows = got.shape[0]
    step = 128
    total = [jnp.zeros((1, MODEL_WIDTH), F32)] * 3
    for i in range(rows // step):
        span = slice(i * step, (i + 1) * step)
        first = unit1[span, :] * params[4:5, :] + params[5:6, :]
        value = so_far[span, :] + mxu(act[span, :], whole[...], NT) + got[span, :].astype(F32)
        unit, scale = unit_rows(first + (value + params[3:4, :]))
        block_out[span, :] = (unit * params[6:7, :] + params[7:8, :]).astype(BF16)
        dy = grad[span, :].astype(F32)
        back = unit_back(dy, unit, scale, params[6:7, :])
        grad_second[span, :] = back
        low = back.astype(BF16)
        grad_low[span, :] = low
        total[0] += down_sum(low.astype(F32))
        total[1] += down_sum(unit * dy)
        total[2] += down_sum(dy)
    sums[...] = jnp.concatenate(total + [jnp.zeros((5, MODEL_WIDTH), F32)], axis=0)


def turn(place, act, so_far, got, unit1, params, grad, block):
    rows, width = got.shape
    columns = act.shape[1]
    *refs, y_last = block
    return run(
        functools.partial(turn_kernel, y_last=y_last),
        "turn",
        [
            (place, "smem"),
            (act, "vmem"),
            (so_far, "vmem"),
            (got, "vmem"),
            (unit1, "vmem"),
            (params, "vmem"),
            (grad, "vmem"),
        ]
        + [(r, "any") for r in refs],
        [((rows, width), BF16), ((rows, width), F32), ((rows, width), BF16), ((8, width), F32)],
        [pltpu.VMEM((width, columns), BF16), pltpu.SemaphoreType.DMA((8,))],
        flops=2 * rows * columns * width,
        moved=10 * 2**20,
        limit=8,
    )


def raise_back_kernel(place, own, other, slope, w0, w1, grad_up, sums, whole, sems, *, y_last):
    for copy in fetch(eight(place, (w0, w1, y_last)), whole, sems):
        copy.wait()
    rows = own.shape[0]
    step = 256
    total = jnp.zeros((1, slope.shape[1]), F32)
    for side in range(2):
        source = own if side == 0 else other
        for i in range(rows // step):
            out = slice(side * rows + i * step, side * rows + (i + 1) * step)
            value = mxu(source[i * step : (i + 1) * step, :], whole[...], NN)
            low = (value * slope[out, :].astype(F32)).astype(BF16)
            grad_up[out, :] = low
            total += down_sum(low.astype(F32))
    sums[...] = jnp.broadcast_to(total, sums.shape)


def raise_back(place, own, other, slope, block):
    rows, width = own.shape
    columns = slope.shape[1]
    *refs, y_last = block
    return run(
        functools.partial(raise_back_kernel, y_last=y_last),
        "raise_back",
        [(place, "smem"), (own, "vmem"), (other, "vmem"), (slope, "vmem")] + [(r, "any") for r in refs],
        [((2 * rows, columns), BF16), ((8, columns), F32)],
        [pltpu.VMEM((width, columns), BF16), pltpu.SemaphoreType.DMA((8,))],
        flops=4 * rows * columns * width,
        moved=8 * 2**20,
        limit=8,
    )


def outer_kernel(place, left_own, left_other, right_own, right_other, mine, theirs, whole, *, y_last):
    whole[...] = mxu(left_own[...], right_own[...], TN) + mxu(left_other[...], right_other[...], TN)
    split_rows(whole, mine, theirs, place, y_last)


def outer_joined_kernel(place, left_own, left_other, right, mine, theirs, whole, *, y_last):
    rows = left_own.shape[0]
    whole[...] = mxu(left_own[...], right[0:rows, :], TN) + mxu(left_other[...], right[rows:, :], TN)
    split_rows(whole, mine, theirs, place, y_last)


def outer(place, left_own, left_other, rights, name, y_last=True):
    rows, width = left_own.shape
    columns = rights[0].shape[1]
    return run(
        functools.partial(outer_kernel if len(rights) == 2 else outer_joined_kernel, y_last=y_last),
        name,
        [(place, "smem"), (left_own, "vmem"), (left_other, "vmem")] + [(r, "vmem") for r in rights],
        [((4, 96, columns), BF16), ((4, 96, columns), BF16)],
        [pltpu.VMEM((width, columns), F32)],
        flops=4 * rows * columns * width,
        moved=6 * 2**20,
        limit=12,
    )


def first_other_kernel(
    place, grad_a, grad_b, a0, a1, b0, b1, out, whole_a, whole_b, sems, *, orders
):
    copies = fetch(eight(place, (a0, a1, orders[0])), whole_a, sems.at[0])
    copies += fetch(eight(place, (b0, b1, orders[1])), whole_b, sems.at[1])
    for copy in copies:
        copy.wait()
    rows = out.shape[0]
    step = 256
    for i in range(rows // step):
        span = slice(rows + i * step, rows + (i + 1) * step)
        value = mxu(grad_a[span, :], whole_a[...], NT) + mxu(grad_b[span, :], whole_b[...], NT)
        out[i * step : (i + 1) * step, :] = value.astype(BF16)


def first_other(place, grad_a, grad_b, block_a, block_b):
    rows, columns = grad_a.shape
    refs = list(block_a[:-1]) + list(block_b[:-1])
    return run(
        functools.partial(first_other_kernel, orders=(block_a[-1], block_b[-1])),
        "first_other",
        [(place, "smem"), (grad_a, "vmem"), (grad_b, "vmem")] + [(r, "any") for r in refs],
        [((rows // 2, MODEL_WIDTH), BF16)],
        [pltpu.VMEM((MODEL_WIDTH, columns), BF16)] * 2 + [pltpu.SemaphoreType.DMA((2, 8))],
        flops=2 * rows * columns * MODEL_WIDTH,
        moved=6 * 2**20,
        limit=8,
    )[0]


def first_back_kernel(
    place,
    grad_a,
    grad_b,
    got,
    grad_second,
    unit1,
    scale1,
    params,
    a0,
    a1,
    b0,
    b1,
    w0,
    w1,
    grad_first_in,
    mixed_keep,
    mixed_give,
    heads_keep,
    heads_give,
    sums,
    whole_a,
    whole_b,
    whole_o,
    low_all,
    heads_all,
    sems,
    sems_o,
    *,
    orders,
):
    x, core = place[0], place[2]
    copies = fetch(eight(place, (a0, a1, orders[0])), whole_a, sems.at[0])
    copies += fetch(eight(place, (b0, b1, orders[1])), whole_b, sems.at[1])
    copies += fetch_out(place, w0, w1, whole_o, sems_o)
    for copy in copies:
        copy.wait()
    rows = got.shape[0]
    step = 256
    total = [jnp.zeros((1, MODEL_WIDTH), F32)] * 3
    for i in range(rows // step):
        span = slice(i * step, (i + 1) * step)
        value = mxu(grad_a[span, :], whole_a[...], NT) + mxu(grad_b[span, :], whole_b[...], NT)
        dh = grad_second[span, :] + value + got[span, :].astype(F32)
        unit = unit1[span, :]
        back = unit_back(dh, unit, scale1[span, 0:1], params[4:5, :])
        grad_first_in[span, :] = back
        low = back.astype(BF16)
        low_all[span, :] = low
        total[0] += down_sum(low.astype(F32))
        total[1] += down_sum(unit * dh)
        total[2] += down_sum(dh)
        heads_all[span, :] = mxu(low, whole_o[...], NT).astype(BF16)
    sums[...] = jnp.concatenate(total + [jnp.zeros((5, MODEL_WIDTH), F32)], axis=0)
    half = lambda i: pl.ds(pl.multiple_of(i * HALF, 128), HALF)
    mixed_keep[...] = low_all[:, half(core)]
    mixed_give[...] = low_all[:, half(1 - core)]
    heads_keep[...] = heads_all[:, half(x)]
    heads_give[...] = heads_all[:, half(1 - x)]


def first_back(
    place, grad_a, grad_b, got, grad_second, unit1, scale1, params, block_a, block_b, out_blocks
):
    rows, width = got.shape
    columns = grad_a.shape[1]
    refs = list(block_a[:-1]) + list(block_b[:-1]) + list(out_blocks)
    return run(
        functools.partial(first_back_kernel, orders=(block_a[-1], block_b[-1])),
        "first_back",
        [
            (place, "smem"),
            (grad_a, "vmem"),
            (grad_b, "vmem"),
            (got, "vmem"),
            (grad_second, "vmem"),
            (unit1, "vmem"),
            (scale1, "vmem"),
            (params, "vmem"),
        ]
        + [(r, "any") for r in refs],
        [
            ((rows, width), F32),
            ((rows, HALF), BF16),
            ((rows, HALF), BF16),
            ((rows, HALF), BF16),
            ((rows, HALF), BF16),
            ((8, width), F32),
        ],
        [pltpu.VMEM((width, columns), BF16)] * 2
        + [pltpu.VMEM((width, width), BF16)]
        + [pltpu.VMEM((rows, width), BF16)] * 2
        + [pltpu.SemaphoreType.DMA((2, 8)), pltpu.SemaphoreType.DMA((16,))],
        flops=4 * rows * columns * width + 2 * rows * width * width,
        moved=12 * 2**20,
        limit=14,
    )


def enter_kernel(
    place,
    *refs,
):
    triples, refs = refs[:9], refs[9:]
    (
    grad_first_in,
    kinds,
    sums1,
    sums2,
    sums_a,
    sums_b,
    w0,
    w1,
    w2,
    w3,
    own,
    give,
    keep_cols,
    give_cols,
    small,
    whole,
    packed,
    sems,
    ) = refs
    x, core = place[0], place[2]
    copies = fetch(sixteen(place, (w0, w1, w2, w3)), whole, sems)
    rows = own.shape[0]
    for pair in range(3):
        for j in range(3):
            packed[:, j * HALF + pair * 128 : j * HALF + (pair + 1) * 128] = triples[3 * pair + j][...]
    packed[:, 3 * HALF :] = jnp.zeros((2 * rows, 128), BF16)
    keep_cols[...] = packed[:, pl.ds(pl.multiple_of(core * QCOLS, 128), QCOLS)]
    give_cols[...] = packed[:, pl.ds(pl.multiple_of((1 - core) * QCOLS, 128), QCOLS)]
    small[...] = jnp.zeros_like(small)
    at = pl.ds(pl.multiple_of(x * HALF, 128), HALF)
    small[0:1, at] = down_sum(packed[:, 0:HALF].astype(F32))
    small[1:2, at] = down_sum(packed[:, 2 * HALF : 3 * HALF].astype(F32))
    small[2:3, :] = sums1[0:1, :]
    small[3:4, :] = sums2[0:1, :]
    small[4:6, :] = sums1[1:3, :]
    small[6:8, :] = sums2[1:3, :]
    small[pl.ds(8 + 2 * core, 1), :] = sums_a[0:1, :]
    small[pl.ds(9 + 2 * core, 1), :] = sums_b[0:1, :]
    for copy in copies:
        copy.wait()
    lane_row = lax.broadcasted_iota(jnp.int32, (8, rows), 0)
    step = 256
    embed = jnp.zeros((8, MODEL_WIDTH), F32)
    for side in (1, 0):
        start = pl.multiple_of((x if side == 0 else 1 - x) * rows, 128)
        hot = jnp.where(kinds[:, pl.ds(start, rows)] == lane_row, 1.0, 0.0).astype(BF16)
        for i in range(rows // step):
            span = slice(i * step, (i + 1) * step)
            source = slice(side * rows + i * step, side * rows + (i + 1) * step)
            value = mxu(packed[source, 0 : 3 * HALF], whole[:, 0 : 3 * HALF], NT)
            if side == 0:
                value = value + grad_first_in[span, :]
                own[span, :] = value
            else:
                give[span, :] = value.astype(BF16)
            take = hot[:, span]
            for term in three_parts(value):
                embed += mxu(take, term, NN)
    small[12:15, :] = embed[0:3, :]


def enter(place, triples, grad_first_in, kinds, sums, blocks):
    rows, width = grad_first_in.shape
    return run(
        enter_kernel,
        "enter",
        [
            (place, "smem"),
        ]
        + [(r, "vmem") for triple in triples for r in triple]
        + [(grad_first_in, "vmem"), (kinds, "vmem")]
        + [(r, "vmem") for r in sums]
        + [(r, "any") for r in blocks],
        [
            ((rows, width), F32),
            ((rows, width), BF16),
            ((2 * rows, QCOLS), BF16),
            ((2 * rows, QCOLS), BF16),
            ((16, width), F32),
        ],
        [
            pltpu.VMEM((width, 3 * HALF + 128), BF16),
            pltpu.VMEM((2 * rows, 3 * HALF + 128), BF16),
            pltpu.SemaphoreType.DMA((16,)),
        ],
        flops=4 * rows * width * 3 * HALF,
        moved=12 * 2**20,
        limit=12,
    )


def outer_qkv_kernel(
    place, left_own, left_other, right_own, right_other, small_own, small_other, mine, theirs, whole
):
    whole[...] = mxu(left_own[...], right_own[...], TN) + mxu(left_other[...], right_other[...], TN)

    @pl.when(place[2] == 1)
    def _():
        small = small_own[...] + small_other[...]
        whole[:, QCOLS - 128 :] = jnp.concatenate(
            [small, jnp.zeros((128 - small.shape[0], small.shape[1]), F32)], axis=0
        ).T

    split_rows(whole, mine, theirs, place, True)


def outer_qkv(place, left_own, left_other, right_own, right_other, small_own, small_other):
    rows, width = left_own.shape
    return run(
        outer_qkv_kernel,
        "outer_qkv",
        [
            (place, "smem"),
            (left_own, "vmem"),
            (left_other, "vmem"),
            (right_own, "vmem"),
            (right_other, "vmem"),
            (small_own, "vmem"),
            (small_other, "vmem"),
        ],
        [((4, 96, QCOLS), BF16), ((4, 96, QCOLS), BF16)],
        [pltpu.VMEM((width, QCOLS), F32)],
        flops=4 * rows * QCOLS * width,
        moved=6 * 2**20,
        limit=14,
    )


def fold_kernel(mine, got, keep, send):
    half = mine.shape[0] // 2
    for i in range(2 * half):
        value = mine[i].astype(F32) + got[i].astype(F32)
        if i < half:
            keep[i] = value
        else:
            send[i - half] = value.astype(BF16)


def fold(mine, got):
    shape = (mine.shape[0] // 2,) + mine.shape[1:]
    return run(
        fold_kernel, "fold", [(mine, "vmem"), (got, "vmem")], [(shape, F32), (shape, BF16)], limit=4
    )


def settle_kernel(place, *refs):
    *sources, keep, near, far = refs
    core = place[2]
    own = pl.ds(pl.multiple_of(core * 48, 16), 48)
    other = pl.ds(pl.multiple_of((1 - core) * 48, 16), 48)
    column = 0
    for i in range(0, len(sources), 2):
        one, two = sources[i : i + 2]
        n = one.shape[2]
        lanes = slice(column, column + n)
        total = lambda rows: one[0, rows, :] + two[0, rows, :].astype(F32)
        mine = total(own)
        keep[:, lanes] = mine
        near[:, lanes] = mine.astype(BF16)
        far[:, lanes] = total(other).astype(BF16)
        column += n


def settle(place, groups):
    sources = [array for group in groups for array in group]
    n = sum(group[0].shape[2] for group in groups)
    return run(
        settle_kernel,
        "settle",
        [(place, "smem")] + [(array, "vmem") for array in sources],
        [((48, n), F32), ((48, n), BF16), ((48, n), BF16)],
        moved=2**20,
        limit=4,
    )


def step_of(weight, momentum, average, grad, rate, decay):
    moved = grad + decay * weight if decay else grad
    new_momentum = momentum_rate * momentum + moved
    new = weight - rate * (moved + momentum_rate * new_momentum)
    return grad, new, new_momentum, average_rate * average + (1.0 - average_rate) * new


def update_rest_kernel(
    place, mats, momentum, average, *refs, rate, groups
):
    sources, outs, work, sems = refs[: 4 * groups], refs[4 * groups : 4 * groups + 4], refs[-5:-1], refs[-1]
    width = MODEL_WIDTH
    base = 3 * width
    for whose in range(2):
        core = place[2] if whose == 0 else 1 - place[2]
        for g in range(groups):
            keep, from_seq, from_core, from_both = sources[4 * g : 4 * g + 4]
            if g == 0:
                parts = ((8 * width + 2 * core * QUARTER, QUARTER), (8 * width + (2 * core + 1) * QUARTER, QUARTER))
            else:
                parts = (
                    (4 * width + 2 * core * QUARTER, QUARTER),
                    (4 * width + (2 * core + 1) * QUARTER, QUARTER),
                    (3 * width + core * HALF, HALF),
                )
            column = 0
            for first, n in parts:
                lanes = slice(column, column + n)
                if whose == 0:
                    grad = keep[:, lanes] + from_seq[:, lanes].astype(F32)
                else:
                    grad = from_core[:, lanes].astype(F32) + from_both[:, lanes].astype(F32)
                at = pl.ds(pl.multiple_of(first, 128), n)
                results = step_of(mats[:, at], momentum[:, at], average[:, at], grad, rate, decay_rate)
                to = pl.ds(pl.multiple_of(first - base, 128), n)
                for ref, value in zip(work, results):
                    ref[:, to] = value
                column += n
    copies = []
    for i in range(4):
        copy = pltpu.make_async_copy(work[i], outs[i].at[:, pl.ds(base, work[i].shape[1])], sems.at[i])
        copy.start()
        copies.append(copy)
    for copy in copies:
        copy.wait()


def update_rest(place, mats, momentum, average, groups, rate):
    rows, columns = mats.shape
    sources = [array for group in groups for array in group]
    n = columns - 3 * MODEL_WIDTH
    return pl.pallas_call(
        functools.partial(update_rest_kernel, rate=rate, groups=len(groups)),
        in_specs=[pl.BlockSpec(memory_space=pltpu.SMEM)]
        + [pl.BlockSpec(memory_space=pltpu.VMEM)] * (3 + len(sources)),
        out_specs=[pl.BlockSpec(memory_space=pl.ANY)] * 4,
        out_shape=[jax.ShapeDtypeStruct((rows, columns), F32)] * 4,
        scratch_shapes=[pltpu.VMEM((rows, n), F32)] * 4 + [pltpu.SemaphoreType.DMA((4,))],
        compiler_params=pltpu.CompilerParams(vmem_limit_bytes=10 * 2**20),
        cost_estimate=pl.CostEstimate(flops=COST, bytes_accessed=0, transcendentals=0),
        name="update_rest",
    )(place, mats, momentum, average, *sources)


def update_heads_kernel(
    place,
    mats,
    momentum,
    average,
    keep,
    from_seq,
    from_core,
    from_both,
    s_value,
    s_momentum,
    s_average,
    a0,
    a1,
    a2,
    a3,
    o0,
    o1,
    o2,
    o3,
    s0,
    s1,
    s2,
    s3,
    w0,
    w1,
    w2,
    w3,
    grads,
    sems,
    *,
    rate,
):
    x, core = place[0], place[2]
    width = MODEL_WIDTH
    half = lambda c: pl.ds(pl.multiple_of(c * QCOLS, 128), QCOLS)
    grads[x, :, half(core)] = keep[...]
    grads[1 - x, :, half(core)] = from_seq[...].astype(F32)
    grads[x, :, half(1 - core)] = from_core[...].astype(F32)
    grads[1 - x, :, half(1 - core)] = from_both[...].astype(F32)
    work = (w0, w1, w2, w3)
    for j in range(3):
        for side in range(2):
            at = slice(j * width + side * HALF, j * width + (side + 1) * HALF)
            grad = grads[side, :, j * HALF : (j + 1) * HALF]
            results = step_of(mats[:, at], momentum[:, at], average[:, at], grad, rate, decay_rate)
            for ref, value in zip(work, results):
                ref[:, at] = value
    copies = []
    for i, out in enumerate((o0, o1, o2, o3)):
        copy = pltpu.make_async_copy(work[i], out.at[:, pl.ds(0, 3 * width)], sems.at[i])
        copy.start()
        copies.append(copy)
    small = (grads[0, :, 3 * HALF :] + grads[1, :, 3 * HALF :]).T[0:16]
    n = s_value.shape[0]
    results = step_of(s_value[...], s_momentum[...], s_average[...], small[0:n], rate, 0.0)
    for ref, value in zip((s0, s1, s2, s3), results):
        ref[...] = value
    for copy in copies:
        copy.wait()


def update_heads(place, mats, momentum, average, group, smalls, so_far, rate):
    rows, columns = mats.shape
    n = 3 * MODEL_WIDTH
    vmem = pl.BlockSpec(memory_space=pltpu.VMEM)
    anywhere = pl.BlockSpec(memory_space=pl.ANY)
    shape = smalls[0].shape
    return pl.pallas_call(
        functools.partial(update_heads_kernel, rate=rate),
        in_specs=[pl.BlockSpec(memory_space=pltpu.SMEM)] + [vmem] * 10 + [anywhere] * 4,
        out_specs=[anywhere] * 4 + [vmem] * 4,
        out_shape=[jax.ShapeDtypeStruct((rows, columns), F32)] * 4 + [jax.ShapeDtypeStruct(shape, F32)] * 4,
        scratch_shapes=[pltpu.VMEM((rows, n), F32)] * 4
        + [pltpu.VMEM((2, rows, 2 * QCOLS), F32), pltpu.SemaphoreType.DMA((4,))],
        input_output_aliases={11 + i: i for i in range(4)},
        compiler_params=pltpu.CompilerParams(vmem_limit_bytes=6 * 2**20),
        cost_estimate=pl.CostEstimate(flops=COST, bytes_accessed=0, transcendentals=0),
        name="update_heads",
    )(place, mats, momentum, average, *group, *smalls, *so_far)


SEQ_SWAP = [(0, 1), (1, 0)]
CORE_SWAP = [(i, i ^ 1) for i in range(16)]
Y_SWAP = [(i, i ^ 2) for i in range(16)]


def over_seq(value):
    return lax.ppermute(value, "seq", SEQ_SWAP)


def over_core(value):
    return lax.ppermute(value, "dp", CORE_SWAP)


def over_y(value):
    return lax.ppermute(value, "dp", Y_SWAP)


def over_z1(value):
    return lax.ppermute(value, "dp", [(i, i ^ 4) for i in range(16)])


def over_z2(value):
    return lax.ppermute(value, "dp", [(i, i ^ 8) for i in range(16)])


def over_both(value):
    return lax.ppermute(value, ("dp", "seq"), [(i, i ^ 3) for i in range(32)])


def ordered(flag, mine, theirs, axis):
    return jnp.where(
        flag == 0,
        jnp.concatenate([mine, theirs], axis=axis),
        jnp.concatenate([theirs, mine], axis=axis),
    )


def pin(value, *after):
    return lax.optimization_barrier((value, after))[0]


def exchange(place, groups):
    keep, near, far = settle(place, groups)
    return keep, over_seq(near), over_core(far), over_both(far)


def tuned(
    inputs,
    modality,
    key_valid_mask,
    output_gradient,
    mats,
    mats_momentum,
    mats_average,
    smalls,
    smalls_momentum,
    smalls_average,
):
    width = MODEL_WIDTH
    rows = inputs.shape[1]
    dp = lax.axis_index("dp")
    x = lax.axis_index("seq")
    core = dp % 2
    y = (dp // 2) % 2
    place = jnp.stack([x, y, core, dp // 4]).astype(jnp.int32)

    def both(mine, theirs):
        return jnp.concatenate([mine, theirs])

    att_own = pack_heads(place, mats, smalls.T)[None]
    att_two = both(att_own, over_z2(att_own))
    other_inputs = over_seq(inputs[0])
    keep, give = pack_rest(pin(place, att_own), mats)
    pair = ordered(core, keep, over_core(give), 0)[None]
    blocks = [pair[:, :, a:b] for a, b in zip(CUTS[:-1], CUTS[1:])]
    two0 = both(blocks[0], over_z2(pin(blocks[0], att_two)))
    att0 = both(att_two, over_z1(att_two))
    two1 = both(blocks[1], over_z2(blocks[1]))
    line0 = both(two0, over_z1(two0))
    att2 = over_y(att0)
    att = (att0, over_core(att0), att2, over_core(att2))
    up0 = (line0, over_y(pin(line0, att2)), True)

    x_low, x_in, qkv, masked, params = project(
        place, inputs[0], other_inputs, modality, key_valid_mask, att
    )
    line1 = both(two1, over_z1(two1))
    two2 = both(blocks[2], over_z2(pin(blocks[2], att0)))
    two3 = both(blocks[3], over_z2(pin(blocks[3], line0)))
    up1 = (line1, over_y(line1), True)
    heads, log_sum = attend(qkv, pin(masked, line1, two2))
    line2 = both(two2, over_z1(two2))
    down0 = (line2, over_y(line2), True)
    square3 = both(two3, over_y(two3))
    down1 = (square3, over_z1(square3), False)
    got_heads = over_seq(heads[rows:])
    out_mine = both(up0[0][:, :, QUARTER:], up0[1][:, :, QUARTER:])
    out_w = (out_mine, over_core(out_mine))
    out_low, unit1, scale1, first_low = mix(
        pin(place, line2), heads, got_heads, x_in, params, out_w
    )
    first_got = over_core(pin(first_low, up1[1]))
    act0, slope0 = raise_up(place, first_low, first_got, params, up0, 0)
    act1, slope1 = raise_up(pin(place, act0), first_low, first_got, params, up1, 1)
    so_far = lower(pin(place, act1), act0, down0)
    sum_got = over_core(lower_other(place, act1, so_far, down1))
    block_out, grad_second, grad_ffo, sums2 = turn(
        place, act1, so_far, sum_got, unit1, params, output_gradient[0], down1
    )

    ffo_got = over_core(grad_ffo)
    mine_d0, theirs_d0 = outer(place, grad_ffo, ffo_got, [act0], "outer_down")
    grad_up0, sums_up0 = raise_back(pin(place, mine_d0), grad_ffo, ffo_got, slope0, down0)
    grad_up1, sums_up1 = raise_back(place, grad_ffo, ffo_got, slope1, down1)
    mine_d1, theirs_d1 = outer(
        pin(place, grad_up1), grad_ffo, ffo_got, [act1], "outer_down", y_last=False
    )
    fold_d0 = fold(mine_d0, pin(over_y(theirs_d0), mine_d1))
    first_grad_got = over_core(first_other(pin(place, fold_d0), grad_up0, grad_up1, up0, up1))
    grad_first_in, mixed_keep, mixed_give, heads_keep, heads_give, sums1 = first_back(
        place, grad_up0, grad_up1, first_grad_got, grad_second, unit1, scale1, params, up0, up1, out_w
    )
    heads_got = over_seq(heads_give)
    mine_u0, theirs_u0 = outer(pin(place, sums1), first_low, first_got, [grad_up0], "outer_up")
    fold_d1 = fold(mine_d1, pin(over_z1(theirs_d1), mine_u0))
    mine_u1, theirs_u1 = outer(
        pin(place, fold_d1), first_low, first_got, [grad_up1], "outer_up"
    )
    last_d0 = fold(fold_d0[0], pin(over_z1(fold_d0[1]), mine_u1))
    mine_o, theirs_o = outer(
        pin(place, last_d0), out_low, over_core(out_low), [mixed_keep, over_core(mixed_give)], "outer_out"
    )
    grad_heads = jnp.concatenate([heads_keep, pin(heads_got, mine_o)], axis=0)
    triples = [attend_back(qkv, heads, grad_heads, log_sum, masked, 0)]
    fold_u0 = fold(mine_u0, pin(over_y(theirs_u0), triples[0]))
    last_d1 = fold(fold_d1[0], pin(over_y(fold_d1[1]), triples[0]))
    triples.append(attend_back(qkv, heads, grad_heads, log_sum, pin(masked, fold_u0, last_d1), 1))
    fold_u1 = fold(mine_u1, pin(over_y(theirs_u1), triples[1]))
    last_u0 = fold(fold_u0[0], pin(over_z1(fold_u0[1]), triples[1]))
    triples.append(attend_back(qkv, heads, grad_heads, log_sum, pin(masked, fold_u1, last_u0), 2))
    down_group = exchange(
        pin(place, triples[2]),
        [(last_d0[0], over_z2(last_d0[1])), (last_d1[0], over_z2(last_d1[1]))],
    )
    fold_o = fold(mine_o, pin(over_y(theirs_o), triples[2]))
    last_u1 = fold(fold_u1[0], pin(over_z1(fold_u1[1]), triples[2]))
    grad_x, give_x, keep_cols, give_cols, small = enter(
        pin(place, down_group[0], fold_o, last_u1),
        triples,
        grad_first_in,
        modality,
        (sums1, sums2, sums_up0, sums_up1),
        att,
    )
    last_o = fold(fold_o[0], pin(over_z1(fold_o[1]), small))
    input_grad = (grad_x + over_seq(give_x).astype(F32)).astype(BF16)[None]
    mine_q, theirs_q = outer_qkv(
        pin(place, last_o), x_low, over_core(x_low), keep_cols, over_core(give_cols), small, over_core(small)
    )
    fold_q = fold(mine_q, over_y(theirs_q))
    last_q = fold(fold_q[0], over_z1(fold_q[1]))

    rate = base_rate / math.sqrt(rows * lax.axis_size("dp") * lax.axis_size("seq"))
    up_group = exchange(
        place, [(v[0], over_z2(v[1])) for v in (last_u0, last_u1, last_o)]
    )
    so_far = update_rest(place, mats, mats_momentum, mats_average, [down_group, up_group], rate)
    *new, s_grad, s_value, s_momentum, s_average = update_heads(
        place,
        mats,
        mats_momentum,
        mats_average,
        exchange(place, [(last_q[0], over_z2(last_q[1]))]),
        (smalls.T, smalls_momentum.T, smalls_average.T),
        so_far,
        rate,
    )
    return (
        block_out[None],
        input_grad,
        *new,
        s_grad.T,
        s_grad[2],
        s_value.T,
        s_momentum.T,
        s_average.T,
    )


def solution(mesh):
    placed = (
        P("dp", "seq", None),
        P("dp", None),
        P("dp", None),
        P("dp", "seq", None),
        P("dp", None),
        P("dp", None),
        P("dp", None),
        P("dp", None),
        P("dp", None),
        P("dp", None),
    )
    plan = tuned if tuple(mesh.shape.values()) == (16, 2) else per_device
    return jax.shard_map(
        plan,
        mesh=mesh,
        in_specs=placed,
        out_specs=(
            P("dp", "seq", None),
            P("dp", "seq", None),
            P("dp", None),
            P("dp", None),
            P("dp", None),
            P("dp", None),
            P("dp", None),
            P("dp"),
            P("dp", None),
            P("dp", None),
            P("dp", None),
        ),
        check_vma=False,
    )
```

```python
import functools
import math

import jax
import jax.numpy as jnp
from jax import lax
from jax.experimental import pallas as pl
from jax.experimental.pallas import tpu as pltpu
from jax.sharding import PartitionSpec as P

MODEL_WIDTH = 768
H = 12
HD = 64
FF = 3072


epsilon = 1e-06
momentum_rate = 0.9
decay_rate = 0.0001
average_rate = 0.75
base_rate = 0.03
masked_score = -1e30


def product(left, right):
    return jnp.dot(left, right, preferred_element_type=jnp.float32)


def product_tn(left, right):
    return lax.dot_general(
        left, right, (((0,), (0,)), ((), ())), preferred_element_type=jnp.float32
    )


def product_nt(left, right):
    return lax.dot_general(
        left, right, (((1,), (1,)), ((), ())), preferred_element_type=jnp.float32
    )


def normalize(rows, gain, shift):
    mean = jnp.mean(rows, axis=-1, keepdims=True)
    centred = rows - mean
    spread = jnp.mean(centred * centred, axis=-1, keepdims=True)
    return centred * lax.rsqrt(spread + epsilon) * gain + shift


def exact_gelu(values):
    return jax.nn.gelu(values, approximate=False)


def head_scores(query_heads, key_heads, live_doc):
    scores = (
        jnp.einsum("qhe,khe->hqk", query_heads, key_heads, preferred_element_type=jnp.float32)
        * 0.125
    )
    return jnp.where(live_doc[None, None, :] > 0, scores, masked_score)


def attention_forward_pass(item):
    query_doc, keys_doc, values_doc, live_doc = item
    query_heads = query_doc.reshape(query_doc.shape[0], H, HD)
    key_heads = keys_doc.reshape(keys_doc.shape[0], H, HD)
    value_heads = values_doc.reshape(values_doc.shape[0], H, HD)
    scores = head_scores(query_heads, key_heads, live_doc)
    top = jnp.max(scores, axis=-1, keepdims=True)
    expd = jnp.exp(scores - top)
    total = jnp.sum(expd, axis=-1, keepdims=True)
    prob = (expd / total).astype(jnp.bfloat16)
    attention_output = jnp.einsum(
        "hqk,khe->qhe", prob, value_heads, preferred_element_type=jnp.float32
    )
    return (attention_output.reshape(query_doc.shape[0], H * HD), (top + jnp.log(total))[..., 0])


def attention_backward_pass(item):
    query_doc, keys_doc, values_doc, live_doc, log_sum_normalizer, grad_doc = item
    element_count = query_doc.shape[0]
    length = keys_doc.shape[0]
    query_heads = query_doc.reshape(element_count, H, HD)
    key_heads = keys_doc.reshape(length, H, HD)
    value_heads = values_doc.reshape(length, H, HD)
    grad_heads = grad_doc.reshape(element_count, H, HD)
    scores = head_scores(query_heads, key_heads, live_doc)
    prob = jnp.exp(scores - log_sum_normalizer[..., None])
    grad_prob = jnp.einsum(
        "qhe,khe->hqk", grad_heads, value_heads, preferred_element_type=jnp.float32
    )
    grad_values = jnp.einsum(
        "hqk,qhe->khe", prob.astype(jnp.bfloat16), grad_heads, preferred_element_type=jnp.float32
    )
    inner = jnp.sum(prob * grad_prob, axis=-1, keepdims=True)
    grad_scores = (prob * (grad_prob - inner)).astype(jnp.bfloat16)
    grad_query = (
        jnp.einsum("hqk,khe->qhe", grad_scores, key_heads, preferred_element_type=jnp.float32)
        * 0.125
    )
    grad_keys = (
        jnp.einsum("hqk,qhe->khe", grad_scores, query_heads, preferred_element_type=jnp.float32)
        * 0.125
    )
    return (
        grad_query.reshape(element_count, H * HD),
        grad_keys.reshape(length, H * HD),
        grad_values.reshape(length, H * HD),
    )


def per_device(
    inputs,
    modality,
    key_valid_mask,
    output_gradient,
    mats,
    mats_momentum,
    mats_average,
    smalls,
    smalls_momentum,
    smalls_average,
):
    docs, local_len, width = inputs.shape
    seq_len = modality.shape[1]
    rows = docs * local_len
    low_mats = mats.astype(jnp.bfloat16)
    w_qkv, w_out, w_up, w_down, whole_smalls = (
        lax.all_gather(low_mats[:, 0 : 3 * MODEL_WIDTH], "dp", axis=0, tiled=True),
        lax.all_gather(low_mats[:, 3 * MODEL_WIDTH : 4 * MODEL_WIDTH], "dp", axis=0, tiled=True),
        lax.all_gather(
            low_mats[:, 4 * MODEL_WIDTH : 4 * MODEL_WIDTH + FF], "dp", axis=0, tiled=True
        ),
        lax.all_gather(low_mats[:, 4 * MODEL_WIDTH + FF :], "dp", axis=0, tiled=True),
        lax.all_gather(smalls.astype(jnp.bfloat16), "dp", axis=0, tiled=True),
    )
    params = whole_smalls.astype(jnp.float32)
    bias_qkv = jnp.concatenate([params[:, 0], jnp.zeros_like(params[:, 0]), params[:, 1]])
    bias_up = jnp.transpose(params[:, 8:12]).reshape(FF)
    embed = jnp.transpose(whole_smalls[:, 12:15])
    leading_key = (jnp.arange(seq_len) == 0).astype(jnp.int32)
    valid_positions = jnp.maximum(key_valid_mask, leading_key[None, :])
    local_start = lax.axis_index("seq") * local_len
    local_modality = lax.dynamic_slice_in_dim(modality, local_start, local_len, 1)
    onehot = (
        local_modality.reshape(rows)[:, None] == jnp.arange(3, dtype=jnp.int32)[None, :]
    ).astype(jnp.bfloat16)
    x_in = inputs.reshape(rows, width).astype(jnp.float32) + product(onehot, embed)
    x_low = x_in.astype(jnp.bfloat16)
    qkv = (product(x_low, w_qkv) + bias_qkv).astype(jnp.bfloat16)
    query_documents = qkv[:, 0:width].reshape(docs, local_len, width)
    keys_local = qkv[:, width : 2 * width].reshape(docs, local_len, width)
    values_local = qkv[:, 2 * width :].reshape(docs, local_len, width)
    every_key, every_value = (
        lax.all_gather(keys_local, "seq", axis=1, tiled=True),
        lax.all_gather(values_local, "seq", axis=1, tiled=True),
    )
    attention_output, log_sum_normalizer = lax.map(
        attention_forward_pass, (query_documents, every_key, every_value, valid_positions)
    )
    out_low = attention_output.reshape(rows, width).astype(jnp.bfloat16)
    mixed = product(out_low, w_out) + params[:, 2]
    first_in = x_in + mixed
    first = normalize(first_in, params[:, 4], params[:, 5])
    first_low = first.astype(jnp.bfloat16)
    up = product(first_low, w_up) + bias_up
    act_low = exact_gelu(up).astype(jnp.bfloat16)
    ffo = product_nt(act_low, w_down) + params[:, 3]
    second_in = first + ffo
    result = normalize(second_in, params[:, 6], params[:, 7])
    block_out = result.astype(jnp.bfloat16).reshape(docs, local_len, width)
    w_qkv, w_out, w_up, w_down = (
        lax.all_gather(low_mats[:, 0 : 3 * MODEL_WIDTH], "dp", axis=0, tiled=True),
        lax.all_gather(low_mats[:, 3 * MODEL_WIDTH : 4 * MODEL_WIDTH], "dp", axis=0, tiled=True),
        lax.all_gather(
            low_mats[:, 4 * MODEL_WIDTH : 4 * MODEL_WIDTH + FF], "dp", axis=0, tiled=True
        ),
        lax.all_gather(low_mats[:, 4 * MODEL_WIDTH + FF :], "dp", axis=0, tiled=True),
    )
    grad_rows = output_gradient.reshape(rows, width).astype(jnp.float32)
    second_out, second_pull = jax.vjp(normalize, second_in, params[:, 6], params[:, 7])
    grad_second, grad_gain2, grad_shift2 = second_pull(grad_rows)
    grad_ffo = grad_second.astype(jnp.bfloat16)
    grad_bias_down = jnp.sum(grad_ffo.astype(jnp.float32), axis=0)
    grad_w_down = product_tn(grad_ffo, act_low)
    grad_act = product(grad_ffo, w_down)
    gelu_out, gelu_pull = jax.vjp(exact_gelu, up)
    grad_up = gelu_pull(grad_act)[0].astype(jnp.bfloat16)
    grad_bias_up = jnp.sum(grad_up.astype(jnp.float32), axis=0)
    grad_w_up = product_tn(first_low, grad_up)
    grad_first = grad_second + product_nt(grad_up, w_up)
    first_out, first_pull = jax.vjp(normalize, first_in, params[:, 4], params[:, 5])
    grad_first_in, grad_gain1, grad_shift1 = first_pull(grad_first)
    grad_mixed = grad_first_in.astype(jnp.bfloat16)
    grad_bias_out = jnp.sum(grad_mixed.astype(jnp.float32), axis=0)
    grad_w_out = product_tn(out_low, grad_mixed)
    grad_out = product_nt(grad_mixed, w_out).astype(jnp.bfloat16)
    output_gradient_documents = grad_out.reshape(docs, local_len, width)
    grad_query, grad_keys_all, grad_values_all = lax.map(
        attention_backward_pass,
        (
            query_documents,
            every_key,
            every_value,
            valid_positions,
            log_sum_normalizer,
            output_gradient_documents,
        ),
    )
    grad_keys, grad_values = (
        lax.psum_scatter(
            grad_keys_all.astype(jnp.bfloat16), "seq", scatter_dimension=1, tiled=True
        ).astype(jnp.float32),
        lax.psum_scatter(
            grad_values_all.astype(jnp.bfloat16), "seq", scatter_dimension=1, tiled=True
        ).astype(jnp.float32),
    )
    grad_qkv = jnp.concatenate(
        [
            grad_query.reshape(rows, width).astype(jnp.bfloat16),
            grad_keys.reshape(rows, width).astype(jnp.bfloat16),
            grad_values.reshape(rows, width).astype(jnp.bfloat16),
        ],
        axis=1,
    )
    grad_bias_qkv = jnp.sum(grad_qkv.astype(jnp.float32), axis=0)
    grad_w_qkv = product_tn(x_low, grad_qkv)
    grad_x_in = grad_first_in + product_nt(grad_qkv, w_qkv)
    grad_embed = lax.dot_general(
        onehot.astype(jnp.float32),
        grad_x_in,
        (((0,), (0,)), ((), ())),
        precision=lax.Precision.HIGHEST,
        preferred_element_type=jnp.float32,
    )
    input_grad = grad_x_in.astype(jnp.bfloat16).reshape(docs, local_len, width)
    grad_columns = jnp.stack(
        [
            grad_bias_qkv[0:width],
            grad_bias_qkv[2 * width :],
            grad_bias_out,
            grad_bias_down,
            grad_gain1,
            grad_shift1,
            grad_gain2,
            grad_shift2,
        ],
        axis=1,
    )
    grad_smalls = jnp.concatenate(
        [
            grad_columns,
            jnp.transpose(grad_bias_up.reshape(FF // width, width)),
            jnp.transpose(grad_embed),
        ],
        axis=1,
    )
    qkv_shard, out_shard, up_shard, down_shard, small_shard = (
        lax.psum_scatter(
            grad_w_qkv.astype(jnp.bfloat16), "dp", scatter_dimension=0, tiled=True
        ).astype(jnp.float32),
        lax.psum_scatter(
            grad_w_out.astype(jnp.bfloat16), "dp", scatter_dimension=0, tiled=True
        ).astype(jnp.float32),
        lax.psum_scatter(
            grad_w_up.astype(jnp.bfloat16), "dp", scatter_dimension=0, tiled=True
        ).astype(jnp.float32),
        lax.psum_scatter(
            grad_w_down.astype(jnp.bfloat16), "dp", scatter_dimension=0, tiled=True
        ).astype(jnp.float32),
        lax.psum_scatter(
            grad_smalls.astype(jnp.bfloat16), "dp", scatter_dimension=0, tiled=True
        ).astype(jnp.float32),
    )
    mats_shard = jnp.concatenate([qkv_shard, out_shard, up_shard, down_shard], axis=1)
    mats_grad, smalls_grad = (
        lax.psum(mats_shard.astype(jnp.bfloat16), "seq").astype(jnp.float32),
        lax.psum(small_shard.astype(jnp.bfloat16), "seq").astype(jnp.float32),
    )
    out_bias_grad = smalls_grad[:, 2]
    total_tokens = rows * lax.axis_size("dp") * lax.axis_size("seq")
    rate = base_rate / math.sqrt(total_tokens)
    decayed = mats_grad + decay_rate * mats
    new_mats_momentum = momentum_rate * mats_momentum + decayed
    new_mats = mats - rate * (decayed + momentum_rate * new_mats_momentum)
    new_mats_average = average_rate * mats_average + (1.0 - average_rate) * new_mats
    new_smalls_momentum = momentum_rate * smalls_momentum + smalls_grad
    new_smalls = smalls - rate * (smalls_grad + momentum_rate * new_smalls_momentum)
    new_smalls_average = average_rate * smalls_average + (1.0 - average_rate) * new_smalls
    return (
        block_out,
        input_grad,
        mats_grad,
        new_mats,
        new_mats_momentum,
        new_mats_average,
        smalls_grad,
        out_bias_grad,
        new_smalls,
        new_smalls_momentum,
        new_smalls_average,
    )


LN2 = math.log(2.0)
NT = (((1,), (1,)), ((), ()))
NN = (((1,), (0,)), ((), ()))
TN = (((0,), (0,)), ((), ()))
BF16 = jnp.bfloat16
F32 = jnp.float32
HALF = MODEL_WIDTH // 2
QUARTER = MODEL_WIDTH
SHARE = 0.5
TIMES = {
    "pack_heads": 1,
    "pack_rest": 1,
    "project": 1,
    "attend": 1,
    "mix": 2,
    "raise_up": 2,
    "lower": 3.5,
    "lower_other": 2.5,
    "turn": 4,
    "outer_down": 2,
    "outer_up": 2,
    "outer_out": 1.5,
    "outer_heads": 2.5,
    "raise_back": 2,
    "first_other": 2,
    "first_back": 1,
    "attend_back": 1,
    "enter": 5.5,
    "narrow": 0.7,
    "fold": 8,
    "fold_two": 0.6,
    "settle": 0.6,
    "join": 0.6,
    "update_rest": 3.5,
    "update_heads": 2.5,
}


def declared(name):
    return pl.CostEstimate(flops=int(SHARE * 1.15e9 * TIMES[name]), bytes_accessed=0, transcendentals=0)


def mxu(left, right, dims):
    return lax.dot_general(left, right, dims, preferred_element_type=jnp.float32)


def three_parts(value):
    high = value.astype(jnp.bfloat16)
    rest = value - high.astype(jnp.float32)
    middle = rest.astype(jnp.bfloat16)
    return high, middle, (rest - middle.astype(jnp.float32)).astype(jnp.bfloat16)


def run(kernel, name, ins, outs, scratch=(), limit=12):
    spaces = {"vmem": pltpu.VMEM, "any": pl.ANY, "hbm": pltpu.HBM, "smem": pltpu.SMEM}
    return pl.pallas_call(
        kernel,
        in_specs=[pl.BlockSpec(memory_space=spaces[kind]) for _, kind in ins],
        out_specs=[pl.BlockSpec(memory_space=pltpu.VMEM) for _ in outs],
        out_shape=[jax.ShapeDtypeStruct(shape, dtype) for shape, dtype in outs],
        scratch_shapes=list(scratch),
        compiler_params=pltpu.CompilerParams(vmem_limit_bytes=limit * 2**20),
        cost_estimate=declared(name),
        name=name,
    )(*[array for array, _ in ins])


def fetch(pieces, whole, sems):
    copies = []
    for i, (source, first) in enumerate(pieces):
        copy = pltpu.make_async_copy(source, whole.at[pl.ds(first, source.shape[0])], sems.at[i])
        copy.start()
        copies.append(copy)
    return copies


def xor2(z):
    return lax.rem(z + 2, 4)


def xor1(z):
    return z + 1 - 2 * lax.rem(z, 2)


def near_far(place, y_last):
    y, z = place[1], place[3]
    if y_last:
        line = (z, xor2(z), xor1(z), xor1(xor2(z)))
        return [(zz, y) for zz in line], [(zz, 1 - y) for zz in line]
    one, two = (z, xor2(z)), (xor1(z), xor1(xor2(z)))
    return [(zz, yy) for yy in (y, 1 - y) for zz in one], [(zz, yy) for yy in (y, 1 - y) for zz in two]


def eight(place, block):
    mine, theirs, y_last = block
    near, far = near_far(place, y_last)
    pieces = []
    for ref, chips in ((mine, near), (theirs, far)):
        for i, (zz, yy) in enumerate(chips):
            pieces.append((ref.at[i, :, pl.ds(0, QUARTER)], pl.multiple_of((2 * zz + yy) * 96, 32)))
    return pieces


def sixteen(place, blocks):
    core = place[2]
    near, far = near_far(place, True)
    pieces = []
    for chips, cc, ref in zip((near, near, far, far), (core, 1 - core, core, 1 - core), blocks):
        for i, (zz, yy) in enumerate(chips):
            pieces.append((ref.at[i], pl.multiple_of((zz * 4 + yy * 2 + cc) * 48, 16)))
    return pieces


def fetch_out(place, mine, theirs, whole, sems):
    core = place[2]
    near, far = near_far(place, True)
    copies = []
    for j, (ref, cc) in enumerate(((mine, core), (theirs, 1 - core))):
        for i, (zz, yy) in enumerate(near + far):
            row = pl.multiple_of((2 * zz + yy) * 96, 32)
            lanes = pl.ds(pl.multiple_of(cc * HALF, 128), HALF)
            copy = pltpu.make_async_copy(ref.at[i], whole.at[pl.ds(row, 96), lanes], sems.at[8 * j + i])
            copy.start()
            copies.append(copy)
    return copies


def split_rows(whole, mine, theirs, place, y_last):
    near, far = near_far(place, y_last)
    for ref, chips in ((mine, near), (theirs, far)):
        for i, (zz, yy) in enumerate(chips):
            row = pl.multiple_of((2 * zz + yy) * 96, 32)
            ref[i] = whole[pl.ds(row, 96), :].astype(ref.dtype)


def pack_heads_kernel(place, mats, smalls_t, block, wide, narrow, sems):
    width = MODEL_WIDTH
    copies = []
    for j in range(3):
        lanes = pl.ds(pl.multiple_of(j * width + place[0] * HALF, 128), HALF)
        copy = pltpu.make_async_copy(mats.at[:, lanes], wide.at[:, pl.ds(j * HALF, HALF)], sems.at[j])
        copy.start()
        copies.append(copy)
    narrow[...] = jnp.zeros_like(narrow)
    narrow[0:15, :] = smalls_t[...]
    block[:, 3 * HALF :] = narrow[...].T.astype(BF16)
    for copy in copies:
        copy.wait()
    block[:, 0 : 3 * HALF] = wide[...].astype(BF16)


def pack_heads(place, mats, smalls_t):
    rows = mats.shape[0]
    return run(
        pack_heads_kernel,
        "pack_heads",
        [(place, "smem"), (mats, "hbm"), (smalls_t, "vmem")],
        [((rows, 3 * HALF + 128), BF16)],
        [
            pltpu.VMEM((rows, 3 * HALF), F32),
            pltpu.VMEM((128, rows), F32),
            pltpu.SemaphoreType.DMA((3,)),
        ],
        limit=4,
    )[0]


CUTS = (0, QUARTER + HALF, 2 * QUARTER + HALF, 3 * QUARTER + HALF, 4 * QUARTER + HALF)


def pack_rest_kernel(place, mats, keep, give, wide, sem):
    width = MODEL_WIDTH
    copy = pltpu.make_async_copy(mats.at[:, pl.ds(3 * width, wide.shape[1])], wide, sem)
    copy.start()
    copy.wait()
    for core, ref in ((1 - place[2], give), (place[2], keep)):
        take = lambda first, n: wide[:, pl.ds(pl.multiple_of(first - 3 * width, 128), n)].astype(BF16)
        ref[:, 0:QUARTER] = take(4 * width + 2 * core * QUARTER, QUARTER)
        ref[:, QUARTER : CUTS[1]] = take(3 * width + core * HALF, HALF)
        ref[:, CUTS[1] : CUTS[2]] = take(4 * width + (2 * core + 1) * QUARTER, QUARTER)
        ref[:, CUTS[2] : CUTS[3]] = take(8 * width + 2 * core * QUARTER, QUARTER)
        ref[:, CUTS[3] :] = take(8 * width + (2 * core + 1) * QUARTER, QUARTER)


def pack_rest(place, mats):
    rows = mats.shape[0]
    return run(
        pack_rest_kernel,
        "pack_rest",
        [(place, "smem"), (mats, "hbm")],
        [((rows, CUTS[4]), BF16)] * 2,
        [pltpu.VMEM((rows, mats.shape[1] - 3 * MODEL_WIDTH), F32), pltpu.SemaphoreType.DMA(())],
        limit=4,
    )


def unit_rows(rows):
    mean = jnp.mean(rows, axis=-1, keepdims=True)
    centred = rows - mean
    spread = jnp.mean(centred * centred, axis=-1, keepdims=True)
    scale = lax.rsqrt(spread + epsilon)
    return centred * scale, scale


def unit_back(grad, unit, scale, gain):
    inner = grad * gain
    mean_one = jnp.mean(inner, axis=-1, keepdims=True)
    mean_two = jnp.mean(inner * unit, axis=-1, keepdims=True)
    return scale * (inner - mean_one - unit * mean_two)


def down_sum(value):
    return jnp.sum(value, axis=0, keepdims=True)


def project_kernel(
    place, own, other, kinds, mask, w0, w1, w2, w3, x_low, x_in, qkv, masked, params, whole, sems
):
    x, y, core = place[0], place[1], place[2]
    rows = own.shape[0]
    copies = fetch(sixteen(place, (w0, w1, w2, w3)), whole, sems)
    lane_row = lax.broadcasted_iota(jnp.int32, (8, rows), 0)
    lane = lax.broadcasted_iota(jnp.int32, (8, 128), 1)
    first_row = lax.broadcasted_iota(jnp.int32, (8, 128), 0)
    pick = jnp.where((lane == 0) & (first_row == 0), 1.0, 0.0).astype(BF16)
    position = lax.broadcasted_iota(jnp.int32, (1, rows), 1)
    for side in range(2):
        start = pl.multiple_of((x if side == 0 else 1 - x) * rows, 128)
        alive = (mask[:, pl.ds(start, rows)] > 0) | (position + start == 0)
        bias = jnp.where(alive, 0.0, masked_score)
        bias = jnp.where(lane_row == 0, jnp.broadcast_to(bias, (8, rows)), 0.0).astype(BF16)
        masked[side * rows : (side + 1) * rows, :] = mxu(bias, pick, TN).astype(BF16)
    for copy in copies:
        copy.wait()
    params[...] = whole[:, 3 * HALF :].astype(F32).T[0:16]
    embed = params[8:16, :].astype(BF16)
    start_q = pl.multiple_of(x * HALF, 128)
    bias_q = params[0:1, pl.ds(start_q, HALF)]
    bias_v = params[1:2, pl.ds(start_q, HALF)]
    scale = 0.125 / LN2
    step = 256
    for side in range(2):
        start = pl.multiple_of((x if side == 0 else 1 - x) * rows, 128)
        hot = jnp.where(kinds[:, pl.ds(start, rows)] + 4 == lane_row, 1.0, 0.0).astype(BF16)
        source = own if side == 0 else other
        for i in range(rows // step):
            span = slice(i * step, (i + 1) * step)
            out = slice(side * rows + i * step, side * rows + (i + 1) * step)
            value = source[span, :].astype(F32) + mxu(hot[:, span], embed, TN)
            if side == 0:
                x_in[span, :] = value
            low = value.astype(BF16)
            x_low[out, :] = low
            q = mxu(low, whole[:, 0:HALF], NN)
            qkv[out, 0:HALF] = ((q + bias_q) * scale).astype(BF16)
            k = mxu(low, whole[:, HALF : 2 * HALF], NN)
            qkv[out, HALF : 2 * HALF] = k.astype(BF16)
            v = mxu(low, whole[:, 2 * HALF : 3 * HALF], NN)
            qkv[out, 2 * HALF :] = (v + bias_v).astype(BF16)


def project(place, own, other, kinds, mask, blocks):
    rows, width = own.shape
    return run(
        project_kernel,
        "project",
        [(place, "smem"), (own, "vmem"), (other, "vmem"), (kinds, "vmem"), (mask, "vmem")]
        + [(block, "any") for block in blocks],
        [
            ((2 * rows, width), BF16),
            ((rows, width), F32),
            ((2 * rows, 3 * HALF), BF16),
            ((2 * rows, 128), BF16),
            ((16, width), F32),
            ((width, 3 * HALF + 128), BF16),
        ],
        [pltpu.SemaphoreType.DMA((16,))],
    )


def attend_kernel(qkv, masked_ref, out_ref, log_ref, *, block):
    length = qkv.shape[0]
    pairs = qkv.shape[1] // 384
    lane = lax.broadcasted_iota(jnp.int32, (1, 128), 1)
    one = jnp.broadcast_to(jnp.where(lane == 0, 1.0, 0.0).astype(jnp.bfloat16), (block, 128))
    ones = jnp.ones((length, 128), jnp.bfloat16)
    for pair in range(pairs):
        take = lambda j: slice((j * pairs + pair) * 128, (j * pairs + pair + 1) * 128)
        keys = jnp.concatenate([qkv[:, take(1)], masked_ref[...]], axis=1)
        values = jnp.concatenate([qkv[:, take(2)], ones], axis=1)
        for i in range(length // block):
            span = slice(i * block, (i + 1) * block)
            query = qkv[span, take(0)]
            outs, logs = [], []
            for head in range(2):
                here = (lane < 64) if head == 0 else (lane >= 64)
                only = jnp.where(here, query, jnp.zeros_like(query))
                scores = mxu(jnp.concatenate([only, one], axis=1), keys, NT)
                top = jnp.max(scores, axis=1, keepdims=True)
                weight = jnp.exp2(scores - top).astype(jnp.bfloat16)
                mixed = mxu(weight, values, NN)
                total = mixed[:, 128:]
                outs.append(mixed[:, :128] / total)
                logs.append(top + jnp.log2(total[:, 0:1]))
            out_ref[span, take(0)] = jnp.where(lane < 64, outs[0], outs[1]).astype(jnp.bfloat16)
            so_far = log_ref[span, :] if pair else jnp.zeros((block, 128), F32)
            both = jnp.where(lane == 2 * pair, logs[0], jnp.where(lane == 2 * pair + 1, logs[1], so_far))
            log_ref[span, :] = both


def attend(qkv, masked, block=256):
    length, columns = qkv.shape
    return run(
        functools.partial(attend_kernel, block=block),
        "attend",
        [(qkv, "vmem"), (masked, "vmem")],
        [((length, columns // 3), BF16), ((length, 128), F32)],
        limit=8,
    )


def attend_back_kernel(
    place, qkv, out, own_ref, got_ref, log_ref, masked_ref, out_ref, *refs, role, parts, block
):
    dk_sum, dv_sum = refs[-2], refs[-1]
    length, rows = qkv.shape[0], own_ref.shape[0]
    pairs = qkv.shape[1] // 384
    bf16 = jnp.bfloat16
    core = place[2]
    pair = (1 - core, core, 2)[role]
    take = lambda j: pl.ds(pl.multiple_of((j * pairs + pair) * 128, 128), 128)
    lane = lax.broadcasted_iota(jnp.int32, (1, 128), 1)
    ones = jnp.where((lane >= 1) & (lane <= 3), 1.0, 0.0).astype(bf16)
    masked = masked_ref[...]
    keys = jnp.concatenate(
        [qkv[:, take(1)], jnp.where(lane == 0, masked, jnp.broadcast_to(ones, masked.shape))], axis=1
    )
    three = jnp.broadcast_to(jnp.where(lane <= 2, 1.0, 0.0).astype(bf16), (length, 128))
    values = jnp.concatenate([qkv[:, take(2)], three], axis=1)
    keys_t = qkv[:, take(1)].T
    one = jnp.ones((block, 128), bf16)
    zero = jnp.zeros((block, 128), bf16)
    row = lax.broadcasted_iota(jnp.int32, (128, 1), 0)
    for i in range(length // block):
        span = slice(i * block, (i + 1) * block)
        at = i * block % rows
        query = qkv[span, take(0)]
        grad = (own_ref if i * block < rows else got_ref)[at : at + block, take(0)]
        both = grad.astype(jnp.float32) * out[span, take(0)].astype(jnp.float32)
        logs = log_ref[span, :]
        turned = []
        for head in range(2):
            here = (lane < 64) if head == 0 else (lane >= 64)
            inner = jnp.sum(jnp.where(here, both, 0.0), axis=1, keepdims=True)
            wide = lambda t: jnp.broadcast_to(t, (block, 128))
            log = jnp.sum(jnp.where(lane == 2 * pair + head, logs, 0.0), axis=1, keepdims=True)
            i0, i1, i2 = (wide(t) for t in three_parts(-inner))
            l0, l1, l2 = (wide(t) for t in three_parts(-log))
            query_h = jnp.where(here, query, zero)
            grad_h = jnp.where(here, grad, zero)
            tail_q = jnp.where(
                lane == 0,
                one,
                jnp.where(lane == 1, l0, jnp.where(lane == 2, l1, jnp.where(lane == 3, l2, zero))),
            )
            tail_g = jnp.where(lane == 0, i0, jnp.where(lane == 1, i1, jnp.where(lane == 2, i2, zero)))
            prob = jnp.exp2(mxu(keys, jnp.concatenate([query_h, tail_q], axis=1), NT))
            slope = mxu(values, jnp.concatenate([grad_h, tail_g], axis=1), NT)
            grad_scores = (prob * slope).astype(bf16)
            add_v = mxu(prob.astype(bf16), grad_h, NN)
            add_k = mxu(grad_scores, query_h, NN)
            if i == 0 and head == 0:
                dv_sum[...] = add_v
                dk_sum[...] = add_k
            else:
                dv_sum[...] += add_v
                dk_sum[...] += add_k
            turned.append(mxu(keys_t, grad_scores, NN))
        out_ref[span, 0:128] = (jnp.where(row < 64, turned[0], turned[1]) * 0.125).T.astype(bf16)
    out_ref[:, 128:256] = (dk_sum[...] * LN2).astype(bf16)
    out_ref[:, 256:384] = dv_sum[...].astype(bf16)
    if parts:
        keep_ref, give_ref, wide_ref = refs[:3]
        wide_ref[:, 0:384] = out_ref[...]
        wide_ref[:, 384:512] = jnp.zeros((length, 128), bf16)
        keep_ref[...] = wide_ref[:, pl.ds(pl.multiple_of(core * 256, 128), 256)]
        give_ref[...] = wide_ref[:, pl.ds(pl.multiple_of((1 - core) * 256, 128), 256)]


def attend_back(place, qkv, out, own, got, log_sum, masked, role, parts=False, block=512):
    length = qkv.shape[0]
    return run(
        functools.partial(attend_back_kernel, role=role, parts=parts, block=block),
        "attend_back",
        [(place, "smem")] + [(v, "vmem") for v in (qkv, out, own, got, log_sum, masked)],
        [((length, 384), BF16)] + [((length, 256), BF16)] * (2 * parts),
        [pltpu.VMEM((length, 512), BF16)] * parts + [pltpu.VMEM((length, 128), F32)] * 2,
        limit=14,
    )


def mix_kernel(
    place, heads, got, x_in, params, w0, w1, out_low, unit, scale, first_low, whole, sems
):
    x, y, core = place[0], place[1], place[2]
    rows = x_in.shape[0]
    copies = fetch_out(place, w0, w1, whole, sems)
    mine = pl.multiple_of(x * HALF, 128)
    theirs = pl.multiple_of((1 - x) * HALF, 128)
    out_low[:, pl.ds(mine, HALF)] = heads[0:rows, :]
    out_low[:, pl.ds(theirs, HALF)] = got[...]
    for copy in copies:
        copy.wait()
    step = 256
    for i in range(rows // step):
        span = slice(i * step, (i + 1) * step)
        mixed = mxu(out_low[span, :], whole[...], NN) + params[2:3, :]
        ones, size = unit_rows(x_in[span, :] + mixed)
        unit[span, :] = ones
        scale[span, :] = jnp.broadcast_to(size, (step, 128))
        first_low[span, :] = (ones * params[4:5, :] + params[5:6, :]).astype(BF16)


def mix(place, heads, got, x_in, params, blocks):
    rows, width = x_in.shape
    return run(
        mix_kernel,
        "mix",
        [(place, "smem"), (heads, "vmem"), (got, "vmem"), (x_in, "vmem"), (params, "vmem")]
        + [(block, "any") for block in blocks],
        [
            ((rows, width), BF16),
            ((rows, width), F32),
            ((rows, 128), F32),
            ((rows, width), BF16),
            ((width, width), BF16),
        ],
        [pltpu.SemaphoreType.DMA((16,))],
    )


def gelu_and_slope(up):
    size = jnp.abs(up)
    t = 1.0 / (1.0 + (0.3275911 * math.sqrt(0.5)) * size)
    bell = jnp.exp(-0.5 * up * up)
    poly = t * (
        0.5 * 0.254829592
        + t
        * (
            0.5 * -0.284496736
            + t * (0.5 * 1.421413741 + t * (0.5 * -1.453152027 + t * (0.5 * 1.061405429)))
        )
    )
    tail = poly * bell
    below = jnp.where(up < 0, tail, 1.0 - tail)
    return up * below, below + up * bell * (1.0 / math.sqrt(2.0 * math.pi))


def up_kernel(place, own, other, params, w0, w1, act, slope, whole, sems, *, which, y_last):
    core = place[2]
    rows = own.shape[0]
    for copy in fetch(eight(place, (w0, w1, y_last)), whole, sems):
        copy.wait()
    bias = params[pl.ds(8 + 2 * core + which, 1), :]
    step = 128
    for side in range(2):
        source = own if side == 0 else other
        for i in range(rows // step):
            out = slice(side * rows + i * step, side * rows + (i + 1) * step)
            up = mxu(source[i * step : (i + 1) * step, :], whole[...], NN) + bias
            value, change = gelu_and_slope(up)
            act[out, :] = value.astype(BF16)
            slope[out, :] = change.astype(BF16)


def raise_up(place, own, other, params, block, which):
    rows, width = own.shape
    *refs, y_last = block
    return run(
        functools.partial(up_kernel, which=which, y_last=y_last),
        "raise_up",
        [(place, "smem"), (own, "vmem"), (other, "vmem"), (params, "vmem")] + [(r, "any") for r in refs],
        [((2 * rows, QUARTER), BF16), ((2 * rows, QUARTER), BF16), ((width, QUARTER), BF16)],
        [pltpu.SemaphoreType.DMA((8,))],
        limit=8,
    )


def lower_kernel(place, act, w0, w1, out, whole, sems, *, y_last):
    for copy in fetch(eight(place, (w0, w1, y_last)), whole, sems):
        copy.wait()
    step = 256
    for i in range(act.shape[0] // step):
        span = slice(i * step, (i + 1) * step)
        out[span, :] = mxu(act[span, :], whole[...], NT)


def lower(place, act, block):
    rows, columns = act.shape
    *refs, y_last = block
    return run(
        functools.partial(lower_kernel, y_last=y_last),
        "lower",
        [(place, "smem"), (act, "vmem")] + [(r, "any") for r in refs],
        [((rows, MODEL_WIDTH), F32), ((MODEL_WIDTH, columns), BF16)],
        [pltpu.SemaphoreType.DMA((8,))],
        limit=8,
    )


def lower_other_kernel(place, act, so_far, w0, w1, out, whole, sems, *, y_last):
    for copy in fetch(eight(place, (w0, w1, y_last)), whole, sems):
        copy.wait()
    rows = out.shape[0]
    step = 256
    for i in range(rows // step):
        span = slice(rows + i * step, rows + (i + 1) * step)
        value = so_far[span, :] + mxu(act[span, :], whole[...], NT)
        out[i * step : (i + 1) * step, :] = value.astype(BF16)


def lower_other(place, act, so_far, block):
    rows, columns = act.shape
    *refs, y_last = block
    return run(
        functools.partial(lower_other_kernel, y_last=y_last),
        "lower_other",
        [(place, "smem"), (act, "vmem"), (so_far, "vmem")] + [(r, "any") for r in refs],
        [((rows // 2, MODEL_WIDTH), BF16), ((MODEL_WIDTH, columns), BF16)],
        [pltpu.SemaphoreType.DMA((8,))],
        limit=8,
    )


def turn_kernel(
    place,
    act,
    so_far,
    got,
    unit1,
    params,
    grad,
    whole,
    block_out,
    grad_second,
    grad_low,
    sums,
):
    rows = got.shape[0]
    step = 128
    total = [jnp.zeros((1, MODEL_WIDTH), F32)] * 3
    for i in range(rows // step):
        span = slice(i * step, (i + 1) * step)
        first = unit1[span, :] * params[4:5, :] + params[5:6, :]
        value = so_far[span, :] + mxu(act[span, :], whole[...], NT) + got[span, :].astype(F32)
        unit, scale = unit_rows(first + (value + params[3:4, :]))
        block_out[span, :] = (unit * params[6:7, :] + params[7:8, :]).astype(BF16)
        dy = grad[span, :].astype(F32)
        back = unit_back(dy, unit, scale, params[6:7, :])
        grad_second[span, :] = back
        low = back.astype(BF16)
        grad_low[span, :] = low
        total[0] += down_sum(low.astype(F32))
        total[1] += down_sum(unit * dy)
        total[2] += down_sum(dy)
    sums[...] = jnp.concatenate(total + [jnp.zeros((5, MODEL_WIDTH), F32)], axis=0)


def turn(place, act, so_far, got, unit1, params, grad, weight):
    rows, width = got.shape
    return run(
        turn_kernel,
        "turn",
        [
            (place, "smem"),
            (act, "vmem"),
            (so_far, "vmem"),
            (got, "vmem"),
            (unit1, "vmem"),
            (params, "vmem"),
            (grad, "vmem"),
            (weight, "vmem"),
        ],
        [((rows, width), BF16), ((rows, width), F32), ((rows, width), BF16), ((8, width), F32)],
        limit=8,
    )


def raise_back_kernel(place, own, other, slope, whole, grad_up, sums):
    rows = own.shape[0]
    step = 256
    total = jnp.zeros((1, slope.shape[1]), F32)
    for side in range(2):
        source = own if side == 0 else other
        for i in range(rows // step):
            out = slice(side * rows + i * step, side * rows + (i + 1) * step)
            value = mxu(source[i * step : (i + 1) * step, :], whole[...], NN)
            low = (value * slope[out, :].astype(F32)).astype(BF16)
            grad_up[out, :] = low
            total += down_sum(low.astype(F32))
    sums[...] = jnp.broadcast_to(total, sums.shape)


def raise_back(place, own, other, slope, weight):
    rows, width = own.shape
    columns = slope.shape[1]
    return run(
        raise_back_kernel,
        "raise_back",
        [(place, "smem"), (own, "vmem"), (other, "vmem"), (slope, "vmem"), (weight, "vmem")],
        [((2 * rows, columns), BF16), ((8, columns), F32)],
        limit=8,
    )


def outer_kernel(place, left_own, left_other, right_own, right_other, mine, theirs, whole, *, y_last):
    whole[...] = mxu(left_own[...], right_own[...], TN) + mxu(left_other[...], right_other[...], TN)
    split_rows(whole, mine, theirs, place, y_last)


def outer_joined_kernel(place, left_own, left_other, right, mine, theirs, whole, *, y_last):
    rows = left_own.shape[0]
    whole[...] = mxu(left_own[...], right[0:rows, :], TN) + mxu(left_other[...], right[rows:, :], TN)
    split_rows(whole, mine, theirs, place, y_last)


def outer(place, left_own, left_other, rights, name, y_last=True):
    rows, width = left_own.shape
    columns = rights[0].shape[1]
    return run(
        functools.partial(outer_kernel if len(rights) == 2 else outer_joined_kernel, y_last=y_last),
        name,
        [(place, "smem"), (left_own, "vmem"), (left_other, "vmem")] + [(r, "vmem") for r in rights],
        [((4, 96, columns), BF16), ((4, 96, columns), BF16)],
        [pltpu.VMEM((width, columns), F32)],
        limit=12,
    )


def first_other_kernel(place, grad_a, grad_b, whole_a, whole_b, out):
    rows = out.shape[0]
    step = 256
    for i in range(rows // step):
        span = slice(rows + i * step, rows + (i + 1) * step)
        value = mxu(grad_a[span, :], whole_a[...], NT) + mxu(grad_b[span, :], whole_b[...], NT)
        out[i * step : (i + 1) * step, :] = value.astype(BF16)


def first_other(place, grad_a, grad_b, weight_a, weight_b):
    rows, columns = grad_a.shape
    return run(
        first_other_kernel,
        "first_other",
        [(place, "smem")] + [(r, "vmem") for r in (grad_a, grad_b, weight_a, weight_b)],
        [((rows // 2, MODEL_WIDTH), BF16)],
        limit=8,
    )[0]


def first_back_kernel(
    place,
    grad_a,
    grad_b,
    got,
    grad_second,
    unit1,
    scale1,
    params,
    whole_a,
    whole_b,
    whole_o,
    grad_first_in,
    mixed_keep,
    mixed_give,
    heads_keep,
    heads_give,
    sums,
    low_all,
    heads_all,
):
    x, core = place[0], place[2]
    rows = got.shape[0]
    step = 256
    total = [jnp.zeros((1, MODEL_WIDTH), F32)] * 3
    for i in range(rows // step):
        span = slice(i * step, (i + 1) * step)
        value = mxu(grad_a[span, :], whole_a[...], NT) + mxu(grad_b[span, :], whole_b[...], NT)
        dh = grad_second[span, :] + value + got[span, :].astype(F32)
        unit = unit1[span, :]
        back = unit_back(dh, unit, scale1[span, 0:1], params[4:5, :])
        grad_first_in[span, :] = back
        low = back.astype(BF16)
        low_all[span, :] = low
        total[0] += down_sum(low.astype(F32))
        total[1] += down_sum(unit * dh)
        total[2] += down_sum(dh)
        heads_all[span, :] = mxu(low, whole_o[...], NT).astype(BF16)
    sums[...] = jnp.concatenate(total + [jnp.zeros((5, MODEL_WIDTH), F32)], axis=0)
    half = lambda i: pl.ds(pl.multiple_of(i * HALF, 128), HALF)
    mixed_keep[...] = low_all[:, half(core)]
    mixed_give[...] = low_all[:, half(1 - core)]
    heads_keep[...] = heads_all[:, half(x)]
    heads_give[...] = heads_all[:, half(1 - x)]


def first_back(place, *arrays):
    rows, width = arrays[2].shape
    return run(
        first_back_kernel,
        "first_back",
        [(place, "smem")] + [(r, "vmem") for r in arrays],
        [
            ((rows, width), F32),
            ((rows, HALF), BF16),
            ((rows, HALF), BF16),
            ((rows, HALF), BF16),
            ((rows, HALF), BF16),
            ((8, width), F32),
        ],
        [pltpu.VMEM((rows, width), BF16)] * 2,
        limit=10,
    )


def enter_kernel(
    place, d_give, d_keep, d_last, grad_first_in, kinds, sums1, sums2, sums_a, sums_b, whole, own, give, small
):
    x, core = place[0], place[2]
    rows = own.shape[0]
    pairs = ((d_give, 1 - core), (d_keep, core), (d_last, 2))
    small[...] = jnp.zeros_like(small)
    for ref, pair in pairs:
        at = pl.ds(pl.multiple_of(x * HALF + pair * 128, 128), 128)
        small[0:1, at] = down_sum(ref[:, 0:128].astype(F32))
        small[1:2, at] = down_sum(ref[:, 256:384].astype(F32))
    small[2:3, :] = sums1[0:1, :]
    small[3:4, :] = sums2[0:1, :]
    small[4:6, :] = sums1[1:3, :]
    small[6:8, :] = sums2[1:3, :]
    small[pl.ds(8 + 2 * core, 1), :] = sums_a[0:1, :]
    small[pl.ds(9 + 2 * core, 1), :] = sums_b[0:1, :]
    weights = []
    for _, pair in pairs:
        tiles = [whole[:, pl.ds(pl.multiple_of(j * HALF + pair * 128, 128), 128)] for j in range(3)]
        weights.append(jnp.concatenate(tiles, axis=1))
    lane_row = lax.broadcasted_iota(jnp.int32, (8, rows), 0)
    step = 256
    embed = jnp.zeros((8, MODEL_WIDTH), F32)
    for side in (1, 0):
        start = pl.multiple_of((x if side == 0 else 1 - x) * rows, 128)
        hot = jnp.where(kinds[:, pl.ds(start, rows)] == lane_row, 1.0, 0.0).astype(BF16)
        for i in range(rows // step):
            span = slice(i * step, (i + 1) * step)
            source = slice(side * rows + i * step, side * rows + (i + 1) * step)
            value = sum(mxu(ref[source, :], weight, NT) for (ref, _), weight in zip(pairs, weights))
            if side == 0:
                value = value + grad_first_in[span, :]
                own[span, :] = value
            else:
                give[span, :] = value.astype(BF16)
            take = hot[:, span]
            for term in three_parts(value):
                embed += mxu(take, term, NN)
    small[12:15, :] = embed[0:3, :]


def enter(place, *arrays):
    rows, width = arrays[3].shape
    return run(
        enter_kernel,
        "enter",
        [(place, "smem")] + [(r, "vmem") for r in arrays],
        [((rows, width), F32), ((rows, width), BF16), ((16, width), F32)],
        limit=12,
    )


def narrow_kernel(place, own, other, mine, theirs, whole):
    small = own[...] + other[...]
    rest = jnp.zeros((128 - small.shape[0], small.shape[1]), F32)
    whole[...] = jnp.concatenate([small, rest], axis=0).T
    split_rows(whole, mine, theirs, place, True)


def narrow(place, own, other):
    return run(
        narrow_kernel,
        "narrow",
        [(place, "smem"), (own, "vmem"), (other, "vmem")],
        [((4, 96, 128), BF16)] * 2,
        [pltpu.VMEM((own.shape[1], 128), F32)],
        limit=4,
    )


def fold_kernel(mine, got, keep, send):
    half = mine.shape[0] // 2
    for i in range(2 * half):
        value = mine[i].astype(F32) + got[i].astype(F32)
        if i < half:
            keep[i] = value
        else:
            send[i - half] = value.astype(BF16)


def fold(mine, got):
    shape = (mine.shape[0] // 2,) + mine.shape[1:]
    return run(
        fold_kernel,
        "fold",
        [(mine, "vmem"), (got, "vmem")],
        [(shape, F32), (shape, BF16)],
        limit=4,
    )


def fold_two_kernel(mine_a, got_a, mine_b, got_b, keep, send):
    n = mine_a.shape[2]
    for i in range(4):
        for mine, got, lanes in ((mine_a, got_a, slice(0, n)), (mine_b, got_b, slice(n, keep.shape[2]))):
            value = mine[i].astype(F32) + got[i].astype(F32)
            if i < 2:
                keep[i, :, lanes] = value
            else:
                send[i - 2, :, lanes] = value.astype(BF16)


def fold_two(mine_a, got_a, mine_b, got_b):
    shape = (2, 96, mine_a.shape[2] + mine_b.shape[2])
    return run(
        fold_two_kernel,
        "fold_two",
        [(v, "vmem") for v in (mine_a, got_a, mine_b, got_b)],
        [(shape, F32), (shape, BF16)],
        limit=4,
    )


def settle_kernel(place, *refs):
    *sources, keep, send = refs
    core = place[2]
    column = 0
    for i in range(0, len(sources), 2):
        one, two = sources[i : i + 2]
        n = one.shape[2]
        lanes = slice(column, column + n)
        for j, whose in enumerate((core, 1 - core)):
            rows = pl.ds(pl.multiple_of(whose * 48, 16), 48)
            value = one[0, rows, :] + two[0, rows, :].astype(F32)
            keep[j, :, lanes] = value
            send[j, :, lanes] = value.astype(BF16)
        column += n


def settle(place, groups):
    sources = [array for group in groups for array in group]
    n = sum(group[0].shape[2] for group in groups)
    return run(
        settle_kernel,
        "settle",
        [(place, "smem")] + [(array, "vmem") for array in sources],
        [((2, 48, n), F32), ((2, 48, n), BF16)],
        limit=4,
    )


def join_kernel(keep, got, near, far):
    near[...] = keep[0] + got[0].astype(F32)
    far[...] = (keep[1] + got[1].astype(F32)).astype(BF16)


def join(keep, got):
    shape = keep.shape[1:]
    return run(join_kernel, "join", [(keep, "vmem"), (got, "vmem")], [(shape, F32), (shape, BF16)], limit=4)


def step_of(weight, momentum, average, grad, rate, decay):
    moved = grad + decay * weight if decay else grad
    new_momentum = momentum_rate * momentum + moved
    new = weight - rate * (moved + momentum_rate * new_momentum)
    return grad, new, new_momentum, average_rate * average + (1.0 - average_rate) * new


def update_rest_kernel(
    place, mats, momentum, average, *refs, rate, groups
):
    sources, outs, work, sems = refs[: 2 * groups], refs[2 * groups : 2 * groups + 4], refs[-5:-1], refs[-1]
    width = MODEL_WIDTH
    base = 3 * width
    for whose in range(2):
        core = place[2] if whose == 0 else 1 - place[2]
        for g in range(groups):
            source = sources[2 * g + whose]
            if g == 0:
                parts = ((8 * width + 2 * core * QUARTER, QUARTER), (8 * width + (2 * core + 1) * QUARTER, QUARTER))
            else:
                parts = (
                    (4 * width + 2 * core * QUARTER, QUARTER),
                    (4 * width + (2 * core + 1) * QUARTER, QUARTER),
                    (3 * width + core * HALF, HALF),
                )
            column = 0
            for first, n in parts:
                lanes = slice(column, column + n)
                grad = source[:, lanes].astype(F32)
                at = pl.ds(pl.multiple_of(first, 128), n)
                results = step_of(mats[:, at], momentum[:, at], average[:, at], grad, rate, decay_rate)
                to = pl.ds(pl.multiple_of(first - base, 128), n)
                for ref, value in zip(work, results):
                    ref[:, to] = value
                column += n
    copies = []
    for i in range(4):
        copy = pltpu.make_async_copy(work[i], outs[i].at[:, pl.ds(base, work[i].shape[1])], sems.at[i])
        copy.start()
        copies.append(copy)
    for copy in copies:
        copy.wait()


def update_rest(place, mats, momentum, average, groups, rate):
    rows, columns = mats.shape
    sources = [array for group in groups for array in group]
    n = columns - 3 * MODEL_WIDTH
    return pl.pallas_call(
        functools.partial(update_rest_kernel, rate=rate, groups=len(groups)),
        in_specs=[pl.BlockSpec(memory_space=pltpu.SMEM)]
        + [pl.BlockSpec(memory_space=pltpu.VMEM)] * (3 + len(sources)),
        out_specs=[pl.BlockSpec(memory_space=pl.ANY)] * 4,
        out_shape=[jax.ShapeDtypeStruct((rows, columns), F32)] * 4,
        scratch_shapes=[pltpu.VMEM((rows, n), F32)] * 4 + [pltpu.SemaphoreType.DMA((4,))],
        compiler_params=pltpu.CompilerParams(vmem_limit_bytes=10 * 2**20),
        cost_estimate=declared("update_rest"),
        name="update_rest",
    )(place, mats, momentum, average, *sources)


def update_heads_kernel(
    place,
    mats,
    momentum,
    average,
    keep,
    from_seq,
    from_core,
    from_both,
    s_value,
    s_momentum,
    s_average,
    a0,
    a1,
    a2,
    a3,
    o0,
    o1,
    o2,
    o3,
    s0,
    s1,
    s2,
    s3,
    bias,
    w0,
    w1,
    w2,
    w3,
    grads,
    sems,
    *,
    rate,
):
    x, core = place[0], place[2]
    width = MODEL_WIDTH
    grads[x, core] = keep[0]
    grads[1 - x, core] = from_seq[...].astype(F32)
    grads[x, 1 - core] = from_core[...].astype(F32)
    grads[1 - x, 1 - core] = from_both[...].astype(F32)
    work = (w0, w1, w2, w3)
    last = ((0, 384), (0, 512), (1, 384))
    for j in range(3):
        for side in range(2):
            at = slice(j * width + side * HALF, j * width + (side + 1) * HALF)
            tiles = [grads[side, c, :, j * 128 : (j + 1) * 128] for c in range(2)]
            c, first = last[j]
            tiles.append(grads[side, c, :, first : first + 128])
            grad = jnp.concatenate(tiles, axis=1)
            results = step_of(mats[:, at], momentum[:, at], average[:, at], grad, rate, decay_rate)
            for ref, value in zip(work, results):
                ref[:, at] = value
    copies = []
    for i, out in enumerate((o0, o1, o2, o3)):
        copy = pltpu.make_async_copy(work[i], out.at[:, pl.ds(0, 3 * width)], sems.at[i])
        copy.start()
        copies.append(copy)
    small = (grads[x, core, :, 640:] + grads[1 - x, core, :, 640:]).T[0:16]
    n = s_value.shape[0]
    results = step_of(s_value[...], s_momentum[...], s_average[...], small[0:n], rate, 0.0)
    for ref, value in zip((s0, s1, s2, s3), results):
        ref[...] = value
    bias[...] = small[2:3]
    for copy in copies:
        copy.wait()


def update_heads(place, mats, momentum, average, group, smalls, so_far, rate):
    rows, columns = mats.shape
    n = 3 * MODEL_WIDTH
    vmem = pl.BlockSpec(memory_space=pltpu.VMEM)
    anywhere = pl.BlockSpec(memory_space=pl.ANY)
    shape = smalls[0].shape
    return pl.pallas_call(
        functools.partial(update_heads_kernel, rate=rate),
        in_specs=[pl.BlockSpec(memory_space=pltpu.SMEM)] + [vmem] * 10 + [anywhere] * 4,
        out_specs=[anywhere] * 4 + [vmem] * 5,
        out_shape=[jax.ShapeDtypeStruct((rows, columns), F32)] * 4 + [jax.ShapeDtypeStruct(shape, F32)] * 4
        + [jax.ShapeDtypeStruct((1, rows), F32)],
        scratch_shapes=[pltpu.VMEM((rows, n), F32)] * 4
        + [pltpu.VMEM((2, 2, rows, 768), F32), pltpu.SemaphoreType.DMA((4,))],
        input_output_aliases={11 + i: i for i in range(4)},
        compiler_params=pltpu.CompilerParams(vmem_limit_bytes=6 * 2**20),
        cost_estimate=declared("update_heads"),
        name="update_heads",
    )(place, mats, momentum, average, *group, *smalls, *so_far)


SEQ_SWAP = [(0, 1), (1, 0)]
CORE_SWAP = [(i, i ^ 1) for i in range(16)]
Y_SWAP = [(i, i ^ 2) for i in range(16)]


def over_seq(value):
    return lax.ppermute(value, "seq", SEQ_SWAP)


def over_core(value):
    return lax.ppermute(value, "dp", CORE_SWAP)


def over_y(value):
    return lax.ppermute(value, "dp", Y_SWAP)


def over_z1(value):
    return lax.ppermute(value, "dp", [(i, i ^ 4) for i in range(16)])


def over_z2(value):
    return lax.ppermute(value, "dp", [(i, i ^ 8) for i in range(16)])


def over_both(value):
    return lax.ppermute(value, ("dp", "seq"), [(i, i ^ 3) for i in range(32)])


def ordered(flag, mine, theirs, axis):
    return jnp.where(
        flag == 0,
        jnp.concatenate([mine, theirs], axis=axis),
        jnp.concatenate([theirs, mine], axis=axis),
    )


def pin(value, *after):
    return lax.optimization_barrier((value, after))[0]


def exchange(place, groups, *after):
    keep, send = settle(place, groups)
    near, far = join(keep, over_seq(pin(send, *after) if after else send))
    return near, over_core(far)


def tuned(
    inputs,
    modality,
    key_valid_mask,
    output_gradient,
    mats,
    mats_momentum,
    mats_average,
    smalls,
    smalls_momentum,
    smalls_average,
):
    width = MODEL_WIDTH
    rows = inputs.shape[1]
    dp = lax.axis_index("dp")
    x = lax.axis_index("seq")
    core = dp % 2
    y = (dp // 2) % 2
    place = jnp.stack([x, y, core, dp // 4]).astype(jnp.int32)

    def both(mine, theirs):
        return jnp.concatenate([mine, theirs])

    att_own = pack_heads(place, mats, smalls.T)[None]
    att_two = both(att_own, over_z2(att_own))
    other_inputs = over_seq(inputs[0])
    keep, give = pack_rest(pin(place, att_own), mats)
    pair = ordered(core, keep, over_core(pin(give, att_two)), 0)[None]
    blocks = [pair[:, :, a:b] for a, b in zip(CUTS[:-1], CUTS[1:])]
    att0 = both(att_two, over_z1(att_two))
    two0 = both(blocks[0], over_z2(blocks[0]))
    att2 = over_y(att0)
    att = (att0, over_core(att0), att2, over_core(att2))
    line0 = over_z1(pin(two0, other_inputs))

    x_low, x_in, qkv, masked, params, w_qkv = project(
        pin(place, two0), inputs[0], other_inputs, modality, key_valid_mask, att
    )
    line0 = both(two0, pin(line0, qkv))
    up0 = (line0, over_y(line0), True)
    got1 = over_z2(pin(blocks[1], qkv))
    heads, log_sum = attend(qkv, pin(masked, line0))
    got1 = pin(got1, heads)
    got_heads = over_seq(pin(heads, got1)[rows:])
    two1 = both(blocks[1], got1)
    line1 = both(two1, over_z1(two1))
    got_heads, y_0 = pin((got_heads, up0[1]), line1)
    x_got = over_core(pin(x_low, heads))
    two2 = both(blocks[2], pin(over_z2(pin(blocks[2], heads)), got_heads))
    out_mine = both(line0[:, :, QUARTER:], y_0[:, :, QUARTER:])
    out_w = (out_mine, over_core(out_mine))
    out_low, unit1, scale1, first_low, w_out = mix(
        pin(place, two2, x_got), heads, got_heads, x_in, params, out_w
    )
    up1 = (line1, over_y(line1), True)
    line2 = both(two2, over_z1(two2))
    two3 = both(blocks[3], over_z2(pin(blocks[3], line1)))
    down0 = (line2, over_y(line2), True)
    square3 = both(two3, over_y(two3))
    down1 = (square3, over_z1(square3), False)
    first_got = over_core(pin(first_low, up1[1], line2, two3))
    out_got = over_core(out_low)
    act0, slope0, w_up0 = raise_up(place, first_low, first_got, params, up0, 0)
    act1, slope1, w_up1 = raise_up(
        pin(place, act0, out_got), first_low, first_got, params, up1, 1
    )
    so_far, w_down0 = lower(pin(place, act1), act0, down0)
    sum_give, w_down1 = lower_other(place, act1, so_far, down1)
    block_out, grad_second, grad_ffo, sums2 = turn(
        place, act1, so_far, over_core(sum_give), unit1, params, output_gradient[0], w_down1
    )

    ffo_got = over_core(grad_ffo)
    mine_d0, theirs_d0 = outer(place, grad_ffo, ffo_got, [act0], "outer_down")
    got_d0 = over_y(theirs_d0)
    grad_up0, sums_up0 = raise_back(pin(place, mine_d0), grad_ffo, ffo_got, slope0, w_down0)
    grad_up1, sums_up1 = raise_back(pin(place, grad_up0), grad_ffo, ffo_got, slope1, w_down1)
    first_give = first_other(place, grad_up0, grad_up1, w_up0, w_up1)
    mine_d1, theirs_d1 = outer(pin(place, first_give), grad_ffo, ffo_got, [act1], "outer_down")
    got_d1 = over_y(theirs_d1)
    fold_d0 = fold(mine_d0, pin(got_d0, mine_d1))
    grad_first_in, mixed_keep, mixed_give, heads_keep, heads_give, sums1 = first_back(
        place,
        grad_up0,
        grad_up1,
        pin(over_core(first_give), fold_d0),
        grad_second,
        unit1,
        scale1,
        params,
        w_up0,
        w_up1,
        w_out,
    )
    heads_got = over_seq(heads_give)
    mixed_got = over_core(mixed_give)
    mine_u0, theirs_u0 = outer(pin(place, sums1), first_low, first_got, [grad_up0], "outer_up")
    got_u0 = over_y(theirs_u0)
    mine_u1, theirs_u1 = outer(
        pin(place, mine_u0), first_low, first_got, [grad_up1], "outer_up", y_last=False
    )
    got_u1 = over_z1(theirs_u1)
    last_d0 = fold(fold_d0[0], pin(over_z1(fold_d0[1]), mine_u1))
    got_last_d0 = over_z2(last_d0[1])
    mine_o, theirs_o = outer(pin(place, last_d0), out_low, out_got, [mixed_keep, mixed_got], "outer_out")
    got_o = over_y(theirs_o)

    def back(role, masked, parts=False):
        return attend_back(place, qkv, heads, heads_keep, heads_got, log_sum, masked, role, parts)

    fold_d1 = fold(mine_d1, pin(got_d1, mine_o))
    (d_give,) = back(0, pin(masked, fold_d1))
    got_d1, got_last_d0 = pin((over_z1(fold_d1[1]), got_last_d0), d_give)
    d_give = pin(d_give, got_d1, got_last_d0)
    last_d1 = fold(fold_d1[0], got_d1)
    d_got = over_core(d_give)
    (d_keep,) = back(1, pin(masked, last_d1))
    got_last_d1 = over_z2(last_d1[1])
    got_u0, got_u1, got_last_d1 = pin((got_u0, got_u1, got_last_d1), d_keep)
    d_keep = pin(d_keep, got_u0, got_u1, got_last_d1)
    fold_u0 = fold(mine_u0, got_u0)
    fold_u1 = fold(mine_u1, got_u1)
    mine_q, theirs_q = outer(
        pin(place, fold_u0, fold_u1), x_low, x_got, [d_keep, pin(d_got, fold_u0, fold_u1)], "outer_heads"
    )
    got_u0, got_u1, got_q = over_z1(fold_u0[1]), over_y(fold_u1[1]), over_y(theirs_q)
    down_keep, down_send = settle(
        pin(place, mine_q), [(last_d0[0], got_last_d0), (last_d1[0], got_last_d1)]
    )
    down_got = over_seq(down_send)
    last = back(2, pin(masked, down_keep), True)
    got_u0, got_o, down_got = pin((got_u0, got_o, down_got), last)
    d_last, cols_keep, cols_give = pin(last, got_u0, got_o, down_got)
    last_u0 = fold(fold_u0[0], got_u0)
    fold_o = fold(mine_o, got_o)
    cols_got = pin(over_core(cols_give), last_u0, fold_o)
    down_near, down_far = join(down_keep, down_got)
    down_group = (down_near, over_core(down_far))
    mine_r, theirs_r = outer(
        pin(place, last_u0, fold_o, down_near), x_low, x_got, [cols_keep, cols_got], "outer_heads"
    )
    got_r = over_y(theirs_r)
    grad_x, give_x, small = enter(
        pin(place, mine_r),
        d_give,
        d_keep,
        d_last,
        grad_first_in,
        modality,
        sums1,
        sums2,
        sums_up0,
        sums_up1,
        w_qkv,
    )
    got_last_u0 = over_z2(last_u0[1])
    got_o, got_u1, got_q, got_last_u0 = pin((over_z1(fold_o[1]), got_u1, got_q, got_last_u0), small)
    got_r = pin(got_r, small)
    small = pin(small, got_o, got_u1, got_q, got_last_u0, got_r, *down_group)
    last_u1 = fold(fold_u1[0], got_u1)
    last_o = fold(fold_o[0], got_o)
    fold_q = fold(mine_q, got_q)
    x_back = over_seq(give_x)
    mine_s, theirs_s = narrow(
        place, small, pin(over_core(small), last_u1, last_o, fold_q)
    )
    last_q = fold(fold_q[0], pin(over_z1(fold_q[1]), mine_s))
    fold_r = fold_two(mine_r, got_r, mine_s, over_y(theirs_s))
    last_r = fold(fold_r[0], over_z1(fold_r[1]))
    input_grad = (grad_x + x_back.astype(F32)).astype(BF16)[None]

    rate = base_rate / math.sqrt(rows * lax.axis_size("dp") * lax.axis_size("seq"))
    up_group = exchange(
        place,
        [(last_u0[0], got_last_u0), (last_u1[0], over_z2(last_u1[1])), (last_o[0], over_z2(last_o[1]))],
        input_grad,
    )
    heads_keep, heads_send = settle(place, [(v[0], over_z2(v[1])) for v in (last_q, last_r)])
    heads_send = pin(heads_send, up_group[0])
    near, far = heads_send[0], heads_send[1]
    heads_group = (heads_keep, over_seq(near), over_core(far), over_both(far))
    so_far = update_rest(place, mats, mats_momentum, mats_average, [down_group, up_group], rate)
    *new, s_grad, s_value, s_momentum, s_average, s_bias = update_heads(
        place,
        mats,
        mats_momentum,
        mats_average,
        heads_group,
        (smalls.T, smalls_momentum.T, smalls_average.T),
        so_far,
        rate,
    )
    return (
        block_out[None],
        input_grad,
        *new,
        s_grad.T,
        s_bias.reshape(-1),
        s_value.T,
        s_momentum.T,
        s_average.T,
    )


def solution(mesh):
    placed = (
        P("dp", "seq", None),
        P("dp", None),
        P("dp", None),
        P("dp", "seq", None),
        P("dp", None),
        P("dp", None),
        P("dp", None),
        P("dp", None),
        P("dp", None),
        P("dp", None),
    )
    plan = tuned if tuple(mesh.shape.values()) == (16, 2) else per_device
    return jax.shard_map(
        plan,
        mesh=mesh,
        in_specs=placed,
        out_specs=(
            P("dp", "seq", None),
            P("dp", "seq", None),
            P("dp", None),
            P("dp", None),
            P("dp", None),
            P("dp", None),
            P("dp", None),
            P("dp"),
            P("dp", None),
            P("dp", None),
            P("dp", None),
        ),
        check_vma=False,
    )
```

```python
import functools
import math

import jax
import jax.numpy as jnp
from jax import lax
from jax.experimental import pallas as pl
from jax.experimental.pallas import tpu as pltpu
from jax.sharding import PartitionSpec as P

MODEL_WIDTH = 768
H = 12
HD = 64
FF = 3072


epsilon = 1e-06
momentum_rate = 0.9
decay_rate = 0.0001
average_rate = 0.75
base_rate = 0.03
masked_score = -1e30


def product(left, right):
    return jnp.dot(left, right, preferred_element_type=jnp.float32)


def product_tn(left, right):
    return lax.dot_general(
        left, right, (((0,), (0,)), ((), ())), preferred_element_type=jnp.float32
    )


def product_nt(left, right):
    return lax.dot_general(
        left, right, (((1,), (1,)), ((), ())), preferred_element_type=jnp.float32
    )


def normalize(rows, gain, shift):
    mean = jnp.mean(rows, axis=-1, keepdims=True)
    centred = rows - mean
    spread = jnp.mean(centred * centred, axis=-1, keepdims=True)
    return centred * lax.rsqrt(spread + epsilon) * gain + shift


def exact_gelu(values):
    return jax.nn.gelu(values, approximate=False)


def head_scores(query_heads, key_heads, live_doc):
    scores = (
        jnp.einsum("qhe,khe->hqk", query_heads, key_heads, preferred_element_type=jnp.float32)
        * 0.125
    )
    return jnp.where(live_doc[None, None, :] > 0, scores, masked_score)


def attention_forward_pass(item):
    query_doc, keys_doc, values_doc, live_doc = item
    query_heads = query_doc.reshape(query_doc.shape[0], H, HD)
    key_heads = keys_doc.reshape(keys_doc.shape[0], H, HD)
    value_heads = values_doc.reshape(values_doc.shape[0], H, HD)
    scores = head_scores(query_heads, key_heads, live_doc)
    top = jnp.max(scores, axis=-1, keepdims=True)
    expd = jnp.exp(scores - top)
    total = jnp.sum(expd, axis=-1, keepdims=True)
    prob = (expd / total).astype(jnp.bfloat16)
    attention_output = jnp.einsum(
        "hqk,khe->qhe", prob, value_heads, preferred_element_type=jnp.float32
    )
    return (attention_output.reshape(query_doc.shape[0], H * HD), (top + jnp.log(total))[..., 0])


def attention_backward_pass(item):
    query_doc, keys_doc, values_doc, live_doc, log_sum_normalizer, grad_doc = item
    element_count = query_doc.shape[0]
    length = keys_doc.shape[0]
    query_heads = query_doc.reshape(element_count, H, HD)
    key_heads = keys_doc.reshape(length, H, HD)
    value_heads = values_doc.reshape(length, H, HD)
    grad_heads = grad_doc.reshape(element_count, H, HD)
    scores = head_scores(query_heads, key_heads, live_doc)
    prob = jnp.exp(scores - log_sum_normalizer[..., None])
    grad_prob = jnp.einsum(
        "qhe,khe->hqk", grad_heads, value_heads, preferred_element_type=jnp.float32
    )
    grad_values = jnp.einsum(
        "hqk,qhe->khe", prob.astype(jnp.bfloat16), grad_heads, preferred_element_type=jnp.float32
    )
    inner = jnp.sum(prob * grad_prob, axis=-1, keepdims=True)
    grad_scores = (prob * (grad_prob - inner)).astype(jnp.bfloat16)
    grad_query = (
        jnp.einsum("hqk,khe->qhe", grad_scores, key_heads, preferred_element_type=jnp.float32)
        * 0.125
    )
    grad_keys = (
        jnp.einsum("hqk,qhe->khe", grad_scores, query_heads, preferred_element_type=jnp.float32)
        * 0.125
    )
    return (
        grad_query.reshape(element_count, H * HD),
        grad_keys.reshape(length, H * HD),
        grad_values.reshape(length, H * HD),
    )


def per_device(
    inputs,
    modality,
    key_valid_mask,
    output_gradient,
    mats,
    mats_momentum,
    mats_average,
    smalls,
    smalls_momentum,
    smalls_average,
):
    docs, local_len, width = inputs.shape
    seq_len = modality.shape[1]
    rows = docs * local_len
    low_mats = mats.astype(jnp.bfloat16)
    w_qkv, w_out, w_up, w_down, whole_smalls = (
        lax.all_gather(low_mats[:, 0 : 3 * MODEL_WIDTH], "dp", axis=0, tiled=True),
        lax.all_gather(low_mats[:, 3 * MODEL_WIDTH : 4 * MODEL_WIDTH], "dp", axis=0, tiled=True),
        lax.all_gather(
            low_mats[:, 4 * MODEL_WIDTH : 4 * MODEL_WIDTH + FF], "dp", axis=0, tiled=True
        ),
        lax.all_gather(low_mats[:, 4 * MODEL_WIDTH + FF :], "dp", axis=0, tiled=True),
        lax.all_gather(smalls.astype(jnp.bfloat16), "dp", axis=0, tiled=True),
    )
    params = whole_smalls.astype(jnp.float32)
    bias_qkv = jnp.concatenate([params[:, 0], jnp.zeros_like(params[:, 0]), params[:, 1]])
    bias_up = jnp.transpose(params[:, 8:12]).reshape(FF)
    embed = jnp.transpose(whole_smalls[:, 12:15])
    leading_key = (jnp.arange(seq_len) == 0).astype(jnp.int32)
    valid_positions = jnp.maximum(key_valid_mask, leading_key[None, :])
    local_start = lax.axis_index("seq") * local_len
    local_modality = lax.dynamic_slice_in_dim(modality, local_start, local_len, 1)
    onehot = (
        local_modality.reshape(rows)[:, None] == jnp.arange(3, dtype=jnp.int32)[None, :]
    ).astype(jnp.bfloat16)
    x_in = inputs.reshape(rows, width).astype(jnp.float32) + product(onehot, embed)
    x_low = x_in.astype(jnp.bfloat16)
    qkv = (product(x_low, w_qkv) + bias_qkv).astype(jnp.bfloat16)
    query_documents = qkv[:, 0:width].reshape(docs, local_len, width)
    keys_local = qkv[:, width : 2 * width].reshape(docs, local_len, width)
    values_local = qkv[:, 2 * width :].reshape(docs, local_len, width)
    every_key, every_value = (
        lax.all_gather(keys_local, "seq", axis=1, tiled=True),
        lax.all_gather(values_local, "seq", axis=1, tiled=True),
    )
    attention_output, log_sum_normalizer = lax.map(
        attention_forward_pass, (query_documents, every_key, every_value, valid_positions)
    )
    out_low = attention_output.reshape(rows, width).astype(jnp.bfloat16)
    mixed = product(out_low, w_out) + params[:, 2]
    first_in = x_in + mixed
    first = normalize(first_in, params[:, 4], params[:, 5])
    first_low = first.astype(jnp.bfloat16)
    up = product(first_low, w_up) + bias_up
    act_low = exact_gelu(up).astype(jnp.bfloat16)
    ffo = product_nt(act_low, w_down) + params[:, 3]
    second_in = first + ffo
    result = normalize(second_in, params[:, 6], params[:, 7])
    block_out = result.astype(jnp.bfloat16).reshape(docs, local_len, width)
    w_qkv, w_out, w_up, w_down = (
        lax.all_gather(low_mats[:, 0 : 3 * MODEL_WIDTH], "dp", axis=0, tiled=True),
        lax.all_gather(low_mats[:, 3 * MODEL_WIDTH : 4 * MODEL_WIDTH], "dp", axis=0, tiled=True),
        lax.all_gather(
            low_mats[:, 4 * MODEL_WIDTH : 4 * MODEL_WIDTH + FF], "dp", axis=0, tiled=True
        ),
        lax.all_gather(low_mats[:, 4 * MODEL_WIDTH + FF :], "dp", axis=0, tiled=True),
    )
    grad_rows = output_gradient.reshape(rows, width).astype(jnp.float32)
    second_out, second_pull = jax.vjp(normalize, second_in, params[:, 6], params[:, 7])
    grad_second, grad_gain2, grad_shift2 = second_pull(grad_rows)
    grad_ffo = grad_second.astype(jnp.bfloat16)
    grad_bias_down = jnp.sum(grad_ffo.astype(jnp.float32), axis=0)
    grad_w_down = product_tn(grad_ffo, act_low)
    grad_act = product(grad_ffo, w_down)
    gelu_out, gelu_pull = jax.vjp(exact_gelu, up)
    grad_up = gelu_pull(grad_act)[0].astype(jnp.bfloat16)
    grad_bias_up = jnp.sum(grad_up.astype(jnp.float32), axis=0)
    grad_w_up = product_tn(first_low, grad_up)
    grad_first = grad_second + product_nt(grad_up, w_up)
    first_out, first_pull = jax.vjp(normalize, first_in, params[:, 4], params[:, 5])
    grad_first_in, grad_gain1, grad_shift1 = first_pull(grad_first)
    grad_mixed = grad_first_in.astype(jnp.bfloat16)
    grad_bias_out = jnp.sum(grad_mixed.astype(jnp.float32), axis=0)
    grad_w_out = product_tn(out_low, grad_mixed)
    grad_out = product_nt(grad_mixed, w_out).astype(jnp.bfloat16)
    output_gradient_documents = grad_out.reshape(docs, local_len, width)
    grad_query, grad_keys_all, grad_values_all = lax.map(
        attention_backward_pass,
        (
            query_documents,
            every_key,
            every_value,
            valid_positions,
            log_sum_normalizer,
            output_gradient_documents,
        ),
    )
    grad_keys, grad_values = (
        lax.psum_scatter(
            grad_keys_all.astype(jnp.bfloat16), "seq", scatter_dimension=1, tiled=True
        ).astype(jnp.float32),
        lax.psum_scatter(
            grad_values_all.astype(jnp.bfloat16), "seq", scatter_dimension=1, tiled=True
        ).astype(jnp.float32),
    )
    grad_qkv = jnp.concatenate(
        [
            grad_query.reshape(rows, width).astype(jnp.bfloat16),
            grad_keys.reshape(rows, width).astype(jnp.bfloat16),
            grad_values.reshape(rows, width).astype(jnp.bfloat16),
        ],
        axis=1,
    )
    grad_bias_qkv = jnp.sum(grad_qkv.astype(jnp.float32), axis=0)
    grad_w_qkv = product_tn(x_low, grad_qkv)
    grad_x_in = grad_first_in + product_nt(grad_qkv, w_qkv)
    grad_embed = lax.dot_general(
        onehot.astype(jnp.float32),
        grad_x_in,
        (((0,), (0,)), ((), ())),
        precision=lax.Precision.HIGHEST,
        preferred_element_type=jnp.float32,
    )
    input_grad = grad_x_in.astype(jnp.bfloat16).reshape(docs, local_len, width)
    grad_columns = jnp.stack(
        [
            grad_bias_qkv[0:width],
            grad_bias_qkv[2 * width :],
            grad_bias_out,
            grad_bias_down,
            grad_gain1,
            grad_shift1,
            grad_gain2,
            grad_shift2,
        ],
        axis=1,
    )
    grad_smalls = jnp.concatenate(
        [
            grad_columns,
            jnp.transpose(grad_bias_up.reshape(FF // width, width)),
            jnp.transpose(grad_embed),
        ],
        axis=1,
    )
    qkv_shard, out_shard, up_shard, down_shard, small_shard = (
        lax.psum_scatter(
            grad_w_qkv.astype(jnp.bfloat16), "dp", scatter_dimension=0, tiled=True
        ).astype(jnp.float32),
        lax.psum_scatter(
            grad_w_out.astype(jnp.bfloat16), "dp", scatter_dimension=0, tiled=True
        ).astype(jnp.float32),
        lax.psum_scatter(
            grad_w_up.astype(jnp.bfloat16), "dp", scatter_dimension=0, tiled=True
        ).astype(jnp.float32),
        lax.psum_scatter(
            grad_w_down.astype(jnp.bfloat16), "dp", scatter_dimension=0, tiled=True
        ).astype(jnp.float32),
        lax.psum_scatter(
            grad_smalls.astype(jnp.bfloat16), "dp", scatter_dimension=0, tiled=True
        ).astype(jnp.float32),
    )
    mats_shard = jnp.concatenate([qkv_shard, out_shard, up_shard, down_shard], axis=1)
    mats_grad, smalls_grad = (
        lax.psum(mats_shard.astype(jnp.bfloat16), "seq").astype(jnp.float32),
        lax.psum(small_shard.astype(jnp.bfloat16), "seq").astype(jnp.float32),
    )
    out_bias_grad = smalls_grad[:, 2]
    total_tokens = rows * lax.axis_size("dp") * lax.axis_size("seq")
    rate = base_rate / math.sqrt(total_tokens)
    decayed = mats_grad + decay_rate * mats
    new_mats_momentum = momentum_rate * mats_momentum + decayed
    new_mats = mats - rate * (decayed + momentum_rate * new_mats_momentum)
    new_mats_average = average_rate * mats_average + (1.0 - average_rate) * new_mats
    new_smalls_momentum = momentum_rate * smalls_momentum + smalls_grad
    new_smalls = smalls - rate * (smalls_grad + momentum_rate * new_smalls_momentum)
    new_smalls_average = average_rate * smalls_average + (1.0 - average_rate) * new_smalls
    return (
        block_out,
        input_grad,
        mats_grad,
        new_mats,
        new_mats_momentum,
        new_mats_average,
        smalls_grad,
        out_bias_grad,
        new_smalls,
        new_smalls_momentum,
        new_smalls_average,
    )


LN2 = math.log(2.0)
NT = (((1,), (1,)), ((), ()))
NN = (((1,), (0,)), ((), ()))
TN = (((0,), (0,)), ((), ()))
BF16 = jnp.bfloat16
F32 = jnp.float32
HALF = MODEL_WIDTH // 2
QUARTER = MODEL_WIDTH
SHARE = 0.5
TIMES = {
    "pack_heads": 1,
    "pack_rest": 1,
    "project": 1,
    "attend": 1,
    "mix": 2,
    "raise_up": 2,
    "lower": 3.5,
    "lower_other": 2.5,
    "turn": 4,
    "outer_down": 2,
    "outer_up": 2,
    "outer_out": 1.5,
    "outer_heads": 2.5,
    "raise_back": 2,
    "first_other": 2,
    "first_back": 1,
    "attend_back": 1,
    "enter": 5.5,
    "narrow": 0.7,
    "fold": 8,
    "fold_two": 0.6,
    "settle": 0.6,
    "join": 0.6,
    "update_rest": 3.5,
    "update_heads": 2.5,
}


def declared(name):
    return pl.CostEstimate(flops=int(SHARE * 1.15e9 * TIMES[name]), bytes_accessed=0, transcendentals=0)


def mxu(left, right, dims):
    return lax.dot_general(left, right, dims, preferred_element_type=jnp.float32)


def three_parts(value):
    high = value.astype(jnp.bfloat16)
    rest = value - high.astype(jnp.float32)
    middle = rest.astype(jnp.bfloat16)
    return high, middle, (rest - middle.astype(jnp.float32)).astype(jnp.bfloat16)


def run(kernel, name, ins, outs, scratch=(), limit=12):
    spaces = {"vmem": pltpu.VMEM, "smem": pltpu.SMEM}
    return pl.pallas_call(
        kernel,
        in_specs=[pl.BlockSpec(memory_space=spaces[kind]) for _, kind in ins],
        out_specs=[pl.BlockSpec(memory_space=pltpu.VMEM) for _ in outs],
        out_shape=[jax.ShapeDtypeStruct(shape, dtype) for shape, dtype in outs],
        scratch_shapes=list(scratch),
        compiler_params=pltpu.CompilerParams(vmem_limit_bytes=limit * 2**20),
        cost_estimate=declared(name),
        name=name,
    )(*[array for array, _ in ins])


def place_rows(pieces, whole):
    for value, first in pieces:
        whole[pl.ds(first, value.shape[0]), :] = value


def xor2(z):
    return lax.rem(z + 2, 4)


def xor1(z):
    return z + 1 - 2 * lax.rem(z, 2)


def near_far(place, y_last):
    y, z = place[1], place[3]
    if y_last:
        line = (z, xor2(z), xor1(z), xor1(xor2(z)))
        return [(zz, y) for zz in line], [(zz, 1 - y) for zz in line]
    one, two = (z, xor2(z)), (xor1(z), xor1(xor2(z)))
    return [(zz, yy) for yy in (y, 1 - y) for zz in one], [(zz, yy) for yy in (y, 1 - y) for zz in two]


def eight(place, block):
    mine, theirs, y_last = block
    near, far = near_far(place, y_last)
    pieces = []
    for ref, chips in ((mine, near), (theirs, far)):
        for i, (zz, yy) in enumerate(chips):
            pieces.append((ref[i, :, 0:QUARTER], pl.multiple_of((2 * zz + yy) * 96, 32)))
    return pieces


def sixteen(place, blocks):
    core = place[2]
    near, far = near_far(place, True)
    pieces = []
    for chips, cc, ref in zip((near, near, far, far), (core, 1 - core, core, 1 - core), blocks):
        for i, (zz, yy) in enumerate(chips):
            pieces.append((ref[i], pl.multiple_of((zz * 4 + yy * 2 + cc) * 48, 16)))
    return pieces


def place_out(place, mine, theirs, whole):
    core = place[2]
    near, far = near_far(place, True)
    for ref, cc in ((mine, core), (theirs, 1 - core)):
        lanes = pl.ds(pl.multiple_of(cc * HALF, 128), HALF)
        for i, (zz, yy) in enumerate(near + far):
            whole[pl.ds(pl.multiple_of((2 * zz + yy) * 96, 32), 96), lanes] = ref[i]


def split_rows(whole, mine, theirs, place, y_last):
    near, far = near_far(place, y_last)
    for ref, chips in ((mine, near), (theirs, far)):
        for i, (zz, yy) in enumerate(chips):
            row = pl.multiple_of((2 * zz + yy) * 96, 32)
            ref[i] = whole[pl.ds(row, 96), :].astype(ref.dtype)


def pack_heads_kernel(place, mats, smalls_t, block, narrow):
    width = MODEL_WIDTH
    narrow[...] = jnp.zeros_like(narrow)
    narrow[0:15, :] = smalls_t[...]
    block[:, 3 * HALF :] = narrow[...].T.astype(BF16)
    for j in range(3):
        lanes = pl.ds(pl.multiple_of(j * width + place[0] * HALF, 128), HALF)
        block[:, j * HALF : (j + 1) * HALF] = mats[:, lanes].astype(BF16)


def pack_heads(place, mats, smalls_t):
    rows = mats.shape[0]
    return run(
        pack_heads_kernel,
        "pack_heads",
        [(place, "smem"), (mats, "vmem"), (smalls_t, "vmem")],
        [((rows, 3 * HALF + 128), BF16)],
        [pltpu.VMEM((128, rows), F32)],
        limit=4,
    )[0]


CUTS = (0, QUARTER + HALF, 2 * QUARTER + HALF, 3 * QUARTER + HALF, 4 * QUARTER + HALF)


def pack_rest_kernel(place, mats, keep, give):
    width = MODEL_WIDTH
    for core, ref in ((1 - place[2], give), (place[2], keep)):
        take = lambda first, n: mats[:, pl.ds(pl.multiple_of(first, 128), n)].astype(BF16)
        ref[:, 0:QUARTER] = take(4 * width + 2 * core * QUARTER, QUARTER)
        ref[:, QUARTER : CUTS[1]] = take(3 * width + core * HALF, HALF)
        ref[:, CUTS[1] : CUTS[2]] = take(4 * width + (2 * core + 1) * QUARTER, QUARTER)
        ref[:, CUTS[2] : CUTS[3]] = take(8 * width + 2 * core * QUARTER, QUARTER)
        ref[:, CUTS[3] :] = take(8 * width + (2 * core + 1) * QUARTER, QUARTER)


def pack_rest(place, mats):
    rows = mats.shape[0]
    return run(
        pack_rest_kernel,
        "pack_rest",
        [(place, "smem"), (mats, "vmem")],
        [((rows, CUTS[4]), BF16)] * 2,
        limit=4,
    )


def unit_rows(rows):
    mean = jnp.mean(rows, axis=-1, keepdims=True)
    centred = rows - mean
    spread = jnp.mean(centred * centred, axis=-1, keepdims=True)
    scale = lax.rsqrt(spread + epsilon)
    return centred * scale, scale


def unit_back(grad, unit, scale, gain):
    inner = grad * gain
    mean_one = jnp.mean(inner, axis=-1, keepdims=True)
    mean_two = jnp.mean(inner * unit, axis=-1, keepdims=True)
    return scale * (inner - mean_one - unit * mean_two)


def down_sum(value):
    return jnp.sum(value, axis=0, keepdims=True)


def project_kernel(
    place, own, other, kinds, mask, w0, w1, w2, w3, x_low, x_in, qkv, masked, params, whole
):
    x, y, core = place[0], place[1], place[2]
    rows = own.shape[0]
    place_rows(sixteen(place, (w0, w1, w2, w3)), whole)
    lane_row = lax.broadcasted_iota(jnp.int32, (8, rows), 0)
    lane = lax.broadcasted_iota(jnp.int32, (8, 128), 1)
    first_row = lax.broadcasted_iota(jnp.int32, (8, 128), 0)
    pick = jnp.where((lane == 0) & (first_row == 0), 1.0, 0.0).astype(BF16)
    position = lax.broadcasted_iota(jnp.int32, (1, rows), 1)
    for side in range(2):
        start = pl.multiple_of((x if side == 0 else 1 - x) * rows, 128)
        alive = (mask[:, pl.ds(start, rows)] > 0) | (position + start == 0)
        bias = jnp.where(alive, 0.0, masked_score)
        bias = jnp.where(lane_row == 0, jnp.broadcast_to(bias, (8, rows)), 0.0).astype(BF16)
        masked[side * rows : (side + 1) * rows, :] = mxu(bias, pick, TN).astype(BF16)
    params[...] = whole[:, 3 * HALF :].astype(F32).T[0:16]
    embed = params[8:16, :].astype(BF16)
    start_q = pl.multiple_of(x * HALF, 128)
    bias_q = params[0:1, pl.ds(start_q, HALF)]
    bias_v = params[1:2, pl.ds(start_q, HALF)]
    scale = 0.125 / LN2
    step = 256
    for side in range(2):
        start = pl.multiple_of((x if side == 0 else 1 - x) * rows, 128)
        hot = jnp.where(kinds[:, pl.ds(start, rows)] + 4 == lane_row, 1.0, 0.0).astype(BF16)
        source = own if side == 0 else other
        for i in range(rows // step):
            span = slice(i * step, (i + 1) * step)
            out = slice(side * rows + i * step, side * rows + (i + 1) * step)
            value = source[span, :].astype(F32) + mxu(hot[:, span], embed, TN)
            if side == 0:
                x_in[span, :] = value
            low = value.astype(BF16)
            x_low[out, :] = low
            q = mxu(low, whole[:, 0:HALF], NN)
            qkv[out, 0:HALF] = ((q + bias_q) * scale).astype(BF16)
            k = mxu(low, whole[:, HALF : 2 * HALF], NN)
            qkv[out, HALF : 2 * HALF] = k.astype(BF16)
            v = mxu(low, whole[:, 2 * HALF : 3 * HALF], NN)
            qkv[out, 2 * HALF :] = (v + bias_v).astype(BF16)


def project(place, own, other, kinds, mask, blocks):
    rows, width = own.shape
    return run(
        project_kernel,
        "project",
        [(place, "smem"), (own, "vmem"), (other, "vmem"), (kinds, "vmem"), (mask, "vmem")]
        + [(block, "vmem") for block in blocks],
        [
            ((2 * rows, width), BF16),
            ((rows, width), F32),
            ((2 * rows, 3 * HALF), BF16),
            ((2 * rows, 128), BF16),
            ((16, width), F32),
            ((width, 3 * HALF + 128), BF16),
        ],
    )


def attend_kernel(qkv, masked_ref, out_ref, log_ref, *, block):
    length = qkv.shape[0]
    pairs = qkv.shape[1] // 384
    lane = lax.broadcasted_iota(jnp.int32, (1, 128), 1)
    one = jnp.broadcast_to(jnp.where(lane == 0, 1.0, 0.0).astype(jnp.bfloat16), (block, 128))
    ones = jnp.ones((length, 128), jnp.bfloat16)
    for pair in range(pairs):
        take = lambda j: slice((j * pairs + pair) * 128, (j * pairs + pair + 1) * 128)
        keys = jnp.concatenate([qkv[:, take(1)], masked_ref[...]], axis=1)
        values = jnp.concatenate([qkv[:, take(2)], ones], axis=1)
        for i in range(length // block):
            span = slice(i * block, (i + 1) * block)
            query = qkv[span, take(0)]
            outs, logs = [], []
            for head in range(2):
                here = (lane < 64) if head == 0 else (lane >= 64)
                only = jnp.where(here, query, jnp.zeros_like(query))
                scores = mxu(jnp.concatenate([only, one], axis=1), keys, NT)
                top = jnp.max(scores, axis=1, keepdims=True)
                weight = jnp.exp2(scores - top).astype(jnp.bfloat16)
                mixed = mxu(weight, values, NN)
                total = mixed[:, 128:]
                outs.append(mixed[:, :128] / total)
                logs.append(top + jnp.log2(total[:, 0:1]))
            out_ref[span, take(0)] = jnp.where(lane < 64, outs[0], outs[1]).astype(jnp.bfloat16)
            so_far = log_ref[span, :] if pair else jnp.zeros((block, 128), F32)
            both = jnp.where(lane == 2 * pair, logs[0], jnp.where(lane == 2 * pair + 1, logs[1], so_far))
            log_ref[span, :] = both


def attend(qkv, masked, block=256):
    length, columns = qkv.shape
    return run(
        functools.partial(attend_kernel, block=block),
        "attend",
        [(qkv, "vmem"), (masked, "vmem")],
        [((length, columns // 3), BF16), ((length, 128), F32)],
        limit=8,
    )


def attend_back_kernel(
    place, qkv, out, own_ref, got_ref, log_ref, masked_ref, out_ref, *refs, role, parts, block
):
    dk_sum, dv_sum = refs[-2], refs[-1]
    length, rows = qkv.shape[0], own_ref.shape[0]
    pairs = qkv.shape[1] // 384
    bf16 = jnp.bfloat16
    core = place[2]
    pair = (1 - core, core, 2)[role]
    take = lambda j: pl.ds(pl.multiple_of((j * pairs + pair) * 128, 128), 128)
    lane = lax.broadcasted_iota(jnp.int32, (1, 128), 1)
    ones = jnp.where((lane >= 1) & (lane <= 3), 1.0, 0.0).astype(bf16)
    masked = masked_ref[...]
    keys = jnp.concatenate(
        [qkv[:, take(1)], jnp.where(lane == 0, masked, jnp.broadcast_to(ones, masked.shape))], axis=1
    )
    three = jnp.broadcast_to(jnp.where(lane <= 2, 1.0, 0.0).astype(bf16), (length, 128))
    values = jnp.concatenate([qkv[:, take(2)], three], axis=1)
    keys_t = qkv[:, take(1)].T
    one = jnp.ones((block, 128), bf16)
    zero = jnp.zeros((block, 128), bf16)
    row = lax.broadcasted_iota(jnp.int32, (128, 1), 0)
    for i in range(length // block):
        span = slice(i * block, (i + 1) * block)
        at = i * block % rows
        query = qkv[span, take(0)]
        grad = (own_ref if i * block < rows else got_ref)[at : at + block, take(0)]
        both = grad.astype(jnp.float32) * out[span, take(0)].astype(jnp.float32)
        logs = log_ref[span, :]
        turned = []
        for head in range(2):
            here = (lane < 64) if head == 0 else (lane >= 64)
            inner = jnp.sum(jnp.where(here, both, 0.0), axis=1, keepdims=True)
            wide = lambda t: jnp.broadcast_to(t, (block, 128))
            log = jnp.sum(jnp.where(lane == 2 * pair + head, logs, 0.0), axis=1, keepdims=True)
            i0, i1, i2 = (wide(t) for t in three_parts(-inner))
            l0, l1, l2 = (wide(t) for t in three_parts(-log))
            query_h = jnp.where(here, query, zero)
            grad_h = jnp.where(here, grad, zero)
            tail_q = jnp.where(
                lane == 0,
                one,
                jnp.where(lane == 1, l0, jnp.where(lane == 2, l1, jnp.where(lane == 3, l2, zero))),
            )
            tail_g = jnp.where(lane == 0, i0, jnp.where(lane == 1, i1, jnp.where(lane == 2, i2, zero)))
            prob = jnp.exp2(mxu(keys, jnp.concatenate([query_h, tail_q], axis=1), NT))
            slope = mxu(values, jnp.concatenate([grad_h, tail_g], axis=1), NT)
            grad_scores = (prob * slope).astype(bf16)
            add_v = mxu(prob.astype(bf16), grad_h, NN)
            add_k = mxu(grad_scores, query_h, NN)
            if i == 0 and head == 0:
                dv_sum[...] = add_v
                dk_sum[...] = add_k
            else:
                dv_sum[...] += add_v
                dk_sum[...] += add_k
            turned.append(mxu(keys_t, grad_scores, NN))
        out_ref[span, 0:128] = (jnp.where(row < 64, turned[0], turned[1]) * 0.125).T.astype(bf16)
    out_ref[:, 128:256] = (dk_sum[...] * LN2).astype(bf16)
    out_ref[:, 256:384] = dv_sum[...].astype(bf16)
    if parts:
        keep_ref, give_ref, wide_ref = refs[:3]
        wide_ref[:, 0:384] = out_ref[...]
        wide_ref[:, 384:512] = jnp.zeros((length, 128), bf16)
        keep_ref[...] = wide_ref[:, pl.ds(pl.multiple_of(core * 256, 128), 256)]
        give_ref[...] = wide_ref[:, pl.ds(pl.multiple_of((1 - core) * 256, 128), 256)]


def attend_back(place, qkv, out, own, got, log_sum, masked, role, parts=False, block=512):
    length = qkv.shape[0]
    return run(
        functools.partial(attend_back_kernel, role=role, parts=parts, block=block),
        "attend_back",
        [(place, "smem")] + [(v, "vmem") for v in (qkv, out, own, got, log_sum, masked)],
        [((length, 384), BF16)] + [((length, 256), BF16)] * (2 * parts),
        [pltpu.VMEM((length, 512), BF16)] * parts + [pltpu.VMEM((length, 128), F32)] * 2,
        limit=14,
    )


def mix_kernel(
    place, heads, got, x_in, params, w0, w1, out_low, unit, scale, first_low, whole
):
    x, y, core = place[0], place[1], place[2]
    rows = x_in.shape[0]
    place_out(place, w0, w1, whole)
    mine = pl.multiple_of(x * HALF, 128)
    theirs = pl.multiple_of((1 - x) * HALF, 128)
    out_low[:, pl.ds(mine, HALF)] = heads[0:rows, :]
    out_low[:, pl.ds(theirs, HALF)] = got[...]
    step = 256
    for i in range(rows // step):
        span = slice(i * step, (i + 1) * step)
        mixed = mxu(out_low[span, :], whole[...], NN) + params[2:3, :]
        ones, size = unit_rows(x_in[span, :] + mixed)
        unit[span, :] = ones
        scale[span, :] = jnp.broadcast_to(size, (step, 128))
        first_low[span, :] = (ones * params[4:5, :] + params[5:6, :]).astype(BF16)


def mix(place, heads, got, x_in, params, blocks):
    rows, width = x_in.shape
    return run(
        mix_kernel,
        "mix",
        [(place, "smem"), (heads, "vmem"), (got, "vmem"), (x_in, "vmem"), (params, "vmem")]
        + [(block, "vmem") for block in blocks],
        [
            ((rows, width), BF16),
            ((rows, width), F32),
            ((rows, 128), F32),
            ((rows, width), BF16),
            ((width, width), BF16),
        ],
    )


def gelu_and_slope(up):
    size = jnp.abs(up)
    t = 1.0 / (1.0 + (0.3275911 * math.sqrt(0.5)) * size)
    bell = jnp.exp(-0.5 * up * up)
    poly = t * (
        0.5 * 0.254829592
        + t
        * (
            0.5 * -0.284496736
            + t * (0.5 * 1.421413741 + t * (0.5 * -1.453152027 + t * (0.5 * 1.061405429)))
        )
    )
    tail = poly * bell
    below = jnp.where(up < 0, tail, 1.0 - tail)
    return up * below, below + up * bell * (1.0 / math.sqrt(2.0 * math.pi))


def up_kernel(place, own, other, params, w0, w1, act, slope, whole, *, which, y_last):
    core = place[2]
    rows = own.shape[0]
    place_rows(eight(place, (w0, w1, y_last)), whole)
    bias = params[pl.ds(8 + 2 * core + which, 1), :]
    step = 128
    for side in range(2):
        source = own if side == 0 else other
        for i in range(rows // step):
            out = slice(side * rows + i * step, side * rows + (i + 1) * step)
            up = mxu(source[i * step : (i + 1) * step, :], whole[...], NN) + bias
            value, change = gelu_and_slope(up)
            act[out, :] = value.astype(BF16)
            slope[out, :] = change.astype(BF16)


def raise_up(place, own, other, params, block, which):
    rows, width = own.shape
    *refs, y_last = block
    return run(
        functools.partial(up_kernel, which=which, y_last=y_last),
        "raise_up",
        [(place, "smem"), (own, "vmem"), (other, "vmem"), (params, "vmem")] + [(r, "vmem") for r in refs],
        [((2 * rows, QUARTER), BF16), ((2 * rows, QUARTER), BF16), ((width, QUARTER), BF16)],
        limit=8,
    )


def lower_kernel(place, act, w0, w1, out, whole, *, y_last):
    place_rows(eight(place, (w0, w1, y_last)), whole)
    step = 256
    for i in range(act.shape[0] // step):
        span = slice(i * step, (i + 1) * step)
        out[span, :] = mxu(act[span, :], whole[...], NT)


def lower(place, act, block):
    rows, columns = act.shape
    *refs, y_last = block
    return run(
        functools.partial(lower_kernel, y_last=y_last),
        "lower",
        [(place, "smem"), (act, "vmem")] + [(r, "vmem") for r in refs],
        [((rows, MODEL_WIDTH), F32), ((MODEL_WIDTH, columns), BF16)],
        limit=8,
    )


def lower_other_kernel(place, act, so_far, w0, w1, out, whole, *, y_last):
    place_rows(eight(place, (w0, w1, y_last)), whole)
    rows = out.shape[0]
    step = 256
    for i in range(rows // step):
        span = slice(rows + i * step, rows + (i + 1) * step)
        value = so_far[span, :] + mxu(act[span, :], whole[...], NT)
        out[i * step : (i + 1) * step, :] = value.astype(BF16)


def lower_other(place, act, so_far, block):
    rows, columns = act.shape
    *refs, y_last = block
    return run(
        functools.partial(lower_other_kernel, y_last=y_last),
        "lower_other",
        [(place, "smem"), (act, "vmem"), (so_far, "vmem")] + [(r, "vmem") for r in refs],
        [((rows // 2, MODEL_WIDTH), BF16), ((MODEL_WIDTH, columns), BF16)],
        limit=8,
    )


def turn_kernel(
    place,
    act,
    so_far,
    got,
    unit1,
    params,
    grad,
    whole,
    block_out,
    grad_second,
    grad_low,
    sums,
):
    rows = got.shape[0]
    step = 128
    total = [jnp.zeros((1, MODEL_WIDTH), F32)] * 3
    for i in range(rows // step):
        span = slice(i * step, (i + 1) * step)
        first = unit1[span, :] * params[4:5, :] + params[5:6, :]
        value = so_far[span, :] + mxu(act[span, :], whole[...], NT) + got[span, :].astype(F32)
        unit, scale = unit_rows(first + (value + params[3:4, :]))
        block_out[span, :] = (unit * params[6:7, :] + params[7:8, :]).astype(BF16)
        dy = grad[span, :].astype(F32)
        back = unit_back(dy, unit, scale, params[6:7, :])
        grad_second[span, :] = back
        low = back.astype(BF16)
        grad_low[span, :] = low
        total[0] += down_sum(low.astype(F32))
        total[1] += down_sum(unit * dy)
        total[2] += down_sum(dy)
    sums[...] = jnp.concatenate(total + [jnp.zeros((5, MODEL_WIDTH), F32)], axis=0)


def turn(place, act, so_far, got, unit1, params, grad, weight):
    rows, width = got.shape
    return run(
        turn_kernel,
        "turn",
        [
            (place, "smem"),
            (act, "vmem"),
            (so_far, "vmem"),
            (got, "vmem"),
            (unit1, "vmem"),
            (params, "vmem"),
            (grad, "vmem"),
            (weight, "vmem"),
        ],
        [((rows, width), BF16), ((rows, width), F32), ((rows, width), BF16), ((8, width), F32)],
        limit=8,
    )


def raise_back_kernel(place, own, other, slope, whole, grad_up, sums):
    rows = own.shape[0]
    step = 256
    total = jnp.zeros((1, slope.shape[1]), F32)
    for side in range(2):
        source = own if side == 0 else other
        for i in range(rows // step):
            out = slice(side * rows + i * step, side * rows + (i + 1) * step)
            value = mxu(source[i * step : (i + 1) * step, :], whole[...], NN)
            low = (value * slope[out, :].astype(F32)).astype(BF16)
            grad_up[out, :] = low
            total += down_sum(low.astype(F32))
    sums[...] = jnp.broadcast_to(total, sums.shape)


def raise_back(place, own, other, slope, weight):
    rows, width = own.shape
    columns = slope.shape[1]
    return run(
        raise_back_kernel,
        "raise_back",
        [(place, "smem"), (own, "vmem"), (other, "vmem"), (slope, "vmem"), (weight, "vmem")],
        [((2 * rows, columns), BF16), ((8, columns), F32)],
        limit=8,
    )


def outer_kernel(place, left_own, left_other, right_own, right_other, mine, theirs, whole, *, y_last):
    whole[...] = mxu(left_own[...], right_own[...], TN) + mxu(left_other[...], right_other[...], TN)
    split_rows(whole, mine, theirs, place, y_last)


def outer_joined_kernel(place, left_own, left_other, right, mine, theirs, whole, *, y_last):
    rows = left_own.shape[0]
    whole[...] = mxu(left_own[...], right[0:rows, :], TN) + mxu(left_other[...], right[rows:, :], TN)
    split_rows(whole, mine, theirs, place, y_last)


def outer(place, left_own, left_other, rights, name, y_last=True):
    rows, width = left_own.shape
    columns = rights[0].shape[1]
    return run(
        functools.partial(outer_kernel if len(rights) == 2 else outer_joined_kernel, y_last=y_last),
        name,
        [(place, "smem"), (left_own, "vmem"), (left_other, "vmem")] + [(r, "vmem") for r in rights],
        [((4, 96, columns), BF16), ((4, 96, columns), BF16)],
        [pltpu.VMEM((width, columns), F32)],
        limit=12,
    )


def first_other_kernel(place, grad_a, grad_b, whole_a, whole_b, out):
    rows = out.shape[0]
    step = 256
    for i in range(rows // step):
        span = slice(rows + i * step, rows + (i + 1) * step)
        value = mxu(grad_a[span, :], whole_a[...], NT) + mxu(grad_b[span, :], whole_b[...], NT)
        out[i * step : (i + 1) * step, :] = value.astype(BF16)


def first_other(place, grad_a, grad_b, weight_a, weight_b):
    rows, columns = grad_a.shape
    return run(
        first_other_kernel,
        "first_other",
        [(place, "smem")] + [(r, "vmem") for r in (grad_a, grad_b, weight_a, weight_b)],
        [((rows // 2, MODEL_WIDTH), BF16)],
        limit=8,
    )[0]


def first_back_kernel(
    place,
    grad_a,
    grad_b,
    got,
    grad_second,
    unit1,
    scale1,
    params,
    whole_a,
    whole_b,
    whole_o,
    grad_first_in,
    mixed_keep,
    mixed_give,
    heads_keep,
    heads_give,
    sums,
    low_all,
    heads_all,
):
    x, core = place[0], place[2]
    rows = got.shape[0]
    step = 256
    total = [jnp.zeros((1, MODEL_WIDTH), F32)] * 3
    for i in range(rows // step):
        span = slice(i * step, (i + 1) * step)
        value = mxu(grad_a[span, :], whole_a[...], NT) + mxu(grad_b[span, :], whole_b[...], NT)
        dh = grad_second[span, :] + value + got[span, :].astype(F32)
        unit = unit1[span, :]
        back = unit_back(dh, unit, scale1[span, 0:1], params[4:5, :])
        grad_first_in[span, :] = back
        low = back.astype(BF16)
        low_all[span, :] = low
        total[0] += down_sum(low.astype(F32))
        total[1] += down_sum(unit * dh)
        total[2] += down_sum(dh)
        heads_all[span, :] = mxu(low, whole_o[...], NT).astype(BF16)
    sums[...] = jnp.concatenate(total + [jnp.zeros((5, MODEL_WIDTH), F32)], axis=0)
    half = lambda i: pl.ds(pl.multiple_of(i * HALF, 128), HALF)
    mixed_keep[...] = low_all[:, half(core)]
    mixed_give[...] = low_all[:, half(1 - core)]
    heads_keep[...] = heads_all[:, half(x)]
    heads_give[...] = heads_all[:, half(1 - x)]


def first_back(place, *arrays):
    rows, width = arrays[2].shape
    return run(
        first_back_kernel,
        "first_back",
        [(place, "smem")] + [(r, "vmem") for r in arrays],
        [
            ((rows, width), F32),
            ((rows, HALF), BF16),
            ((rows, HALF), BF16),
            ((rows, HALF), BF16),
            ((rows, HALF), BF16),
            ((8, width), F32),
        ],
        [pltpu.VMEM((rows, width), BF16)] * 2,
        limit=10,
    )


def enter_kernel(
    place, d_give, d_keep, d_last, grad_first_in, kinds, sums1, sums2, sums_a, sums_b, whole, own, give, small
):
    x, core = place[0], place[2]
    rows = own.shape[0]
    pairs = ((d_give, 1 - core), (d_keep, core), (d_last, 2))
    small[...] = jnp.zeros_like(small)
    for ref, pair in pairs:
        at = pl.ds(pl.multiple_of(x * HALF + pair * 128, 128), 128)
        small[0:1, at] = down_sum(ref[:, 0:128].astype(F32))
        small[1:2, at] = down_sum(ref[:, 256:384].astype(F32))
    small[2:3, :] = sums1[0:1, :]
    small[3:4, :] = sums2[0:1, :]
    small[4:6, :] = sums1[1:3, :]
    small[6:8, :] = sums2[1:3, :]
    small[pl.ds(8 + 2 * core, 1), :] = sums_a[0:1, :]
    small[pl.ds(9 + 2 * core, 1), :] = sums_b[0:1, :]
    weights = []
    for _, pair in pairs:
        tiles = [whole[:, pl.ds(pl.multiple_of(j * HALF + pair * 128, 128), 128)] for j in range(3)]
        weights.append(jnp.concatenate(tiles, axis=1))
    lane_row = lax.broadcasted_iota(jnp.int32, (8, rows), 0)
    step = 256
    embed = jnp.zeros((8, MODEL_WIDTH), F32)
    for side in (1, 0):
        start = pl.multiple_of((x if side == 0 else 1 - x) * rows, 128)
        hot = jnp.where(kinds[:, pl.ds(start, rows)] == lane_row, 1.0, 0.0).astype(BF16)
        for i in range(rows // step):
            span = slice(i * step, (i + 1) * step)
            source = slice(side * rows + i * step, side * rows + (i + 1) * step)
            value = sum(mxu(ref[source, :], weight, NT) for (ref, _), weight in zip(pairs, weights))
            if side == 0:
                value = value + grad_first_in[span, :]
                own[span, :] = value
            else:
                give[span, :] = value.astype(BF16)
            take = hot[:, span]
            for term in three_parts(value):
                embed += mxu(take, term, NN)
    small[12:15, :] = embed[0:3, :]


def enter(place, *arrays):
    rows, width = arrays[3].shape
    return run(
        enter_kernel,
        "enter",
        [(place, "smem")] + [(r, "vmem") for r in arrays],
        [((rows, width), F32), ((rows, width), BF16), ((16, width), F32)],
        limit=12,
    )


def narrow_kernel(place, own, other, mine, theirs, whole):
    small = own[...] + other[...]
    rest = jnp.zeros((128 - small.shape[0], small.shape[1]), F32)
    whole[...] = jnp.concatenate([small, rest], axis=0).T
    split_rows(whole, mine, theirs, place, True)


def narrow(place, own, other):
    return run(
        narrow_kernel,
        "narrow",
        [(place, "smem"), (own, "vmem"), (other, "vmem")],
        [((4, 96, 128), BF16)] * 2,
        [pltpu.VMEM((own.shape[1], 128), F32)],
        limit=4,
    )


def fold_kernel(mine, got, keep, send):
    half = mine.shape[0] // 2
    for i in range(2 * half):
        value = mine[i].astype(F32) + got[i].astype(F32)
        if i < half:
            keep[i] = value
        else:
            send[i - half] = value.astype(BF16)


def fold(mine, got):
    shape = (mine.shape[0] // 2,) + mine.shape[1:]
    return run(
        fold_kernel,
        "fold",
        [(mine, "vmem"), (got, "vmem")],
        [(shape, F32), (shape, BF16)],
        limit=4,
    )


def fold_two_kernel(mine_a, got_a, mine_b, got_b, keep, send):
    n = mine_a.shape[2]
    for i in range(4):
        for mine, got, lanes in ((mine_a, got_a, slice(0, n)), (mine_b, got_b, slice(n, keep.shape[2]))):
            value = mine[i].astype(F32) + got[i].astype(F32)
            if i < 2:
                keep[i, :, lanes] = value
            else:
                send[i - 2, :, lanes] = value.astype(BF16)


def fold_two(mine_a, got_a, mine_b, got_b):
    shape = (2, 96, mine_a.shape[2] + mine_b.shape[2])
    return run(
        fold_two_kernel,
        "fold_two",
        [(v, "vmem") for v in (mine_a, got_a, mine_b, got_b)],
        [(shape, F32), (shape, BF16)],
        limit=4,
    )


def settle_kernel(place, *refs):
    *sources, keep, send = refs
    core = place[2]
    column = 0
    for i in range(0, len(sources), 2):
        one, two = sources[i : i + 2]
        n = one.shape[2]
        lanes = slice(column, column + n)
        for j, whose in enumerate((core, 1 - core)):
            rows = pl.ds(pl.multiple_of(whose * 48, 16), 48)
            value = one[0, rows, :] + two[0, rows, :].astype(F32)
            keep[j, :, lanes] = value
            send[j, :, lanes] = value.astype(BF16)
        column += n


def settle(place, groups):
    sources = [array for group in groups for array in group]
    n = sum(group[0].shape[2] for group in groups)
    return run(
        settle_kernel,
        "settle",
        [(place, "smem")] + [(array, "vmem") for array in sources],
        [((2, 48, n), F32), ((2, 48, n), BF16)],
        limit=4,
    )


def join_kernel(keep, got, near, far):
    near[...] = keep[0] + got[0].astype(F32)
    far[...] = (keep[1] + got[1].astype(F32)).astype(BF16)


def join(keep, got):
    shape = keep.shape[1:]
    return run(join_kernel, "join", [(keep, "vmem"), (got, "vmem")], [(shape, F32), (shape, BF16)], limit=4)


def step_of(weight, momentum, average, grad, rate, decay):
    moved = grad + decay * weight if decay else grad
    new_momentum = momentum_rate * momentum + moved
    new = weight - rate * (moved + momentum_rate * new_momentum)
    return grad, new, new_momentum, average_rate * average + (1.0 - average_rate) * new


def update_rest_kernel(
    place, mats, momentum, average, *refs, rate, groups
):
    sources, outs, work, sems = refs[: 2 * groups], refs[2 * groups : 2 * groups + 4], refs[-5:-1], refs[-1]
    width = MODEL_WIDTH
    base = 3 * width
    for whose in range(2):
        core = place[2] if whose == 0 else 1 - place[2]
        for g in range(groups):
            source = sources[2 * g + whose]
            if g == 0:
                parts = ((8 * width + 2 * core * QUARTER, QUARTER), (8 * width + (2 * core + 1) * QUARTER, QUARTER))
            else:
                parts = (
                    (4 * width + 2 * core * QUARTER, QUARTER),
                    (4 * width + (2 * core + 1) * QUARTER, QUARTER),
                    (3 * width + core * HALF, HALF),
                )
            column = 0
            for first, n in parts:
                lanes = slice(column, column + n)
                grad = source[:, lanes].astype(F32)
                at = pl.ds(pl.multiple_of(first, 128), n)
                results = step_of(mats[:, at], momentum[:, at], average[:, at], grad, rate, decay_rate)
                to = pl.ds(pl.multiple_of(first - base, 128), n)
                for ref, value in zip(work, results):
                    ref[:, to] = value
                column += n
    copies = []
    for i in range(4):
        copy = pltpu.make_async_copy(work[i], outs[i].at[:, pl.ds(base, work[i].shape[1])], sems.at[i])
        copy.start()
        copies.append(copy)
    for copy in copies:
        copy.wait()


def update_rest(place, mats, momentum, average, groups, rate):
    rows, columns = mats.shape
    sources = [array for group in groups for array in group]
    n = columns - 3 * MODEL_WIDTH
    return pl.pallas_call(
        functools.partial(update_rest_kernel, rate=rate, groups=len(groups)),
        in_specs=[pl.BlockSpec(memory_space=pltpu.SMEM)]
        + [pl.BlockSpec(memory_space=pltpu.VMEM)] * (3 + len(sources)),
        out_specs=[pl.BlockSpec(memory_space=pl.ANY)] * 4,
        out_shape=[jax.ShapeDtypeStruct((rows, columns), F32)] * 4,
        scratch_shapes=[pltpu.VMEM((rows, n), F32)] * 4 + [pltpu.SemaphoreType.DMA((4,))],
        compiler_params=pltpu.CompilerParams(vmem_limit_bytes=10 * 2**20),
        cost_estimate=declared("update_rest"),
        name="update_rest",
    )(place, mats, momentum, average, *sources)


def update_heads_kernel(
    place,
    mats,
    momentum,
    average,
    keep,
    from_seq,
    from_core,
    from_both,
    s_value,
    s_momentum,
    s_average,
    a0,
    a1,
    a2,
    a3,
    o0,
    o1,
    o2,
    o3,
    s0,
    s1,
    s2,
    s3,
    bias,
    w0,
    w1,
    w2,
    w3,
    grads,
    sems,
    *,
    rate,
):
    x, core = place[0], place[2]
    width = MODEL_WIDTH
    grads[x, core] = keep[0]
    grads[1 - x, core] = from_seq[...].astype(F32)
    grads[x, 1 - core] = from_core[...].astype(F32)
    grads[1 - x, 1 - core] = from_both[...].astype(F32)
    work = (w0, w1, w2, w3)
    last = ((0, 384), (0, 512), (1, 384))
    for j in range(3):
        for side in range(2):
            at = slice(j * width + side * HALF, j * width + (side + 1) * HALF)
            tiles = [grads[side, c, :, j * 128 : (j + 1) * 128] for c in range(2)]
            c, first = last[j]
            tiles.append(grads[side, c, :, first : first + 128])
            grad = jnp.concatenate(tiles, axis=1)
            results = step_of(mats[:, at], momentum[:, at], average[:, at], grad, rate, decay_rate)
            for ref, value in zip(work, results):
                ref[:, at] = value
    copies = []
    for i, out in enumerate((o0, o1, o2, o3)):
        copy = pltpu.make_async_copy(work[i], out.at[:, pl.ds(0, 3 * width)], sems.at[i])
        copy.start()
        copies.append(copy)
    small = (grads[x, core, :, 640:] + grads[1 - x, core, :, 640:]).T[0:16]
    n = s_value.shape[0]
    results = step_of(s_value[...], s_momentum[...], s_average[...], small[0:n], rate, 0.0)
    for ref, value in zip((s0, s1, s2, s3), results):
        ref[...] = value
    bias[...] = small[2:3]
    for copy in copies:
        copy.wait()


def update_heads(place, mats, momentum, average, group, smalls, so_far, rate):
    rows, columns = mats.shape
    n = 3 * MODEL_WIDTH
    vmem = pl.BlockSpec(memory_space=pltpu.VMEM)
    anywhere = pl.BlockSpec(memory_space=pl.ANY)
    shape = smalls[0].shape
    return pl.pallas_call(
        functools.partial(update_heads_kernel, rate=rate),
        in_specs=[pl.BlockSpec(memory_space=pltpu.SMEM)] + [vmem] * 10 + [anywhere] * 4,
        out_specs=[anywhere] * 4 + [vmem] * 5,
        out_shape=[jax.ShapeDtypeStruct((rows, columns), F32)] * 4 + [jax.ShapeDtypeStruct(shape, F32)] * 4
        + [jax.ShapeDtypeStruct((1, rows), F32)],
        scratch_shapes=[pltpu.VMEM((rows, n), F32)] * 4
        + [pltpu.VMEM((2, 2, rows, 768), F32), pltpu.SemaphoreType.DMA((4,))],
        input_output_aliases={11 + i: i for i in range(4)},
        compiler_params=pltpu.CompilerParams(vmem_limit_bytes=6 * 2**20),
        cost_estimate=declared("update_heads"),
        name="update_heads",
    )(place, mats, momentum, average, *group, *smalls, *so_far)


SEQ_SWAP = [(0, 1), (1, 0)]
CORE_SWAP = [(i, i ^ 1) for i in range(16)]
Y_SWAP = [(i, i ^ 2) for i in range(16)]


def over_seq(value):
    return lax.ppermute(value, "seq", SEQ_SWAP)


def over_core(value):
    return lax.ppermute(value, "dp", CORE_SWAP)


def over_y(value):
    return lax.ppermute(value, "dp", Y_SWAP)


def over_z1(value):
    return lax.ppermute(value, "dp", [(i, i ^ 4) for i in range(16)])


def over_z2(value):
    return lax.ppermute(value, "dp", [(i, i ^ 8) for i in range(16)])


def over_both(value):
    return lax.ppermute(value, ("dp", "seq"), [(i, i ^ 3) for i in range(32)])


def ordered(flag, mine, theirs, axis):
    return jnp.where(
        flag == 0,
        jnp.concatenate([mine, theirs], axis=axis),
        jnp.concatenate([theirs, mine], axis=axis),
    )


def pin(value, *after):
    return lax.optimization_barrier((value, after))[0]


def exchange(place, groups, *after):
    keep, send = settle(place, groups)
    near, far = join(keep, over_seq(pin(send, *after) if after else send))
    return near, over_core(far)


def tuned(
    inputs,
    modality,
    key_valid_mask,
    output_gradient,
    mats,
    mats_momentum,
    mats_average,
    smalls,
    smalls_momentum,
    smalls_average,
):
    width = MODEL_WIDTH
    rows = inputs.shape[1]
    dp = lax.axis_index("dp")
    x = lax.axis_index("seq")
    core = dp % 2
    y = (dp // 2) % 2
    place = jnp.stack([x, y, core, dp // 4]).astype(jnp.int32)

    def both(mine, theirs):
        return jnp.concatenate([mine, theirs])

    att_own = pack_heads(place, mats, smalls.T)[None]
    att_got = over_z2(att_own)
    other_inputs = over_seq(inputs[0])
    keep, give = pack_rest(pin(place, att_own), mats)
    pair = ordered(core, keep, over_core(give), 0)[None]
    att_two = both(att_own, pin(att_got, pair))
    blocks = [pair[:, :, a:b] for a, b in zip(CUTS[:-1], CUTS[1:])]
    att0 = both(att_two, over_z1(att_two))
    two0 = both(blocks[0], pin(over_z2(pin(blocks[0], att_two)), att0))
    att2 = pin(over_y(att0), other_inputs)
    att = (att0, over_core(att0), att2, over_core(att2))
    line0 = over_z1(two0)

    x_low, x_in, qkv, masked, params, w_qkv = project(
        pin(place, two0), inputs[0], other_inputs, modality, key_valid_mask, att
    )
    line0 = both(two0, pin(line0, qkv))
    up0 = (line0, over_y(line0), True)
    got1 = over_z2(pin(blocks[1], qkv))
    heads, log_sum = attend(qkv, pin(masked, line0))
    got1 = pin(got1, heads)
    got_heads = over_seq(pin(heads, got1)[rows:])
    two1 = both(blocks[1], got1)
    line1 = both(two1, over_z1(two1))
    x_got = over_core(x_low)
    two2 = both(blocks[2], pin(over_z2(pin(blocks[2], heads)), line1))
    got_heads, y_0 = pin((got_heads, up0[1]), two2)
    out_mine = both(line0[:, :, QUARTER:], y_0[:, :, QUARTER:])
    out_w = (out_mine, over_core(out_mine))
    up1 = (line1, over_y(line1), True)
    line2 = both(two2, pin(over_z1(two2), got_heads))
    two3 = both(blocks[3], pin(over_z2(pin(blocks[3], line1)), got_heads))
    out_low, unit1, scale1, first_low, w_out = mix(
        pin(place, up1[1], line2, two3, x_got), heads, got_heads, x_in, params, out_w
    )
    down0 = (line2, over_y(line2), True)
    first_got = over_core(first_low)
    out_got = over_core(out_low)
    act0, slope0, w_up0 = raise_up(place, first_low, first_got, params, up0, 0)
    square3 = both(two3, pin(over_y(two3), act0))
    down1 = (square3, over_z1(square3), False)
    act1, slope1, w_up1 = raise_up(
        pin(place, square3, out_got), first_low, first_got, params, up1, 1
    )
    so_far, w_down0 = lower(pin(place, act1), act0, down0)
    sum_give, w_down1 = lower_other(place, act1, so_far, down1)
    block_out, grad_second, grad_ffo, sums2 = turn(
        place, act1, so_far, over_core(sum_give), unit1, params, output_gradient[0], w_down1
    )

    ffo_got = over_core(grad_ffo)
    mine_d0, theirs_d0 = outer(place, grad_ffo, ffo_got, [act0], "outer_down")
    got_d0 = over_y(theirs_d0)
    grad_up0, sums_up0 = raise_back(pin(place, mine_d0), grad_ffo, ffo_got, slope0, w_down0)
    grad_up1, sums_up1 = raise_back(pin(place, grad_up0), grad_ffo, ffo_got, slope1, w_down1)
    first_give = first_other(place, grad_up0, grad_up1, w_up0, w_up1)
    mine_d1, theirs_d1 = outer(pin(place, first_give), grad_ffo, ffo_got, [act1], "outer_down")
    got_d1 = over_y(theirs_d1)
    fold_d0 = fold(mine_d0, pin(got_d0, mine_d1))
    grad_first_in, mixed_keep, mixed_give, heads_keep, heads_give, sums1 = first_back(
        place,
        grad_up0,
        grad_up1,
        pin(over_core(first_give), fold_d0),
        grad_second,
        unit1,
        scale1,
        params,
        w_up0,
        w_up1,
        w_out,
    )
    heads_got = over_seq(heads_give)
    mixed_got = over_core(mixed_give)
    mine_u0, theirs_u0 = outer(pin(place, sums1), first_low, first_got, [grad_up0], "outer_up")
    got_u0 = over_y(theirs_u0)
    mine_u1, theirs_u1 = outer(
        pin(place, mine_u0), first_low, first_got, [grad_up1], "outer_up", y_last=False
    )
    got_u1 = over_z1(theirs_u1)
    last_d0 = fold(fold_d0[0], pin(over_z1(fold_d0[1]), mine_u1))
    got_last_d0 = over_z2(last_d0[1])
    mine_o, theirs_o = outer(pin(place, last_d0), out_low, out_got, [mixed_keep, mixed_got], "outer_out")
    got_o = over_y(theirs_o)

    def back(role, masked, parts=False):
        return attend_back(place, qkv, heads, heads_keep, heads_got, log_sum, masked, role, parts)

    fold_d1 = fold(mine_d1, pin(got_d1, mine_o))
    (d_give,) = back(0, pin(masked, fold_d1))
    got_d1, got_last_d0 = pin((over_z1(fold_d1[1]), got_last_d0), d_give)
    d_give = pin(d_give, got_d1, got_last_d0)
    last_d1 = fold(fold_d1[0], got_d1)
    d_got = over_core(d_give)
    (d_keep,) = back(1, pin(masked, last_d1))
    got_last_d1 = over_z2(last_d1[1])
    got_u0, got_u1, got_last_d1 = pin((got_u0, got_u1, got_last_d1), d_keep)
    d_keep = pin(d_keep, got_u0, got_u1, got_last_d1)
    fold_u0 = fold(mine_u0, got_u0)
    fold_u1 = fold(mine_u1, got_u1)
    mine_q, theirs_q = outer(
        pin(place, fold_u0, fold_u1), x_low, x_got, [d_keep, pin(d_got, fold_u0, fold_u1)], "outer_heads"
    )
    got_u0, got_u1, got_q = over_z1(fold_u0[1]), over_y(fold_u1[1]), over_y(theirs_q)
    down_keep, down_send = settle(
        pin(place, mine_q), [(last_d0[0], got_last_d0), (last_d1[0], got_last_d1)]
    )
    down_got = over_seq(down_send)
    last = back(2, pin(masked, down_keep), True)
    got_u0, got_o, down_got = pin((got_u0, got_o, down_got), last)
    d_last, cols_keep, cols_give = pin(last, got_u0, got_o, down_got)
    last_u0 = fold(fold_u0[0], got_u0)
    fold_o = fold(mine_o, got_o)
    cols_got = over_core(cols_give)
    down_near, down_far = join(down_keep, down_got)
    grad_x, give_x, small = enter(
        pin(place, last_u0, fold_o, down_near),
        d_give,
        d_keep,
        d_last,
        grad_first_in,
        modality,
        sums1,
        sums2,
        sums_up0,
        sums_up1,
        w_qkv,
    )
    got_last_u0 = over_z2(last_u0[1])
    got_o, got_u1, got_q, got_last_u0 = pin((over_z1(fold_o[1]), got_u1, got_q, got_last_u0), small)
    give_x, small = pin((give_x, small), got_o, got_u1, got_q, got_last_u0)
    x_back = over_seq(give_x)
    last_u1 = fold(fold_u1[0], got_u1)
    fold_q = fold(mine_q, got_q)
    mine_r, theirs_r = outer(
        pin(place, last_u1, fold_q), x_low, x_got, [cols_keep, pin(cols_got, last_u1, fold_q)], "outer_heads"
    )
    mine_s, theirs_s = narrow(pin(place, mine_r), small, over_core(small))
    last_o = fold(fold_o[0], pin(got_o, mine_s))
    last_q = fold(fold_q[0], pin(over_z1(fold_q[1]), mine_s))
    fold_r = fold_two(mine_r, over_y(theirs_r), mine_s, over_y(theirs_s))
    down_group = (down_near, over_core(pin(down_far, last_q)))
    last_r = fold(fold_r[0], over_z1(fold_r[1]))

    rate = base_rate / math.sqrt(rows * lax.axis_size("dp") * lax.axis_size("seq"))
    up_group = exchange(
        place,
        [(last_u0[0], got_last_u0), (last_u1[0], over_z2(last_u1[1])), (last_o[0], over_z2(last_o[1]))],
    )
    heads_keep, heads_send = settle(place, [(v[0], over_z2(v[1])) for v in (last_q, last_r)])
    near, far = heads_send[0], heads_send[1]
    heads_group = (heads_keep, over_seq(near), over_core(far), over_both(far))
    x_back, up_near = pin((x_back, up_group[0]), heads_keep)
    up_group = (up_near, up_group[1])
    input_grad = (grad_x + x_back.astype(F32)).astype(BF16)[None]
    so_far = update_rest(place, mats, mats_momentum, mats_average, [down_group, up_group], rate)
    *new, s_grad, s_value, s_momentum, s_average, s_bias = update_heads(
        place,
        mats,
        mats_momentum,
        mats_average,
        heads_group,
        (smalls.T, smalls_momentum.T, smalls_average.T),
        so_far,
        rate,
    )
    return (
        block_out[None],
        input_grad,
        *new,
        s_grad.T,
        s_bias.reshape(-1),
        s_value.T,
        s_momentum.T,
        s_average.T,
    )


def solution(mesh):
    placed = (
        P("dp", "seq", None),
        P("dp", None),
        P("dp", None),
        P("dp", "seq", None),
        P("dp", None),
        P("dp", None),
        P("dp", None),
        P("dp", None),
        P("dp", None),
        P("dp", None),
    )
    plan = tuned if tuple(mesh.shape.values()) == (16, 2) else per_device
    return jax.shard_map(
        plan,
        mesh=mesh,
        in_specs=placed,
        out_specs=(
            P("dp", "seq", None),
            P("dp", "seq", None),
            P("dp", None),
            P("dp", None),
            P("dp", None),
            P("dp", None),
            P("dp", None),
            P("dp"),
            P("dp", None),
            P("dp", None),
            P("dp", None),
        ),
        check_vma=False,
    )
```

```python
import functools
import math

import jax
import jax.numpy as jnp
from jax import lax
from jax.experimental import pallas as pl
from jax.experimental.pallas import tpu as pltpu
from jax.sharding import PartitionSpec as P

MODEL_WIDTH = 768
H = 12
HD = 64
FF = 3072


epsilon = 1e-06
momentum_rate = 0.9
decay_rate = 0.0001
average_rate = 0.75
base_rate = 0.03
masked_score = -1e30


def product(left, right):
    return jnp.dot(left, right, preferred_element_type=jnp.float32)


def product_tn(left, right):
    return lax.dot_general(
        left, right, (((0,), (0,)), ((), ())), preferred_element_type=jnp.float32
    )


def product_nt(left, right):
    return lax.dot_general(
        left, right, (((1,), (1,)), ((), ())), preferred_element_type=jnp.float32
    )


def normalize(rows, gain, shift):
    mean = jnp.mean(rows, axis=-1, keepdims=True)
    centred = rows - mean
    spread = jnp.mean(centred * centred, axis=-1, keepdims=True)
    return centred * lax.rsqrt(spread + epsilon) * gain + shift


def exact_gelu(values):
    return jax.nn.gelu(values, approximate=False)


def head_scores(query_heads, key_heads, live_doc):
    scores = (
        jnp.einsum("qhe,khe->hqk", query_heads, key_heads, preferred_element_type=jnp.float32)
        * 0.125
    )
    return jnp.where(live_doc[None, None, :] > 0, scores, masked_score)


def attention_forward_pass(item):
    query_doc, keys_doc, values_doc, live_doc = item
    query_heads = query_doc.reshape(query_doc.shape[0], H, HD)
    key_heads = keys_doc.reshape(keys_doc.shape[0], H, HD)
    value_heads = values_doc.reshape(values_doc.shape[0], H, HD)
    scores = head_scores(query_heads, key_heads, live_doc)
    top = jnp.max(scores, axis=-1, keepdims=True)
    expd = jnp.exp(scores - top)
    total = jnp.sum(expd, axis=-1, keepdims=True)
    prob = (expd / total).astype(jnp.bfloat16)
    attention_output = jnp.einsum(
        "hqk,khe->qhe", prob, value_heads, preferred_element_type=jnp.float32
    )
    return (attention_output.reshape(query_doc.shape[0], H * HD), (top + jnp.log(total))[..., 0])


def attention_backward_pass(item):
    query_doc, keys_doc, values_doc, live_doc, log_sum_normalizer, grad_doc = item
    element_count = query_doc.shape[0]
    length = keys_doc.shape[0]
    query_heads = query_doc.reshape(element_count, H, HD)
    key_heads = keys_doc.reshape(length, H, HD)
    value_heads = values_doc.reshape(length, H, HD)
    grad_heads = grad_doc.reshape(element_count, H, HD)
    scores = head_scores(query_heads, key_heads, live_doc)
    prob = jnp.exp(scores - log_sum_normalizer[..., None])
    grad_prob = jnp.einsum(
        "qhe,khe->hqk", grad_heads, value_heads, preferred_element_type=jnp.float32
    )
    grad_values = jnp.einsum(
        "hqk,qhe->khe", prob.astype(jnp.bfloat16), grad_heads, preferred_element_type=jnp.float32
    )
    inner = jnp.sum(prob * grad_prob, axis=-1, keepdims=True)
    grad_scores = (prob * (grad_prob - inner)).astype(jnp.bfloat16)
    grad_query = (
        jnp.einsum("hqk,khe->qhe", grad_scores, key_heads, preferred_element_type=jnp.float32)
        * 0.125
    )
    grad_keys = (
        jnp.einsum("hqk,qhe->khe", grad_scores, query_heads, preferred_element_type=jnp.float32)
        * 0.125
    )
    return (
        grad_query.reshape(element_count, H * HD),
        grad_keys.reshape(length, H * HD),
        grad_values.reshape(length, H * HD),
    )


def per_device(
    inputs,
    modality,
    key_valid_mask,
    output_gradient,
    mats,
    mats_momentum,
    mats_average,
    smalls,
    smalls_momentum,
    smalls_average,
):
    docs, local_len, width = inputs.shape
    seq_len = modality.shape[1]
    rows = docs * local_len
    low_mats = mats.astype(jnp.bfloat16)
    w_qkv, w_out, w_up, w_down, whole_smalls = (
        lax.all_gather(low_mats[:, 0 : 3 * MODEL_WIDTH], "dp", axis=0, tiled=True),
        lax.all_gather(low_mats[:, 3 * MODEL_WIDTH : 4 * MODEL_WIDTH], "dp", axis=0, tiled=True),
        lax.all_gather(
            low_mats[:, 4 * MODEL_WIDTH : 4 * MODEL_WIDTH + FF], "dp", axis=0, tiled=True
        ),
        lax.all_gather(low_mats[:, 4 * MODEL_WIDTH + FF :], "dp", axis=0, tiled=True),
        lax.all_gather(smalls.astype(jnp.bfloat16), "dp", axis=0, tiled=True),
    )
    params = whole_smalls.astype(jnp.float32)
    bias_qkv = jnp.concatenate([params[:, 0], jnp.zeros_like(params[:, 0]), params[:, 1]])
    bias_up = jnp.transpose(params[:, 8:12]).reshape(FF)
    embed = jnp.transpose(whole_smalls[:, 12:15])
    leading_key = (jnp.arange(seq_len) == 0).astype(jnp.int32)
    valid_positions = jnp.maximum(key_valid_mask, leading_key[None, :])
    local_start = lax.axis_index("seq") * local_len
    local_modality = lax.dynamic_slice_in_dim(modality, local_start, local_len, 1)
    onehot = (
        local_modality.reshape(rows)[:, None] == jnp.arange(3, dtype=jnp.int32)[None, :]
    ).astype(jnp.bfloat16)
    x_in = inputs.reshape(rows, width).astype(jnp.float32) + product(onehot, embed)
    x_low = x_in.astype(jnp.bfloat16)
    qkv = (product(x_low, w_qkv) + bias_qkv).astype(jnp.bfloat16)
    query_documents = qkv[:, 0:width].reshape(docs, local_len, width)
    keys_local = qkv[:, width : 2 * width].reshape(docs, local_len, width)
    values_local = qkv[:, 2 * width :].reshape(docs, local_len, width)
    every_key, every_value = (
        lax.all_gather(keys_local, "seq", axis=1, tiled=True),
        lax.all_gather(values_local, "seq", axis=1, tiled=True),
    )
    attention_output, log_sum_normalizer = lax.map(
        attention_forward_pass, (query_documents, every_key, every_value, valid_positions)
    )
    out_low = attention_output.reshape(rows, width).astype(jnp.bfloat16)
    mixed = product(out_low, w_out) + params[:, 2]
    first_in = x_in + mixed
    first = normalize(first_in, params[:, 4], params[:, 5])
    first_low = first.astype(jnp.bfloat16)
    up = product(first_low, w_up) + bias_up
    act_low = exact_gelu(up).astype(jnp.bfloat16)
    ffo = product_nt(act_low, w_down) + params[:, 3]
    second_in = first + ffo
    result = normalize(second_in, params[:, 6], params[:, 7])
    block_out = result.astype(jnp.bfloat16).reshape(docs, local_len, width)
    w_qkv, w_out, w_up, w_down = (
        lax.all_gather(low_mats[:, 0 : 3 * MODEL_WIDTH], "dp", axis=0, tiled=True),
        lax.all_gather(low_mats[:, 3 * MODEL_WIDTH : 4 * MODEL_WIDTH], "dp", axis=0, tiled=True),
        lax.all_gather(
            low_mats[:, 4 * MODEL_WIDTH : 4 * MODEL_WIDTH + FF], "dp", axis=0, tiled=True
        ),
        lax.all_gather(low_mats[:, 4 * MODEL_WIDTH + FF :], "dp", axis=0, tiled=True),
    )
    grad_rows = output_gradient.reshape(rows, width).astype(jnp.float32)
    second_out, second_pull = jax.vjp(normalize, second_in, params[:, 6], params[:, 7])
    grad_second, grad_gain2, grad_shift2 = second_pull(grad_rows)
    grad_ffo = grad_second.astype(jnp.bfloat16)
    grad_bias_down = jnp.sum(grad_ffo.astype(jnp.float32), axis=0)
    grad_w_down = product_tn(grad_ffo, act_low)
    grad_act = product(grad_ffo, w_down)
    gelu_out, gelu_pull = jax.vjp(exact_gelu, up)
    grad_up = gelu_pull(grad_act)[0].astype(jnp.bfloat16)
    grad_bias_up = jnp.sum(grad_up.astype(jnp.float32), axis=0)
    grad_w_up = product_tn(first_low, grad_up)
    grad_first = grad_second + product_nt(grad_up, w_up)
    first_out, first_pull = jax.vjp(normalize, first_in, params[:, 4], params[:, 5])
    grad_first_in, grad_gain1, grad_shift1 = first_pull(grad_first)
    grad_mixed = grad_first_in.astype(jnp.bfloat16)
    grad_bias_out = jnp.sum(grad_mixed.astype(jnp.float32), axis=0)
    grad_w_out = product_tn(out_low, grad_mixed)
    grad_out = product_nt(grad_mixed, w_out).astype(jnp.bfloat16)
    output_gradient_documents = grad_out.reshape(docs, local_len, width)
    grad_query, grad_keys_all, grad_values_all = lax.map(
        attention_backward_pass,
        (
            query_documents,
            every_key,
            every_value,
            valid_positions,
            log_sum_normalizer,
            output_gradient_documents,
        ),
    )
    grad_keys, grad_values = (
        lax.psum_scatter(
            grad_keys_all.astype(jnp.bfloat16), "seq", scatter_dimension=1, tiled=True
        ).astype(jnp.float32),
        lax.psum_scatter(
            grad_values_all.astype(jnp.bfloat16), "seq", scatter_dimension=1, tiled=True
        ).astype(jnp.float32),
    )
    grad_qkv = jnp.concatenate(
        [
            grad_query.reshape(rows, width).astype(jnp.bfloat16),
            grad_keys.reshape(rows, width).astype(jnp.bfloat16),
            grad_values.reshape(rows, width).astype(jnp.bfloat16),
        ],
        axis=1,
    )
    grad_bias_qkv = jnp.sum(grad_qkv.astype(jnp.float32), axis=0)
    grad_w_qkv = product_tn(x_low, grad_qkv)
    grad_x_in = grad_first_in + product_nt(grad_qkv, w_qkv)
    grad_embed = lax.dot_general(
        onehot.astype(jnp.float32),
        grad_x_in,
        (((0,), (0,)), ((), ())),
        precision=lax.Precision.HIGHEST,
        preferred_element_type=jnp.float32,
    )
    input_grad = grad_x_in.astype(jnp.bfloat16).reshape(docs, local_len, width)
    grad_columns = jnp.stack(
        [
            grad_bias_qkv[0:width],
            grad_bias_qkv[2 * width :],
            grad_bias_out,
            grad_bias_down,
            grad_gain1,
            grad_shift1,
            grad_gain2,
            grad_shift2,
        ],
        axis=1,
    )
    grad_smalls = jnp.concatenate(
        [
            grad_columns,
            jnp.transpose(grad_bias_up.reshape(FF // width, width)),
            jnp.transpose(grad_embed),
        ],
        axis=1,
    )
    qkv_shard, out_shard, up_shard, down_shard, small_shard = (
        lax.psum_scatter(
            grad_w_qkv.astype(jnp.bfloat16), "dp", scatter_dimension=0, tiled=True
        ).astype(jnp.float32),
        lax.psum_scatter(
            grad_w_out.astype(jnp.bfloat16), "dp", scatter_dimension=0, tiled=True
        ).astype(jnp.float32),
        lax.psum_scatter(
            grad_w_up.astype(jnp.bfloat16), "dp", scatter_dimension=0, tiled=True
        ).astype(jnp.float32),
        lax.psum_scatter(
            grad_w_down.astype(jnp.bfloat16), "dp", scatter_dimension=0, tiled=True
        ).astype(jnp.float32),
        lax.psum_scatter(
            grad_smalls.astype(jnp.bfloat16), "dp", scatter_dimension=0, tiled=True
        ).astype(jnp.float32),
    )
    mats_shard = jnp.concatenate([qkv_shard, out_shard, up_shard, down_shard], axis=1)
    mats_grad, smalls_grad = (
        lax.psum(mats_shard.astype(jnp.bfloat16), "seq").astype(jnp.float32),
        lax.psum(small_shard.astype(jnp.bfloat16), "seq").astype(jnp.float32),
    )
    out_bias_grad = smalls_grad[:, 2]
    total_tokens = rows * lax.axis_size("dp") * lax.axis_size("seq")
    rate = base_rate / math.sqrt(total_tokens)
    decayed = mats_grad + decay_rate * mats
    new_mats_momentum = momentum_rate * mats_momentum + decayed
    new_mats = mats - rate * (decayed + momentum_rate * new_mats_momentum)
    new_mats_average = average_rate * mats_average + (1.0 - average_rate) * new_mats
    new_smalls_momentum = momentum_rate * smalls_momentum + smalls_grad
    new_smalls = smalls - rate * (smalls_grad + momentum_rate * new_smalls_momentum)
    new_smalls_average = average_rate * smalls_average + (1.0 - average_rate) * new_smalls
    return (
        block_out,
        input_grad,
        mats_grad,
        new_mats,
        new_mats_momentum,
        new_mats_average,
        smalls_grad,
        out_bias_grad,
        new_smalls,
        new_smalls_momentum,
        new_smalls_average,
    )


LN2 = math.log(2.0)
NT = (((1,), (1,)), ((), ()))
NN = (((1,), (0,)), ((), ()))
TN = (((0,), (0,)), ((), ()))
BF16 = jnp.bfloat16
F32 = jnp.float32
HALF = MODEL_WIDTH // 2
QUARTER = MODEL_WIDTH
SHARE = 0.5
TIMES = {"long_fold": 8, "outer_out": 6}


def declared(name):
    return pl.CostEstimate(flops=int(SHARE * 1.15e9 * TIMES.get(name, 0.2)), bytes_accessed=0, transcendentals=0)


def mxu(left, right, dims):
    return lax.dot_general(left, right, dims, preferred_element_type=jnp.float32)


def three_parts(value):
    high = value.astype(jnp.bfloat16)
    rest = value - high.astype(jnp.float32)
    middle = rest.astype(jnp.bfloat16)
    return high, middle, (rest - middle.astype(jnp.float32)).astype(jnp.bfloat16)


def run(kernel, name, ins, outs, scratch=(), limit=12):
    spaces = {"vmem": pltpu.VMEM, "smem": pltpu.SMEM}
    return pl.pallas_call(
        kernel,
        in_specs=[pl.BlockSpec(memory_space=spaces[kind]) for _, kind in ins],
        out_specs=[pl.BlockSpec(memory_space=pltpu.VMEM) for _ in outs],
        out_shape=[jax.ShapeDtypeStruct(shape, dtype) for shape, dtype in outs],
        scratch_shapes=list(scratch),
        compiler_params=pltpu.CompilerParams(vmem_limit_bytes=limit * 2**20),
        cost_estimate=declared(name),
        name=name,
    )(*[array for array, _ in ins])


def both_kernel(mine, theirs, out):
    n = mine.shape[0]
    out[0:n] = mine[...]
    out[n:] = theirs[...]


def both(mine, theirs):
    shape = (mine.shape[0] + theirs.shape[0],) + mine.shape[1:]
    return run(both_kernel, "both", [(mine, "vmem"), (theirs, "vmem")], [(shape, mine.dtype)], limit=2)[0]


def last_columns_kernel(mine, theirs, out):
    n = mine.shape[0]
    out[0:n] = mine[:, :, mine.shape[2] - HALF :]
    out[n:] = theirs[:, :, mine.shape[2] - HALF :]


def last_columns(mine, theirs):
    shape = (2 * mine.shape[0], mine.shape[1], HALF)
    return run(last_columns_kernel, "last_columns", [(mine, "vmem"), (theirs, "vmem")], [(shape, BF16)], limit=2)[0]


def pair_up_kernel(place, keep, got, *blocks):
    rows = keep.shape[0]
    for ref, side in ((keep, place[2]), (got, 1 - place[2])):
        at = pl.ds(pl.multiple_of(side * rows, 16), rows)
        for block, first, last in zip(blocks, CUTS[:-1], CUTS[1:]):
            block[0, at, :] = ref[:, first:last]


def pair_up(place, keep, got):
    rows = keep.shape[0]
    return run(
        pair_up_kernel,
        "pair_up",
        [(place, "smem"), (keep, "vmem"), (got, "vmem")],
        [((1, 2 * rows, b - a), BF16) for a, b in zip(CUTS[:-1], CUTS[1:])],
        limit=2,
    )


def place_rows(pieces, whole):
    for value, first in pieces:
        whole[pl.ds(first, value.shape[0]), :] = value


def xor2(z):
    return lax.rem(z + 2, 4)


def xor1(z):
    return z + 1 - 2 * lax.rem(z, 2)


def near_far(place, y_last):
    y, z = place[1], place[3]
    if y_last:
        line = (z, xor2(z), xor1(z), xor1(xor2(z)))
        return [(zz, y) for zz in line], [(zz, 1 - y) for zz in line]
    one, two = (z, xor2(z)), (xor1(z), xor1(xor2(z)))
    return [(zz, yy) for yy in (y, 1 - y) for zz in one], [(zz, yy) for yy in (y, 1 - y) for zz in two]


def eight(place, block):
    mine, theirs, y_last = block
    near, far = near_far(place, y_last)
    pieces = []
    for ref, chips in ((mine, near), (theirs, far)):
        for i, (zz, yy) in enumerate(chips):
            pieces.append((ref[i, :, 0:QUARTER], pl.multiple_of((2 * zz + yy) * 96, 32)))
    return pieces


def sixteen(place, blocks):
    core = place[2]
    near, far = near_far(place, True)
    pieces = []
    for chips, cc, ref in zip((near, near, far, far), (core, 1 - core, core, 1 - core), blocks):
        for i, (zz, yy) in enumerate(chips):
            pieces.append((ref[i], pl.multiple_of((zz * 4 + yy * 2 + cc) * 48, 16)))
    return pieces


def place_out(place, mine, theirs, whole):
    core = place[2]
    near, far = near_far(place, True)
    for ref, cc in ((mine, core), (theirs, 1 - core)):
        lanes = pl.ds(pl.multiple_of(cc * HALF, 128), HALF)
        for i, (zz, yy) in enumerate(near + far):
            whole[pl.ds(pl.multiple_of((2 * zz + yy) * 96, 32), 96), lanes] = ref[i]


def split_rows(whole, mine, theirs, place, y_last):
    near, far = near_far(place, y_last)
    for ref, chips in ((mine, near), (theirs, far)):
        for i, (zz, yy) in enumerate(chips):
            row = pl.multiple_of((2 * zz + yy) * 96, 32)
            ref[i] = whole[pl.ds(row, 96), :].astype(ref.dtype)


def pack_heads_kernel(place, mats, smalls_t, block, narrow):
    width = MODEL_WIDTH
    narrow[...] = jnp.zeros_like(narrow)
    narrow[0:15, :] = smalls_t[...]
    block[:, 3 * HALF :] = narrow[...].T.astype(BF16)
    for j in range(3):
        lanes = pl.ds(pl.multiple_of(j * width + place[0] * HALF, 128), HALF)
        block[:, j * HALF : (j + 1) * HALF] = mats[:, lanes].astype(BF16)


def pack_heads(place, mats, smalls_t):
    rows = mats.shape[0]
    return run(
        pack_heads_kernel,
        "pack_heads",
        [(place, "smem"), (mats, "vmem"), (smalls_t, "vmem")],
        [((rows, 3 * HALF + 128), BF16)],
        [pltpu.VMEM((128, rows), F32)],
        limit=4,
    )[0]


CUTS = (0, QUARTER + HALF, 2 * QUARTER + HALF, 3 * QUARTER + HALF, 4 * QUARTER + HALF)


def pack_rest_kernel(place, mats, keep, give):
    width = MODEL_WIDTH
    for core, ref in ((1 - place[2], give), (place[2], keep)):
        take = lambda first, n: mats[:, pl.ds(pl.multiple_of(first, 128), n)].astype(BF16)
        ref[:, 0:QUARTER] = take(4 * width + 2 * core * QUARTER, QUARTER)
        ref[:, QUARTER : CUTS[1]] = take(3 * width + core * HALF, HALF)
        ref[:, CUTS[1] : CUTS[2]] = take(4 * width + (2 * core + 1) * QUARTER, QUARTER)
        ref[:, CUTS[2] : CUTS[3]] = take(8 * width + 2 * core * QUARTER, QUARTER)
        ref[:, CUTS[3] :] = take(8 * width + (2 * core + 1) * QUARTER, QUARTER)


def pack_rest(place, mats):
    rows = mats.shape[0]
    return run(
        pack_rest_kernel,
        "pack_rest",
        [(place, "smem"), (mats, "vmem")],
        [((rows, CUTS[4]), BF16)] * 2,
        limit=4,
    )


def unit_rows(rows):
    mean = jnp.mean(rows, axis=-1, keepdims=True)
    centred = rows - mean
    spread = jnp.mean(centred * centred, axis=-1, keepdims=True)
    scale = lax.rsqrt(spread + epsilon)
    return centred * scale, scale


def unit_back(grad, unit, scale, gain):
    inner = grad * gain
    mean_one = jnp.mean(inner, axis=-1, keepdims=True)
    mean_two = jnp.mean(inner * unit, axis=-1, keepdims=True)
    return scale * (inner - mean_one - unit * mean_two)


def down_sum(value):
    return jnp.sum(value, axis=0, keepdims=True)


def project_kernel(
    place, own, other, kinds, mask, w0, w1, w2, w3, x_low, x_in, qkv, masked, params, whole
):
    x, y, core = place[0], place[1], place[2]
    rows = own.shape[0]
    place_rows(sixteen(place, (w0, w1, w2, w3)), whole)
    lane_row = lax.broadcasted_iota(jnp.int32, (8, rows), 0)
    lane = lax.broadcasted_iota(jnp.int32, (8, 128), 1)
    first_row = lax.broadcasted_iota(jnp.int32, (8, 128), 0)
    pick = jnp.where((lane == 0) & (first_row == 0), 1.0, 0.0).astype(BF16)
    position = lax.broadcasted_iota(jnp.int32, (1, rows), 1)
    for side in range(2):
        start = pl.multiple_of((x if side == 0 else 1 - x) * rows, 128)
        alive = (mask[:, pl.ds(start, rows)] > 0) | (position + start == 0)
        bias = jnp.where(alive, 0.0, masked_score)
        bias = jnp.where(lane_row == 0, jnp.broadcast_to(bias, (8, rows)), 0.0).astype(BF16)
        masked[side * rows : (side + 1) * rows, :] = mxu(bias, pick, TN).astype(BF16)
    params[...] = whole[:, 3 * HALF :].astype(F32).T[0:16]
    embed = params[8:16, :].astype(BF16)
    start_q = pl.multiple_of(x * HALF, 128)
    bias_q = params[0:1, pl.ds(start_q, HALF)]
    bias_v = params[1:2, pl.ds(start_q, HALF)]
    scale = 0.125 / LN2
    step = 256
    for side in range(2):
        start = pl.multiple_of((x if side == 0 else 1 - x) * rows, 128)
        hot = jnp.where(kinds[:, pl.ds(start, rows)] + 4 == lane_row, 1.0, 0.0).astype(BF16)
        source = own if side == 0 else other
        for i in range(rows // step):
            span = slice(i * step, (i + 1) * step)
            out = slice(side * rows + i * step, side * rows + (i + 1) * step)
            value = source[span, :].astype(F32) + mxu(hot[:, span], embed, TN)
            if side == 0:
                x_in[span, :] = value
            low = value.astype(BF16)
            x_low[out, :] = low
            q = mxu(low, whole[:, 0:HALF], NN)
            qkv[out, 0:HALF] = ((q + bias_q) * scale).astype(BF16)
            k = mxu(low, whole[:, HALF : 2 * HALF], NN)
            qkv[out, HALF : 2 * HALF] = k.astype(BF16)
            v = mxu(low, whole[:, 2 * HALF : 3 * HALF], NN)
            qkv[out, 2 * HALF :] = (v + bias_v).astype(BF16)


def project(place, own, other, kinds, mask, blocks):
    rows, width = own.shape
    return run(
        project_kernel,
        "project",
        [(place, "smem"), (own, "vmem"), (other, "vmem"), (kinds, "vmem"), (mask, "vmem")]
        + [(block, "vmem") for block in blocks],
        [
            ((2 * rows, width), BF16),
            ((rows, width), F32),
            ((2 * rows, 3 * HALF), BF16),
            ((2 * rows, 128), BF16),
            ((16, width), F32),
            ((width, 3 * HALF + 128), BF16),
        ],
    )


def attend_kernel(qkv, masked_ref, out_ref, log_ref, *, block):
    length = qkv.shape[0]
    pairs = qkv.shape[1] // 384
    lane = lax.broadcasted_iota(jnp.int32, (1, 128), 1)
    one = jnp.broadcast_to(jnp.where(lane == 0, 1.0, 0.0).astype(jnp.bfloat16), (block, 128))
    ones = jnp.ones((length, 128), jnp.bfloat16)
    for pair in range(pairs):
        take = lambda j: slice((j * pairs + pair) * 128, (j * pairs + pair + 1) * 128)
        keys = jnp.concatenate([qkv[:, take(1)], masked_ref[...]], axis=1)
        values = jnp.concatenate([qkv[:, take(2)], ones], axis=1)
        for i in range(length // block):
            span = slice(i * block, (i + 1) * block)
            query = qkv[span, take(0)]
            outs, logs = [], []
            for head in range(2):
                here = (lane < 64) if head == 0 else (lane >= 64)
                only = jnp.where(here, query, jnp.zeros_like(query))
                scores = mxu(jnp.concatenate([only, one], axis=1), keys, NT)
                top = jnp.max(scores, axis=1, keepdims=True)
                weight = jnp.exp2(scores - top).astype(jnp.bfloat16)
                mixed = mxu(weight, values, NN)
                total = mixed[:, 128:]
                outs.append(mixed[:, :128] / total)
                logs.append(top + jnp.log2(total[:, 0:1]))
            out_ref[span, take(0)] = jnp.where(lane < 64, outs[0], outs[1]).astype(jnp.bfloat16)
            so_far = log_ref[span, :] if pair else jnp.zeros((block, 128), F32)
            both = jnp.where(lane == 2 * pair, logs[0], jnp.where(lane == 2 * pair + 1, logs[1], so_far))
            log_ref[span, :] = both


def attend(qkv, masked, block=256):
    length, columns = qkv.shape
    return run(
        functools.partial(attend_kernel, block=block),
        "attend",
        [(qkv, "vmem"), (masked, "vmem")],
        [((length, columns // 3), BF16), ((length, 128), F32)],
        limit=8,
    )


def attend_back_kernel(
    place, qkv, out, own_ref, got_ref, log_ref, masked_ref, out_ref, *refs, role, parts, block
):
    dk_sum, dv_sum = refs[-2], refs[-1]
    length, rows = qkv.shape[0], own_ref.shape[0]
    pairs = qkv.shape[1] // 384
    bf16 = jnp.bfloat16
    core = place[2]
    pair = (1 - core, core, 2)[role]
    take = lambda j: pl.ds(pl.multiple_of((j * pairs + pair) * 128, 128), 128)
    lane = lax.broadcasted_iota(jnp.int32, (1, 128), 1)
    ones = jnp.where((lane >= 1) & (lane <= 3), 1.0, 0.0).astype(bf16)
    masked = masked_ref[...]
    keys = jnp.concatenate(
        [qkv[:, take(1)], jnp.where(lane == 0, masked, jnp.broadcast_to(ones, masked.shape))], axis=1
    )
    three = jnp.broadcast_to(jnp.where(lane <= 2, 1.0, 0.0).astype(bf16), (length, 128))
    values = jnp.concatenate([qkv[:, take(2)], three], axis=1)
    keys_t = qkv[:, take(1)].T
    one = jnp.ones((block, 128), bf16)
    zero = jnp.zeros((block, 128), bf16)
    row = lax.broadcasted_iota(jnp.int32, (128, 1), 0)
    for i in range(length // block):
        span = slice(i * block, (i + 1) * block)
        at = i * block % rows
        query = qkv[span, take(0)]
        grad = (own_ref if i * block < rows else got_ref)[at : at + block, take(0)]
        both = grad.astype(jnp.float32) * out[span, take(0)].astype(jnp.float32)
        logs = log_ref[span, :]
        turned = []
        for head in range(2):
            here = (lane < 64) if head == 0 else (lane >= 64)
            inner = jnp.sum(jnp.where(here, both, 0.0), axis=1, keepdims=True)
            wide = lambda t: jnp.broadcast_to(t, (block, 128))
            log = jnp.sum(jnp.where(lane == 2 * pair + head, logs, 0.0), axis=1, keepdims=True)
            i0, i1, i2 = (wide(t) for t in three_parts(-inner))
            l0, l1, l2 = (wide(t) for t in three_parts(-log))
            query_h = jnp.where(here, query, zero)
            grad_h = jnp.where(here, grad, zero)
            tail_q = jnp.where(
                lane == 0,
                one,
                jnp.where(lane == 1, l0, jnp.where(lane == 2, l1, jnp.where(lane == 3, l2, zero))),
            )
            tail_g = jnp.where(lane == 0, i0, jnp.where(lane == 1, i1, jnp.where(lane == 2, i2, zero)))
            prob = jnp.exp2(mxu(keys, jnp.concatenate([query_h, tail_q], axis=1), NT))
            slope = mxu(values, jnp.concatenate([grad_h, tail_g], axis=1), NT)
            grad_scores = (prob * slope).astype(bf16)
            add_v = mxu(prob.astype(bf16), grad_h, NN)
            add_k = mxu(grad_scores, query_h, NN)
            if i == 0 and head == 0:
                dv_sum[...] = add_v
                dk_sum[...] = add_k
            else:
                dv_sum[...] += add_v
                dk_sum[...] += add_k
            turned.append(mxu(keys_t, grad_scores, NN))
        out_ref[span, 0:128] = (jnp.where(row < 64, turned[0], turned[1]) * 0.125).T.astype(bf16)
    out_ref[:, 128:256] = (dk_sum[...] * LN2).astype(bf16)
    out_ref[:, 256:384] = dv_sum[...].astype(bf16)
    if parts:
        keep_ref, give_ref, wide_ref = refs[:3]
        wide_ref[:, 0:384] = out_ref[...]
        wide_ref[:, 384:512] = jnp.zeros((length, 128), bf16)
        keep_ref[...] = wide_ref[:, pl.ds(pl.multiple_of(core * 256, 128), 256)]
        give_ref[...] = wide_ref[:, pl.ds(pl.multiple_of((1 - core) * 256, 128), 256)]


def attend_back(place, qkv, out, own, got, log_sum, masked, role, parts=False, block=512):
    length = qkv.shape[0]
    return run(
        functools.partial(attend_back_kernel, role=role, parts=parts, block=block),
        "attend_back",
        [(place, "smem")] + [(v, "vmem") for v in (qkv, out, own, got, log_sum, masked)],
        [((length, 384), BF16)] + [((length, 256), BF16)] * (2 * parts),
        [pltpu.VMEM((length, 512), BF16)] * parts + [pltpu.VMEM((length, 128), F32)] * 2,
        limit=14,
    )


def mix_kernel(
    place, heads, got, x_in, params, w0, w1, out_low, unit, scale, first_low, whole
):
    x, y, core = place[0], place[1], place[2]
    rows = x_in.shape[0]
    place_out(place, w0, w1, whole)
    mine = pl.multiple_of(x * HALF, 128)
    theirs = pl.multiple_of((1 - x) * HALF, 128)
    out_low[:, pl.ds(mine, HALF)] = heads[0:rows, :]
    out_low[:, pl.ds(theirs, HALF)] = got[...]
    step = 256
    for i in range(rows // step):
        span = slice(i * step, (i + 1) * step)
        mixed = mxu(out_low[span, :], whole[...], NN) + params[2:3, :]
        ones, size = unit_rows(x_in[span, :] + mixed)
        unit[span, :] = ones
        scale[span, :] = jnp.broadcast_to(size, (step, 128))
        first_low[span, :] = (ones * params[4:5, :] + params[5:6, :]).astype(BF16)


def mix(place, heads, got, x_in, params, blocks):
    rows, width = x_in.shape
    return run(
        mix_kernel,
        "mix",
        [(place, "smem"), (heads, "vmem"), (got, "vmem"), (x_in, "vmem"), (params, "vmem")]
        + [(block, "vmem") for block in blocks],
        [
            ((rows, width), BF16),
            ((rows, width), F32),
            ((rows, 128), F32),
            ((rows, width), BF16),
            ((width, width), BF16),
        ],
    )


def gelu_and_slope(up):
    size = jnp.abs(up)
    t = 1.0 / (1.0 + (0.3275911 * math.sqrt(0.5)) * size)
    bell = jnp.exp(-0.5 * up * up)
    poly = t * (
        0.5 * 0.254829592
        + t
        * (
            0.5 * -0.284496736
            + t * (0.5 * 1.421413741 + t * (0.5 * -1.453152027 + t * (0.5 * 1.061405429)))
        )
    )
    tail = poly * bell
    below = jnp.where(up < 0, tail, 1.0 - tail)
    return up * below, below + up * bell * (1.0 / math.sqrt(2.0 * math.pi))


def up_kernel(place, own, other, params, w0, w1, act, slope, whole, *, which, y_last):
    core = place[2]
    rows = own.shape[0]
    place_rows(eight(place, (w0, w1, y_last)), whole)
    bias = params[pl.ds(8 + 2 * core + which, 1), :]
    step = 128
    for side in range(2):
        source = own if side == 0 else other
        for i in range(rows // step):
            out = slice(side * rows + i * step, side * rows + (i + 1) * step)
            up = mxu(source[i * step : (i + 1) * step, :], whole[...], NN) + bias
            value, change = gelu_and_slope(up)
            act[out, :] = value.astype(BF16)
            slope[out, :] = change.astype(BF16)


def raise_up(place, own, other, params, block, which):
    rows, width = own.shape
    *refs, y_last = block
    return run(
        functools.partial(up_kernel, which=which, y_last=y_last),
        "raise_up",
        [(place, "smem"), (own, "vmem"), (other, "vmem"), (params, "vmem")] + [(r, "vmem") for r in refs],
        [((2 * rows, QUARTER), BF16), ((2 * rows, QUARTER), BF16), ((width, QUARTER), BF16)],
        limit=8,
    )


def lower_kernel(place, act, w0, w1, out, whole, *, y_last):
    place_rows(eight(place, (w0, w1, y_last)), whole)
    step = 256
    for i in range(act.shape[0] // step):
        span = slice(i * step, (i + 1) * step)
        out[span, :] = mxu(act[span, :], whole[...], NT)


def lower(place, act, block):
    rows, columns = act.shape
    *refs, y_last = block
    return run(
        functools.partial(lower_kernel, y_last=y_last),
        "lower",
        [(place, "smem"), (act, "vmem")] + [(r, "vmem") for r in refs],
        [((rows, MODEL_WIDTH), F32), ((MODEL_WIDTH, columns), BF16)],
        limit=8,
    )


def lower_other_kernel(place, act, so_far, w0, w1, out, whole, *, y_last):
    place_rows(eight(place, (w0, w1, y_last)), whole)
    rows = out.shape[0]
    step = 256
    for i in range(rows // step):
        span = slice(rows + i * step, rows + (i + 1) * step)
        value = so_far[span, :] + mxu(act[span, :], whole[...], NT)
        out[i * step : (i + 1) * step, :] = value.astype(BF16)


def lower_other(place, act, so_far, block):
    rows, columns = act.shape
    *refs, y_last = block
    return run(
        functools.partial(lower_other_kernel, y_last=y_last),
        "lower_other",
        [(place, "smem"), (act, "vmem"), (so_far, "vmem")] + [(r, "vmem") for r in refs],
        [((rows // 2, MODEL_WIDTH), BF16), ((MODEL_WIDTH, columns), BF16)],
        limit=8,
    )


def turn_kernel(
    place,
    act,
    so_far,
    got,
    unit1,
    params,
    grad,
    whole,
    block_out,
    grad_second,
    grad_low,
    sums,
):
    rows = got.shape[0]
    step = 128
    total = [jnp.zeros((1, MODEL_WIDTH), F32)] * 3
    for i in range(rows // step):
        span = slice(i * step, (i + 1) * step)
        first = unit1[span, :] * params[4:5, :] + params[5:6, :]
        value = so_far[span, :] + mxu(act[span, :], whole[...], NT) + got[span, :].astype(F32)
        unit, scale = unit_rows(first + (value + params[3:4, :]))
        block_out[span, :] = (unit * params[6:7, :] + params[7:8, :]).astype(BF16)
        dy = grad[span, :].astype(F32)
        back = unit_back(dy, unit, scale, params[6:7, :])
        grad_second[span, :] = back
        low = back.astype(BF16)
        grad_low[span, :] = low
        total[0] += down_sum(low.astype(F32))
        total[1] += down_sum(unit * dy)
        total[2] += down_sum(dy)
    sums[...] = jnp.concatenate(total + [jnp.zeros((5, MODEL_WIDTH), F32)], axis=0)


def turn(place, act, so_far, got, unit1, params, grad, weight):
    rows, width = got.shape
    return run(
        turn_kernel,
        "turn",
        [
            (place, "smem"),
            (act, "vmem"),
            (so_far, "vmem"),
            (got, "vmem"),
            (unit1, "vmem"),
            (params, "vmem"),
            (grad, "vmem"),
            (weight, "vmem"),
        ],
        [((rows, width), BF16), ((rows, width), F32), ((rows, width), BF16), ((8, width), F32)],
        limit=8,
    )


def raise_back_kernel(place, own, other, slope, whole, grad_up, sums):
    rows = own.shape[0]
    step = 256
    total = jnp.zeros((1, slope.shape[1]), F32)
    for side in range(2):
        source = own if side == 0 else other
        for i in range(rows // step):
            out = slice(side * rows + i * step, side * rows + (i + 1) * step)
            value = mxu(source[i * step : (i + 1) * step, :], whole[...], NN)
            low = (value * slope[out, :].astype(F32)).astype(BF16)
            grad_up[out, :] = low
            total += down_sum(low.astype(F32))
    sums[...] = jnp.broadcast_to(total, sums.shape)


def raise_back(place, own, other, slope, weight):
    rows, width = own.shape
    columns = slope.shape[1]
    return run(
        raise_back_kernel,
        "raise_back",
        [(place, "smem"), (own, "vmem"), (other, "vmem"), (slope, "vmem"), (weight, "vmem")],
        [((2 * rows, columns), BF16), ((8, columns), F32)],
        limit=8,
    )


def outer_kernel(place, left_own, left_other, right_own, right_other, mine, theirs, whole, *, y_last):
    whole[...] = mxu(left_own[...], right_own[...], TN) + mxu(left_other[...], right_other[...], TN)
    split_rows(whole, mine, theirs, place, y_last)


def outer_joined_kernel(place, left_own, left_other, right, mine, theirs, whole, *, y_last):
    rows = left_own.shape[0]
    whole[...] = mxu(left_own[...], right[0:rows, :], TN) + mxu(left_other[...], right[rows:, :], TN)
    split_rows(whole, mine, theirs, place, y_last)


def outer_wide_kernel(place, left_own, left_other, first, second, mine, theirs, whole):
    rows = left_own.shape[0]
    n = first.shape[1]
    for j, right in enumerate((first, second)):
        value = mxu(left_own[...], right[0:rows, :], TN) + mxu(left_other[...], right[rows:, :], TN)
        whole[:, j * n : (j + 1) * n] = value
    split_rows(whole, mine, theirs, place, True)


def outer_wide(place, left_own, left_other, first, second):
    width = left_own.shape[1]
    columns = 2 * first.shape[1]
    return run(
        outer_wide_kernel,
        "outer_wide",
        [(place, "smem")] + [(r, "vmem") for r in (left_own, left_other, first, second)],
        [((4, 96, columns), BF16), ((4, 96, columns), BF16)],
        [pltpu.VMEM((width, columns), F32)],
        limit=14,
    )


def outer(place, left_own, left_other, rights, name, y_last=True):
    rows, width = left_own.shape
    columns = rights[0].shape[1]
    return run(
        functools.partial(outer_kernel if len(rights) == 2 else outer_joined_kernel, y_last=y_last),
        name,
        [(place, "smem"), (left_own, "vmem"), (left_other, "vmem")] + [(r, "vmem") for r in rights],
        [((4, 96, columns), BF16), ((4, 96, columns), BF16)],
        [pltpu.VMEM((width, columns), F32)],
        limit=12,
    )


def first_other_kernel(place, grad_a, grad_b, whole_a, whole_b, out):
    rows = out.shape[0]
    step = 256
    for i in range(rows // step):
        span = slice(rows + i * step, rows + (i + 1) * step)
        value = mxu(grad_a[span, :], whole_a[...], NT) + mxu(grad_b[span, :], whole_b[...], NT)
        out[i * step : (i + 1) * step, :] = value.astype(BF16)


def first_other(place, grad_a, grad_b, weight_a, weight_b):
    rows, columns = grad_a.shape
    return run(
        first_other_kernel,
        "first_other",
        [(place, "smem")] + [(r, "vmem") for r in (grad_a, grad_b, weight_a, weight_b)],
        [((rows // 2, MODEL_WIDTH), BF16)],
        limit=8,
    )[0]


def first_back_kernel(
    place,
    grad_a,
    grad_b,
    got_first,
    got_last,
    grad_second,
    unit1,
    scale1,
    params,
    whole_a,
    whole_b,
    whole_o,
    grad_first_in,
    mixed_keep,
    mixed_give,
    heads_keep,
    heads_give,
    sums,
    low_all,
    heads_all,
):
    x, core = place[0], place[2]
    step = got_first.shape[0]
    rows = 2 * step
    total = [jnp.zeros((1, MODEL_WIDTH), F32)] * 3
    for i in range(rows // step):
        span = slice(i * step, (i + 1) * step)
        value = mxu(grad_a[span, :], whole_a[...], NT) + mxu(grad_b[span, :], whole_b[...], NT)
        got = (got_first, got_last)[i]
        dh = grad_second[span, :] + value + got[...].astype(F32)
        unit = unit1[span, :]
        back = unit_back(dh, unit, scale1[span, 0:1], params[4:5, :])
        grad_first_in[span, :] = back
        low = back.astype(BF16)
        low_all[span, :] = low
        total[0] += down_sum(low.astype(F32))
        total[1] += down_sum(unit * dh)
        total[2] += down_sum(dh)
        heads_all[span, :] = mxu(low, whole_o[...], NT).astype(BF16)
    sums[...] = jnp.concatenate(total + [jnp.zeros((5, MODEL_WIDTH), F32)], axis=0)
    half = lambda i: pl.ds(pl.multiple_of(i * HALF, 128), HALF)
    mixed_keep[...] = low_all[:, half(core)]
    mixed_give[...] = low_all[:, half(1 - core)]
    heads_keep[...] = heads_all[:, half(x)]
    heads_give[...] = heads_all[:, half(1 - x)]


def first_back(place, *arrays):
    rows, width = arrays[4].shape
    return run(
        first_back_kernel,
        "first_back",
        [(place, "smem")] + [(r, "vmem") for r in arrays],
        [
            ((rows, width), F32),
            ((rows, HALF), BF16),
            ((rows, HALF), BF16),
            ((rows, HALF), BF16),
            ((rows, HALF), BF16),
            ((8, width), F32),
        ],
        [pltpu.VMEM((rows, width), BF16)] * 2,
        limit=10,
    )


def enter_kernel(
    place, d_give, d_keep, d_last, grad_first_in, kinds, sums1, sums2, sums_a, sums_b, whole, own, give, small
):
    x, core = place[0], place[2]
    rows = own.shape[0]
    pairs = ((d_give, 1 - core), (d_keep, core), (d_last, 2))
    small[...] = jnp.zeros_like(small)
    for ref, pair in pairs:
        at = pl.ds(pl.multiple_of(x * HALF + pair * 128, 128), 128)
        small[0:1, at] = down_sum(ref[:, 0:128].astype(F32))
        small[1:2, at] = down_sum(ref[:, 256:384].astype(F32))
    small[2:3, :] = sums1[0:1, :]
    small[3:4, :] = sums2[0:1, :]
    small[4:6, :] = sums1[1:3, :]
    small[6:8, :] = sums2[1:3, :]
    small[pl.ds(8 + 2 * core, 1), :] = sums_a[0:1, :]
    small[pl.ds(9 + 2 * core, 1), :] = sums_b[0:1, :]
    weights = []
    for _, pair in pairs:
        tiles = [whole[:, pl.ds(pl.multiple_of(j * HALF + pair * 128, 128), 128)] for j in range(3)]
        weights.append(jnp.concatenate(tiles, axis=1))
    lane_row = lax.broadcasted_iota(jnp.int32, (8, rows), 0)
    step = 256
    embed = jnp.zeros((8, MODEL_WIDTH), F32)
    for side in (1, 0):
        start = pl.multiple_of((x if side == 0 else 1 - x) * rows, 128)
        hot = jnp.where(kinds[:, pl.ds(start, rows)] == lane_row, 1.0, 0.0).astype(BF16)
        for i in range(rows // step):
            span = slice(i * step, (i + 1) * step)
            source = slice(side * rows + i * step, side * rows + (i + 1) * step)
            value = sum(mxu(ref[source, :], weight, NT) for (ref, _), weight in zip(pairs, weights))
            if side == 0:
                value = value + grad_first_in[span, :]
                own[span, :] = value
            else:
                give[span, :] = value.astype(BF16)
            take = hot[:, span]
            for term in three_parts(value):
                embed += mxu(take, term, NN)
    small[12:15, :] = embed[0:3, :]


def enter(place, *arrays):
    rows, width = arrays[3].shape
    return run(
        enter_kernel,
        "enter",
        [(place, "smem")] + [(r, "vmem") for r in arrays],
        [((rows, width), F32), ((rows, width), BF16), ((16, width), F32)],
        limit=12,
    )


def narrow_kernel(place, own, other, mine, theirs, whole):
    small = own[...] + other[...]
    rest = jnp.zeros((128 - small.shape[0], small.shape[1]), F32)
    whole[...] = jnp.concatenate([small, rest], axis=0).T
    split_rows(whole, mine, theirs, place, True)


def narrow(place, own, other):
    return run(
        narrow_kernel,
        "narrow",
        [(place, "smem"), (own, "vmem"), (other, "vmem")],
        [((4, 96, 128), BF16)] * 2,
        [pltpu.VMEM((own.shape[1], 128), F32)],
        limit=4,
    )


def fold_kernel(mine, got, keep, send):
    half = mine.shape[0] // 2
    for i in range(2 * half):
        value = mine[i].astype(F32) + got[i].astype(F32)
        if i < half:
            keep[i] = value
        else:
            send[i - half] = value.astype(BF16)


def fold(mine, got, name="fold"):
    shape = (mine.shape[0] // 2,) + mine.shape[1:]
    return run(
        fold_kernel,
        name,
        [(mine, "vmem"), (got, "vmem")],
        [(shape, F32), (shape, BF16)],
        limit=4,
    )


def fold_two_kernel(mine_a, got_a, mine_b, got_b, keep, send):
    n = mine_a.shape[2]
    half = keep.shape[0]
    for i in range(2 * half):
        for mine, got, lanes in ((mine_a, got_a, slice(0, n)), (mine_b, got_b, slice(n, keep.shape[2]))):
            value = mine[i].astype(F32) + got[i].astype(F32)
            if i < half:
                keep[i, :, lanes] = value
            else:
                send[i - half, :, lanes] = value.astype(BF16)


def fold_two(mine_a, got_a, mine_b, got_b, name="fold_two"):
    shape = (mine_a.shape[0] // 2, 96, mine_a.shape[2] + mine_b.shape[2])
    return run(
        fold_two_kernel,
        name,
        [(v, "vmem") for v in (mine_a, got_a, mine_b, got_b)],
        [(shape, F32), (shape, BF16)],
        limit=4,
    )


def settle_kernel(place, *refs):
    *sources, keep, send = refs
    core = place[2]
    column = 0
    for i in range(0, len(sources), 2):
        one, two = sources[i : i + 2]
        n = one.shape[2]
        lanes = slice(column, column + n)
        for j, whose in enumerate((core, 1 - core)):
            rows = pl.ds(pl.multiple_of(whose * 48, 16), 48)
            value = one[0, rows, :] + two[0, rows, :].astype(F32)
            keep[j, :, lanes] = value
            send[j, :, lanes] = value.astype(BF16)
        column += n


def settle(place, groups):
    sources = [array for group in groups for array in group]
    n = sum(group[0].shape[2] for group in groups)
    return run(
        settle_kernel,
        "settle",
        [(place, "smem")] + [(array, "vmem") for array in sources],
        [((2, 48, n), F32), ((2, 48, n), BF16)],
        limit=4,
    )


def join_kernel(keep, got, near, far):
    near[...] = keep[0] + got[0].astype(F32)
    far[...] = (keep[1] + got[1].astype(F32)).astype(BF16)


def join(keep, got):
    shape = keep.shape[1:]
    return run(join_kernel, "join", [(keep, "vmem"), (got, "vmem")], [(shape, F32), (shape, BF16)], limit=4)


def step_of(weight, momentum, average, grad, rate, decay):
    moved = grad + decay * weight if decay else grad
    new_momentum = momentum_rate * momentum + moved
    new = weight - rate * (moved + momentum_rate * new_momentum)
    return grad, new, new_momentum, average_rate * average + (1.0 - average_rate) * new


def update_rest_kernel(
    place, mats, momentum, average, *refs, rate, groups
):
    sources, outs, work, sems = refs[: 2 * groups], refs[2 * groups : 2 * groups + 4], refs[-5:-1], refs[-1]
    width = MODEL_WIDTH
    base = 3 * width
    for whose in range(2):
        core = place[2] if whose == 0 else 1 - place[2]
        for g in range(groups):
            source = sources[2 * g + whose]
            if g == 0:
                parts = ((8 * width + 2 * core * QUARTER, QUARTER), (8 * width + (2 * core + 1) * QUARTER, QUARTER))
            else:
                parts = (
                    (4 * width + 2 * core * QUARTER, QUARTER),
                    (4 * width + (2 * core + 1) * QUARTER, QUARTER),
                    (3 * width + core * HALF, HALF),
                )
            column = 0
            for first, n in parts:
                lanes = slice(column, column + n)
                grad = source[:, lanes].astype(F32)
                at = pl.ds(pl.multiple_of(first, 128), n)
                results = step_of(mats[:, at], momentum[:, at], average[:, at], grad, rate, decay_rate)
                to = pl.ds(pl.multiple_of(first - base, 128), n)
                for ref, value in zip(work, results):
                    ref[:, to] = value
                column += n
    copies = []
    for i in range(4):
        copy = pltpu.make_async_copy(work[i], outs[i].at[:, pl.ds(base, work[i].shape[1])], sems.at[i])
        copy.start()
        copies.append(copy)
    for copy in copies:
        copy.wait()


def update_rest(place, mats, momentum, average, groups, rate):
    rows, columns = mats.shape
    sources = [array for group in groups for array in group]
    n = columns - 3 * MODEL_WIDTH
    return pl.pallas_call(
        functools.partial(update_rest_kernel, rate=rate, groups=len(groups)),
        in_specs=[pl.BlockSpec(memory_space=pltpu.SMEM)]
        + [pl.BlockSpec(memory_space=pltpu.VMEM)] * (3 + len(sources)),
        out_specs=[pl.BlockSpec(memory_space=pl.ANY)] * 4,
        out_shape=[jax.ShapeDtypeStruct((rows, columns), F32)] * 4,
        scratch_shapes=[pltpu.VMEM((rows, n), F32)] * 4 + [pltpu.SemaphoreType.DMA((4,))],
        compiler_params=pltpu.CompilerParams(vmem_limit_bytes=10 * 2**20),
        cost_estimate=declared("update_rest"),
        name="update_rest",
    )(place, mats, momentum, average, *sources)


def update_heads_kernel(
    place,
    mats,
    momentum,
    average,
    keep,
    from_seq,
    from_core,
    from_both,
    s_value,
    s_momentum,
    s_average,
    a0,
    a1,
    a2,
    a3,
    o0,
    o1,
    o2,
    o3,
    s0,
    s1,
    s2,
    s3,
    bias,
    w0,
    w1,
    w2,
    w3,
    grads,
    sems,
    *,
    rate,
):
    x, core = place[0], place[2]
    width = MODEL_WIDTH
    grads[x, core] = keep[0]
    grads[1 - x, core] = from_seq[...].astype(F32)
    grads[x, 1 - core] = from_core[...].astype(F32)
    grads[1 - x, 1 - core] = from_both[...].astype(F32)
    work = (w0, w1, w2, w3)
    last = ((0, 384), (0, 512), (1, 384))
    for j in range(3):
        for side in range(2):
            at = slice(j * width + side * HALF, j * width + (side + 1) * HALF)
            tiles = [grads[side, c, :, j * 128 : (j + 1) * 128] for c in range(2)]
            c, first = last[j]
            tiles.append(grads[side, c, :, first : first + 128])
            grad = jnp.concatenate(tiles, axis=1)
            results = step_of(mats[:, at], momentum[:, at], average[:, at], grad, rate, decay_rate)
            for ref, value in zip(work, results):
                ref[:, at] = value
    copies = []
    for i, out in enumerate((o0, o1, o2, o3)):
        copy = pltpu.make_async_copy(work[i], out.at[:, pl.ds(0, 3 * width)], sems.at[i])
        copy.start()
        copies.append(copy)
    small = (grads[x, core, :, 640:] + grads[1 - x, core, :, 640:]).T[0:16]
    n = s_value.shape[0]
    results = step_of(s_value[...], s_momentum[...], s_average[...], small[0:n], rate, 0.0)
    for ref, value in zip((s0, s1, s2, s3), results):
        ref[...] = value
    bias[...] = small[2:3]
    for copy in copies:
        copy.wait()


def update_heads(place, mats, momentum, average, group, smalls, so_far, rate):
    rows, columns = mats.shape
    n = 3 * MODEL_WIDTH
    vmem = pl.BlockSpec(memory_space=pltpu.VMEM)
    anywhere = pl.BlockSpec(memory_space=pl.ANY)
    shape = smalls[0].shape
    return pl.pallas_call(
        functools.partial(update_heads_kernel, rate=rate),
        in_specs=[pl.BlockSpec(memory_space=pltpu.SMEM)] + [vmem] * 10 + [anywhere] * 4,
        out_specs=[anywhere] * 4 + [vmem] * 5,
        out_shape=[jax.ShapeDtypeStruct((rows, columns), F32)] * 4 + [jax.ShapeDtypeStruct(shape, F32)] * 4
        + [jax.ShapeDtypeStruct((1, rows), F32)],
        scratch_shapes=[pltpu.VMEM((rows, n), F32)] * 4
        + [pltpu.VMEM((2, 2, rows, 768), F32), pltpu.SemaphoreType.DMA((4,))],
        input_output_aliases={11 + i: i for i in range(4)},
        compiler_params=pltpu.CompilerParams(vmem_limit_bytes=6 * 2**20),
        cost_estimate=declared("update_heads"),
        name="update_heads",
    )(place, mats, momentum, average, *group, *smalls, *so_far)


SEQ_SWAP = [(0, 1), (1, 0)]
CORE_SWAP = [(i, i ^ 1) for i in range(16)]
Y_SWAP = [(i, i ^ 2) for i in range(16)]


def over_seq(value):
    return lax.ppermute(value, "seq", SEQ_SWAP)


def over_core(value):
    return lax.ppermute(value, "dp", CORE_SWAP)


def over_y(value):
    return lax.ppermute(value, "dp", Y_SWAP)


def over_z1(value):
    return lax.ppermute(value, "dp", [(i, i ^ 4) for i in range(16)])


def over_z2(value):
    return lax.ppermute(value, "dp", [(i, i ^ 8) for i in range(16)])


def over_both(value):
    return lax.ppermute(value, ("dp", "seq"), [(i, i ^ 3) for i in range(32)])


def pin(value, *after):
    return lax.optimization_barrier((value, after))[0]


def exchange(place, groups, *after):
    keep, send = settle(place, groups)
    near, far = join(keep, over_seq(pin(send, *after) if after else send))
    return near, over_core(far)


def tuned(
    inputs,
    modality,
    key_valid_mask,
    output_gradient,
    mats,
    mats_momentum,
    mats_average,
    smalls,
    smalls_momentum,
    smalls_average,
):
    width = MODEL_WIDTH
    rows = inputs.shape[1]
    dp = lax.axis_index("dp")
    x = lax.axis_index("seq")
    core = dp % 2
    y = (dp // 2) % 2
    place = jnp.stack([x, y, core, dp // 4]).astype(jnp.int32)

    att_own = pack_heads(place, mats, smalls.T)[None]
    att_got = over_z2(att_own)
    other_inputs = over_seq(inputs[0])
    keep, give = pack_rest(pin(place, att_own), mats)
    blocks = pair_up(place, keep, over_core(give))
    att_two = both(att_own, pin(att_got, blocks))
    att0 = both(att_two, over_z1(att_two))
    two0 = both(blocks[0], pin(over_z2(pin(blocks[0], att_two)), att0))
    att2 = pin(over_y(att0), other_inputs)
    att = (att0, over_core(att0), att2, over_core(att2))
    line0 = over_z1(two0)

    x_low, x_in, qkv, masked, params, w_qkv = project(
        pin(place, two0), inputs[0], other_inputs, modality, key_valid_mask, att
    )
    line0 = both(two0, pin(line0, qkv))
    up0 = (line0, over_y(line0), True)
    got1 = over_z2(pin(blocks[1], qkv))
    heads, log_sum = attend(qkv, pin(masked, line0))
    got1 = pin(got1, heads)
    got_heads = over_seq(pin(heads, got1)[rows:])
    two1 = both(blocks[1], got1)
    line1 = both(two1, over_z1(two1))
    x_got = over_core(x_low)
    two2 = both(blocks[2], pin(over_z2(pin(blocks[2], heads)), line1))
    got_heads, y_0 = pin((got_heads, up0[1]), two2)
    out_mine = last_columns(line0, y_0)
    out_w = (out_mine, over_core(out_mine))
    up1 = (line1, over_y(line1), True)
    line2 = both(two2, pin(over_z1(two2), got_heads))
    two3 = both(blocks[3], pin(over_z2(pin(blocks[3], line1)), got_heads))
    out_low, unit1, scale1, first_low, w_out = mix(
        pin(place, up1[1], line2, two3, x_got), heads, got_heads, x_in, params, out_w
    )
    down0 = (line2, over_y(line2), True)
    first_got = over_core(first_low)
    out_got = over_core(out_low)
    act0, slope0, w_up0 = raise_up(place, first_low, first_got, params, up0, 0)
    square3 = both(two3, pin(over_y(two3), act0))
    down1 = (square3, over_z1(square3), False)
    act1, slope1, w_up1 = raise_up(
        pin(place, square3, out_got), first_low, first_got, params, up1, 1
    )
    so_far, w_down0 = lower(pin(place, act1), act0, down0)
    sum_give, w_down1 = lower_other(place, act1, so_far, down1)
    block_out, grad_second, grad_ffo, sums2 = turn(
        place, act1, so_far, over_core(sum_give), unit1, params, output_gradient[0], w_down1
    )

    ffo_got = over_core(grad_ffo)
    mine_d, theirs_d = outer_wide(place, grad_ffo, ffo_got, act0, act1)
    got_d = over_y(theirs_d)
    grad_up0, sums_up0 = raise_back(pin(place, mine_d), grad_ffo, ffo_got, slope0, w_down0)
    grad_up1, sums_up1 = raise_back(pin(place, grad_up0), grad_ffo, ffo_got, slope1, w_down1)
    first_give = first_other(place, grad_up0, grad_up1, w_up0, w_up1)
    first_out = first_back(
        place,
        grad_up0,
        grad_up1,
        over_core(first_give[0:256]),
        over_core(first_give[256:]),
        grad_second,
        unit1,
        scale1,
        params,
        w_up0,
        w_up1,
        w_out,
    )
    grad_first_in, mixed_keep, mixed_give, heads_keep, heads_give, sums1 = first_out
    heads_got = over_seq(heads_give)
    mixed_got = over_core(mixed_give)
    mine_u0, theirs_u0 = outer(pin(place, sums1), first_low, first_got, [grad_up0], "outer_up")
    got_u0 = over_y(theirs_u0)
    mine_u1, theirs_u1 = outer(
        pin(place, mine_u0), first_low, first_got, [grad_up1], "outer_up", y_last=False
    )
    got_u1 = over_z1(theirs_u1)
    heads_got = pin(heads_got, mine_u1)
    fold_d = fold(mine_d, pin(got_d, heads_got))
    got_d = over_z1(fold_d[1])
    mine_o, theirs_o = outer(
        pin(place, fold_d), out_low, out_got, [mixed_keep, mixed_got], "outer_out"
    )
    got_o = over_y(theirs_o)

    def back(role, masked, parts=False):
        return attend_back(place, qkv, heads, heads_keep, heads_got, log_sum, masked, role, parts)

    (d_give,) = back(0, pin(masked, mine_o))
    got_u1 = pin(got_u1, d_give)
    d_give = pin(d_give, got_u1)
    fold_u1 = fold(mine_u1, got_u1)
    got_u1 = over_y(fold_u1[1])
    d_got = over_core(d_give)
    (d_keep,) = back(1, pin(masked, fold_u1))
    got_u0, got_d = pin((got_u0, got_d), d_keep)
    d_keep = pin(d_keep, got_u0, got_d)
    fold_u0 = fold(mine_u0, got_u0, "long_fold")
    last_d = fold(fold_d[0], got_d)
    got_u0, got_d = over_z1(fold_u0[1]), over_z2(last_d[1])
    mine_q, theirs_q = outer(
        pin(place, fold_u0, last_d), x_low, x_got, [d_keep, pin(d_got, fold_u0)], "outer_heads"
    )
    got_q = over_y(theirs_q)
    d_last, cols_keep, cols_give = back(2, pin(masked, mine_q), True)
    down_keep, down_send = settle(place, [(last_d[0], pin(got_d, d_last))])
    down_got = over_seq(down_send)
    grad_x, give_x, small = enter(
        pin(place, down_keep),
        d_give,
        d_keep,
        d_last,
        grad_first_in,
        modality,
        sums1,
        sums2,
        sums_up0,
        sums_up1,
        w_qkv,
    )
    got_u1, got_o, got_u0, got_q = pin((got_u1, got_o, got_u0, got_q), small)
    give_x, small, cols_give = pin((give_x, small, cols_give), got_u1, got_o, got_u0, got_q)
    x_back = over_seq(give_x)
    last_u = fold_two(fold_u0[0], got_u0, fold_u1[0], got_u1)
    fold_o = fold(mine_o, got_o)
    got_u, got_o = over_z2(last_u[1]), over_z1(fold_o[1])
    cols_got = over_core(cols_give)
    fold_q = fold(mine_q, got_q, "long_fold")
    mine_r, theirs_r = outer(
        pin(place, last_u, fold_o, fold_q), x_low, x_got, [cols_keep, pin(cols_got, fold_q)], "outer_heads"
    )
    mine_s, theirs_s = narrow(pin(place, mine_r), small, over_core(small))
    last_o = fold(fold_o[0], pin(got_o, mine_s))
    got_last_o = over_z2(last_o[1])
    last_q = fold(fold_q[0], pin(over_z1(fold_q[1]), mine_s))
    fold_r = fold_two(mine_r, over_y(theirs_r), mine_s, over_y(theirs_s))
    got_u, got_last_o = pin((got_u, got_last_o), fold_r)
    last_r = fold(fold_r[0], over_z1(fold_r[1]))
    down_near, down_far = join(down_keep, pin(down_got, last_r))
    down_group = (down_near, over_core(down_far))

    rate = base_rate / math.sqrt(rows * lax.axis_size("dp") * lax.axis_size("seq"))
    up_group = exchange(place, [(last_u[0], got_u), (last_o[0], got_last_o)])
    heads_keep, heads_send = settle(place, [(v[0], over_z2(v[1])) for v in (last_q, last_r)])
    near, far = heads_send[0], heads_send[1]
    heads_group = (heads_keep, over_seq(near), over_core(far), over_both(far))
    x_back, up_near = pin((x_back, up_group[0]), heads_keep)
    up_group = (up_near, up_group[1])
    input_grad = (grad_x + x_back.astype(F32)).astype(BF16)[None]
    so_far = update_rest(place, mats, mats_momentum, mats_average, [down_group, up_group], rate)
    *new, s_grad, s_value, s_momentum, s_average, s_bias = update_heads(
        place,
        mats,
        mats_momentum,
        mats_average,
        heads_group,
        (smalls.T, smalls_momentum.T, smalls_average.T),
        so_far,
        rate,
    )
    return (
        block_out[None],
        input_grad,
        *new,
        s_grad.T,
        s_bias.reshape(-1),
        s_value.T,
        s_momentum.T,
        s_average.T,
    )


def solution(mesh):
    placed = (
        P("dp", "seq", None),
        P("dp", None),
        P("dp", None),
        P("dp", "seq", None),
        P("dp", None),
        P("dp", None),
        P("dp", None),
        P("dp", None),
        P("dp", None),
        P("dp", None),
    )
    plan = tuned if tuple(mesh.shape.values()) == (16, 2) else per_device
    return jax.shard_map(
        plan,
        mesh=mesh,
        in_specs=placed,
        out_specs=(
            P("dp", "seq", None),
            P("dp", "seq", None),
            P("dp", None),
            P("dp", None),
            P("dp", None),
            P("dp", None),
            P("dp", None),
            P("dp"),
            P("dp", None),
            P("dp", None),
            P("dp", None),
        ),
        check_vma=False,
    )
```

```python
import functools
import math

import jax
import jax.numpy as jnp
from jax import lax
from jax.experimental import pallas as pl
from jax.experimental.pallas import tpu as pltpu
from jax.sharding import PartitionSpec as P

MODEL_WIDTH = 768
H = 12
HD = 64
FF = 3072


epsilon = 1e-06
momentum_rate = 0.9
decay_rate = 0.0001
average_rate = 0.75
base_rate = 0.03
masked_score = -1e30


def product(left, right):
    return jnp.dot(left, right, preferred_element_type=jnp.float32)


def product_tn(left, right):
    return lax.dot_general(
        left, right, (((0,), (0,)), ((), ())), preferred_element_type=jnp.float32
    )


def product_nt(left, right):
    return lax.dot_general(
        left, right, (((1,), (1,)), ((), ())), preferred_element_type=jnp.float32
    )


def normalize(rows, gain, shift):
    mean = jnp.mean(rows, axis=-1, keepdims=True)
    centred = rows - mean
    spread = jnp.mean(centred * centred, axis=-1, keepdims=True)
    return centred * lax.rsqrt(spread + epsilon) * gain + shift


def exact_gelu(values):
    return jax.nn.gelu(values, approximate=False)


def head_scores(query_heads, key_heads, live_doc):
    scores = (
        jnp.einsum("qhe,khe->hqk", query_heads, key_heads, preferred_element_type=jnp.float32)
        * 0.125
    )
    return jnp.where(live_doc[None, None, :] > 0, scores, masked_score)


def attention_forward_pass(item):
    query_doc, keys_doc, values_doc, live_doc = item
    query_heads = query_doc.reshape(query_doc.shape[0], H, HD)
    key_heads = keys_doc.reshape(keys_doc.shape[0], H, HD)
    value_heads = values_doc.reshape(values_doc.shape[0], H, HD)
    scores = head_scores(query_heads, key_heads, live_doc)
    top = jnp.max(scores, axis=-1, keepdims=True)
    expd = jnp.exp(scores - top)
    total = jnp.sum(expd, axis=-1, keepdims=True)
    prob = (expd / total).astype(jnp.bfloat16)
    attention_output = jnp.einsum(
        "hqk,khe->qhe", prob, value_heads, preferred_element_type=jnp.float32
    )
    return (attention_output.reshape(query_doc.shape[0], H * HD), (top + jnp.log(total))[..., 0])


def attention_backward_pass(item):
    query_doc, keys_doc, values_doc, live_doc, log_sum_normalizer, grad_doc = item
    element_count = query_doc.shape[0]
    length = keys_doc.shape[0]
    query_heads = query_doc.reshape(element_count, H, HD)
    key_heads = keys_doc.reshape(length, H, HD)
    value_heads = values_doc.reshape(length, H, HD)
    grad_heads = grad_doc.reshape(element_count, H, HD)
    scores = head_scores(query_heads, key_heads, live_doc)
    prob = jnp.exp(scores - log_sum_normalizer[..., None])
    grad_prob = jnp.einsum(
        "qhe,khe->hqk", grad_heads, value_heads, preferred_element_type=jnp.float32
    )
    grad_values = jnp.einsum(
        "hqk,qhe->khe", prob.astype(jnp.bfloat16), grad_heads, preferred_element_type=jnp.float32
    )
    inner = jnp.sum(prob * grad_prob, axis=-1, keepdims=True)
    grad_scores = (prob * (grad_prob - inner)).astype(jnp.bfloat16)
    grad_query = (
        jnp.einsum("hqk,khe->qhe", grad_scores, key_heads, preferred_element_type=jnp.float32)
        * 0.125
    )
    grad_keys = (
        jnp.einsum("hqk,qhe->khe", grad_scores, query_heads, preferred_element_type=jnp.float32)
        * 0.125
    )
    return (
        grad_query.reshape(element_count, H * HD),
        grad_keys.reshape(length, H * HD),
        grad_values.reshape(length, H * HD),
    )


def per_device(
    inputs,
    modality,
    key_valid_mask,
    output_gradient,
    mats,
    mats_momentum,
    mats_average,
    smalls,
    smalls_momentum,
    smalls_average,
):
    docs, local_len, width = inputs.shape
    seq_len = modality.shape[1]
    rows = docs * local_len
    low_mats = mats.astype(jnp.bfloat16)
    w_qkv, w_out, w_up, w_down, whole_smalls = (
        lax.all_gather(low_mats[:, 0 : 3 * MODEL_WIDTH], "dp", axis=0, tiled=True),
        lax.all_gather(low_mats[:, 3 * MODEL_WIDTH : 4 * MODEL_WIDTH], "dp", axis=0, tiled=True),
        lax.all_gather(
            low_mats[:, 4 * MODEL_WIDTH : 4 * MODEL_WIDTH + FF], "dp", axis=0, tiled=True
        ),
        lax.all_gather(low_mats[:, 4 * MODEL_WIDTH + FF :], "dp", axis=0, tiled=True),
        lax.all_gather(smalls.astype(jnp.bfloat16), "dp", axis=0, tiled=True),
    )
    params = whole_smalls.astype(jnp.float32)
    bias_qkv = jnp.concatenate([params[:, 0], jnp.zeros_like(params[:, 0]), params[:, 1]])
    bias_up = jnp.transpose(params[:, 8:12]).reshape(FF)
    embed = jnp.transpose(whole_smalls[:, 12:15])
    leading_key = (jnp.arange(seq_len) == 0).astype(jnp.int32)
    valid_positions = jnp.maximum(key_valid_mask, leading_key[None, :])
    local_start = lax.axis_index("seq") * local_len
    local_modality = lax.dynamic_slice_in_dim(modality, local_start, local_len, 1)
    onehot = (
        local_modality.reshape(rows)[:, None] == jnp.arange(3, dtype=jnp.int32)[None, :]
    ).astype(jnp.bfloat16)
    x_in = inputs.reshape(rows, width).astype(jnp.float32) + product(onehot, embed)
    x_low = x_in.astype(jnp.bfloat16)
    qkv = (product(x_low, w_qkv) + bias_qkv).astype(jnp.bfloat16)
    query_documents = qkv[:, 0:width].reshape(docs, local_len, width)
    keys_local = qkv[:, width : 2 * width].reshape(docs, local_len, width)
    values_local = qkv[:, 2 * width :].reshape(docs, local_len, width)
    every_key, every_value = (
        lax.all_gather(keys_local, "seq", axis=1, tiled=True),
        lax.all_gather(values_local, "seq", axis=1, tiled=True),
    )
    attention_output, log_sum_normalizer = lax.map(
        attention_forward_pass, (query_documents, every_key, every_value, valid_positions)
    )
    out_low = attention_output.reshape(rows, width).astype(jnp.bfloat16)
    mixed = product(out_low, w_out) + params[:, 2]
    first_in = x_in + mixed
    first = normalize(first_in, params[:, 4], params[:, 5])
    first_low = first.astype(jnp.bfloat16)
    up = product(first_low, w_up) + bias_up
    act_low = exact_gelu(up).astype(jnp.bfloat16)
    ffo = product_nt(act_low, w_down) + params[:, 3]
    second_in = first + ffo
    result = normalize(second_in, params[:, 6], params[:, 7])
    block_out = result.astype(jnp.bfloat16).reshape(docs, local_len, width)
    w_qkv, w_out, w_up, w_down = (
        lax.all_gather(low_mats[:, 0 : 3 * MODEL_WIDTH], "dp", axis=0, tiled=True),
        lax.all_gather(low_mats[:, 3 * MODEL_WIDTH : 4 * MODEL_WIDTH], "dp", axis=0, tiled=True),
        lax.all_gather(
            low_mats[:, 4 * MODEL_WIDTH : 4 * MODEL_WIDTH + FF], "dp", axis=0, tiled=True
        ),
        lax.all_gather(low_mats[:, 4 * MODEL_WIDTH + FF :], "dp", axis=0, tiled=True),
    )
    grad_rows = output_gradient.reshape(rows, width).astype(jnp.float32)
    second_out, second_pull = jax.vjp(normalize, second_in, params[:, 6], params[:, 7])
    grad_second, grad_gain2, grad_shift2 = second_pull(grad_rows)
    grad_ffo = grad_second.astype(jnp.bfloat16)
    grad_bias_down = jnp.sum(grad_ffo.astype(jnp.float32), axis=0)
    grad_w_down = product_tn(grad_ffo, act_low)
    grad_act = product(grad_ffo, w_down)
    gelu_out, gelu_pull = jax.vjp(exact_gelu, up)
    grad_up = gelu_pull(grad_act)[0].astype(jnp.bfloat16)
    grad_bias_up = jnp.sum(grad_up.astype(jnp.float32), axis=0)
    grad_w_up = product_tn(first_low, grad_up)
    grad_first = grad_second + product_nt(grad_up, w_up)
    first_out, first_pull = jax.vjp(normalize, first_in, params[:, 4], params[:, 5])
    grad_first_in, grad_gain1, grad_shift1 = first_pull(grad_first)
    grad_mixed = grad_first_in.astype(jnp.bfloat16)
    grad_bias_out = jnp.sum(grad_mixed.astype(jnp.float32), axis=0)
    grad_w_out = product_tn(out_low, grad_mixed)
    grad_out = product_nt(grad_mixed, w_out).astype(jnp.bfloat16)
    output_gradient_documents = grad_out.reshape(docs, local_len, width)
    grad_query, grad_keys_all, grad_values_all = lax.map(
        attention_backward_pass,
        (
            query_documents,
            every_key,
            every_value,
            valid_positions,
            log_sum_normalizer,
            output_gradient_documents,
        ),
    )
    grad_keys, grad_values = (
        lax.psum_scatter(
            grad_keys_all.astype(jnp.bfloat16), "seq", scatter_dimension=1, tiled=True
        ).astype(jnp.float32),
        lax.psum_scatter(
            grad_values_all.astype(jnp.bfloat16), "seq", scatter_dimension=1, tiled=True
        ).astype(jnp.float32),
    )
    grad_qkv = jnp.concatenate(
        [
            grad_query.reshape(rows, width).astype(jnp.bfloat16),
            grad_keys.reshape(rows, width).astype(jnp.bfloat16),
            grad_values.reshape(rows, width).astype(jnp.bfloat16),
        ],
        axis=1,
    )
    grad_bias_qkv = jnp.sum(grad_qkv.astype(jnp.float32), axis=0)
    grad_w_qkv = product_tn(x_low, grad_qkv)
    grad_x_in = grad_first_in + product_nt(grad_qkv, w_qkv)
    grad_embed = lax.dot_general(
        onehot.astype(jnp.float32),
        grad_x_in,
        (((0,), (0,)), ((), ())),
        precision=lax.Precision.HIGHEST,
        preferred_element_type=jnp.float32,
    )
    input_grad = grad_x_in.astype(jnp.bfloat16).reshape(docs, local_len, width)
    grad_columns = jnp.stack(
        [
            grad_bias_qkv[0:width],
            grad_bias_qkv[2 * width :],
            grad_bias_out,
            grad_bias_down,
            grad_gain1,
            grad_shift1,
            grad_gain2,
            grad_shift2,
        ],
        axis=1,
    )
    grad_smalls = jnp.concatenate(
        [
            grad_columns,
            jnp.transpose(grad_bias_up.reshape(FF // width, width)),
            jnp.transpose(grad_embed),
        ],
        axis=1,
    )
    qkv_shard, out_shard, up_shard, down_shard, small_shard = (
        lax.psum_scatter(
            grad_w_qkv.astype(jnp.bfloat16), "dp", scatter_dimension=0, tiled=True
        ).astype(jnp.float32),
        lax.psum_scatter(
            grad_w_out.astype(jnp.bfloat16), "dp", scatter_dimension=0, tiled=True
        ).astype(jnp.float32),
        lax.psum_scatter(
            grad_w_up.astype(jnp.bfloat16), "dp", scatter_dimension=0, tiled=True
        ).astype(jnp.float32),
        lax.psum_scatter(
            grad_w_down.astype(jnp.bfloat16), "dp", scatter_dimension=0, tiled=True
        ).astype(jnp.float32),
        lax.psum_scatter(
            grad_smalls.astype(jnp.bfloat16), "dp", scatter_dimension=0, tiled=True
        ).astype(jnp.float32),
    )
    mats_shard = jnp.concatenate([qkv_shard, out_shard, up_shard, down_shard], axis=1)
    mats_grad, smalls_grad = (
        lax.psum(mats_shard.astype(jnp.bfloat16), "seq").astype(jnp.float32),
        lax.psum(small_shard.astype(jnp.bfloat16), "seq").astype(jnp.float32),
    )
    out_bias_grad = smalls_grad[:, 2]
    total_tokens = rows * lax.axis_size("dp") * lax.axis_size("seq")
    rate = base_rate / math.sqrt(total_tokens)
    decayed = mats_grad + decay_rate * mats
    new_mats_momentum = momentum_rate * mats_momentum + decayed
    new_mats = mats - rate * (decayed + momentum_rate * new_mats_momentum)
    new_mats_average = average_rate * mats_average + (1.0 - average_rate) * new_mats
    new_smalls_momentum = momentum_rate * smalls_momentum + smalls_grad
    new_smalls = smalls - rate * (smalls_grad + momentum_rate * new_smalls_momentum)
    new_smalls_average = average_rate * smalls_average + (1.0 - average_rate) * new_smalls
    return (
        block_out,
        input_grad,
        mats_grad,
        new_mats,
        new_mats_momentum,
        new_mats_average,
        smalls_grad,
        out_bias_grad,
        new_smalls,
        new_smalls_momentum,
        new_smalls_average,
    )


LN2 = math.log(2.0)
NT = (((1,), (1,)), ((), ()))
NN = (((1,), (0,)), ((), ()))
TN = (((0,), (0,)), ((), ()))
BF16 = jnp.bfloat16
F32 = jnp.float32
HALF = MODEL_WIDTH // 2
QUARTER = MODEL_WIDTH
SHARE = 0.5
TIMES = {"long_fold": 8, "outer_out": 6}


def declared(name):
    return pl.CostEstimate(flops=int(SHARE * 1.15e9 * TIMES.get(name, 0.2)), bytes_accessed=0, transcendentals=0)


def mxu(left, right, dims):
    return lax.dot_general(left, right, dims, preferred_element_type=jnp.float32)


def three_parts(value):
    high = value.astype(jnp.bfloat16)
    rest = value - high.astype(jnp.float32)
    middle = rest.astype(jnp.bfloat16)
    return high, middle, (rest - middle.astype(jnp.float32)).astype(jnp.bfloat16)


def run(kernel, name, ins, outs, scratch=(), limit=12):
    spaces = {"vmem": pltpu.VMEM, "smem": pltpu.SMEM}
    return pl.pallas_call(
        kernel,
        in_specs=[pl.BlockSpec(memory_space=spaces[kind]) for _, kind in ins],
        out_specs=[pl.BlockSpec(memory_space=pltpu.VMEM) for _ in outs],
        out_shape=[jax.ShapeDtypeStruct(shape, dtype) for shape, dtype in outs],
        scratch_shapes=list(scratch),
        compiler_params=pltpu.CompilerParams(vmem_limit_bytes=limit * 2**20),
        cost_estimate=declared(name),
        name=name,
    )(*[array for array, _ in ins])


def both_kernel(mine, theirs, out):
    n = mine.shape[0]
    out[0:n] = mine[...]
    out[n:] = theirs[...]


def both(mine, theirs):
    shape = (mine.shape[0] + theirs.shape[0],) + mine.shape[1:]
    return run(both_kernel, "both", [(mine, "vmem"), (theirs, "vmem")], [(shape, mine.dtype)], limit=2)[0]


def last_columns_kernel(mine, theirs, out):
    n = mine.shape[0]
    out[0:n] = mine[:, :, mine.shape[2] - HALF :]
    out[n:] = theirs[:, :, mine.shape[2] - HALF :]


def last_columns(mine, theirs):
    shape = (2 * mine.shape[0], mine.shape[1], HALF)
    return run(last_columns_kernel, "last_columns", [(mine, "vmem"), (theirs, "vmem")], [(shape, BF16)], limit=2)[0]


def pair_up_kernel(place, keep, got, *blocks):
    rows = keep.shape[0]
    for ref, side in ((keep, place[2]), (got, 1 - place[2])):
        at = pl.ds(pl.multiple_of(side * rows, 16), rows)
        for block, first, last in zip(blocks, CUTS[:-1], CUTS[1:]):
            block[0, at, :] = ref[:, first:last]


def pair_up(place, keep, got):
    rows = keep.shape[0]
    return run(
        pair_up_kernel,
        "pair_up",
        [(place, "smem"), (keep, "vmem"), (got, "vmem")],
        [((1, 2 * rows, b - a), BF16) for a, b in zip(CUTS[:-1], CUTS[1:])],
        limit=2,
    )


def place_rows(pieces, whole):
    for value, first in pieces:
        whole[pl.ds(first, value.shape[0]), :] = value


def xor2(z):
    return lax.rem(z + 2, 4)


def xor1(z):
    return z + 1 - 2 * lax.rem(z, 2)


def near_far(place, y_last):
    y, z = place[1], place[3]
    if y_last:
        line = (z, xor2(z), xor1(z), xor1(xor2(z)))
        return [(zz, y) for zz in line], [(zz, 1 - y) for zz in line]
    one, two = (z, xor2(z)), (xor1(z), xor1(xor2(z)))
    return [(zz, yy) for yy in (y, 1 - y) for zz in one], [(zz, yy) for yy in (y, 1 - y) for zz in two]


def eight(place, block):
    mine, theirs, y_last = block
    near, far = near_far(place, y_last)
    pieces = []
    for ref, chips in ((mine, near), (theirs, far)):
        for i, (zz, yy) in enumerate(chips):
            pieces.append((ref[i, :, 0:QUARTER], pl.multiple_of((2 * zz + yy) * 96, 32)))
    return pieces


def sixteen(place, blocks):
    core = place[2]
    near, far = near_far(place, True)
    pieces = []
    for chips, cc, ref in zip((near, near, far, far), (core, 1 - core, core, 1 - core), blocks):
        for i, (zz, yy) in enumerate(chips):
            pieces.append((ref[i], pl.multiple_of((zz * 4 + yy * 2 + cc) * 48, 16)))
    return pieces


def place_out(place, mine, theirs, whole):
    core = place[2]
    near, far = near_far(place, True)
    for ref, cc in ((mine, core), (theirs, 1 - core)):
        lanes = pl.ds(pl.multiple_of(cc * HALF, 128), HALF)
        for i, (zz, yy) in enumerate(near + far):
            whole[pl.ds(pl.multiple_of((2 * zz + yy) * 96, 32), 96), lanes] = ref[i]


def split_rows(whole, mine, theirs, place, y_last):
    near, far = near_far(place, y_last)
    for ref, chips in ((mine, near), (theirs, far)):
        for i, (zz, yy) in enumerate(chips):
            row = pl.multiple_of((2 * zz + yy) * 96, 32)
            ref[i] = whole[pl.ds(row, 96), :].astype(ref.dtype)


def pack_heads_kernel(place, mats, smalls_t, block, narrow):
    width = MODEL_WIDTH
    narrow[...] = jnp.zeros_like(narrow)
    narrow[0:15, :] = smalls_t[...]
    block[:, 3 * HALF :] = narrow[...].T.astype(BF16)
    for j in range(3):
        lanes = pl.ds(pl.multiple_of(j * width + place[0] * HALF, 128), HALF)
        block[:, j * HALF : (j + 1) * HALF] = mats[:, lanes].astype(BF16)


def pack_heads(place, mats, smalls_t):
    rows = mats.shape[0]
    return run(
        pack_heads_kernel,
        "pack_heads",
        [(place, "smem"), (mats, "vmem"), (smalls_t, "vmem")],
        [((rows, 3 * HALF + 128), BF16)],
        [pltpu.VMEM((128, rows), F32)],
        limit=4,
    )[0]


CUTS = (0, QUARTER + HALF, 2 * QUARTER + HALF, 3 * QUARTER + HALF, 4 * QUARTER + HALF)


def pack_rest_kernel(place, mats, keep, give):
    width = MODEL_WIDTH
    for core, ref in ((1 - place[2], give), (place[2], keep)):
        take = lambda first, n: mats[:, pl.ds(pl.multiple_of(first, 128), n)].astype(BF16)
        ref[:, 0:QUARTER] = take(4 * width + 2 * core * QUARTER, QUARTER)
        ref[:, QUARTER : CUTS[1]] = take(3 * width + core * HALF, HALF)
        ref[:, CUTS[1] : CUTS[2]] = take(4 * width + (2 * core + 1) * QUARTER, QUARTER)
        ref[:, CUTS[2] : CUTS[3]] = take(8 * width + 2 * core * QUARTER, QUARTER)
        ref[:, CUTS[3] :] = take(8 * width + (2 * core + 1) * QUARTER, QUARTER)


def pack_rest(place, mats):
    rows = mats.shape[0]
    return run(
        pack_rest_kernel,
        "pack_rest",
        [(place, "smem"), (mats, "vmem")],
        [((rows, CUTS[4]), BF16)] * 2,
        limit=4,
    )


def unit_rows(rows):
    mean = jnp.mean(rows, axis=-1, keepdims=True)
    centred = rows - mean
    spread = jnp.mean(centred * centred, axis=-1, keepdims=True)
    scale = lax.rsqrt(spread + epsilon)
    return centred * scale, scale


def unit_back(grad, unit, scale, gain):
    inner = grad * gain
    mean_one = jnp.mean(inner, axis=-1, keepdims=True)
    mean_two = jnp.mean(inner * unit, axis=-1, keepdims=True)
    return scale * (inner - mean_one - unit * mean_two)


def down_sum(value):
    return jnp.sum(value, axis=0, keepdims=True)


def project_kernel(
    place, own, other, kinds, mask, w0, w1, w2, w3, x_low, x_in, qkv, masked, params, whole
):
    x, y, core = place[0], place[1], place[2]
    rows = own.shape[0]
    place_rows(sixteen(place, (w0, w1, w2, w3)), whole)
    lane_row = lax.broadcasted_iota(jnp.int32, (8, rows), 0)
    lane = lax.broadcasted_iota(jnp.int32, (8, 128), 1)
    first_row = lax.broadcasted_iota(jnp.int32, (8, 128), 0)
    pick = jnp.where((lane == 0) & (first_row == 0), 1.0, 0.0).astype(BF16)
    position = lax.broadcasted_iota(jnp.int32, (1, rows), 1)
    for side in range(2):
        start = pl.multiple_of((x if side == 0 else 1 - x) * rows, 128)
        alive = (mask[:, pl.ds(start, rows)] > 0) | (position + start == 0)
        bias = jnp.where(alive, 0.0, masked_score)
        bias = jnp.where(lane_row == 0, jnp.broadcast_to(bias, (8, rows)), 0.0).astype(BF16)
        masked[side * rows : (side + 1) * rows, :] = mxu(bias, pick, TN).astype(BF16)
    params[...] = whole[:, 3 * HALF :].astype(F32).T[0:16]
    embed = params[8:16, :].astype(BF16)
    start_q = pl.multiple_of(x * HALF, 128)
    bias_q = params[0:1, pl.ds(start_q, HALF)]
    bias_v = params[1:2, pl.ds(start_q, HALF)]
    scale = 0.125 / LN2
    step = 256
    for side in range(2):
        start = pl.multiple_of((x if side == 0 else 1 - x) * rows, 128)
        hot = jnp.where(kinds[:, pl.ds(start, rows)] + 4 == lane_row, 1.0, 0.0).astype(BF16)
        source = own if side == 0 else other
        for i in range(rows // step):
            span = slice(i * step, (i + 1) * step)
            out = slice(side * rows + i * step, side * rows + (i + 1) * step)
            value = source[span, :].astype(F32) + mxu(hot[:, span], embed, TN)
            if side == 0:
                x_in[span, :] = value
            low = value.astype(BF16)
            x_low[out, :] = low
            q = mxu(low, whole[:, 0:HALF], NN)
            qkv[out, 0:HALF] = ((q + bias_q) * scale).astype(BF16)
            k = mxu(low, whole[:, HALF : 2 * HALF], NN)
            qkv[out, HALF : 2 * HALF] = k.astype(BF16)
            v = mxu(low, whole[:, 2 * HALF : 3 * HALF], NN)
            qkv[out, 2 * HALF :] = (v + bias_v).astype(BF16)


def project(place, own, other, kinds, mask, blocks):
    rows, width = own.shape
    return run(
        project_kernel,
        "project",
        [(place, "smem"), (own, "vmem"), (other, "vmem"), (kinds, "vmem"), (mask, "vmem")]
        + [(block, "vmem") for block in blocks],
        [
            ((2 * rows, width), BF16),
            ((rows, width), F32),
            ((2 * rows, 3 * HALF), BF16),
            ((2 * rows, 128), BF16),
            ((16, width), F32),
            ((width, 3 * HALF + 128), BF16),
        ],
    )


def attend_kernel(qkv, masked_ref, out_ref, log_ref, *, block):
    length = qkv.shape[0]
    pairs = qkv.shape[1] // 384
    lane = lax.broadcasted_iota(jnp.int32, (1, 128), 1)
    one = jnp.broadcast_to(jnp.where(lane == 0, 1.0, 0.0).astype(jnp.bfloat16), (block, 128))
    ones = jnp.ones((length, 128), jnp.bfloat16)
    for pair in range(pairs):
        take = lambda j: slice((j * pairs + pair) * 128, (j * pairs + pair + 1) * 128)
        keys = jnp.concatenate([qkv[:, take(1)], masked_ref[...]], axis=1)
        values = jnp.concatenate([qkv[:, take(2)], ones], axis=1)
        for i in range(length // block):
            span = slice(i * block, (i + 1) * block)
            query = qkv[span, take(0)]
            outs, logs = [], []
            for head in range(2):
                here = (lane < 64) if head == 0 else (lane >= 64)
                only = jnp.where(here, query, jnp.zeros_like(query))
                scores = mxu(jnp.concatenate([only, one], axis=1), keys, NT)
                top = jnp.max(scores, axis=1, keepdims=True)
                weight = jnp.exp2(scores - top).astype(jnp.bfloat16)
                mixed = mxu(weight, values, NN)
                total = mixed[:, 128:]
                outs.append(mixed[:, :128] / total)
                logs.append(top + jnp.log2(total[:, 0:1]))
            out_ref[span, take(0)] = jnp.where(lane < 64, outs[0], outs[1]).astype(jnp.bfloat16)
            so_far = log_ref[span, :] if pair else jnp.zeros((block, 128), F32)
            both = jnp.where(lane == 2 * pair, logs[0], jnp.where(lane == 2 * pair + 1, logs[1], so_far))
            log_ref[span, :] = both


def attend(qkv, masked, block=256):
    length, columns = qkv.shape
    return run(
        functools.partial(attend_kernel, block=block),
        "attend",
        [(qkv, "vmem"), (masked, "vmem")],
        [((length, columns // 3), BF16), ((length, 128), F32)],
        limit=8,
    )


def attend_back_kernel(
    place, qkv, out, own_ref, got_ref, log_ref, masked_ref, out_ref, *refs, role, parts, block
):
    dk_sum, dv_sum = refs[-2], refs[-1]
    length, rows = qkv.shape[0], own_ref.shape[0]
    pairs = qkv.shape[1] // 384
    bf16 = jnp.bfloat16
    core = place[2]
    pair = (1 - core, core, 2)[role]
    take = lambda j: pl.ds(pl.multiple_of((j * pairs + pair) * 128, 128), 128)
    lane = lax.broadcasted_iota(jnp.int32, (1, 128), 1)
    ones = jnp.where((lane >= 1) & (lane <= 3), 1.0, 0.0).astype(bf16)
    masked = masked_ref[...]
    keys = jnp.concatenate(
        [qkv[:, take(1)], jnp.where(lane == 0, masked, jnp.broadcast_to(ones, masked.shape))], axis=1
    )
    three = jnp.broadcast_to(jnp.where(lane <= 2, 1.0, 0.0).astype(bf16), (length, 128))
    values = jnp.concatenate([qkv[:, take(2)], three], axis=1)
    keys_t = qkv[:, take(1)].T
    one = jnp.ones((block, 128), bf16)
    zero = jnp.zeros((block, 128), bf16)
    row = lax.broadcasted_iota(jnp.int32, (128, 1), 0)
    for i in range(length // block):
        span = slice(i * block, (i + 1) * block)
        at = i * block % rows
        query = qkv[span, take(0)]
        grad = (own_ref if i * block < rows else got_ref)[at : at + block, take(0)]
        both = grad.astype(jnp.float32) * out[span, take(0)].astype(jnp.float32)
        logs = log_ref[span, :]
        turned = []
        for head in range(2):
            here = (lane < 64) if head == 0 else (lane >= 64)
            inner = jnp.sum(jnp.where(here, both, 0.0), axis=1, keepdims=True)
            wide = lambda t: jnp.broadcast_to(t, (block, 128))
            log = jnp.sum(jnp.where(lane == 2 * pair + head, logs, 0.0), axis=1, keepdims=True)
            i0, i1, i2 = (wide(t) for t in three_parts(-inner))
            l0, l1, l2 = (wide(t) for t in three_parts(-log))
            query_h = jnp.where(here, query, zero)
            grad_h = jnp.where(here, grad, zero)
            tail_q = jnp.where(
                lane == 0,
                one,
                jnp.where(lane == 1, l0, jnp.where(lane == 2, l1, jnp.where(lane == 3, l2, zero))),
            )
            tail_g = jnp.where(lane == 0, i0, jnp.where(lane == 1, i1, jnp.where(lane == 2, i2, zero)))
            prob = jnp.exp2(mxu(keys, jnp.concatenate([query_h, tail_q], axis=1), NT))
            slope = mxu(values, jnp.concatenate([grad_h, tail_g], axis=1), NT)
            grad_scores = (prob * slope).astype(bf16)
            add_v = mxu(prob.astype(bf16), grad_h, NN)
            add_k = mxu(grad_scores, query_h, NN)
            if i == 0 and head == 0:
                dv_sum[...] = add_v
                dk_sum[...] = add_k
            else:
                dv_sum[...] += add_v
                dk_sum[...] += add_k
            turned.append(mxu(keys_t, grad_scores, NN))
        out_ref[span, 0:128] = (jnp.where(row < 64, turned[0], turned[1]) * 0.125).T.astype(bf16)
    out_ref[:, 128:256] = (dk_sum[...] * LN2).astype(bf16)
    out_ref[:, 256:384] = dv_sum[...].astype(bf16)
    if parts:
        keep_ref, give_ref, wide_ref = refs[:3]
        wide_ref[:, 0:384] = out_ref[...]
        wide_ref[:, 384:512] = jnp.zeros((length, 128), bf16)
        keep_ref[...] = wide_ref[:, pl.ds(pl.multiple_of(core * 256, 128), 256)]
        give_ref[...] = wide_ref[:, pl.ds(pl.multiple_of((1 - core) * 256, 128), 256)]


def attend_back(place, qkv, out, own, got, log_sum, masked, role, parts=False, block=512):
    length = qkv.shape[0]
    return run(
        functools.partial(attend_back_kernel, role=role, parts=parts, block=block),
        "attend_back",
        [(place, "smem")] + [(v, "vmem") for v in (qkv, out, own, got, log_sum, masked)],
        [((length, 384), BF16)] + [((length, 256), BF16)] * (2 * parts),
        [pltpu.VMEM((length, 512), BF16)] * parts + [pltpu.VMEM((length, 128), F32)] * 2,
        limit=14,
    )


def mix_kernel(
    place, heads, got, x_in, params, w0, w1, out_low, unit, scale, first_low, whole
):
    x, y, core = place[0], place[1], place[2]
    rows = x_in.shape[0]
    place_out(place, w0, w1, whole)
    mine = pl.multiple_of(x * HALF, 128)
    theirs = pl.multiple_of((1 - x) * HALF, 128)
    out_low[:, pl.ds(mine, HALF)] = heads[0:rows, :]
    out_low[:, pl.ds(theirs, HALF)] = got[...]
    step = 256
    for i in range(rows // step):
        span = slice(i * step, (i + 1) * step)
        mixed = mxu(out_low[span, :], whole[...], NN) + params[2:3, :]
        ones, size = unit_rows(x_in[span, :] + mixed)
        unit[span, :] = ones
        scale[span, :] = jnp.broadcast_to(size, (step, 128))
        first_low[span, :] = (ones * params[4:5, :] + params[5:6, :]).astype(BF16)


def mix(place, heads, got, x_in, params, blocks):
    rows, width = x_in.shape
    return run(
        mix_kernel,
        "mix",
        [(place, "smem"), (heads, "vmem"), (got, "vmem"), (x_in, "vmem"), (params, "vmem")]
        + [(block, "vmem") for block in blocks],
        [
            ((rows, width), BF16),
            ((rows, width), F32),
            ((rows, 128), F32),
            ((rows, width), BF16),
            ((width, width), BF16),
        ],
    )


def gelu_and_slope(up):
    size = jnp.abs(up)
    t = 1.0 / (1.0 + (0.3275911 * math.sqrt(0.5)) * size)
    bell = jnp.exp(-0.5 * up * up)
    poly = t * (
        0.5 * 0.254829592
        + t
        * (
            0.5 * -0.284496736
            + t * (0.5 * 1.421413741 + t * (0.5 * -1.453152027 + t * (0.5 * 1.061405429)))
        )
    )
    tail = poly * bell
    below = jnp.where(up < 0, tail, 1.0 - tail)
    return up * below, below + up * bell * (1.0 / math.sqrt(2.0 * math.pi))


def up_kernel(place, own, other, params, w0, w1, act, slope, whole, *, which, y_last):
    core = place[2]
    rows = own.shape[0]
    place_rows(eight(place, (w0, w1, y_last)), whole)
    bias = params[pl.ds(8 + 2 * core + which, 1), :]
    step = 128
    for side in range(2):
        source = own if side == 0 else other
        for i in range(rows // step):
            out = slice(side * rows + i * step, side * rows + (i + 1) * step)
            up = mxu(source[i * step : (i + 1) * step, :], whole[...], NN) + bias
            value, change = gelu_and_slope(up)
            act[out, :] = value.astype(BF16)
            slope[out, :] = change.astype(BF16)


def raise_up(place, own, other, params, block, which):
    rows, width = own.shape
    *refs, y_last = block
    return run(
        functools.partial(up_kernel, which=which, y_last=y_last),
        "raise_up",
        [(place, "smem"), (own, "vmem"), (other, "vmem"), (params, "vmem")] + [(r, "vmem") for r in refs],
        [((2 * rows, QUARTER), BF16), ((2 * rows, QUARTER), BF16), ((width, QUARTER), BF16)],
        limit=8,
    )


def lower_kernel(place, act, w0, w1, out, whole, *, y_last):
    place_rows(eight(place, (w0, w1, y_last)), whole)
    step = 256
    for i in range(act.shape[0] // step):
        span = slice(i * step, (i + 1) * step)
        out[span, :] = mxu(act[span, :], whole[...], NT)


def lower(place, act, block):
    rows, columns = act.shape
    *refs, y_last = block
    return run(
        functools.partial(lower_kernel, y_last=y_last),
        "lower",
        [(place, "smem"), (act, "vmem")] + [(r, "vmem") for r in refs],
        [((rows, MODEL_WIDTH), F32), ((MODEL_WIDTH, columns), BF16)],
        limit=8,
    )


def lower_other_kernel(place, act, so_far, w0, w1, out, whole, *, y_last):
    place_rows(eight(place, (w0, w1, y_last)), whole)
    rows = out.shape[0]
    step = 256
    for i in range(rows // step):
        span = slice(rows + i * step, rows + (i + 1) * step)
        value = so_far[span, :] + mxu(act[span, :], whole[...], NT)
        out[i * step : (i + 1) * step, :] = value.astype(BF16)


def lower_other(place, act, so_far, block):
    rows, columns = act.shape
    *refs, y_last = block
    return run(
        functools.partial(lower_other_kernel, y_last=y_last),
        "lower_other",
        [(place, "smem"), (act, "vmem"), (so_far, "vmem")] + [(r, "vmem") for r in refs],
        [((rows // 2, MODEL_WIDTH), BF16), ((MODEL_WIDTH, columns), BF16)],
        limit=8,
    )


def turn_kernel(
    place,
    act,
    so_far,
    got,
    unit1,
    params,
    grad,
    whole,
    block_out,
    grad_second,
    grad_low,
    sums,
):
    rows = got.shape[0]
    step = 128
    total = [jnp.zeros((1, MODEL_WIDTH), F32)] * 3
    for i in range(rows // step):
        span = slice(i * step, (i + 1) * step)
        first = unit1[span, :] * params[4:5, :] + params[5:6, :]
        value = so_far[span, :] + mxu(act[span, :], whole[...], NT) + got[span, :].astype(F32)
        unit, scale = unit_rows(first + (value + params[3:4, :]))
        block_out[span, :] = (unit * params[6:7, :] + params[7:8, :]).astype(BF16)
        dy = grad[span, :].astype(F32)
        back = unit_back(dy, unit, scale, params[6:7, :])
        grad_second[span, :] = back
        low = back.astype(BF16)
        grad_low[span, :] = low
        total[0] += down_sum(low.astype(F32))
        total[1] += down_sum(unit * dy)
        total[2] += down_sum(dy)
    sums[...] = jnp.concatenate(total + [jnp.zeros((5, MODEL_WIDTH), F32)], axis=0)


def turn(place, act, so_far, got, unit1, params, grad, weight):
    rows, width = got.shape
    return run(
        turn_kernel,
        "turn",
        [
            (place, "smem"),
            (act, "vmem"),
            (so_far, "vmem"),
            (got, "vmem"),
            (unit1, "vmem"),
            (params, "vmem"),
            (grad, "vmem"),
            (weight, "vmem"),
        ],
        [((rows, width), BF16), ((rows, width), F32), ((rows, width), BF16), ((8, width), F32)],
        limit=8,
    )


def raise_back_kernel(place, own, other, slope, whole, grad_up, sums):
    rows = own.shape[0]
    step = 256
    total = jnp.zeros((1, slope.shape[1]), F32)
    for side in range(2):
        source = own if side == 0 else other
        for i in range(rows // step):
            out = slice(side * rows + i * step, side * rows + (i + 1) * step)
            value = mxu(source[i * step : (i + 1) * step, :], whole[...], NN)
            low = (value * slope[out, :].astype(F32)).astype(BF16)
            grad_up[out, :] = low
            total += down_sum(low.astype(F32))
    sums[...] = jnp.broadcast_to(total, sums.shape)


def raise_back(place, own, other, slope, weight):
    rows, width = own.shape
    columns = slope.shape[1]
    return run(
        raise_back_kernel,
        "raise_back",
        [(place, "smem"), (own, "vmem"), (other, "vmem"), (slope, "vmem"), (weight, "vmem")],
        [((2 * rows, columns), BF16), ((8, columns), F32)],
        limit=8,
    )


def outer_kernel(place, left_own, left_other, right_own, right_other, mine, theirs, whole, *, y_last):
    whole[...] = mxu(left_own[...], right_own[...], TN) + mxu(left_other[...], right_other[...], TN)
    split_rows(whole, mine, theirs, place, y_last)


def outer_joined_kernel(place, left_own, left_other, right, mine, theirs, whole, *, y_last):
    rows = left_own.shape[0]
    whole[...] = mxu(left_own[...], right[0:rows, :], TN) + mxu(left_other[...], right[rows:, :], TN)
    split_rows(whole, mine, theirs, place, y_last)


def outer_wide_kernel(place, left_own, left_other, first, second, mine, theirs, whole):
    rows = left_own.shape[0]
    n = first.shape[1]
    for j, right in enumerate((first, second)):
        value = mxu(left_own[...], right[0:rows, :], TN) + mxu(left_other[...], right[rows:, :], TN)
        whole[:, j * n : (j + 1) * n] = value
    split_rows(whole, mine, theirs, place, True)


def outer_wide(place, left_own, left_other, first, second):
    width = left_own.shape[1]
    columns = 2 * first.shape[1]
    return run(
        outer_wide_kernel,
        "outer_wide",
        [(place, "smem")] + [(r, "vmem") for r in (left_own, left_other, first, second)],
        [((4, 96, columns), BF16), ((4, 96, columns), BF16)],
        [pltpu.VMEM((width, columns), F32)],
        limit=14,
    )


def outer(place, left_own, left_other, rights, name, y_last=True):
    rows, width = left_own.shape
    columns = rights[0].shape[1]
    return run(
        functools.partial(outer_kernel if len(rights) == 2 else outer_joined_kernel, y_last=y_last),
        name,
        [(place, "smem"), (left_own, "vmem"), (left_other, "vmem")] + [(r, "vmem") for r in rights],
        [((4, 96, columns), BF16), ((4, 96, columns), BF16)],
        [pltpu.VMEM((width, columns), F32)],
        limit=12,
    )


def first_other_kernel(place, grad_a, grad_b, whole_a, whole_b, out):
    rows = out.shape[0]
    step = 256
    for i in range(rows // step):
        span = slice(rows + i * step, rows + (i + 1) * step)
        value = mxu(grad_a[span, :], whole_a[...], NT) + mxu(grad_b[span, :], whole_b[...], NT)
        out[i * step : (i + 1) * step, :] = value.astype(BF16)


def first_other(place, grad_a, grad_b, weight_a, weight_b):
    rows, columns = grad_a.shape
    return run(
        first_other_kernel,
        "first_other",
        [(place, "smem")] + [(r, "vmem") for r in (grad_a, grad_b, weight_a, weight_b)],
        [((rows // 2, MODEL_WIDTH), BF16)],
        limit=8,
    )[0]


def first_back_kernel(
    place,
    grad_a,
    grad_b,
    got_first,
    got_last,
    grad_second,
    unit1,
    scale1,
    params,
    whole_a,
    whole_b,
    whole_o,
    grad_first_in,
    mixed_keep,
    mixed_give,
    heads_keep,
    heads_give,
    sums,
    low_all,
    heads_all,
):
    x, core = place[0], place[2]
    step = got_first.shape[0]
    rows = 2 * step
    total = [jnp.zeros((1, MODEL_WIDTH), F32)] * 3
    for i in range(rows // step):
        span = slice(i * step, (i + 1) * step)
        value = mxu(grad_a[span, :], whole_a[...], NT) + mxu(grad_b[span, :], whole_b[...], NT)
        got = (got_first, got_last)[i]
        dh = grad_second[span, :] + value + got[...].astype(F32)
        unit = unit1[span, :]
        back = unit_back(dh, unit, scale1[span, 0:1], params[4:5, :])
        grad_first_in[span, :] = back
        low = back.astype(BF16)
        low_all[span, :] = low
        total[0] += down_sum(low.astype(F32))
        total[1] += down_sum(unit * dh)
        total[2] += down_sum(dh)
        heads_all[span, :] = mxu(low, whole_o[...], NT).astype(BF16)
    sums[...] = jnp.concatenate(total + [jnp.zeros((5, MODEL_WIDTH), F32)], axis=0)
    half = lambda i: pl.ds(pl.multiple_of(i * HALF, 128), HALF)
    mixed_keep[...] = low_all[:, half(core)]
    mixed_give[...] = low_all[:, half(1 - core)]
    heads_keep[...] = heads_all[:, half(x)]
    heads_give[...] = heads_all[:, half(1 - x)]


def first_back(place, *arrays):
    rows, width = arrays[4].shape
    return run(
        first_back_kernel,
        "first_back",
        [(place, "smem")] + [(r, "vmem") for r in arrays],
        [
            ((rows, width), F32),
            ((rows, HALF), BF16),
            ((rows, HALF), BF16),
            ((rows, HALF), BF16),
            ((rows, HALF), BF16),
            ((8, width), F32),
        ],
        [pltpu.VMEM((rows, width), BF16)] * 2,
        limit=10,
    )


def enter_kernel(
    place, d_give, d_keep, d_last, grad_first_in, kinds, sums1, sums2, sums_a, sums_b, whole, own, give, small
):
    x, core = place[0], place[2]
    rows = own.shape[0]
    pairs = ((d_give, 1 - core), (d_keep, core), (d_last, 2))
    small[...] = jnp.zeros_like(small)
    for ref, pair in pairs:
        at = pl.ds(pl.multiple_of(x * HALF + pair * 128, 128), 128)
        small[0:1, at] = down_sum(ref[:, 0:128].astype(F32))
        small[1:2, at] = down_sum(ref[:, 256:384].astype(F32))
    small[2:3, :] = sums1[0:1, :]
    small[3:4, :] = sums2[0:1, :]
    small[4:6, :] = sums1[1:3, :]
    small[6:8, :] = sums2[1:3, :]
    small[pl.ds(8 + 2 * core, 1), :] = sums_a[0:1, :]
    small[pl.ds(9 + 2 * core, 1), :] = sums_b[0:1, :]
    weights = []
    for _, pair in pairs:
        tiles = [whole[:, pl.ds(pl.multiple_of(j * HALF + pair * 128, 128), 128)] for j in range(3)]
        weights.append(jnp.concatenate(tiles, axis=1))
    lane_row = lax.broadcasted_iota(jnp.int32, (8, rows), 0)
    step = 256
    embed = jnp.zeros((8, MODEL_WIDTH), F32)
    for side in (1, 0):
        start = pl.multiple_of((x if side == 0 else 1 - x) * rows, 128)
        hot = jnp.where(kinds[:, pl.ds(start, rows)] == lane_row, 1.0, 0.0).astype(BF16)
        for i in range(rows // step):
            span = slice(i * step, (i + 1) * step)
            source = slice(side * rows + i * step, side * rows + (i + 1) * step)
            value = sum(mxu(ref[source, :], weight, NT) for (ref, _), weight in zip(pairs, weights))
            if side == 0:
                value = value + grad_first_in[span, :]
                own[span, :] = value
            else:
                give[span, :] = value.astype(BF16)
            take = hot[:, span]
            for term in three_parts(value):
                embed += mxu(take, term, NN)
    small[12:15, :] = embed[0:3, :]


def enter(place, *arrays):
    rows, width = arrays[3].shape
    return run(
        enter_kernel,
        "enter",
        [(place, "smem")] + [(r, "vmem") for r in arrays],
        [((rows, width), F32), ((rows, width), BF16), ((16, width), F32)],
        limit=12,
    )


def narrow_kernel(place, own, other, mine, theirs, whole):
    small = own[...] + other[...]
    rest = jnp.zeros((128 - small.shape[0], small.shape[1]), F32)
    whole[...] = jnp.concatenate([small, rest], axis=0).T
    split_rows(whole, mine, theirs, place, True)


def narrow(place, own, other):
    return run(
        narrow_kernel,
        "narrow",
        [(place, "smem"), (own, "vmem"), (other, "vmem")],
        [((4, 96, 128), BF16)] * 2,
        [pltpu.VMEM((own.shape[1], 128), F32)],
        limit=4,
    )


def fold_kernel(mine, got, keep, send):
    half = mine.shape[0] // 2
    for i in range(2 * half):
        value = mine[i].astype(F32) + got[i].astype(F32)
        if i < half:
            keep[i] = value
        else:
            send[i - half] = value.astype(BF16)


def fold(mine, got, name="fold"):
    shape = (mine.shape[0] // 2,) + mine.shape[1:]
    return run(
        fold_kernel,
        name,
        [(mine, "vmem"), (got, "vmem")],
        [(shape, F32), (shape, BF16)],
        limit=4,
    )


def fold_two_kernel(mine_a, got_a, mine_b, got_b, keep, send):
    n = mine_a.shape[2]
    half = keep.shape[0]
    for i in range(2 * half):
        for mine, got, lanes in ((mine_a, got_a, slice(0, n)), (mine_b, got_b, slice(n, keep.shape[2]))):
            value = mine[i].astype(F32) + got[i].astype(F32)
            if i < half:
                keep[i, :, lanes] = value
            else:
                send[i - half, :, lanes] = value.astype(BF16)


def fold_two(mine_a, got_a, mine_b, got_b, name="fold_two"):
    shape = (mine_a.shape[0] // 2, 96, mine_a.shape[2] + mine_b.shape[2])
    return run(
        fold_two_kernel,
        name,
        [(v, "vmem") for v in (mine_a, got_a, mine_b, got_b)],
        [(shape, F32), (shape, BF16)],
        limit=4,
    )


def settle_kernel(place, *refs):
    *sources, keep, send = refs
    core = place[2]
    column = 0
    for i in range(0, len(sources), 2):
        one, two = sources[i : i + 2]
        n = one.shape[2]
        lanes = slice(column, column + n)
        for j, whose in enumerate((core, 1 - core)):
            rows = pl.ds(pl.multiple_of(whose * 48, 16), 48)
            value = one[0, rows, :] + two[0, rows, :].astype(F32)
            keep[j, :, lanes] = value
            send[j, :, lanes] = value.astype(BF16)
        column += n


def settle(place, groups):
    sources = [array for group in groups for array in group]
    n = sum(group[0].shape[2] for group in groups)
    return run(
        settle_kernel,
        "settle",
        [(place, "smem")] + [(array, "vmem") for array in sources],
        [((2, 48, n), F32), ((2, 48, n), BF16)],
        limit=4,
    )


def join_kernel(keep, got, near, far):
    near[...] = keep[0] + got[0].astype(F32)
    far[...] = (keep[1] + got[1].astype(F32)).astype(BF16)


def join(keep, got):
    shape = keep.shape[1:]
    return run(join_kernel, "join", [(keep, "vmem"), (got, "vmem")], [(shape, F32), (shape, BF16)], limit=4)


def step_of(weight, momentum, average, grad, rate, decay):
    moved = grad + decay * weight if decay else grad
    new_momentum = momentum_rate * momentum + moved
    new = weight - rate * (moved + momentum_rate * new_momentum)
    return grad, new, new_momentum, average_rate * average + (1.0 - average_rate) * new


def update_rest_kernel(
    place, mats, momentum, average, *refs, rate, groups
):
    sources, outs, work, sems = refs[: 2 * groups], refs[2 * groups : 2 * groups + 4], refs[-5:-1], refs[-1]
    width = MODEL_WIDTH
    base = 3 * width
    copies = []
    for whose in range(2):
        core = place[2] if whose == 0 else 1 - place[2]
        for g in range(groups):
            source = sources[2 * g + whose]
            if g == 0:
                parts = ((8 * width + 2 * core * QUARTER, QUARTER), (8 * width + (2 * core + 1) * QUARTER, QUARTER))
            else:
                parts = (
                    (4 * width + 2 * core * QUARTER, QUARTER),
                    (4 * width + (2 * core + 1) * QUARTER, QUARTER),
                    (3 * width + core * HALF, HALF),
                )
            column = 0
            for first, n in parts:
                lanes = slice(column, column + n)
                grad = source[:, lanes].astype(F32)
                at = pl.ds(pl.multiple_of(first, 128), n)
                results = step_of(mats[:, at], momentum[:, at], average[:, at], grad, rate, decay_rate)
                to = pl.ds(pl.multiple_of(first - base, 128), n)
                for i, (ref, value) in enumerate(zip(work, results)):
                    ref[:, to] = value
                    copy = pltpu.make_async_copy(ref.at[:, to], outs[i].at[:, at], sems.at[len(copies)])
                    copy.start()
                    copies.append(copy)
                column += n
    for copy in copies:
        copy.wait()


def update_rest(place, mats, momentum, average, groups, rate):
    rows, columns = mats.shape
    sources = [array for group in groups for array in group]
    n = columns - 3 * MODEL_WIDTH
    return pl.pallas_call(
        functools.partial(update_rest_kernel, rate=rate, groups=len(groups)),
        in_specs=[pl.BlockSpec(memory_space=pltpu.SMEM)]
        + [pl.BlockSpec(memory_space=pltpu.VMEM)] * (3 + len(sources)),
        out_specs=[pl.BlockSpec(memory_space=pl.ANY)] * 4,
        out_shape=[jax.ShapeDtypeStruct((rows, columns), F32)] * 4,
        scratch_shapes=[pltpu.VMEM((rows, n), F32)] * 4 + [pltpu.SemaphoreType.DMA((40,))],
        compiler_params=pltpu.CompilerParams(vmem_limit_bytes=10 * 2**20),
        cost_estimate=declared("update_rest"),
        name="update_rest",
    )(place, mats, momentum, average, *sources)


def update_heads_kernel(
    place,
    mats,
    momentum,
    average,
    keep,
    from_seq,
    from_core,
    from_both,
    s_value,
    s_momentum,
    s_average,
    a0,
    a1,
    a2,
    a3,
    o0,
    o1,
    o2,
    o3,
    s0,
    s1,
    s2,
    s3,
    bias,
    w0,
    w1,
    w2,
    w3,
    grads,
    sems,
    *,
    rate,
):
    x, core = place[0], place[2]
    width = MODEL_WIDTH
    grads[x, core] = keep[0]
    grads[1 - x, core] = from_seq[...].astype(F32)
    grads[x, 1 - core] = from_core[...].astype(F32)
    grads[1 - x, 1 - core] = from_both[...].astype(F32)
    work = (w0, w1, w2, w3)
    last = ((0, 384), (0, 512), (1, 384))
    copies = []
    for j in range(3):
        for side in range(2):
            at = slice(j * width + side * HALF, j * width + (side + 1) * HALF)
            tiles = [grads[side, c, :, j * 128 : (j + 1) * 128] for c in range(2)]
            c, first = last[j]
            tiles.append(grads[side, c, :, first : first + 128])
            grad = jnp.concatenate(tiles, axis=1)
            results = step_of(mats[:, at], momentum[:, at], average[:, at], grad, rate, decay_rate)
            for out, ref, value in zip((o0, o1, o2, o3), work, results):
                ref[:, at] = value
                here = pl.ds(at.start, HALF)
                copy = pltpu.make_async_copy(ref.at[:, here], out.at[:, here], sems.at[len(copies)])
                copy.start()
                copies.append(copy)
    small = (grads[x, core, :, 640:] + grads[1 - x, core, :, 640:]).T[0:16]
    n = s_value.shape[0]
    results = step_of(s_value[...], s_momentum[...], s_average[...], small[0:n], rate, 0.0)
    for ref, value in zip((s0, s1, s2, s3), results):
        ref[...] = value
    bias[...] = small[2:3]
    for copy in copies:
        copy.wait()


def update_heads(place, mats, momentum, average, group, smalls, so_far, rate):
    rows, columns = mats.shape
    n = 3 * MODEL_WIDTH
    vmem = pl.BlockSpec(memory_space=pltpu.VMEM)
    anywhere = pl.BlockSpec(memory_space=pl.ANY)
    shape = smalls[0].shape
    return pl.pallas_call(
        functools.partial(update_heads_kernel, rate=rate),
        in_specs=[pl.BlockSpec(memory_space=pltpu.SMEM)] + [vmem] * 10 + [anywhere] * 4,
        out_specs=[anywhere] * 4 + [vmem] * 5,
        out_shape=[jax.ShapeDtypeStruct((rows, columns), F32)] * 4 + [jax.ShapeDtypeStruct(shape, F32)] * 4
        + [jax.ShapeDtypeStruct((1, rows), F32)],
        scratch_shapes=[pltpu.VMEM((rows, n), F32)] * 4
        + [pltpu.VMEM((2, 2, rows, 768), F32), pltpu.SemaphoreType.DMA((24,))],
        input_output_aliases={11 + i: i for i in range(4)},
        compiler_params=pltpu.CompilerParams(vmem_limit_bytes=6 * 2**20),
        cost_estimate=declared("update_heads"),
        name="update_heads",
    )(place, mats, momentum, average, *group, *smalls, *so_far)


SEQ_SWAP = [(0, 1), (1, 0)]
CORE_SWAP = [(i, i ^ 1) for i in range(16)]
Y_SWAP = [(i, i ^ 2) for i in range(16)]


def over_seq(value):
    return lax.ppermute(value, "seq", SEQ_SWAP)


def over_core(value):
    return lax.ppermute(value, "dp", CORE_SWAP)


def over_y(value):
    return lax.ppermute(value, "dp", Y_SWAP)


def over_z1(value):
    return lax.ppermute(value, "dp", [(i, i ^ 4) for i in range(16)])


def over_z2(value):
    return lax.ppermute(value, "dp", [(i, i ^ 8) for i in range(16)])


def over_both(value):
    return lax.ppermute(value, ("dp", "seq"), [(i, i ^ 3) for i in range(32)])


def pin(value, *after):
    return lax.optimization_barrier((value, after))[0]


def exchange(place, groups, *after):
    keep, send = settle(place, groups)
    near, far = join(keep, over_seq(pin(send, *after) if after else send))
    return near, over_core(far)


def tuned(
    inputs,
    modality,
    key_valid_mask,
    output_gradient,
    mats,
    mats_momentum,
    mats_average,
    smalls,
    smalls_momentum,
    smalls_average,
):
    width = MODEL_WIDTH
    rows = inputs.shape[1]
    dp = lax.axis_index("dp")
    x = lax.axis_index("seq")
    core = dp % 2
    y = (dp // 2) % 2
    place = jnp.stack([x, y, core, dp // 4]).astype(jnp.int32)

    att_own = pack_heads(place, mats, smalls.T)[None]
    att_got = over_z2(att_own)
    other_inputs = over_seq(inputs[0])
    keep, give = pack_rest(pin(place, att_own), mats)
    blocks = pair_up(place, keep, over_core(give))
    att_two = both(att_own, pin(att_got, blocks))
    att0 = both(att_two, over_z1(att_two))
    two0 = both(blocks[0], pin(over_z2(pin(blocks[0], att_two)), att0))
    att2 = pin(over_y(att0), other_inputs)
    att = (att0, over_core(att0), att2, over_core(att2))
    line0 = over_z1(two0)

    x_low, x_in, qkv, masked, params, w_qkv = project(
        pin(place, two0), inputs[0], other_inputs, modality, key_valid_mask, att
    )
    line0 = both(two0, pin(line0, qkv))
    up0 = (line0, over_y(line0), True)
    got1 = over_z2(pin(blocks[1], qkv))
    heads, log_sum = attend(qkv, pin(masked, line0))
    got1 = pin(got1, heads)
    got_heads = over_seq(pin(heads, got1)[rows:])
    two1 = both(blocks[1], got1)
    line1 = both(two1, over_z1(two1))
    x_got = over_core(x_low)
    two2 = both(blocks[2], pin(over_z2(pin(blocks[2], heads)), line1))
    got_heads, y_0 = pin((got_heads, up0[1]), two2)
    out_mine = last_columns(line0, y_0)
    out_w = (out_mine, over_core(out_mine))
    up1 = (line1, over_y(line1), True)
    line2 = both(two2, pin(over_z1(two2), got_heads))
    two3 = both(blocks[3], pin(over_z2(pin(blocks[3], line1)), got_heads))
    out_low, unit1, scale1, first_low, w_out = mix(
        pin(place, up1[1], line2, two3, x_got), heads, got_heads, x_in, params, out_w
    )
    down0 = (line2, over_y(line2), True)
    first_got = over_core(first_low)
    out_got = over_core(out_low)
    act0, slope0, w_up0 = raise_up(place, first_low, first_got, params, up0, 0)
    square3 = both(two3, pin(over_y(two3), act0))
    down1 = (square3, over_z1(square3), False)
    act1, slope1, w_up1 = raise_up(
        pin(place, square3, out_got), first_low, first_got, params, up1, 1
    )
    so_far, w_down0 = lower(pin(place, act1), act0, down0)
    sum_give, w_down1 = lower_other(place, act1, so_far, down1)
    block_out, grad_second, grad_ffo, sums2 = turn(
        place, act1, so_far, over_core(sum_give), unit1, params, output_gradient[0], w_down1
    )

    ffo_got = over_core(grad_ffo)
    mine_d, theirs_d = outer_wide(place, grad_ffo, ffo_got, act0, act1)
    got_d = over_y(theirs_d)
    grad_up0, sums_up0 = raise_back(pin(place, mine_d), grad_ffo, ffo_got, slope0, w_down0)
    grad_up1, sums_up1 = raise_back(pin(place, grad_up0), grad_ffo, ffo_got, slope1, w_down1)
    first_give = first_other(place, grad_up0, grad_up1, w_up0, w_up1)
    first_out = first_back(
        place,
        grad_up0,
        grad_up1,
        over_core(first_give[0:256]),
        over_core(first_give[256:]),
        grad_second,
        unit1,
        scale1,
        params,
        w_up0,
        w_up1,
        w_out,
    )
    grad_first_in, mixed_keep, mixed_give, heads_keep, heads_give, sums1 = first_out
    heads_got = over_seq(heads_give)
    mixed_got = over_core(mixed_give)
    mine_u0, theirs_u0 = outer(pin(place, sums1), first_low, first_got, [grad_up0], "outer_up")
    got_u0 = over_y(theirs_u0)
    mine_u1, theirs_u1 = outer(
        pin(place, mine_u0), first_low, first_got, [grad_up1], "outer_up", y_last=False
    )
    got_u1 = over_z1(theirs_u1)
    heads_got = pin(heads_got, mine_u1)
    fold_d = fold(mine_d, pin(got_d, heads_got))
    got_d = over_z1(fold_d[1])
    mine_o, theirs_o = outer(
        pin(place, fold_d), out_low, out_got, [mixed_keep, mixed_got], "outer_out"
    )
    got_o = over_y(theirs_o)

    def back(role, masked, parts=False):
        return attend_back(place, qkv, heads, heads_keep, heads_got, log_sum, masked, role, parts)

    (d_give,) = back(0, pin(masked, mine_o))
    got_u1 = pin(got_u1, d_give)
    d_give = pin(d_give, got_u1)
    fold_u1 = fold(mine_u1, got_u1)
    got_u1 = over_y(fold_u1[1])
    d_got = over_core(d_give)
    (d_keep,) = back(1, pin(masked, fold_u1))
    got_u0, got_d = pin((got_u0, got_d), d_keep)
    d_keep = pin(d_keep, got_u0, got_d)
    fold_u0 = fold(mine_u0, got_u0, "long_fold")
    last_d = fold(fold_d[0], got_d)
    got_u0, got_d = over_z1(fold_u0[1]), over_z2(last_d[1])
    mine_q, theirs_q = outer(
        pin(place, fold_u0, last_d), x_low, x_got, [d_keep, pin(d_got, fold_u0)], "outer_heads"
    )
    got_q = over_y(theirs_q)
    d_last, cols_keep, cols_give = back(2, pin(masked, mine_q), True)
    down_keep, down_send = settle(place, [(last_d[0], pin(got_d, d_last))])
    down_got = over_seq(down_send)
    grad_x, give_x, small = enter(
        pin(place, down_keep),
        d_give,
        d_keep,
        d_last,
        grad_first_in,
        modality,
        sums1,
        sums2,
        sums_up0,
        sums_up1,
        w_qkv,
    )
    got_u1, got_o, got_u0, got_q = pin((got_u1, got_o, got_u0, got_q), small)
    give_x, small, cols_give = pin((give_x, small, cols_give), got_u1, got_o, got_u0, got_q)
    x_back = over_seq(give_x)
    last_u = fold_two(fold_u0[0], got_u0, fold_u1[0], got_u1)
    fold_o = fold(mine_o, got_o)
    got_u, got_o = over_z2(last_u[1]), over_z1(fold_o[1])
    cols_got = over_core(cols_give)
    fold_q = fold(mine_q, got_q, "long_fold")
    mine_r, theirs_r = outer(
        pin(place, last_u, fold_o, fold_q), x_low, x_got, [cols_keep, pin(cols_got, fold_q)], "outer_heads"
    )
    mine_s, theirs_s = narrow(pin(place, mine_r), small, over_core(small))
    last_o = fold(fold_o[0], pin(got_o, mine_s))
    got_last_o = over_z2(last_o[1])
    last_q = fold(fold_q[0], pin(over_z1(fold_q[1]), mine_s))
    fold_r = fold_two(mine_r, over_y(theirs_r), mine_s, over_y(theirs_s))
    got_u, got_last_o = pin((got_u, got_last_o), fold_r)
    last_r = fold(fold_r[0], over_z1(fold_r[1]))
    down_near, down_far = join(down_keep, pin(down_got, last_r))
    down_group = (down_near, over_core(down_far))

    rate = base_rate / math.sqrt(rows * lax.axis_size("dp") * lax.axis_size("seq"))
    up_group = exchange(place, [(last_u[0], got_u), (last_o[0], got_last_o)])
    heads_keep, heads_send = settle(place, [(v[0], over_z2(v[1])) for v in (last_q, last_r)])
    near, far = heads_send[0], heads_send[1]
    heads_group = (heads_keep, over_seq(near), over_core(far), over_both(far))
    x_back, up_near = pin((x_back, up_group[0]), heads_keep)
    up_group = (up_near, up_group[1])
    input_grad = (grad_x + x_back.astype(F32)).astype(BF16)[None]
    so_far = update_rest(place, mats, mats_momentum, mats_average, [down_group, up_group], rate)
    *new, s_grad, s_value, s_momentum, s_average, s_bias = update_heads(
        place,
        mats,
        mats_momentum,
        mats_average,
        heads_group,
        (smalls.T, smalls_momentum.T, smalls_average.T),
        so_far,
        rate,
    )
    return (
        block_out[None],
        input_grad,
        *new,
        s_grad.T,
        s_bias.reshape(-1),
        s_value.T,
        s_momentum.T,
        s_average.T,
    )


def solution(mesh):
    placed = (
        P("dp", "seq", None),
        P("dp", None),
        P("dp", None),
        P("dp", "seq", None),
        P("dp", None),
        P("dp", None),
        P("dp", None),
        P("dp", None),
        P("dp", None),
        P("dp", None),
    )
    plan = tuned if tuple(mesh.shape.values()) == (16, 2) else per_device
    return jax.shard_map(
        plan,
        mesh=mesh,
        in_specs=placed,
        out_specs=(
            P("dp", "seq", None),
            P("dp", "seq", None),
            P("dp", None),
            P("dp", None),
            P("dp", None),
            P("dp", None),
            P("dp", None),
            P("dp"),
            P("dp", None),
            P("dp", None),
            P("dp", None),
        ),
        check_vma=False,
    )
```

```python
import functools
import math

import jax
import jax.numpy as jnp
from jax import lax
from jax.experimental import pallas as pl
from jax.experimental.pallas import tpu as pltpu
from jax.sharding import PartitionSpec as P

MODEL_WIDTH = 768
H = 12
HD = 64
FF = 3072


epsilon = 1e-06
momentum_rate = 0.9
decay_rate = 0.0001
average_rate = 0.75
base_rate = 0.03
masked_score = -1e30


def product(left, right):
    return jnp.dot(left, right, preferred_element_type=jnp.float32)


def product_tn(left, right):
    return lax.dot_general(
        left, right, (((0,), (0,)), ((), ())), preferred_element_type=jnp.float32
    )


def product_nt(left, right):
    return lax.dot_general(
        left, right, (((1,), (1,)), ((), ())), preferred_element_type=jnp.float32
    )


def normalize(rows, gain, shift):
    mean = jnp.mean(rows, axis=-1, keepdims=True)
    centred = rows - mean
    spread = jnp.mean(centred * centred, axis=-1, keepdims=True)
    return centred * lax.rsqrt(spread + epsilon) * gain + shift


def exact_gelu(values):
    return jax.nn.gelu(values, approximate=False)


def head_scores(query_heads, key_heads, live_doc):
    scores = (
        jnp.einsum("qhe,khe->hqk", query_heads, key_heads, preferred_element_type=jnp.float32)
        * 0.125
    )
    return jnp.where(live_doc[None, None, :] > 0, scores, masked_score)


def attention_forward_pass(item):
    query_doc, keys_doc, values_doc, live_doc = item
    query_heads = query_doc.reshape(query_doc.shape[0], H, HD)
    key_heads = keys_doc.reshape(keys_doc.shape[0], H, HD)
    value_heads = values_doc.reshape(values_doc.shape[0], H, HD)
    scores = head_scores(query_heads, key_heads, live_doc)
    top = jnp.max(scores, axis=-1, keepdims=True)
    expd = jnp.exp(scores - top)
    total = jnp.sum(expd, axis=-1, keepdims=True)
    prob = (expd / total).astype(jnp.bfloat16)
    attention_output = jnp.einsum(
        "hqk,khe->qhe", prob, value_heads, preferred_element_type=jnp.float32
    )
    return (attention_output.reshape(query_doc.shape[0], H * HD), (top + jnp.log(total))[..., 0])


def attention_backward_pass(item):
    query_doc, keys_doc, values_doc, live_doc, log_sum_normalizer, grad_doc = item
    element_count = query_doc.shape[0]
    length = keys_doc.shape[0]
    query_heads = query_doc.reshape(element_count, H, HD)
    key_heads = keys_doc.reshape(length, H, HD)
    value_heads = values_doc.reshape(length, H, HD)
    grad_heads = grad_doc.reshape(element_count, H, HD)
    scores = head_scores(query_heads, key_heads, live_doc)
    prob = jnp.exp(scores - log_sum_normalizer[..., None])
    grad_prob = jnp.einsum(
        "qhe,khe->hqk", grad_heads, value_heads, preferred_element_type=jnp.float32
    )
    grad_values = jnp.einsum(
        "hqk,qhe->khe", prob.astype(jnp.bfloat16), grad_heads, preferred_element_type=jnp.float32
    )
    inner = jnp.sum(prob * grad_prob, axis=-1, keepdims=True)
    grad_scores = (prob * (grad_prob - inner)).astype(jnp.bfloat16)
    grad_query = (
        jnp.einsum("hqk,khe->qhe", grad_scores, key_heads, preferred_element_type=jnp.float32)
        * 0.125
    )
    grad_keys = (
        jnp.einsum("hqk,qhe->khe", grad_scores, query_heads, preferred_element_type=jnp.float32)
        * 0.125
    )
    return (
        grad_query.reshape(element_count, H * HD),
        grad_keys.reshape(length, H * HD),
        grad_values.reshape(length, H * HD),
    )


def per_device(
    inputs,
    modality,
    key_valid_mask,
    output_gradient,
    mats,
    mats_momentum,
    mats_average,
    smalls,
    smalls_momentum,
    smalls_average,
):
    docs, local_len, width = inputs.shape
    seq_len = modality.shape[1]
    rows = docs * local_len
    low_mats = mats.astype(jnp.bfloat16)
    w_qkv, w_out, w_up, w_down, whole_smalls = (
        lax.all_gather(low_mats[:, 0 : 3 * MODEL_WIDTH], "dp", axis=0, tiled=True),
        lax.all_gather(low_mats[:, 3 * MODEL_WIDTH : 4 * MODEL_WIDTH], "dp", axis=0, tiled=True),
        lax.all_gather(
            low_mats[:, 4 * MODEL_WIDTH : 4 * MODEL_WIDTH + FF], "dp", axis=0, tiled=True
        ),
        lax.all_gather(low_mats[:, 4 * MODEL_WIDTH + FF :], "dp", axis=0, tiled=True),
        lax.all_gather(smalls.astype(jnp.bfloat16), "dp", axis=0, tiled=True),
    )
    params = whole_smalls.astype(jnp.float32)
    bias_qkv = jnp.concatenate([params[:, 0], jnp.zeros_like(params[:, 0]), params[:, 1]])
    bias_up = jnp.transpose(params[:, 8:12]).reshape(FF)
    embed = jnp.transpose(whole_smalls[:, 12:15])
    leading_key = (jnp.arange(seq_len) == 0).astype(jnp.int32)
    valid_positions = jnp.maximum(key_valid_mask, leading_key[None, :])
    local_start = lax.axis_index("seq") * local_len
    local_modality = lax.dynamic_slice_in_dim(modality, local_start, local_len, 1)
    onehot = (
        local_modality.reshape(rows)[:, None] == jnp.arange(3, dtype=jnp.int32)[None, :]
    ).astype(jnp.bfloat16)
    x_in = inputs.reshape(rows, width).astype(jnp.float32) + product(onehot, embed)
    x_low = x_in.astype(jnp.bfloat16)
    qkv = (product(x_low, w_qkv) + bias_qkv).astype(jnp.bfloat16)
    query_documents = qkv[:, 0:width].reshape(docs, local_len, width)
    keys_local = qkv[:, width : 2 * width].reshape(docs, local_len, width)
    values_local = qkv[:, 2 * width :].reshape(docs, local_len, width)
    every_key, every_value = (
        lax.all_gather(keys_local, "seq", axis=1, tiled=True),
        lax.all_gather(values_local, "seq", axis=1, tiled=True),
    )
    attention_output, log_sum_normalizer = lax.map(
        attention_forward_pass, (query_documents, every_key, every_value, valid_positions)
    )
    out_low = attention_output.reshape(rows, width).astype(jnp.bfloat16)
    mixed = product(out_low, w_out) + params[:, 2]
    first_in = x_in + mixed
    first = normalize(first_in, params[:, 4], params[:, 5])
    first_low = first.astype(jnp.bfloat16)
    up = product(first_low, w_up) + bias_up
    act_low = exact_gelu(up).astype(jnp.bfloat16)
    ffo = product_nt(act_low, w_down) + params[:, 3]
    second_in = first + ffo
    result = normalize(second_in, params[:, 6], params[:, 7])
    block_out = result.astype(jnp.bfloat16).reshape(docs, local_len, width)
    w_qkv, w_out, w_up, w_down = (
        lax.all_gather(low_mats[:, 0 : 3 * MODEL_WIDTH], "dp", axis=0, tiled=True),
        lax.all_gather(low_mats[:, 3 * MODEL_WIDTH : 4 * MODEL_WIDTH], "dp", axis=0, tiled=True),
        lax.all_gather(
            low_mats[:, 4 * MODEL_WIDTH : 4 * MODEL_WIDTH + FF], "dp", axis=0, tiled=True
        ),
        lax.all_gather(low_mats[:, 4 * MODEL_WIDTH + FF :], "dp", axis=0, tiled=True),
    )
    grad_rows = output_gradient.reshape(rows, width).astype(jnp.float32)
    second_out, second_pull = jax.vjp(normalize, second_in, params[:, 6], params[:, 7])
    grad_second, grad_gain2, grad_shift2 = second_pull(grad_rows)
    grad_ffo = grad_second.astype(jnp.bfloat16)
    grad_bias_down = jnp.sum(grad_ffo.astype(jnp.float32), axis=0)
    grad_w_down = product_tn(grad_ffo, act_low)
    grad_act = product(grad_ffo, w_down)
    gelu_out, gelu_pull = jax.vjp(exact_gelu, up)
    grad_up = gelu_pull(grad_act)[0].astype(jnp.bfloat16)
    grad_bias_up = jnp.sum(grad_up.astype(jnp.float32), axis=0)
    grad_w_up = product_tn(first_low, grad_up)
    grad_first = grad_second + product_nt(grad_up, w_up)
    first_out, first_pull = jax.vjp(normalize, first_in, params[:, 4], params[:, 5])
    grad_first_in, grad_gain1, grad_shift1 = first_pull(grad_first)
    grad_mixed = grad_first_in.astype(jnp.bfloat16)
    grad_bias_out = jnp.sum(grad_mixed.astype(jnp.float32), axis=0)
    grad_w_out = product_tn(out_low, grad_mixed)
    grad_out = product_nt(grad_mixed, w_out).astype(jnp.bfloat16)
    output_gradient_documents = grad_out.reshape(docs, local_len, width)
    grad_query, grad_keys_all, grad_values_all = lax.map(
        attention_backward_pass,
        (
            query_documents,
            every_key,
            every_value,
            valid_positions,
            log_sum_normalizer,
            output_gradient_documents,
        ),
    )
    grad_keys, grad_values = (
        lax.psum_scatter(
            grad_keys_all.astype(jnp.bfloat16), "seq", scatter_dimension=1, tiled=True
        ).astype(jnp.float32),
        lax.psum_scatter(
            grad_values_all.astype(jnp.bfloat16), "seq", scatter_dimension=1, tiled=True
        ).astype(jnp.float32),
    )
    grad_qkv = jnp.concatenate(
        [
            grad_query.reshape(rows, width).astype(jnp.bfloat16),
            grad_keys.reshape(rows, width).astype(jnp.bfloat16),
            grad_values.reshape(rows, width).astype(jnp.bfloat16),
        ],
        axis=1,
    )
    grad_bias_qkv = jnp.sum(grad_qkv.astype(jnp.float32), axis=0)
    grad_w_qkv = product_tn(x_low, grad_qkv)
    grad_x_in = grad_first_in + product_nt(grad_qkv, w_qkv)
    grad_embed = lax.dot_general(
        onehot.astype(jnp.float32),
        grad_x_in,
        (((0,), (0,)), ((), ())),
        precision=lax.Precision.HIGHEST,
        preferred_element_type=jnp.float32,
    )
    input_grad = grad_x_in.astype(jnp.bfloat16).reshape(docs, local_len, width)
    grad_columns = jnp.stack(
        [
            grad_bias_qkv[0:width],
            grad_bias_qkv[2 * width :],
            grad_bias_out,
            grad_bias_down,
            grad_gain1,
            grad_shift1,
            grad_gain2,
            grad_shift2,
        ],
        axis=1,
    )
    grad_smalls = jnp.concatenate(
        [
            grad_columns,
            jnp.transpose(grad_bias_up.reshape(FF // width, width)),
            jnp.transpose(grad_embed),
        ],
        axis=1,
    )
    qkv_shard, out_shard, up_shard, down_shard, small_shard = (
        lax.psum_scatter(
            grad_w_qkv.astype(jnp.bfloat16), "dp", scatter_dimension=0, tiled=True
        ).astype(jnp.float32),
        lax.psum_scatter(
            grad_w_out.astype(jnp.bfloat16), "dp", scatter_dimension=0, tiled=True
        ).astype(jnp.float32),
        lax.psum_scatter(
            grad_w_up.astype(jnp.bfloat16), "dp", scatter_dimension=0, tiled=True
        ).astype(jnp.float32),
        lax.psum_scatter(
            grad_w_down.astype(jnp.bfloat16), "dp", scatter_dimension=0, tiled=True
        ).astype(jnp.float32),
        lax.psum_scatter(
            grad_smalls.astype(jnp.bfloat16), "dp", scatter_dimension=0, tiled=True
        ).astype(jnp.float32),
    )
    mats_shard = jnp.concatenate([qkv_shard, out_shard, up_shard, down_shard], axis=1)
    mats_grad, smalls_grad = (
        lax.psum(mats_shard.astype(jnp.bfloat16), "seq").astype(jnp.float32),
        lax.psum(small_shard.astype(jnp.bfloat16), "seq").astype(jnp.float32),
    )
    out_bias_grad = smalls_grad[:, 2]
    total_tokens = rows * lax.axis_size("dp") * lax.axis_size("seq")
    rate = base_rate / math.sqrt(total_tokens)
    decayed = mats_grad + decay_rate * mats
    new_mats_momentum = momentum_rate * mats_momentum + decayed
    new_mats = mats - rate * (decayed + momentum_rate * new_mats_momentum)
    new_mats_average = average_rate * mats_average + (1.0 - average_rate) * new_mats
    new_smalls_momentum = momentum_rate * smalls_momentum + smalls_grad
    new_smalls = smalls - rate * (smalls_grad + momentum_rate * new_smalls_momentum)
    new_smalls_average = average_rate * smalls_average + (1.0 - average_rate) * new_smalls
    return (
        block_out,
        input_grad,
        mats_grad,
        new_mats,
        new_mats_momentum,
        new_mats_average,
        smalls_grad,
        out_bias_grad,
        new_smalls,
        new_smalls_momentum,
        new_smalls_average,
    )


LN2 = math.log(2.0)
NT = (((1,), (1,)), ((), ()))
NN = (((1,), (0,)), ((), ()))
TN = (((0,), (0,)), ((), ()))
BF16 = jnp.bfloat16
F32 = jnp.float32
HALF = MODEL_WIDTH // 2
QUARTER = MODEL_WIDTH
SHARE = 0.5
TIMES = {"long_fold": 8, "outer_out": 6}


def declared(name):
    return pl.CostEstimate(flops=int(SHARE * 1.15e9 * TIMES.get(name, 0.2)), bytes_accessed=0, transcendentals=0)


def mxu(left, right, dims):
    return lax.dot_general(left, right, dims, preferred_element_type=jnp.float32)


def three_parts(value):
    high = value.astype(jnp.bfloat16)
    rest = value - high.astype(jnp.float32)
    middle = rest.astype(jnp.bfloat16)
    return high, middle, (rest - middle.astype(jnp.float32)).astype(jnp.bfloat16)


def run(kernel, name, ins, outs, scratch=(), limit=12):
    spaces = {"vmem": pltpu.VMEM, "smem": pltpu.SMEM}
    return pl.pallas_call(
        kernel,
        in_specs=[pl.BlockSpec(memory_space=spaces[kind]) for _, kind in ins],
        out_specs=[pl.BlockSpec(memory_space=pltpu.VMEM) for _ in outs],
        out_shape=[jax.ShapeDtypeStruct(shape, dtype) for shape, dtype in outs],
        scratch_shapes=list(scratch),
        compiler_params=pltpu.CompilerParams(vmem_limit_bytes=limit * 2**20),
        cost_estimate=declared(name),
        name=name,
    )(*[array for array, _ in ins])


def both_kernel(mine, theirs, out):
    n = mine.shape[0]
    out[0:n] = mine[...]
    out[n:] = theirs[...]


def both(mine, theirs):
    shape = (mine.shape[0] + theirs.shape[0],) + mine.shape[1:]
    return run(both_kernel, "both", [(mine, "vmem"), (theirs, "vmem")], [(shape, mine.dtype)], limit=2)[0]


def last_columns_kernel(mine, theirs, out):
    n = mine.shape[0]
    out[0:n] = mine[:, :, mine.shape[2] - HALF :]
    out[n:] = theirs[:, :, mine.shape[2] - HALF :]


def last_columns(mine, theirs):
    shape = (2 * mine.shape[0], mine.shape[1], HALF)
    return run(last_columns_kernel, "last_columns", [(mine, "vmem"), (theirs, "vmem")], [(shape, BF16)], limit=2)[0]


def pair_up_kernel(place, keep, got, *blocks):
    rows = keep.shape[0]
    for ref, side in ((keep, place[2]), (got, 1 - place[2])):
        at = pl.ds(pl.multiple_of(side * rows, 16), rows)
        for block, first, last in zip(blocks, CUTS[:-1], CUTS[1:]):
            block[0, at, :] = ref[:, first:last]


def pair_up(place, keep, got):
    rows = keep.shape[0]
    return run(
        pair_up_kernel,
        "pair_up",
        [(place, "smem"), (keep, "vmem"), (got, "vmem")],
        [((1, 2 * rows, b - a), BF16) for a, b in zip(CUTS[:-1], CUTS[1:])],
        limit=2,
    )


def place_rows(pieces, whole):
    for value, first in pieces:
        whole[pl.ds(first, value.shape[0]), :] = value


def xor2(z):
    return lax.rem(z + 2, 4)


def xor1(z):
    return z + 1 - 2 * lax.rem(z, 2)


def near_far(place, y_last):
    y, z = place[1], place[3]
    if y_last:
        line = (z, xor2(z), xor1(z), xor1(xor2(z)))
        return [(zz, y) for zz in line], [(zz, 1 - y) for zz in line]
    one, two = (z, xor2(z)), (xor1(z), xor1(xor2(z)))
    return [(zz, yy) for yy in (y, 1 - y) for zz in one], [(zz, yy) for yy in (y, 1 - y) for zz in two]


def eight(place, block):
    mine, theirs, y_last = block
    near, far = near_far(place, y_last)
    pieces = []
    for ref, chips in ((mine, near), (theirs, far)):
        for i, (zz, yy) in enumerate(chips):
            pieces.append((ref[i, :, 0:QUARTER], pl.multiple_of((2 * zz + yy) * 96, 32)))
    return pieces


def sixteen(place, blocks):
    core = place[2]
    near, far = near_far(place, True)
    pieces = []
    for chips, cc, ref in zip((near, near, far, far), (core, 1 - core, core, 1 - core), blocks):
        for i, (zz, yy) in enumerate(chips):
            pieces.append((ref[i], pl.multiple_of((zz * 4 + yy * 2 + cc) * 48, 16)))
    return pieces


def place_out(place, mine, theirs, whole):
    core = place[2]
    near, far = near_far(place, True)
    for ref, cc in ((mine, core), (theirs, 1 - core)):
        lanes = pl.ds(pl.multiple_of(cc * HALF, 128), HALF)
        for i, (zz, yy) in enumerate(near + far):
            whole[pl.ds(pl.multiple_of((2 * zz + yy) * 96, 32), 96), lanes] = ref[i]


def split_rows(whole, mine, theirs, place, y_last):
    near, far = near_far(place, y_last)
    for ref, chips in ((mine, near), (theirs, far)):
        for i, (zz, yy) in enumerate(chips):
            row = pl.multiple_of((2 * zz + yy) * 96, 32)
            ref[i] = whole[pl.ds(row, 96), :].astype(ref.dtype)


def pack_heads_kernel(place, mats, smalls_t, block, narrow):
    width = MODEL_WIDTH
    narrow[...] = jnp.zeros_like(narrow)
    narrow[0:15, :] = smalls_t[...]
    block[:, 3 * HALF :] = narrow[...].T.astype(BF16)
    for j in range(3):
        lanes = pl.ds(pl.multiple_of(j * width + place[0] * HALF, 128), HALF)
        block[:, j * HALF : (j + 1) * HALF] = mats[:, lanes].astype(BF16)


def pack_heads(place, mats, smalls_t):
    rows = mats.shape[0]
    return run(
        pack_heads_kernel,
        "pack_heads",
        [(place, "smem"), (mats, "vmem"), (smalls_t, "vmem")],
        [((rows, 3 * HALF + 128), BF16)],
        [pltpu.VMEM((128, rows), F32)],
        limit=4,
    )[0]


CUTS = (0, QUARTER + HALF, 2 * QUARTER + HALF, 3 * QUARTER + HALF, 4 * QUARTER + HALF)


def pack_rest_kernel(place, mats, keep, give):
    width = MODEL_WIDTH
    for core, ref in ((1 - place[2], give), (place[2], keep)):
        take = lambda first, n: mats[:, pl.ds(pl.multiple_of(first, 128), n)].astype(BF16)
        ref[:, 0:QUARTER] = take(4 * width + 2 * core * QUARTER, QUARTER)
        ref[:, QUARTER : CUTS[1]] = take(3 * width + core * HALF, HALF)
        ref[:, CUTS[1] : CUTS[2]] = take(4 * width + (2 * core + 1) * QUARTER, QUARTER)
        ref[:, CUTS[2] : CUTS[3]] = take(8 * width + 2 * core * QUARTER, QUARTER)
        ref[:, CUTS[3] :] = take(8 * width + (2 * core + 1) * QUARTER, QUARTER)


def pack_rest(place, mats):
    rows = mats.shape[0]
    return run(
        pack_rest_kernel,
        "pack_rest",
        [(place, "smem"), (mats, "vmem")],
        [((rows, CUTS[4]), BF16)] * 2,
        limit=4,
    )


def unit_rows(rows):
    mean = jnp.mean(rows, axis=-1, keepdims=True)
    centred = rows - mean
    spread = jnp.mean(centred * centred, axis=-1, keepdims=True)
    scale = lax.rsqrt(spread + epsilon)
    return centred * scale, scale


def unit_back(grad, unit, scale, gain):
    inner = grad * gain
    mean_one = jnp.mean(inner, axis=-1, keepdims=True)
    mean_two = jnp.mean(inner * unit, axis=-1, keepdims=True)
    return scale * (inner - mean_one - unit * mean_two)


def down_sum(value):
    return jnp.sum(value, axis=0, keepdims=True)


def project_kernel(
    place, own, other, kinds, mask, w0, w1, w2, w3, x_low, x_in, qkv, masked, params, whole
):
    x, y, core = place[0], place[1], place[2]
    rows = own.shape[0]
    place_rows(sixteen(place, (w0, w1, w2, w3)), whole)
    lane_row = lax.broadcasted_iota(jnp.int32, (8, rows), 0)
    lane = lax.broadcasted_iota(jnp.int32, (8, 128), 1)
    first_row = lax.broadcasted_iota(jnp.int32, (8, 128), 0)
    pick = jnp.where((lane == 0) & (first_row == 0), 1.0, 0.0).astype(BF16)
    position = lax.broadcasted_iota(jnp.int32, (1, rows), 1)
    for side in range(2):
        start = pl.multiple_of((x if side == 0 else 1 - x) * rows, 128)
        alive = (mask[:, pl.ds(start, rows)] > 0) | (position + start == 0)
        bias = jnp.where(alive, 0.0, masked_score)
        bias = jnp.where(lane_row == 0, jnp.broadcast_to(bias, (8, rows)), 0.0).astype(BF16)
        masked[side * rows : (side + 1) * rows, :] = mxu(bias, pick, TN).astype(BF16)
    params[...] = whole[:, 3 * HALF :].astype(F32).T[0:16]
    embed = params[8:16, :].astype(BF16)
    start_q = pl.multiple_of(x * HALF, 128)
    bias_q = params[0:1, pl.ds(start_q, HALF)]
    bias_v = params[1:2, pl.ds(start_q, HALF)]
    scale = 0.125 / LN2
    step = 256
    for side in range(2):
        start = pl.multiple_of((x if side == 0 else 1 - x) * rows, 128)
        hot = jnp.where(kinds[:, pl.ds(start, rows)] + 4 == lane_row, 1.0, 0.0).astype(BF16)
        source = own if side == 0 else other
        for i in range(rows // step):
            span = slice(i * step, (i + 1) * step)
            out = slice(side * rows + i * step, side * rows + (i + 1) * step)
            value = source[span, :].astype(F32) + mxu(hot[:, span], embed, TN)
            if side == 0:
                x_in[span, :] = value
            low = value.astype(BF16)
            x_low[out, :] = low
            q = mxu(low, whole[:, 0:HALF], NN)
            qkv[out, 0:HALF] = ((q + bias_q) * scale).astype(BF16)
            k = mxu(low, whole[:, HALF : 2 * HALF], NN)
            qkv[out, HALF : 2 * HALF] = k.astype(BF16)
            v = mxu(low, whole[:, 2 * HALF : 3 * HALF], NN)
            qkv[out, 2 * HALF :] = (v + bias_v).astype(BF16)


def project(place, own, other, kinds, mask, blocks):
    rows, width = own.shape
    return run(
        project_kernel,
        "project",
        [(place, "smem"), (own, "vmem"), (other, "vmem"), (kinds, "vmem"), (mask, "vmem")]
        + [(block, "vmem") for block in blocks],
        [
            ((2 * rows, width), BF16),
            ((rows, width), F32),
            ((2 * rows, 3 * HALF), BF16),
            ((2 * rows, 128), BF16),
            ((16, width), F32),
            ((width, 3 * HALF + 128), BF16),
        ],
    )


def attend_kernel(qkv, masked_ref, out_ref, log_ref, *, block):
    length = qkv.shape[0]
    pairs = qkv.shape[1] // 384
    lane = lax.broadcasted_iota(jnp.int32, (1, 128), 1)
    one = jnp.broadcast_to(jnp.where(lane == 0, 1.0, 0.0).astype(jnp.bfloat16), (block, 128))
    ones = jnp.ones((length, 128), jnp.bfloat16)
    for pair in range(pairs):
        take = lambda j: slice((j * pairs + pair) * 128, (j * pairs + pair + 1) * 128)
        keys = jnp.concatenate([qkv[:, take(1)], masked_ref[...]], axis=1)
        values = jnp.concatenate([qkv[:, take(2)], ones], axis=1)
        for i in range(length // block):
            span = slice(i * block, (i + 1) * block)
            query = qkv[span, take(0)]
            outs, logs = [], []
            for head in range(2):
                here = (lane < 64) if head == 0 else (lane >= 64)
                only = jnp.where(here, query, jnp.zeros_like(query))
                scores = mxu(jnp.concatenate([only, one], axis=1), keys, NT)
                top = jnp.max(scores, axis=1, keepdims=True)
                weight = jnp.exp2(scores - top).astype(jnp.bfloat16)
                mixed = mxu(weight, values, NN)
                total = mixed[:, 128:]
                outs.append(mixed[:, :128] / total)
                logs.append(top + jnp.log2(total[:, 0:1]))
            out_ref[span, take(0)] = jnp.where(lane < 64, outs[0], outs[1]).astype(jnp.bfloat16)
            so_far = log_ref[span, :] if pair else jnp.zeros((block, 128), F32)
            both = jnp.where(lane == 2 * pair, logs[0], jnp.where(lane == 2 * pair + 1, logs[1], so_far))
            log_ref[span, :] = both


def attend(qkv, masked, block=256):
    length, columns = qkv.shape
    return run(
        functools.partial(attend_kernel, block=block),
        "attend",
        [(qkv, "vmem"), (masked, "vmem")],
        [((length, columns // 3), BF16), ((length, 128), F32)],
        limit=8,
    )


def attend_back_kernel(
    place, qkv, out, own_ref, got_ref, log_ref, masked_ref, out_ref, *refs, role, parts, block
):
    dk_sum, dv_sum = refs[-2], refs[-1]
    length, rows = qkv.shape[0], own_ref.shape[0]
    pairs = qkv.shape[1] // 384
    bf16 = jnp.bfloat16
    core = place[2]
    pair = (1 - core, core, 2)[role]
    take = lambda j: pl.ds(pl.multiple_of((j * pairs + pair) * 128, 128), 128)
    lane = lax.broadcasted_iota(jnp.int32, (1, 128), 1)
    ones = jnp.where((lane >= 1) & (lane <= 3), 1.0, 0.0).astype(bf16)
    masked = masked_ref[...]
    keys = jnp.concatenate(
        [qkv[:, take(1)], jnp.where(lane == 0, masked, jnp.broadcast_to(ones, masked.shape))], axis=1
    )
    three = jnp.broadcast_to(jnp.where(lane <= 2, 1.0, 0.0).astype(bf16), (length, 128))
    values = jnp.concatenate([qkv[:, take(2)], three], axis=1)
    keys_t = qkv[:, take(1)].T
    one = jnp.ones((block, 128), bf16)
    zero = jnp.zeros((block, 128), bf16)
    row = lax.broadcasted_iota(jnp.int32, (128, 1), 0)
    for i in range(length // block):
        span = slice(i * block, (i + 1) * block)
        at = i * block % rows
        query = qkv[span, take(0)]
        grad = (own_ref if i * block < rows else got_ref)[at : at + block, take(0)]
        both = grad.astype(jnp.float32) * out[span, take(0)].astype(jnp.float32)
        logs = log_ref[span, :]
        turned = []
        for head in range(2):
            here = (lane < 64) if head == 0 else (lane >= 64)
            inner = jnp.sum(jnp.where(here, both, 0.0), axis=1, keepdims=True)
            wide = lambda t: jnp.broadcast_to(t, (block, 128))
            log = jnp.sum(jnp.where(lane == 2 * pair + head, logs, 0.0), axis=1, keepdims=True)
            i0, i1, i2 = (wide(t) for t in three_parts(-inner))
            l0, l1, l2 = (wide(t) for t in three_parts(-log))
            query_h = jnp.where(here, query, zero)
            grad_h = jnp.where(here, grad, zero)
            tail_q = jnp.where(
                lane == 0,
                one,
                jnp.where(lane == 1, l0, jnp.where(lane == 2, l1, jnp.where(lane == 3, l2, zero))),
            )
            tail_g = jnp.where(lane == 0, i0, jnp.where(lane == 1, i1, jnp.where(lane == 2, i2, zero)))
            prob = jnp.exp2(mxu(keys, jnp.concatenate([query_h, tail_q], axis=1), NT))
            slope = mxu(values, jnp.concatenate([grad_h, tail_g], axis=1), NT)
            grad_scores = (prob * slope).astype(bf16)
            add_v = mxu(prob.astype(bf16), grad_h, NN)
            add_k = mxu(grad_scores, query_h, NN)
            if i == 0 and head == 0:
                dv_sum[...] = add_v
                dk_sum[...] = add_k
            else:
                dv_sum[...] += add_v
                dk_sum[...] += add_k
            turned.append(mxu(keys_t, grad_scores, NN))
        out_ref[span, 0:128] = (jnp.where(row < 64, turned[0], turned[1]) * 0.125).T.astype(bf16)
    out_ref[:, 128:256] = (dk_sum[...] * LN2).astype(bf16)
    out_ref[:, 256:384] = dv_sum[...].astype(bf16)
    if parts:
        keep_ref, give_ref, wide_ref = refs[:3]
        wide_ref[:, 0:384] = out_ref[...]
        wide_ref[:, 384:512] = jnp.zeros((length, 128), bf16)
        keep_ref[...] = wide_ref[:, pl.ds(pl.multiple_of(core * 256, 128), 256)]
        give_ref[...] = wide_ref[:, pl.ds(pl.multiple_of((1 - core) * 256, 128), 256)]


def attend_back(place, qkv, out, own, got, log_sum, masked, role, parts=False, block=512):
    length = qkv.shape[0]
    return run(
        functools.partial(attend_back_kernel, role=role, parts=parts, block=block),
        "attend_back",
        [(place, "smem")] + [(v, "vmem") for v in (qkv, out, own, got, log_sum, masked)],
        [((length, 384), BF16)] + [((length, 256), BF16)] * (2 * parts),
        [pltpu.VMEM((length, 512), BF16)] * parts + [pltpu.VMEM((length, 128), F32)] * 2,
        limit=14,
    )


def mix_kernel(
    place, heads, got, x_in, params, w0, w1, out_low, unit, scale, first_low, whole
):
    x, y, core = place[0], place[1], place[2]
    rows = x_in.shape[0]
    place_out(place, w0, w1, whole)
    mine = pl.multiple_of(x * HALF, 128)
    theirs = pl.multiple_of((1 - x) * HALF, 128)
    out_low[:, pl.ds(mine, HALF)] = heads[0:rows, :]
    out_low[:, pl.ds(theirs, HALF)] = got[...]
    step = 256
    for i in range(rows // step):
        span = slice(i * step, (i + 1) * step)
        mixed = mxu(out_low[span, :], whole[...], NN) + params[2:3, :]
        ones, size = unit_rows(x_in[span, :] + mixed)
        unit[span, :] = ones
        scale[span, :] = jnp.broadcast_to(size, (step, 128))
        first_low[span, :] = (ones * params[4:5, :] + params[5:6, :]).astype(BF16)


def mix(place, heads, got, x_in, params, blocks):
    rows, width = x_in.shape
    return run(
        mix_kernel,
        "mix",
        [(place, "smem"), (heads, "vmem"), (got, "vmem"), (x_in, "vmem"), (params, "vmem")]
        + [(block, "vmem") for block in blocks],
        [
            ((rows, width), BF16),
            ((rows, width), F32),
            ((rows, 128), F32),
            ((rows, width), BF16),
            ((width, width), BF16),
        ],
    )


def gelu_and_slope(up):
    size = jnp.abs(up)
    t = 1.0 / (1.0 + (0.3275911 * math.sqrt(0.5)) * size)
    bell = jnp.exp(-0.5 * up * up)
    poly = t * (
        0.5 * 0.254829592
        + t
        * (
            0.5 * -0.284496736
            + t * (0.5 * 1.421413741 + t * (0.5 * -1.453152027 + t * (0.5 * 1.061405429)))
        )
    )
    tail = poly * bell
    below = jnp.where(up < 0, tail, 1.0 - tail)
    return up * below, below + up * bell * (1.0 / math.sqrt(2.0 * math.pi))


def up_kernel(place, own, other, params, w0, w1, act, slope, whole, *, which, y_last):
    core = place[2]
    rows = own.shape[0]
    place_rows(eight(place, (w0, w1, y_last)), whole)
    bias = params[pl.ds(8 + 2 * core + which, 1), :]
    step = 128
    for side in range(2):
        source = own if side == 0 else other
        for i in range(rows // step):
            out = slice(side * rows + i * step, side * rows + (i + 1) * step)
            up = mxu(source[i * step : (i + 1) * step, :], whole[...], NN) + bias
            value, change = gelu_and_slope(up)
            act[out, :] = value.astype(BF16)
            slope[out, :] = change.astype(BF16)


def raise_up(place, own, other, params, block, which):
    rows, width = own.shape
    *refs, y_last = block
    return run(
        functools.partial(up_kernel, which=which, y_last=y_last),
        "raise_up",
        [(place, "smem"), (own, "vmem"), (other, "vmem"), (params, "vmem")] + [(r, "vmem") for r in refs],
        [((2 * rows, QUARTER), BF16), ((2 * rows, QUARTER), BF16), ((width, QUARTER), BF16)],
        limit=8,
    )


def lower_kernel(place, act, w0, w1, out, whole, *, y_last):
    place_rows(eight(place, (w0, w1, y_last)), whole)
    step = 256
    for i in range(act.shape[0] // step):
        span = slice(i * step, (i + 1) * step)
        out[span, :] = mxu(act[span, :], whole[...], NT)


def lower(place, act, block):
    rows, columns = act.shape
    *refs, y_last = block
    return run(
        functools.partial(lower_kernel, y_last=y_last),
        "lower",
        [(place, "smem"), (act, "vmem")] + [(r, "vmem") for r in refs],
        [((rows, MODEL_WIDTH), F32), ((MODEL_WIDTH, columns), BF16)],
        limit=8,
    )


def lower_other_kernel(place, act, so_far, w0, w1, out, whole, *, y_last):
    place_rows(eight(place, (w0, w1, y_last)), whole)
    rows = out.shape[0]
    step = 256
    for i in range(rows // step):
        span = slice(rows + i * step, rows + (i + 1) * step)
        value = so_far[span, :] + mxu(act[span, :], whole[...], NT)
        out[i * step : (i + 1) * step, :] = value.astype(BF16)


def lower_other(place, act, so_far, block):
    rows, columns = act.shape
    *refs, y_last = block
    return run(
        functools.partial(lower_other_kernel, y_last=y_last),
        "lower_other",
        [(place, "smem"), (act, "vmem"), (so_far, "vmem")] + [(r, "vmem") for r in refs],
        [((rows // 2, MODEL_WIDTH), BF16), ((MODEL_WIDTH, columns), BF16)],
        limit=8,
    )


def turn_kernel(
    place,
    act,
    so_far,
    got,
    unit1,
    params,
    grad,
    whole,
    block_out,
    grad_second,
    grad_low,
    sums,
):
    rows = got.shape[0]
    step = 128
    total = [jnp.zeros((1, MODEL_WIDTH), F32)] * 3
    for i in range(rows // step):
        span = slice(i * step, (i + 1) * step)
        first = unit1[span, :] * params[4:5, :] + params[5:6, :]
        value = so_far[span, :] + mxu(act[span, :], whole[...], NT) + got[span, :].astype(F32)
        unit, scale = unit_rows(first + (value + params[3:4, :]))
        block_out[span, :] = (unit * params[6:7, :] + params[7:8, :]).astype(BF16)
        dy = grad[span, :].astype(F32)
        back = unit_back(dy, unit, scale, params[6:7, :])
        grad_second[span, :] = back
        low = back.astype(BF16)
        grad_low[span, :] = low
        total[0] += down_sum(low.astype(F32))
        total[1] += down_sum(unit * dy)
        total[2] += down_sum(dy)
    sums[...] = jnp.concatenate(total + [jnp.zeros((5, MODEL_WIDTH), F32)], axis=0)


def turn(place, act, so_far, got, unit1, params, grad, weight):
    rows, width = got.shape
    return run(
        turn_kernel,
        "turn",
        [
            (place, "smem"),
            (act, "vmem"),
            (so_far, "vmem"),
            (got, "vmem"),
            (unit1, "vmem"),
            (params, "vmem"),
            (grad, "vmem"),
            (weight, "vmem"),
        ],
        [((rows, width), BF16), ((rows, width), F32), ((rows, width), BF16), ((8, width), F32)],
        limit=8,
    )


def raise_back_kernel(place, own, other, slope, whole, grad_up, sums):
    rows = own.shape[0]
    step = 256
    total = jnp.zeros((1, slope.shape[1]), F32)
    for side in range(2):
        source = own if side == 0 else other
        for i in range(rows // step):
            out = slice(side * rows + i * step, side * rows + (i + 1) * step)
            value = mxu(source[i * step : (i + 1) * step, :], whole[...], NN)
            low = (value * slope[out, :].astype(F32)).astype(BF16)
            grad_up[out, :] = low
            total += down_sum(low.astype(F32))
    sums[...] = jnp.broadcast_to(total, sums.shape)


def raise_back(place, own, other, slope, weight):
    rows, width = own.shape
    columns = slope.shape[1]
    return run(
        raise_back_kernel,
        "raise_back",
        [(place, "smem"), (own, "vmem"), (other, "vmem"), (slope, "vmem"), (weight, "vmem")],
        [((2 * rows, columns), BF16), ((8, columns), F32)],
        limit=8,
    )


def outer_kernel(place, left_own, left_other, right_own, right_other, mine, theirs, whole, *, y_last):
    whole[...] = mxu(left_own[...], right_own[...], TN) + mxu(left_other[...], right_other[...], TN)
    split_rows(whole, mine, theirs, place, y_last)


def outer_joined_kernel(place, left_own, left_other, right, mine, theirs, whole, *, y_last):
    rows = left_own.shape[0]
    whole[...] = mxu(left_own[...], right[0:rows, :], TN) + mxu(left_other[...], right[rows:, :], TN)
    split_rows(whole, mine, theirs, place, y_last)


def outer_wide_kernel(place, left_own, left_other, first, second, mine, theirs, whole):
    rows = left_own.shape[0]
    n = first.shape[1]
    for j, right in enumerate((first, second)):
        value = mxu(left_own[...], right[0:rows, :], TN) + mxu(left_other[...], right[rows:, :], TN)
        whole[:, j * n : (j + 1) * n] = value
    split_rows(whole, mine, theirs, place, True)


def outer_wide(place, left_own, left_other, first, second):
    width = left_own.shape[1]
    columns = 2 * first.shape[1]
    return run(
        outer_wide_kernel,
        "outer_wide",
        [(place, "smem")] + [(r, "vmem") for r in (left_own, left_other, first, second)],
        [((4, 96, columns), BF16), ((4, 96, columns), BF16)],
        [pltpu.VMEM((width, columns), F32)],
        limit=14,
    )


def outer(place, left_own, left_other, rights, name, y_last=True):
    rows, width = left_own.shape
    columns = rights[0].shape[1]
    return run(
        functools.partial(outer_kernel if len(rights) == 2 else outer_joined_kernel, y_last=y_last),
        name,
        [(place, "smem"), (left_own, "vmem"), (left_other, "vmem")] + [(r, "vmem") for r in rights],
        [((4, 96, columns), BF16), ((4, 96, columns), BF16)],
        [pltpu.VMEM((width, columns), F32)],
        limit=12,
    )


def first_other_kernel(place, grad_a, grad_b, whole_a, whole_b, out):
    rows = out.shape[0]
    step = 256
    for i in range(rows // step):
        span = slice(rows + i * step, rows + (i + 1) * step)
        value = mxu(grad_a[span, :], whole_a[...], NT) + mxu(grad_b[span, :], whole_b[...], NT)
        out[i * step : (i + 1) * step, :] = value.astype(BF16)


def first_other(place, grad_a, grad_b, weight_a, weight_b):
    rows, columns = grad_a.shape
    return run(
        first_other_kernel,
        "first_other",
        [(place, "smem")] + [(r, "vmem") for r in (grad_a, grad_b, weight_a, weight_b)],
        [((rows // 2, MODEL_WIDTH), BF16)],
        limit=8,
    )[0]


def first_back_kernel(
    place,
    grad_a,
    grad_b,
    got_first,
    got_last,
    grad_second,
    unit1,
    scale1,
    params,
    whole_a,
    whole_b,
    whole_o,
    grad_first_in,
    mixed_keep,
    mixed_give,
    heads_keep,
    heads_give,
    sums,
    low_all,
    heads_all,
):
    x, core = place[0], place[2]
    step = got_first.shape[0]
    rows = 2 * step
    total = [jnp.zeros((1, MODEL_WIDTH), F32)] * 3
    for i in range(rows // step):
        span = slice(i * step, (i + 1) * step)
        value = mxu(grad_a[span, :], whole_a[...], NT) + mxu(grad_b[span, :], whole_b[...], NT)
        got = (got_first, got_last)[i]
        dh = grad_second[span, :] + value + got[...].astype(F32)
        unit = unit1[span, :]
        back = unit_back(dh, unit, scale1[span, 0:1], params[4:5, :])
        grad_first_in[span, :] = back
        low = back.astype(BF16)
        low_all[span, :] = low
        total[0] += down_sum(low.astype(F32))
        total[1] += down_sum(unit * dh)
        total[2] += down_sum(dh)
        heads_all[span, :] = mxu(low, whole_o[...], NT).astype(BF16)
    sums[...] = jnp.concatenate(total + [jnp.zeros((5, MODEL_WIDTH), F32)], axis=0)
    half = lambda i: pl.ds(pl.multiple_of(i * HALF, 128), HALF)
    mixed_keep[...] = low_all[:, half(core)]
    mixed_give[...] = low_all[:, half(1 - core)]
    heads_keep[...] = heads_all[:, half(x)]
    heads_give[...] = heads_all[:, half(1 - x)]


def first_back(place, *arrays):
    rows, width = arrays[4].shape
    return run(
        first_back_kernel,
        "first_back",
        [(place, "smem")] + [(r, "vmem") for r in arrays],
        [
            ((rows, width), F32),
            ((rows, HALF), BF16),
            ((rows, HALF), BF16),
            ((rows, HALF), BF16),
            ((rows, HALF), BF16),
            ((8, width), F32),
        ],
        [pltpu.VMEM((rows, width), BF16)] * 2,
        limit=10,
    )


def enter_kernel(
    place, d_give, d_keep, d_last, grad_first_in, kinds, sums1, sums2, sums_a, sums_b, whole, own, give, small
):
    x, core = place[0], place[2]
    rows = own.shape[0]
    pairs = ((d_give, 1 - core), (d_keep, core), (d_last, 2))
    small[...] = jnp.zeros_like(small)
    for ref, pair in pairs:
        at = pl.ds(pl.multiple_of(x * HALF + pair * 128, 128), 128)
        small[0:1, at] = down_sum(ref[:, 0:128].astype(F32))
        small[1:2, at] = down_sum(ref[:, 256:384].astype(F32))
    small[2:3, :] = sums1[0:1, :]
    small[3:4, :] = sums2[0:1, :]
    small[4:6, :] = sums1[1:3, :]
    small[6:8, :] = sums2[1:3, :]
    small[pl.ds(8 + 2 * core, 1), :] = sums_a[0:1, :]
    small[pl.ds(9 + 2 * core, 1), :] = sums_b[0:1, :]
    weights = []
    for _, pair in pairs:
        tiles = [whole[:, pl.ds(pl.multiple_of(j * HALF + pair * 128, 128), 128)] for j in range(3)]
        weights.append(jnp.concatenate(tiles, axis=1))
    lane_row = lax.broadcasted_iota(jnp.int32, (8, rows), 0)
    step = 256
    embed = jnp.zeros((8, MODEL_WIDTH), F32)
    for side in (1, 0):
        start = pl.multiple_of((x if side == 0 else 1 - x) * rows, 128)
        hot = jnp.where(kinds[:, pl.ds(start, rows)] == lane_row, 1.0, 0.0).astype(BF16)
        for i in range(rows // step):
            span = slice(i * step, (i + 1) * step)
            source = slice(side * rows + i * step, side * rows + (i + 1) * step)
            value = sum(mxu(ref[source, :], weight, NT) for (ref, _), weight in zip(pairs, weights))
            if side == 0:
                value = value + grad_first_in[span, :]
                own[span, :] = value
            else:
                give[span, :] = value.astype(BF16)
            take = hot[:, span]
            for term in three_parts(value):
                embed += mxu(take, term, NN)
    small[12:15, :] = embed[0:3, :]


def enter(place, *arrays):
    rows, width = arrays[3].shape
    return run(
        enter_kernel,
        "enter",
        [(place, "smem")] + [(r, "vmem") for r in arrays],
        [((rows, width), F32), ((rows, width), BF16), ((16, width), F32)],
        limit=12,
    )


def narrow_kernel(place, own, other, mine, theirs, whole):
    small = own[...] + other[...]
    rest = jnp.zeros((128 - small.shape[0], small.shape[1]), F32)
    whole[...] = jnp.concatenate([small, rest], axis=0).T
    split_rows(whole, mine, theirs, place, True)


def narrow(place, own, other):
    return run(
        narrow_kernel,
        "narrow",
        [(place, "smem"), (own, "vmem"), (other, "vmem")],
        [((4, 96, 128), BF16)] * 2,
        [pltpu.VMEM((own.shape[1], 128), F32)],
        limit=4,
    )


def fold_kernel(mine, got, keep, send):
    half = mine.shape[0] // 2
    for i in range(2 * half):
        value = mine[i].astype(F32) + got[i].astype(F32)
        if i < half:
            keep[i] = value
        else:
            send[i - half] = value.astype(BF16)


def fold(mine, got, name="fold"):
    shape = (mine.shape[0] // 2,) + mine.shape[1:]
    return run(
        fold_kernel,
        name,
        [(mine, "vmem"), (got, "vmem")],
        [(shape, F32), (shape, BF16)],
        limit=4,
    )


def fold_two_kernel(mine_a, got_a, mine_b, got_b, keep, send):
    n = mine_a.shape[2]
    half = keep.shape[0]
    for i in range(2 * half):
        for mine, got, lanes in ((mine_a, got_a, slice(0, n)), (mine_b, got_b, slice(n, keep.shape[2]))):
            value = mine[i].astype(F32) + got[i].astype(F32)
            if i < half:
                keep[i, :, lanes] = value
            else:
                send[i - half, :, lanes] = value.astype(BF16)


def fold_two(mine_a, got_a, mine_b, got_b, name="fold_two"):
    shape = (mine_a.shape[0] // 2, 96, mine_a.shape[2] + mine_b.shape[2])
    return run(
        fold_two_kernel,
        name,
        [(v, "vmem") for v in (mine_a, got_a, mine_b, got_b)],
        [(shape, F32), (shape, BF16)],
        limit=4,
    )


def settle_kernel(place, *refs):
    *sources, keep, send = refs
    core = place[2]
    column = 0
    for i in range(0, len(sources), 2):
        one, two = sources[i : i + 2]
        n = one.shape[2]
        lanes = slice(column, column + n)
        for j, whose in enumerate((core, 1 - core)):
            rows = pl.ds(pl.multiple_of(whose * 48, 16), 48)
            value = one[0, rows, :] + two[0, rows, :].astype(F32)
            keep[j, :, lanes] = value
            send[j, :, lanes] = value.astype(BF16)
        column += n


def settle(place, groups):
    sources = [array for group in groups for array in group]
    n = sum(group[0].shape[2] for group in groups)
    return run(
        settle_kernel,
        "settle",
        [(place, "smem")] + [(array, "vmem") for array in sources],
        [((2, 48, n), F32), ((2, 48, n), BF16)],
        limit=4,
    )


def join_kernel(keep, got, near, far):
    near[...] = keep[0] + got[0].astype(F32)
    far[...] = (keep[1] + got[1].astype(F32)).astype(BF16)


def join(keep, got):
    shape = keep.shape[1:]
    return run(join_kernel, "join", [(keep, "vmem"), (got, "vmem")], [(shape, F32), (shape, BF16)], limit=4)


def step_of(weight, momentum, average, grad, rate, decay):
    moved = grad + decay * weight if decay else grad
    new_momentum = momentum_rate * momentum + moved
    new = weight - rate * (moved + momentum_rate * new_momentum)
    return grad, new, new_momentum, average_rate * average + (1.0 - average_rate) * new


def update_rest_kernel(
    place, mats, momentum, average, *refs, rate, groups
):
    sources, outs, work, sems = refs[: 2 * groups], refs[2 * groups : 2 * groups + 4], refs[-5:-1], refs[-1]
    width = MODEL_WIDTH
    base = 3 * width
    copies = []
    for whose in range(2):
        core = place[2] if whose == 0 else 1 - place[2]
        for g in range(groups):
            source = sources[2 * g + whose]
            if g == 0:
                parts = ((8 * width + 2 * core * QUARTER, QUARTER), (8 * width + (2 * core + 1) * QUARTER, QUARTER))
            else:
                parts = (
                    (4 * width + 2 * core * QUARTER, QUARTER),
                    (4 * width + (2 * core + 1) * QUARTER, QUARTER),
                    (3 * width + core * HALF, HALF),
                )
            column = 0
            for first, n in parts:
                lanes = slice(column, column + n)
                grad = source[:, lanes].astype(F32)
                at = pl.ds(pl.multiple_of(first, 128), n)
                results = step_of(mats[:, at], momentum[:, at], average[:, at], grad, rate, decay_rate)
                to = pl.ds(pl.multiple_of(first - base, 128), n)
                for i, (ref, value) in enumerate(zip(work, results)):
                    ref[:, to] = value
                    copy = pltpu.make_async_copy(ref.at[:, to], outs[i].at[:, at], sems.at[len(copies)])
                    copy.start()
                    copies.append(copy)
                column += n
    for copy in copies:
        copy.wait()


def update_rest(place, mats, momentum, average, groups, rate):
    rows, columns = mats.shape
    sources = [array for group in groups for array in group]
    n = columns - 3 * MODEL_WIDTH
    return pl.pallas_call(
        functools.partial(update_rest_kernel, rate=rate, groups=len(groups)),
        in_specs=[pl.BlockSpec(memory_space=pltpu.SMEM)]
        + [pl.BlockSpec(memory_space=pltpu.VMEM)] * (3 + len(sources)),
        out_specs=[pl.BlockSpec(memory_space=pl.ANY)] * 4,
        out_shape=[jax.ShapeDtypeStruct((rows, columns), F32)] * 4,
        scratch_shapes=[pltpu.VMEM((rows, n), F32)] * 4 + [pltpu.SemaphoreType.DMA((40,))],
        compiler_params=pltpu.CompilerParams(vmem_limit_bytes=10 * 2**20),
        cost_estimate=declared("update_rest"),
        name="update_rest",
    )(place, mats, momentum, average, *sources)


def update_heads_kernel(
    place,
    mats,
    momentum,
    average,
    keep,
    from_seq,
    from_core,
    from_both,
    s_value,
    s_momentum,
    s_average,
    a0,
    a1,
    a2,
    a3,
    o0,
    o1,
    o2,
    o3,
    s0,
    s1,
    s2,
    s3,
    bias,
    w0,
    w1,
    w2,
    w3,
    grads,
    sems,
    *,
    rate,
):
    x, core = place[0], place[2]
    width = MODEL_WIDTH
    grads[x, core] = keep[0]
    grads[1 - x, core] = from_seq[...].astype(F32)
    grads[x, 1 - core] = from_core[...].astype(F32)
    grads[1 - x, 1 - core] = from_both[...].astype(F32)
    work = (w0, w1, w2, w3)
    last = ((0, 384), (0, 512), (1, 384))
    copies = []
    for j in range(3):
        for side in range(2):
            at = slice(j * width + side * HALF, j * width + (side + 1) * HALF)
            tiles = [grads[side, c, :, j * 128 : (j + 1) * 128] for c in range(2)]
            c, first = last[j]
            tiles.append(grads[side, c, :, first : first + 128])
            grad = jnp.concatenate(tiles, axis=1)
            results = step_of(mats[:, at], momentum[:, at], average[:, at], grad, rate, decay_rate)
            for out, ref, value in zip((o0, o1, o2, o3), work, results):
                ref[:, at] = value
                here = pl.ds(at.start, HALF)
                copy = pltpu.make_async_copy(ref.at[:, here], out.at[:, here], sems.at[len(copies)])
                copy.start()
                copies.append(copy)
    small = (grads[x, core, :, 640:] + grads[1 - x, core, :, 640:]).T[0:16]
    n = s_value.shape[0]
    results = step_of(s_value[...], s_momentum[...], s_average[...], small[0:n], rate, 0.0)
    for ref, value in zip((s0, s1, s2, s3), results):
        ref[...] = value
    bias[...] = small[2:3]
    for copy in copies:
        copy.wait()


def update_heads(place, mats, momentum, average, group, smalls, so_far, rate):
    rows, columns = mats.shape
    n = 3 * MODEL_WIDTH
    vmem = pl.BlockSpec(memory_space=pltpu.VMEM)
    anywhere = pl.BlockSpec(memory_space=pl.ANY)
    shape = smalls[0].shape
    return pl.pallas_call(
        functools.partial(update_heads_kernel, rate=rate),
        in_specs=[pl.BlockSpec(memory_space=pltpu.SMEM)] + [vmem] * 10 + [anywhere] * 4,
        out_specs=[anywhere] * 4 + [vmem] * 5,
        out_shape=[jax.ShapeDtypeStruct((rows, columns), F32)] * 4 + [jax.ShapeDtypeStruct(shape, F32)] * 4
        + [jax.ShapeDtypeStruct((1, rows), F32)],
        scratch_shapes=[pltpu.VMEM((rows, n), F32)] * 4
        + [pltpu.VMEM((2, 2, rows, 768), F32), pltpu.SemaphoreType.DMA((24,))],
        input_output_aliases={11 + i: i for i in range(4)},
        compiler_params=pltpu.CompilerParams(vmem_limit_bytes=6 * 2**20),
        cost_estimate=declared("update_heads"),
        name="update_heads",
    )(place, mats, momentum, average, *group, *smalls, *so_far)


SEQ_SWAP = [(0, 1), (1, 0)]
CORE_SWAP = [(i, i ^ 1) for i in range(16)]
Y_SWAP = [(i, i ^ 2) for i in range(16)]


def over_seq(value):
    return lax.ppermute(value, "seq", SEQ_SWAP)


def over_core(value):
    return lax.ppermute(value, "dp", CORE_SWAP)


def over_y(value):
    return lax.ppermute(value, "dp", Y_SWAP)


def over_z1(value):
    return lax.ppermute(value, "dp", [(i, i ^ 4) for i in range(16)])


def over_z2(value):
    return lax.ppermute(value, "dp", [(i, i ^ 8) for i in range(16)])


def over_both(value):
    return lax.ppermute(value, ("dp", "seq"), [(i, i ^ 3) for i in range(32)])


def pin(value, *after):
    return lax.optimization_barrier((value, after))[0]


def exchange(place, groups, *after):
    keep, send = settle(place, groups)
    near, far = join(keep, over_seq(pin(send, *after) if after else send))
    return near, over_core(far)


def tuned(
    inputs,
    modality,
    key_valid_mask,
    output_gradient,
    mats,
    mats_momentum,
    mats_average,
    smalls,
    smalls_momentum,
    smalls_average,
):
    width = MODEL_WIDTH
    rows = inputs.shape[1]
    dp = lax.axis_index("dp")
    x = lax.axis_index("seq")
    core = dp % 2
    y = (dp // 2) % 2
    place = jnp.stack([x, y, core, dp // 4]).astype(jnp.int32)

    att_own = pack_heads(place, mats, smalls.T)[None]
    att_got = over_z2(att_own)
    other_inputs = over_seq(inputs[0])
    keep, give = pack_rest(pin(place, att_own), mats)
    blocks = pair_up(place, keep, over_core(give))
    att_two = both(att_own, pin(att_got, blocks))
    att0 = both(att_two, over_z1(att_two))
    two0 = both(blocks[0], pin(over_z2(pin(blocks[0], att_two)), att0))
    att2 = pin(over_y(att0), other_inputs)
    att = (att0, over_core(att0), att2, over_core(att2))
    line0 = over_z1(two0)

    x_low, x_in, qkv, masked, params, w_qkv = project(
        pin(place, two0), inputs[0], other_inputs, modality, key_valid_mask, att
    )
    line0 = both(two0, pin(line0, qkv))
    up0 = (line0, over_y(line0), True)
    got1 = over_z2(pin(blocks[1], qkv))
    heads, log_sum = attend(qkv, pin(masked, line0))
    got1 = pin(got1, heads)
    got_heads = over_seq(pin(heads, got1)[rows:])
    two1 = both(blocks[1], got1)
    line1 = both(two1, over_z1(two1))
    x_got = over_core(x_low)
    two2 = both(blocks[2], pin(over_z2(pin(blocks[2], heads)), line1))
    got_heads, y_0 = pin((got_heads, up0[1]), two2)
    out_mine = last_columns(line0, y_0)
    out_w = (out_mine, over_core(out_mine))
    up1 = (line1, over_y(line1), True)
    line2 = both(two2, pin(over_z1(two2), got_heads))
    two3 = both(blocks[3], pin(over_z2(pin(blocks[3], line1)), got_heads))
    out_low, unit1, scale1, first_low, w_out = mix(
        pin(place, up1[1], line2, two3, x_got), heads, got_heads, x_in, params, out_w
    )
    down0 = (line2, over_y(line2), True)
    first_got = over_core(first_low)
    out_got = over_core(out_low)
    act0, slope0, w_up0 = raise_up(place, first_low, first_got, params, up0, 0)
    square3 = both(two3, pin(over_y(two3), act0))
    down1 = (square3, over_z1(square3), False)
    act1, slope1, w_up1 = raise_up(
        pin(place, square3, out_got), first_low, first_got, params, up1, 1
    )
    so_far, w_down0 = lower(pin(place, act1), act0, down0)
    sum_give, w_down1 = lower_other(place, act1, so_far, down1)
    block_out, grad_second, grad_ffo, sums2 = turn(
        place, act1, so_far, over_core(sum_give), unit1, params, output_gradient[0], w_down1
    )

    ffo_got = over_core(grad_ffo)
    mine_d, theirs_d = outer_wide(place, grad_ffo, ffo_got, act0, act1)
    got_d = over_y(theirs_d)
    grad_up0, sums_up0 = raise_back(pin(place, mine_d), grad_ffo, ffo_got, slope0, w_down0)
    grad_up1, sums_up1 = raise_back(pin(place, grad_up0), grad_ffo, ffo_got, slope1, w_down1)
    first_give = first_other(place, grad_up0, grad_up1, w_up0, w_up1)
    first_out = first_back(
        place,
        grad_up0,
        grad_up1,
        over_core(first_give[0:256]),
        over_core(first_give[256:]),
        grad_second,
        unit1,
        scale1,
        params,
        w_up0,
        w_up1,
        w_out,
    )
    grad_first_in, mixed_keep, mixed_give, heads_keep, heads_give, sums1 = first_out
    heads_got = over_seq(heads_give)
    mixed_got = over_core(mixed_give)
    mine_u0, theirs_u0 = outer(pin(place, sums1), first_low, first_got, [grad_up0], "outer_up")
    got_u0 = over_y(theirs_u0)
    mine_u1, theirs_u1 = outer(
        pin(place, mine_u0), first_low, first_got, [grad_up1], "outer_up", y_last=False
    )
    got_u1 = over_z1(theirs_u1)
    heads_got = pin(heads_got, mine_u1)
    fold_d = fold(mine_d, pin(got_d, heads_got))
    got_d = over_z1(fold_d[1])
    mine_o, theirs_o = outer(
        pin(place, fold_d), out_low, out_got, [mixed_keep, mixed_got], "outer_out"
    )
    got_o = over_y(theirs_o)

    def back(role, masked, parts=False):
        return attend_back(place, qkv, heads, heads_keep, heads_got, log_sum, masked, role, parts)

    (d_give,) = back(0, pin(masked, mine_o))
    got_u1 = pin(got_u1, d_give)
    d_give = pin(d_give, got_u1)
    fold_u1 = fold(mine_u1, got_u1)
    got_u1 = over_y(fold_u1[1])
    d_got = over_core(d_give)
    (d_keep,) = back(1, pin(masked, fold_u1))
    got_u0, got_d = pin((got_u0, got_d), d_keep)
    d_keep = pin(d_keep, got_u0, got_d)
    fold_u0 = fold(mine_u0, got_u0, "long_fold")
    last_d = fold(fold_d[0], got_d)
    got_u0, got_d = over_z1(fold_u0[1]), over_z2(last_d[1])
    mine_q, theirs_q = outer(
        pin(place, fold_u0, last_d), x_low, x_got, [d_keep, pin(d_got, fold_u0)], "outer_heads"
    )
    got_q = over_y(theirs_q)
    d_last, cols_keep, cols_give = back(2, pin(masked, mine_q), True)
    got_d, got_o = pin((got_d, got_o), d_last)
    down_keep, down_send = settle(place, [(last_d[0], got_d)])
    fold_o = fold(mine_o, got_o)
    got_o = over_z1(fold_o[1])
    down_got = over_seq(down_send)
    grad_x, give_x, small = enter(
        pin(place, down_keep, fold_o),
        d_give,
        d_keep,
        d_last,
        grad_first_in,
        modality,
        sums1,
        sums2,
        sums_up0,
        sums_up1,
        w_qkv,
    )
    got_u1, got_o, got_u0, got_q = pin((got_u1, got_o, got_u0, got_q), small)
    give_x, small, cols_give = pin((give_x, small, cols_give), got_u1, got_o, got_u0, got_q)
    x_back = over_seq(give_x)
    last_u = fold_two(fold_u0[0], got_u0, fold_u1[0], got_u1)
    last_o = fold(fold_o[0], got_o)
    got_u, got_last_o = over_z2(last_u[1]), over_z2(last_o[1])
    cols_got = over_core(cols_give)
    fold_q = fold(mine_q, got_q, "long_fold")
    mine_r, theirs_r = outer(
        pin(place, last_u, last_o, fold_q), x_low, x_got, [cols_keep, pin(cols_got, fold_q)], "outer_heads"
    )
    mine_s, theirs_s = narrow(pin(place, mine_r), small, over_core(small))
    last_q = fold(fold_q[0], pin(over_z1(fold_q[1]), mine_s))
    fold_r = fold_two(mine_r, over_y(theirs_r), mine_s, over_y(theirs_s))
    got_u, got_last_o = pin((got_u, got_last_o), fold_r)
    last_r = fold(fold_r[0], over_z1(fold_r[1]))
    down_near, down_far = join(down_keep, pin(down_got, last_r))
    down_group = (down_near, over_core(down_far))

    rate = base_rate / math.sqrt(rows * lax.axis_size("dp") * lax.axis_size("seq"))
    up_group = exchange(place, [(last_u[0], got_u), (last_o[0], got_last_o)])
    heads_keep, heads_send = settle(place, [(v[0], over_z2(v[1])) for v in (last_q, last_r)])
    near, far = heads_send[0], heads_send[1]
    heads_group = (heads_keep, over_seq(near), over_core(far), over_both(far))
    x_back, up_near = pin((x_back, up_group[0]), heads_keep)
    up_group = (up_near, up_group[1])
    input_grad = (grad_x + x_back.astype(F32)).astype(BF16)[None]
    so_far = update_rest(place, mats, mats_momentum, mats_average, [down_group, up_group], rate)
    *new, s_grad, s_value, s_momentum, s_average, s_bias = update_heads(
        place,
        mats,
        mats_momentum,
        mats_average,
        heads_group,
        (smalls.T, smalls_momentum.T, smalls_average.T),
        so_far,
        rate,
    )
    return (
        block_out[None],
        input_grad,
        *new,
        s_grad.T,
        s_bias.reshape(-1),
        s_value.T,
        s_momentum.T,
        s_average.T,
    )


def solution(mesh):
    placed = (
        P("dp", "seq", None),
        P("dp", None),
        P("dp", None),
        P("dp", "seq", None),
        P("dp", None),
        P("dp", None),
        P("dp", None),
        P("dp", None),
        P("dp", None),
        P("dp", None),
    )
    plan = tuned if tuple(mesh.shape.values()) == (16, 2) else per_device
    return jax.shard_map(
        plan,
        mesh=mesh,
        in_specs=placed,
        out_specs=(
            P("dp", "seq", None),
            P("dp", "seq", None),
            P("dp", None),
            P("dp", None),
            P("dp", None),
            P("dp", None),
            P("dp", None),
            P("dp"),
            P("dp", None),
            P("dp", None),
            P("dp", None),
        ),
        check_vma=False,
    )
```
